128 devices in a mesh: rep: 16 (over z_lo, x, core), grp: 8 (over z_hi, y).
Axes of the slice: x: 4, y: 4, z: 4 (z_hi: 2, z_lo: 2; z = z_hi * 2 + z_lo), core: 2. Of those that a mesh axis runs over, the one named last changes fastest.
Arguments:
- tokens: bfloat16 [32, 1024, 1024], P('rep', 'grp'), may hold values from -6 to 6
- segments: int32 [32, 1024], P('rep'), may hold values from 0 to 2, as said below
- routes: int32 [32, 1024, 2], P('rep', 'grp'), may hold values from 0 to 5, all different within a row
- cotangent: bfloat16 [32, 1024, 1024], P('rep', 'grp'), may hold values from -6 to 6
- w_qkv: float32 [1024, 2048], P('grp'), may hold values from -0.1875 to 0.1875
- w_out: float32 [1024, 1024], P('grp'), may hold values from -1.5 to 1.5
- w_gateup: float32 [6, 1024, 1024], P(None, 'grp'), may hold values from -0.1875 to 0.1875
- w_down: float32 [6, 512, 1024], P(None, None, 'grp'), may hold values from -0.5 to 0.5
- w_router: float32 [1024, 6], P('grp'), may hold values from -0.09375 to 0.09375
- w_gains: float32 [2, 1024], P(None, 'grp'), may hold values from 0.5 to 1.5
- qkv_first: float32 [1024, 2048], P('grp'), may hold values from -192 to 192
- qkv_second: float32 [1024, 2048], P('grp'), may hold values from 1966.08 to 15400.96
- out_first: float32 [1024, 1024], P('grp'), may hold values from -20 to 20
- out_second: float32 [1024, 1024], P('grp'), may hold values from 19.6608 to 154.0096
- gateup_first: float32 [6, 1024, 1024], P(None, 'grp'), may hold values from -48 to 48
- gateup_second: float32 [6, 1024, 1024], P(None, 'grp'), may hold values from 137.6256 to 1114.112
- down_first: float32 [6, 512, 1024], P(None, None, 'grp'), may hold values from -20 to 20
- down_second: float32 [6, 512, 1024], P(None, None, 'grp'), may hold values from 19.6608 to 154.0096
- router_first: float32 [1024, 6], P('grp'), may hold values from -1280 to 1280
- router_second: float32 [1024, 6], P('grp'), may hold values from 107374.18 to 872415.25
- gains_first: float32 [2, 1024], P(None, 'grp'), may hold values from -192 to 192
- gains_second: float32 [2, 1024], P(None, 'grp'), may hold values from 1966.08 to 15400.96
Outputs:
- layer_out: bfloat16 [32, 1024, 1024], P('rep', 'grp')
- input_grad: float32 [32, 1024, 1024], P('rep', 'grp')
- qkv_moment: float32 [1024, 2048], P('grp')
- qkv_square: float32 [1024, 2048], P('grp')
- qkv_updated: float32 [1024, 2048], P('grp')
- out_moment: float32 [1024, 1024], P('grp')
- out_square: float32 [1024, 1024], P('grp')
- out_updated: float32 [1024, 1024], P('grp')
- gateup_moment: float32 [6, 1024, 1024], P(None, 'grp')
- gateup_square: float32 [6, 1024, 1024], P(None, 'grp')
- gateup_updated: float32 [6, 1024, 1024], P(None, 'grp')
- down_moment: float32 [6, 512, 1024], P(None, None, 'grp')
- down_square: float32 [6, 512, 1024], P(None, None, 'grp')
- down_updated: float32 [6, 512, 1024], P(None, None, 'grp')
- router_moment: float32 [1024, 6], P('grp')
- router_square: float32 [1024, 6], P('grp')
- router_updated: float32 [1024, 6], P('grp')
- gains_moment: float32 [2, 1024], P(None, 'grp')
- gains_square: float32 [2, 1024], P(None, 'grp')
- gains_updated: float32 [2, 1024], P(None, 'grp')
The draws below stay inside these ranges and needn't reach their ends.
Inputs may be any that keep to these rules, and one draw needn't show every extreme that they name: `routes`: each token names 2 different experts. `segments`: a sequence's segment numbers start at 0 and never fall; of each 2 consecutive sequences one is a single document.
All inputs are finite; a program needn't handle non-finite values.
Results may differ from the reference program's by a relative error of at most 0.034.
Values may be sent and summed in bfloat16 or wider, within the bound.
A program may use at most 256 MiB of HBM per device.

```python
import math
import jax
import jax.numpy as jnp
from jax import lax

D = 1024
HQ = 16
HK = 8
HD = 64
FF = 512
EXPERTS = 6
TOPK = 2
SEQ_LEN = 1024
SEQS = 2
STEP = 10
BATCH = 32
TOKENS = 32768
QKV = 2048


def draw_segments(key, part):
    key = jax.random.fold_in(key, 7)
    key_first, key_second, key_whole = jax.random.split(key, 3)
    reach = SEQ_LEN // 8
    first_cut = SEQ_LEN // 3 + jax.random.randint(key_first, (BATCH, 1), -reach, reach)
    second_cut = 2 * SEQ_LEN // 3 + jax.random.randint(key_second, (BATCH, 1), -reach, reach)
    places = jnp.arange(SEQ_LEN)[None, :]
    segment_ids = (places >= first_cut).astype(jnp.int32) + (places >= second_cut).astype(jnp.int32)
    whole_pick = jax.random.randint(key_whole, (BATCH // SEQS, 1), 0, SEQS)
    row_number = jnp.arange(BATCH).reshape(BATCH // SEQS, SEQS) % SEQS
    single = (row_number == whole_pick).reshape(BATCH, 1)
    return jnp.where(single, 0, segment_ids).astype(jnp.int32)


def levels(rng, shape, pieces, smallest, top_value):
    level = 1.0
    for dim, blocks in pieces:
        draws = jax.random.uniform(jax.random.fold_in(jax.random.fold_in(rng, 6), dim), (blocks,), jnp.float32, smallest / len(pieces), top_value / len(pieces))
        level = level * jnp.repeat(jnp.exp(draws), shape[dim] // blocks).reshape((-1,) + (1,) * (len(shape) - 1 - dim))
    return level


def different_ones(stream_key, rows, amount, top, lift):
    ranking = jax.random.permutation(jax.random.fold_in(stream_key, 1), amount)
    boost = ranking
    for power in range(3):
        boost = boost * boost // amount
    boost = boost * lift // amount
    chance = jax.random.randint(jax.random.fold_in(stream_key, 2), (rows, amount), 0, 4096) + boost
    holders = jax.random.permutation(jax.random.fold_in(stream_key, 3), rows)[jnp.arange(amount) % rows]
    chance = jnp.where(jnp.arange(rows)[:, None] == holders[None, :], 1 << 14, chance)
    merit = chance * amount + jnp.arange(amount)
    return lax.top_k(merit.astype(jnp.int32), top)[1].astype(jnp.int32)


def scatter_about(key, extent, width, limit, cuts=(), kind=jnp.bfloat16):
    gain = levels(key, extent, cuts, -0.22, 0.18) if cuts else 1.0
    values = jax.random.normal(key, extent, jnp.float32) * width * gain
    return jnp.minimum(jnp.maximum(values, -limit), limit).astype(kind)


def setup_inputs(seed: int = 0) -> dict:
    splits = jax.random.split(jax.random.key(seed), 23)
    tokens = scatter_about(splits[0], (BATCH, SEQ_LEN, D), 1.0, 6.0, ((0, 16), (1, 8)))
    segments = draw_segments(jax.random.fold_in(splits[22], 71), 0)
    routes = different_ones(splits[2], BATCH * SEQ_LEN, EXPERTS, TOPK, 2730).reshape((BATCH, SEQ_LEN, TOPK))
    cotangent = scatter_about(splits[3], (BATCH, SEQ_LEN, D), 1.0, 6.0, ((0, 16), (1, 8)))
    w_qkv = scatter_about(splits[4], (D, QKV), D ** -0.5, 0.1875, ((0, 8),), jnp.float32)
    w_out = scatter_about(splits[5], (HQ * HD, D), (D // 64) ** -0.5, 1.5, ((0, 8),), jnp.float32)
    w_gateup = scatter_about(splits[6], (EXPERTS, D, 2 * FF), D ** -0.5, 0.1875, ((1, 8),), jnp.float32)
    w_down = scatter_about(splits[7], (EXPERTS, FF, D), (FF // 4) ** -0.5, 0.5, ((2, 8),), jnp.float32)
    w_router = scatter_about(splits[8], (D, EXPERTS), (4 * D) ** -0.5, 0.09375, ((0, 8),), jnp.float32)
    w_gains = jnp.clip(1.0 + 0.1 * jax.random.normal(splits[9], (2, D), jnp.float32), 0.5, 1.5)
    qkv_first = scatter_about(splits[10], (D, QKV), (0.17 * TOKENS ** 0.5), 192.0, ((0, 8),), jnp.float32)
    qkv_second = jnp.clip(jnp.exp(math.log(15400.96) - 2.0583882 * jax.random.uniform(splits[11], (D, QKV), jnp.float32) ** levels(splits[11], (D, QKV), ((0, 8),), -0.2, 0.2)), 1966.08, 15400.96)
    out_first = scatter_about(splits[12], (HQ * HD, D), (0.017 * TOKENS ** 0.5), 20.0, ((0, 8),), jnp.float32)
    out_second = jnp.clip(jnp.exp(math.log(154.0096) - 2.058388 * jax.random.uniform(splits[13], (HQ * HD, D), jnp.float32) ** levels(splits[13], (HQ * HD, D), ((0, 8),), -0.2, 0.2)), 19.6608, 154.0096)
    gateup_first = scatter_about(splits[14], (EXPERTS, D, 2 * FF), (0.044 * TOKENS ** 0.5), 48.0, ((1, 8),), jnp.float32)
    gateup_second = jnp.clip(jnp.exp(math.log(1114.112) - 2.0912761 * jax.random.uniform(splits[15], (EXPERTS, D, 2 * FF), jnp.float32) ** levels(splits[15], (EXPERTS, D, 2 * FF), ((1, 8),), -0.2, 0.2)), 137.6256, 1114.112)
    down_first = scatter_about(splits[16], (EXPERTS, FF, D), (0.017 * TOKENS ** 0.5), 20.0, ((2, 8),), jnp.float32)
    down_second = jnp.clip(jnp.exp(math.log(154.0096) - 2.058388 * jax.random.uniform(splits[17], (EXPERTS, FF, D), jnp.float32) ** levels(splits[17], (EXPERTS, FF, D), ((2, 8),), -0.2, 0.2)), 19.6608, 154.0096)
    router_first = scatter_about(splits[18], (D, EXPERTS), (0.04 * (D * TOKENS) ** 0.5), 1280.0, ((0, 8),), jnp.float32)
    router_second = jnp.clip(jnp.exp(math.log(872415.25) - 2.09494577 * jax.random.uniform(splits[19], (D, EXPERTS), jnp.float32) ** levels(splits[19], (D, EXPERTS), ((0, 8),), -0.2, 0.2)), 107374.18, 872415.25)
    gains_first = scatter_about(splits[20], (2, D), (0.17 * TOKENS ** 0.5), 192.0, ((1, 8),), jnp.float32)
    gains_second = jnp.clip(jnp.exp(math.log(15400.96) - 2.0583882 * jax.random.uniform(splits[21], (2, D), jnp.float32) ** levels(splits[21], (2, D), ((1, 8),), -0.2, 0.2)), 1966.08, 15400.96)
    return dict(tokens=tokens, segments=segments, routes=routes, cotangent=cotangent, w_qkv=w_qkv, w_out=w_out, w_gateup=w_gateup, w_down=w_down, w_router=w_router, w_gains=w_gains, qkv_first=qkv_first, qkv_second=qkv_second, out_first=out_first, out_second=out_second, gateup_first=gateup_first, gateup_second=gateup_second, down_first=down_first, down_second=down_second, router_first=router_first, router_second=router_second, gains_first=gains_first, gains_second=gains_second)


beta_one = 0.9
beta_two = 0.95
adam_epsilon = 1e-08
norm_epsilon = 1e-06
HIGHEST = lax.Precision.HIGHEST

@jax.custom_vjp
def low(v):
    return lax.optimization_barrier(v.astype(jnp.bfloat16)).astype(jnp.float32)

@jax.custom_vjp
def low_back(v):
    return v

def low_keep(v):
    return (low(v), None)

def low_pass(kept, grad):
    return (grad,)

def back_keep(v):
    return (v, None)

def back_low(kept, grad):
    return (low(grad),)
low.defvjp(low_keep, low_pass)
low_back.defvjp(back_keep, back_low)

def normed(values, gain_vec):
    return values * lax.rsqrt(lax.optimization_barrier(jnp.mean(values * values, axis=-1, keepdims=True)) + norm_epsilon) * gain_vec

def rotary_tables(positions, head_width):
    freqs = 10000.0 ** (-jnp.arange(head_width // 2).astype(jnp.float32) * 2.0 / head_width)
    angles = positions.astype(jnp.float32)[:, None] * freqs[None, :]
    return (jnp.cos(angles), jnp.sin(angles))

def rotate(tensor, cosine, sine_part):
    half_width = tensor.shape[-1] // 2
    front_half = tensor[..., :half_width]
    back_half = tensor[..., half_width:]
    return jnp.concatenate([front_half * cosine - back_half * sine_part, back_half * cosine + front_half * sine_part], axis=-1)

def attend(queries, keys_in, values_in, segment_ids):
    scores = jnp.einsum('qhgd,khd->hgqk', queries, keys_in, precision=HIGHEST)
    scores = low_back(scores) * HD ** (-0.5)
    places = jnp.arange(SEQ_LEN)
    allowed = (places[:, None] >= places[None, :]) & (segment_ids[:, None] == segment_ids[None, :])
    scores = jnp.where(allowed, scores, -1e+30)
    highest = lax.optimization_barrier(jnp.max(scores, axis=-1, keepdims=True))
    powers = jnp.exp(scores - highest)
    probs = low(powers / lax.optimization_barrier(jnp.sum(powers, axis=-1, keepdims=True)))
    return jnp.einsum('hgqk,khd->qhgd', probs, values_in, precision=HIGHEST)

def forward(inputs, w_qkv, w_out, w_gateup, w_down, w_router, w_gains, route_ids, segment_ids):
    w_qkv = low(w_qkv)
    w_out = low(w_out)
    w_gateup = low(w_gateup)
    w_down = low(w_down)
    w_router = low(w_router)
    w_gains = low(w_gains)
    act_one = low(normed(inputs, w_gains[0]))
    projected = low_back(jnp.dot(act_one, w_qkv, precision=HIGHEST))
    cosine, sine_part = rotary_tables(jnp.arange(SEQ_LEN), HD)
    cosine = cosine[:, None, :]
    sine_part = sine_part[:, None, :]
    query_width = HQ * HD
    key_width = HK * HD
    queries = projected[:, :query_width].reshape(SEQ_LEN, HQ, HD)
    keys_in = projected[:, query_width:query_width + key_width].reshape(SEQ_LEN, HK, HD)
    values_in = projected[:, query_width + key_width:].reshape(SEQ_LEN, HK, HD)
    queries = low(rotate(queries, cosine, sine_part)).reshape(SEQ_LEN, HK, HQ // HK, HD)
    keys_in = low(rotate(keys_in, cosine, sine_part))
    values_in = low(values_in)
    heads_out = jax.checkpoint(attend)(queries, keys_in, values_in, segment_ids).reshape(SEQ_LEN, query_width)
    heads_out = low(low_back(heads_out))
    hidden = inputs + low_back(jnp.dot(heads_out, w_out, precision=HIGHEST))
    act_two = low(normed(hidden, w_gains[1]))
    logits = low_back(jnp.dot(act_two, w_router, precision=HIGHEST))
    chosen = (route_ids[:, :, None] == jnp.arange(EXPERTS)[None, None, :]).astype(jnp.float32)
    picked = jnp.einsum('ske,se->sk', chosen, logits, precision=HIGHEST)
    highest = lax.optimization_barrier(jnp.max(picked, axis=-1, keepdims=True))
    powers = jnp.exp(picked - highest)
    gate_probs = powers / lax.optimization_barrier(jnp.sum(powers, axis=-1, keepdims=True))
    mixing = jnp.einsum('sk,ske->se', gate_probs, chosen, precision=HIGHEST)
    gate_up = low_back(jnp.einsum('sd,edf->sef', act_two, w_gateup, precision=HIGHEST))
    gate_part = gate_up[..., :FF]
    inner = low(gate_part * jax.nn.sigmoid(gate_part) * gate_up[..., FF:])
    expert_out = low_back(jnp.einsum('sef,efd->sed', inner, w_down, precision=HIGHEST))
    return hidden + jnp.einsum('se,sed->sd', mixing, expert_out, precision=HIGHEST)

def learning_rates():
    return (D ** (-0.5), 8.0 * D ** (-0.5), D ** (-0.5), 2.0 * FF ** (-0.5), 0.5 * D ** (-0.5), 0.5)

def adamw(weight, gradient, moment, square, step_rate, decay_rate):
    moment_new = beta_one * moment + (1.0 - beta_one) * gradient
    square_new = beta_two * square + (1.0 - beta_two) * gradient * gradient
    corrected = moment_new / (1.0 - beta_one ** STEP)
    spread = jnp.sqrt(square_new / (1.0 - beta_two ** STEP)) + adam_epsilon
    updated = weight - step_rate * (corrected / spread + decay_rate * weight)
    return (moment_new, square_new, updated)

def reference(tokens, segments, routes, cotangent, w_qkv, w_out, w_gateup, w_down, w_router, w_gains, qkv_first, qkv_second, out_first, out_second, gateup_first, gateup_second, down_first, down_second, router_first, router_second, gains_first, gains_second):
    masters = (w_qkv, w_out, w_gateup, w_down, w_router, w_gains)

    def one_sequence(totals, item):
        token_rows, segment_ids, route_ids, back_rows = item

        def wrapped(inputs, *params):
            return forward(inputs, *params, route_ids, segment_ids)
        result, pull = jax.vjp(wrapped, token_rows.astype(jnp.float32), *masters)
        gradients = pull(back_rows.astype(jnp.float32))
        totals = tuple((total_grad + new_grad for total_grad, new_grad in zip(totals, gradients[1:])))
        return (totals, (result.astype(jnp.bfloat16), gradients[0]))
    start = tuple((jnp.zeros_like(master) for master in masters))
    totals, (outputs, input_grad) = lax.scan(one_sequence, start, (tokens, segments, routes, cotangent))
    first_moments = (qkv_first, out_first, gateup_first, down_first, router_first, gains_first)
    second_moments = (qkv_second, out_second, gateup_second, down_second, router_second, gains_second)
    step_rates = learning_rates()
    decay_rates = (0.1, 0.1, 0.1, 0.1, 0.1, 0.0)
    results = []
    for slot_index in range(6):
        results.extend(adamw(masters[slot_index], totals[slot_index], first_moments[slot_index], second_moments[slot_index], step_rates[slot_index], decay_rates[slot_index]))
    return (outputs, input_grad, results[0], results[1], results[2], results[3], results[4], results[5], results[6], results[7], results[8], results[9], results[10], results[11], results[12], results[13], results[14], results[15], results[16], results[17])
```

```python
import functools

import jax
import jax.numpy as jnp
from jax import lax
from jax.experimental import pallas as pl
from jax.experimental.pallas import tpu as pltpu
from jax.sharding import PartitionSpec as P

D = 1024
HQ = 16
HK = 8
HD = 64
FF = 512
EXPERTS = 6
TOPK = 2
STEP = 10
ROWS = 256
SLICE = 64
WIDE = EXPERTS * SLICE

beta_one = 0.9
beta_two = 0.95
adam_epsilon = 1e-08
norm_epsilon = 1e-06

f32 = jnp.float32
b16 = jnp.bfloat16
MESH = pl.DeviceIdType.MESH
ANY = pl.BlockSpec(memory_space=pl.ANY)
VMEM = pl.BlockSpec(memory_space=pltpu.VMEM)
MIB = 2**20


def place():
    rep = lax.axis_index("rep")
    grp = lax.axis_index("grp")
    z_lo, x, c = rep // 8, lax.rem(rep // 2, 4), lax.rem(rep, 2)
    z_hi, y = grp // 4, lax.rem(grp, 4)
    return x, y, z_hi * 2 + z_lo, c


def dev(x, y, z, c):
    x, y, z = lax.rem(x + 4, 4), lax.rem(y + 4, 4), lax.rem(z + 4, 4)
    return (lax.rem(z, 2) * 8 + x * 2 + c, (z // 2) * 4 + y)


class Net:
    def __init__(self, send_sems, recv_sems, local_sems):
        self.sems = (send_sems, recv_sems, local_sems)
        self.count = 0
        self.locals = 0
        self.open = []

    def greet(self, peers):
        bar = pltpu.get_barrier_semaphore()
        for peer in peers:
            pl.semaphore_signal(bar, inc=1, device_id=peer, device_id_type=MESH)
        pl.semaphore_wait(bar, len(peers))

    def send(self, src, dst, peer):
        copy = pltpu.make_async_remote_copy(
            src_ref=src,
            dst_ref=dst,
            send_sem=self.sems[0].at[self.count],
            recv_sem=self.sems[1].at[self.count],
            device_id=peer,
            device_id_type=MESH,
        )
        copy.start()
        self.count += 1
        self.open.append(copy)
        return copy

    def local(self, src, dst):
        copy = pltpu.make_async_copy(src, dst, self.sems[2].at[self.locals])
        copy.start()
        self.locals += 1
        return copy

    def got(self, copy):
        copy.wait_recv()
        copy.seen = True

    def finish(self):
        for copy in self.open:
            if not getattr(copy, "seen", False):
                copy.wait_recv()
            copy.wait_send()


def sems(n, n_local=1):
    return [
        pltpu.SemaphoreType.DMA((n,)),
        pltpu.SemaphoreType.DMA((n,)),
        pltpu.SemaphoreType.DMA((n_local,)),
    ]


def params(cid=None, mib=56):
    if cid is None:
        return pltpu.CompilerParams(vmem_limit_bytes=mib * MIB)
    return pltpu.CompilerParams(
        vmem_limit_bytes=mib * MIB, collective_id=cid, has_side_effects=True
    )


def shape(dims, dtype):
    return jax.ShapeDtypeStruct(dims, dtype)


def ring_gather(net, part, right, left, me, src=None):
    src = src or (lambda half: part(me, half))
    a1 = net.send(src(0), part(me, 0), right)
    b1 = net.send(src(1), part(me, 1), left)
    a2 = net.send(src(1), part(me, 1), right)
    b2 = net.send(src(0), part(me, 0), left)
    before, after = lax.rem(me + 3, 4), lax.rem(me + 1, 4)
    net.got(a1)
    a3 = net.send(part(before, 0), part(before, 0), right)
    net.got(b1)
    b3 = net.send(part(after, 1), part(after, 1), left)
    for copy in (a2, b2, a3, b3):
        net.got(copy)


def add_into(dst, one, two, rows, step):
    def body(i, carry):
        at = pl.ds(pl.multiple_of(i * step, step), step)
        dst[at] = (one[at].astype(f32) + two[at].astype(f32)).astype(b16)
        return carry

    lax.fori_loop(0, rows // step, body, 0)


def ring_scatter(net, part, tmp, got, right, left, me, rows, step):
    half = rows // 2
    lo, hi = pl.ds(0, half), pl.ds(half, half)
    after, before, across = lax.rem(me + 1, 4), lax.rem(me + 3, 4), lax.rem(me + 2, 4)
    s1 = net.send(part(across).at[lo], tmp.at[0], right)
    s2 = net.send(part(across).at[hi], tmp.at[1], left)
    s3 = net.send(part(after).at[hi], got.at[0, hi], right)
    s4 = net.send(part(before).at[lo], got.at[1, lo], left)
    net.got(s1)
    add_into(tmp.at[0], tmp.at[0], part(after).at[lo], half, step)
    s5 = net.send(tmp.at[0], got.at[0, lo], right)
    net.got(s2)
    add_into(tmp.at[1], tmp.at[1], part(before).at[hi], half, step)
    s6 = net.send(tmp.at[1], got.at[1, hi], left)
    for copy in (s3, s4, s5, s6):
        net.got(copy)


def dot(a, b):
    return lax.dot_general(a, b, (((1,), (0,)), ((), ())), preferred_element_type=f32)


def dot_t(a, b):
    return lax.dot_general(a, b, (((1,), (1,)), ((), ())), preferred_element_type=f32)


def t_dot(a, b):
    return lax.dot_general(a, b, (((0,), (0,)), ((), ())), preferred_element_type=f32)


def gather_kernel(xl, gl, rl, wq, wo, gu, dn, X, R, G, WQ, WO, GU, DN, ss, rs, ls):
    x, y, z, c = place()
    z_hi = z // 2
    shard = z_hi * 4 + y
    slot = x * 2 + c
    net = Net(ss, rs, ls)
    partner = dev(x, y, z + 2, c)
    twin = dev(x, y, z, 1 - c)
    right, left = dev(x + 1, y, z, c), dev(x - 1, y, z, c)
    offsets = [(0, 1), (0, 3), (1, 0), (0, 2), (1, 1), (1, 3), (1, 2)]
    peers = [dev(x, y + dy, (3 - z) if dz else z, c) for dz, dy in offsets]
    net.greet(peers + [partner, twin, right, left])
    rows_of = lambda n: pl.ds(pl.multiple_of(n * 128, 128), 128)
    mine = rows_of(z_hi)
    swaps = [
        net.send(gl.at[1 - z_hi], G.at[slot, mine], partner),
        net.send(xl.at[1 - z_hi], X.at[mine], partner),
        net.send(rl.at[1 - z_hi], R.at[mine], partner),
    ]
    locs = [net.local(gl.at[z_hi], G.at[slot, mine])]
    at = rows_of(shard)
    wq_in = [net.send(wq, WQ.at[c, at], p) for p in peers]
    wo_in = [net.send(wo, WO.at[c, at], p) for p in peers]
    rest = [net.send(gu, GU.at[at], p) for p in peers]
    rest += [net.send(dn, DN.at[:, at], p) for p in peers]
    locs += [
        net.local(xl.at[z_hi], X.at[mine]),
        net.local(rl.at[z_hi], R.at[mine]),
        net.local(wq, WQ.at[c, at]),
        net.local(wo, WO.at[c, at]),
        net.local(gu, GU.at[at]),
        net.local(dn, DN.at[:, at]),
    ]
    net.send(wq, WQ.at[c, at], twin)
    net.send(wo, WO.at[c, at], twin)
    net.got(swaps[0])
    locs[0].wait()
    gpart = lambda n, h: G.at[n * 2 + c, pl.ds(h * 128, 128)]
    ring_gather(net, gpart, right, left, x)
    for n in range(4):
        net.send(G.at[n * 2 + c], G.at[n * 2 + c], twin)
    sources = [
        rows_of((lax.rem(1 - z_hi if dz else z_hi, 2)) * 4 + lax.rem(y + 4 - dy, 4))
        for dz, dy in offsets
    ]
    for copies, whole in ((wq_in, WQ), (wo_in, WO)):
        for copy, src in zip(copies, sources):
            net.got(copy)
            net.send(whole.at[c, src], whole.at[c, src], twin)
    for copy in locs[1:]:
        copy.wait()
    net.finish()


def gather(xl, gl, rl, wq, wo, gu, dn):
    return pl.pallas_call(
        gather_kernel,
        out_shape=(
            shape((ROWS, D), b16),
            shape((ROWS, 128), f32),
            shape((8, ROWS, D), b16),
            shape((2, D, 1024), b16),
            shape((2, D, 512), b16),
            shape((D, 2 * WIDE), b16),
            shape((WIDE + 16, D), b16),
        ),
        in_specs=[ANY] * 7,
        out_specs=(ANY,) * 7,
        scratch_shapes=sems(64, 8),
        compiler_params=params(0),
        name="gather",
    )(xl, gl, rl, wq, wo, gu, dn)


def partner_lanes(v):
    lane = lax.broadcasted_iota(jnp.int32, v.shape, 1)
    return jnp.where(lane % HD < HD // 2, pltpu.roll(v, 96, 1), pltpu.roll(v, 32, 1))


def project_kernel(x, wq, gains, cos, sin, act, q, kv):
    v = x[...].astype(f32)
    gain = gains[6:7, :].astype(f32)
    r = lax.rsqrt(jnp.mean(v * v, axis=-1, keepdims=True) + norm_epsilon)
    a = (v * r * gain).astype(b16)
    act[...] = a
    cosine, sine = cos[...], sin[...]
    for half in range(2):
        for t in range(4):
            out = dot(a, wq[half, :, 256 * t : 256 * (t + 1)])
            for u in range(2):
                tile = out[:, 128 * u : 128 * (u + 1)]
                at = slice(256 * t + 128 * u, 256 * t + 128 * (u + 1))
                if half == 0 or t < 2:
                    tile = tile * cosine + partner_lanes(tile) * sine
                if half == 0:
                    q[:, at] = (tile * 0.125).astype(b16)
                else:
                    kv[:, at] = tile.astype(b16)


def project(x, wq, dn, cos, sin):
    return pl.pallas_call(
        project_kernel,
        grid=(1,),
        out_shape=(shape((ROWS, D), b16),) * 3,
        in_specs=[
            pl.BlockSpec((ROWS, D), lambda i: (0, 0)),
            pl.BlockSpec((2, D, 1024), lambda i: (0, 0, 0)),
            pl.BlockSpec((16, D), lambda i: (WIDE // 16, 0)),
            pl.BlockSpec((ROWS, 128), lambda i: (0, 0)),
            pl.BlockSpec((ROWS, 128), lambda i: (0, 0)),
        ],
        out_specs=(pl.BlockSpec((ROWS, D), lambda i: (0, 0)),) * 3,
        compiler_params=params(),
        name="project",
    )(x, wq, dn, cos, sin)


def keys_kernel(kv, KV, ss, rs, ls):
    x, y, z, c = place()
    net = Net(ss, rs, ls)
    right, left = dev(x, y + 1, z, c), dev(x, y - 1, z, c)
    net.greet([right, left])
    own = net.local(kv, KV.at[y])
    part = lambda n, h: KV.at[n, pl.ds(h * 128, 128)]
    ring_gather(net, part, right, left, y, src=lambda h: kv.at[pl.ds(h * 128, 128)])
    own.wait()
    net.finish()


def gather_keys(kv):
    return pl.pallas_call(
        keys_kernel,
        out_shape=shape((4, ROWS, D), b16),
        in_specs=[ANY],
        out_specs=ANY,
        scratch_shapes=sems(8),
        compiler_params=params(1),
        name="gather_keys",
    )(kv)


def half_mask(rows, half):
    lane = lax.broadcasted_iota(jnp.int32, (rows, 128), 1)
    return (lane < HD) if half == 0 else (lane >= HD)


def spread(tile, half):
    keep = half_mask(ROWS, half)
    heads = []
    for g in range(2):
        v = tile if g == half else pltpu.roll(tile, HD, 1)
        heads.append(jnp.where(keep, v, 0.0).astype(b16))
    low = jnp.concatenate([h[:128] for h in heads], axis=0)
    high = jnp.concatenate([h[128:] for h in heads], axis=0)
    return low, high


def collect(low, high, half):
    heads = []
    for g in range(2):
        v = jnp.concatenate([low[g * 128 : g * 128 + 128], high[g * 128 : g * 128 + 128]], axis=0)
        heads.append(v if g == half else pltpu.roll(v, HD, 1))
    return jnp.where(half_mask(ROWS, 0), heads[0], heads[1])


def attend_kernel(q, k, v, posq, segq, segk, o, p, bias):
    @pl.when(pl.program_id(0) == 0)
    def _():
        place_k = lax.broadcasted_iota(jnp.int32, (128, D), 1)
        for h in range(2):
            at = slice(128 * h, 128 * h + 128)
            fine = (posq[at, :] >= place_k) & (segq[at, :] == segk[...])
            bias[at, :] = jnp.where(fine, 0.0, -1e30)

    keys = [k[:, :128].reshape(512, 128), k[:, 128:].reshape(512, 128)]
    vals = [v[:, :128].reshape(512, 128), v[:, 128:].reshape(512, 128)]
    keys_all = jnp.concatenate(keys, axis=0)
    vals_all = jnp.concatenate(vals, axis=0)
    low_bias = jnp.concatenate([bias[:128, :512]] * 2, axis=0)
    high_bias = jnp.concatenate([bias[128:, :]] * 2, axis=0)
    for half in range(2):
        tile = q[:, 128 * half : 128 * half + 128].astype(f32)
        low, high = spread(tile, half)
        outs = []
        for rows, kk, vv, bb, lo in (
            (low, keys[0], vals[0], low_bias, True),
            (high, keys_all, vals_all, high_bias, False),
        ):
            s = dot_t(rows, kk) + bb
            top = jnp.max(s, axis=-1, keepdims=True)
            e = jnp.exp(s - top)
            probs = (e * (1.0 / jnp.sum(e, axis=-1, keepdims=True))).astype(b16)
            if lo:
                p[half, :, :512] = probs
            else:
                p[half, :, 512:] = probs
            outs.append(dot(probs, vv))
        o[:, 128 * half : 128 * half + 128] = collect(outs[0], outs[1], half).astype(b16)


def attend(q, KV, posq, segq, segk):
    return pl.pallas_call(
        attend_kernel,
        grid=(4,),
        out_shape=(shape((ROWS, D), b16), shape((8, ROWS, 1536), b16)),
        in_specs=[
            pl.BlockSpec((ROWS, 256), lambda i: (0, i)),
            pl.BlockSpec((4, ROWS, 128), lambda i: (0, 0, i)),
            pl.BlockSpec((4, ROWS, 128), lambda i: (0, 0, 4 + i)),
            pl.BlockSpec((ROWS, 1), lambda i: (0, 0)),
            pl.BlockSpec((ROWS, 1), lambda i: (0, 0)),
            pl.BlockSpec((1, D), lambda i: (0, 0)),
        ],
        out_specs=(
            pl.BlockSpec((ROWS, 256), lambda i: (0, i)),
            pl.BlockSpec((2, ROWS, 1536), lambda i: (i, 0, 0)),
        ),
        scratch_shapes=[pltpu.VMEM((ROWS, D), f32)],
        compiler_params=params(),
        name="attend",
    )(q, KV, KV, posq, segq, segk)


def router_rows(tail):
    row = lax.broadcasted_iota(jnp.int32, (16, D), 0)
    kept = jnp.where(row < EXPERTS, tail.astype(f32), 0.0).astype(b16)
    return jnp.concatenate([kept, jnp.zeros((112, D), b16)], axis=0)


def one_hot(routes, slot):
    lane = lax.broadcasted_iota(jnp.int32, (ROWS, 128), 1).astype(f32)
    return (routes[:, slot : slot + 1] == lane).astype(f32)


def after_kernel(x, o, wo, tail, routes, hidden, act):
    heads = o[...]
    for half in range(2):
        for t in range(2):
            cols = slice(512 * half + 256 * t, 512 * half + 256 * (t + 1))
            hidden[:, cols] = x[:, cols].astype(f32) + dot(heads, wo[half, :, 256 * t : 256 * (t + 1)])
    h = hidden[...]
    r = lax.rsqrt(jnp.mean(h * h, axis=-1, keepdims=True) + norm_epsilon)
    a = (h * r * tail[7:8, :].astype(f32)).astype(b16)
    act[:, :D] = a
    logits = dot_t(a, router_rows(tail[...]))
    hots = [one_hot(routes, k) for k in range(TOPK)]
    picked = [jnp.sum(hot * logits, axis=-1, keepdims=True) for hot in hots]
    top = jnp.maximum(picked[0], picked[1])
    powers = [jnp.exp(v - top) for v in picked]
    total = powers[0] + powers[1]
    mixing = hots[0] * (powers[0] / total) + hots[1] * (powers[1] / total)
    big = mixing.astype(b16).astype(f32)
    act[:, D:] = (big + pltpu.roll(mixing - big, 16, 1)).astype(b16)


def after(x, o, wo, dn, routes):
    return pl.pallas_call(
        after_kernel,
        grid=(1,),
        out_shape=(shape((ROWS, D), f32), shape((ROWS, D + 128), b16)),
        in_specs=[
            pl.BlockSpec((ROWS, D), lambda i: (0, 0)),
            pl.BlockSpec((ROWS, D), lambda i: (0, 0)),
            pl.BlockSpec((2, D, 512), lambda i: (0, 0, 0)),
            pl.BlockSpec((16, D), lambda i: (WIDE // 16, 0)),
            pl.BlockSpec((ROWS, 128), lambda i: (0, 0)),
        ],
        out_specs=(
            pl.BlockSpec((ROWS, D), lambda i: (0, 0)),
            pl.BlockSpec((ROWS, D + 128), lambda i: (0, 0)),
        ),
        compiler_params=params(),
        name="after_attention",
    )(x, o, wo, dn, routes)


def tokens_kernel(act, ACT, ss, rs, ls):
    x, y, z, c = place()
    net = Net(ss, rs, ls)
    right, left, twin = dev(x + 1, y, z, c), dev(x - 1, y, z, c), dev(x, y, z, 1 - c)
    net.greet([right, left, twin])
    own = net.local(act, ACT.at[x * 2 + c])
    net.send(act, ACT.at[x * 2 + c], twin)
    part = lambda n, h: ACT.at[n * 2 + c, pl.ds(h * 128, 128)]
    ring_gather(net, part, right, left, x, src=lambda h: act.at[pl.ds(h * 128, 128)])
    for d in range(1, 4):
        block = ACT.at[lax.rem(x + d, 4) * 2 + c]
        net.send(block, block, twin)
    own.wait()
    net.finish()


def gather_tokens(act):
    return pl.pallas_call(
        tokens_kernel,
        out_shape=shape((8, ROWS, D + 128), b16),
        in_specs=[ANY],
        out_specs=ANY,
        scratch_shapes=sems(16),
        compiler_params=params(2),
        name="gather_tokens",
    )(act)


def experts_kernel(act, g, gu, dn, part, grads, gu_acc, dn_acc):
    step = pl.program_id(0)
    row = lax.broadcasted_iota(jnp.int32, (128, WIDE), 0)
    lane = lax.broadcasted_iota(jnp.int32, (128, WIDE), 1)
    pick = ((row % 16 == lane // SLICE) & (row < 32)).astype(b16)
    a = act[0, :, :D]
    mix = dot(act[0, :, D:], pick)
    gt = g[0]
    down = dn[:WIDE, :]
    h = dot(a, gu[...])
    gate, up = h[:, :WIDE], h[:, WIDE:]
    gw = dot_t(gt, down)
    s = 1.0 / (1.0 + jnp.exp(-gate))
    silu = gate * s
    inner = silu * up
    scaled = (inner * mix).astype(b16)
    part[0, :, :D] = dot(scaled, down).astype(b16)
    part[0, :, 2 * D :] = dot_t((inner * gw).astype(b16), pick).astype(b16)
    gi = gw * mix
    ggu = jnp.concatenate(
        [(gi * up * s * (1.0 + gate * (1.0 - s))).astype(b16), (gi * silu).astype(b16)], axis=1
    )
    part[0, :, D : 2 * D] = dot_t(ggu, gu[...]).astype(b16)

    @pl.when(step == 0)
    def _():
        gu_acc[...] = jnp.zeros_like(gu_acc)
        dn_acc[...] = jnp.zeros_like(dn_acc)

    gu_acc[...] += t_dot(a, ggu)
    dn_acc[...] += t_dot(scaled, gt)

    @pl.when(step == 7)
    def _():
        for n in range(8):
            at = slice(128 * n, 128 * n + 128)
            for b in range(6):
                grads[n, b] = gu_acc[at, 128 * b : 128 * b + 128].astype(b16)
            for b in range(3):
                grads[n, 6 + b] = dn_acc[128 * b : 128 * b + 128, at].astype(b16)


def experts(ACT, G, GU, DN):
    return pl.pallas_call(
        experts_kernel,
        grid=(8,),
        out_shape=(shape((8, ROWS, 2 * D + 128), b16), shape((8, 9, 128, 128), b16)),
        in_specs=[
            pl.BlockSpec((1, ROWS, D + 128), lambda i: (i, 0, 0)),
            pl.BlockSpec((1, ROWS, D), lambda i: (i, 0, 0)),
            pl.BlockSpec((D, 2 * WIDE), lambda i: (0, 0)),
            pl.BlockSpec((WIDE + 16, D), lambda i: (0, 0)),
        ],
        out_specs=(
            pl.BlockSpec((1, ROWS, 2 * D + 128), lambda i: (i, 0, 0)),
            pl.BlockSpec((8, 9, 128, 128), lambda i: (0, 0, 0, 0)),
        ),
        scratch_shapes=[pltpu.VMEM((D, 2 * WIDE), f32), pltpu.VMEM((WIDE, D), f32)],
        compiler_params=params(),
        name="experts",
    )(ACT, G, GU, DN)


def home_kernel(part, total, twin_got, tmp, got, ss, rs, ls):
    x, y, z, c = place()
    net = Net(ss, rs, ls)
    right, left, twin = dev(x + 1, y, z, c), dev(x - 1, y, z, c), dev(x, y, z, 1 - c)
    net.greet([right, left, twin])
    order = [lax.rem(x + d, 4) for d in (2, 1, 3, 0)]
    sent = [net.send(part.at[n * 2 + 1 - c], twin_got.at[n], twin) for n in order]
    for n, copy in zip(order, sent):
        net.got(copy)
        add_into(twin_got.at[n], twin_got.at[n], part.at[n * 2 + c], ROWS, 16)
    ring_scatter(net, lambda n: twin_got.at[n], tmp, got, right, left, x, ROWS, 16)

    def body(i, carry):
        at = pl.ds(pl.multiple_of(i * 16, 16), 16)
        total[at] = twin_got[x, at].astype(f32) + got[0, at].astype(f32) + got[1, at].astype(f32)
        return carry

    lax.fori_loop(0, ROWS // 16, body, 0)
    net.finish()


def send_home(part):
    wide = 2 * D + 128
    return pl.pallas_call(
        home_kernel,
        out_shape=shape((ROWS, wide), f32),
        in_specs=[VMEM],
        out_specs=VMEM,
        scratch_shapes=[
            pltpu.VMEM((4, ROWS, wide), b16),
            pltpu.VMEM((2, ROWS // 2, wide), b16),
            pltpu.VMEM((2, ROWS, wide), b16),
        ]
        + sems(16),
        compiler_params=params(3),
        name="send_home",
    )(part)


def middle_kernel(total, hidden, act, g, tail, routes, heads, wo, out, gh_ref, ghi, og, small):
    h = hidden[...]
    out[...] = (h + total[:, :D]).astype(b16)
    a = act[:, :D]
    mix = act[:, D:].astype(f32)
    lane = lax.broadcasted_iota(jnp.int32, (ROWS, 128), 1)
    mixing = jnp.where(lane < 16, mix + pltpu.roll(mix, 112, 1), 0.0)
    dg = total[:, 2 * D :]
    hots = [one_hot(routes, k) for k in range(TOPK)]
    probs = [jnp.sum(hot * mixing, axis=-1, keepdims=True) for hot in hots]
    dgs = [jnp.sum(hot * dg, axis=-1, keepdims=True) for hot in hots]
    mean = probs[0] * dgs[0] + probs[1] * dgs[1]
    grad_logits = sum(hot * (p * (d - mean)) for hot, p, d in zip(hots, probs, dgs)).astype(b16)
    ga = total[:, D : 2 * D] + dot(grad_logits, router_rows(tail[...]))
    small[0:6, :] = t_dot(grad_logits, a)[0:6, :]
    r = lax.rsqrt(jnp.mean(h * h, axis=-1, keepdims=True) + norm_epsilon)
    u = ga * tail[7:8, :].astype(f32)
    small[6:7, :] = jnp.sum(ga * h * r, axis=0, keepdims=True)
    small[7:8, :] = jnp.zeros((1, D), f32)
    gh = g[0].astype(f32) + r * (u - h * (r * r * jnp.mean(u * h, axis=-1, keepdims=True)))
    gh_ref[...] = gh
    low = gh.astype(b16)
    ghi[...] = (dot_t(low[:, :512], wo[0]) + dot_t(low[:, 512:], wo[1])).astype(b16)
    o = heads[...]
    for k in range(8):
        piece = t_dot(o, low[:, 128 * k : 128 * k + 128]).astype(b16)
        for n in range(8):
            og[k, n, 0] = piece[128 * n : 128 * n + 128]


def middle(slot, total, hidden, act, G, dn, routes, heads, wo):
    whole = lambda *dims: pl.BlockSpec(dims, lambda i, s: (0,) * len(dims))
    return pl.pallas_call(
        middle_kernel_with_slot,
        grid_spec=pltpu.PrefetchScalarGridSpec(
            num_scalar_prefetch=1,
            grid=(1,),
            in_specs=[
                whole(ROWS, 2 * D + 128),
                whole(ROWS, D),
                whole(ROWS, D + 128),
                pl.BlockSpec((1, ROWS, D), lambda i, s: (s[0], 0, 0)),
                pl.BlockSpec((16, D), lambda i, s: (WIDE // 16, 0)),
                whole(ROWS, 128),
                whole(ROWS, D),
                whole(2, D, 512),
            ],
            out_specs=(
                whole(ROWS, D),
                whole(ROWS, D),
                whole(ROWS, D),
                whole(8, 8, 1, 128, 128),
                whole(8, D),
            ),
        ),
        out_shape=(
            shape((ROWS, D), b16),
            shape((ROWS, D), f32),
            shape((ROWS, D), b16),
            shape((8, 8, 1, 128, 128), b16),
            shape((8, D), f32),
        ),
        compiler_params=params(),
        name="middle",
    )(slot, total, hidden, act, G, dn, routes, heads, wo)


def middle_kernel_with_slot(slot, *refs):
    middle_kernel(*refs)


def attend_back_kernel(q, k, v, p, do, dq, dk, dv):
    keys = [k[:, :128].reshape(512, 128), k[:, 128:].reshape(512, 128)]
    vals = [v[:, :128].reshape(512, 128), v[:, 128:].reshape(512, 128)]
    keys_all = jnp.concatenate(keys, axis=0)
    vals_all = jnp.concatenate(vals, axis=0)
    dk_sum = dv_sum = None
    for half in range(2):
        at = slice(128 * half, 128 * half + 128)
        q_low, q_high = spread(q[:, at].astype(f32), half)
        do_low, do_high = spread(do[:, at].astype(f32), half)
        outs, dks, dvs = [], [], []
        for qq, dd, kk, vv, cols in (
            (q_low, do_low, keys[0], vals[0], slice(0, 512)),
            (q_high, do_high, keys_all, vals_all, slice(512, 1536)),
        ):
            probs = p[half, :, cols]
            dp = dot_t(dd, vv)
            pf = probs.astype(f32)
            prod = pf * dp
            ds = (prod - pf * jnp.sum(prod, axis=-1, keepdims=True)).astype(b16)
            outs.append(dot(ds, kk) * 0.125)
            dks.append(t_dot(ds, qq))
            dvs.append(t_dot(probs, dd))
        dq[:, at] = collect(outs[0], outs[1], half)
        if half == 0:
            dk_sum, dv_sum = dks, dvs
        else:
            dk_sum = [a + b for a, b in zip(dk_sum, dks)]
            dv_sum = [a + b for a, b in zip(dv_sum, dvs)]
    for ref, (low, whole) in ((dk, dk_sum), (dv, dv_sum)):
        ref[:, :128] = (low + whole[:512]).reshape(4, 128, 128).astype(b16)
        ref[:, 128:] = whole[512:].reshape(4, 128, 128).astype(b16)


def attend_back(q, KV, p, do):
    return pl.pallas_call(
        attend_back_kernel,
        grid=(4,),
        out_shape=(shape((ROWS, D), f32), shape((4, ROWS, 512), b16), shape((4, ROWS, 512), b16)),
        in_specs=[
            pl.BlockSpec((ROWS, 256), lambda i: (0, i)),
            pl.BlockSpec((4, ROWS, 128), lambda i: (0, 0, i)),
            pl.BlockSpec((4, ROWS, 128), lambda i: (0, 0, 4 + i)),
            pl.BlockSpec((2, ROWS, 1536), lambda i: (i, 0, 0)),
            pl.BlockSpec((ROWS, 256), lambda i: (0, i)),
        ],
        out_specs=(
            pl.BlockSpec((ROWS, 256), lambda i: (0, i)),
            pl.BlockSpec((4, ROWS, 128), lambda i: (0, 0, i)),
            pl.BlockSpec((4, ROWS, 128), lambda i: (0, 0, i)),
        ),
        compiler_params=params(),
        name="attend_back",
    )(q, KV, KV, p, do)


def keys_home_kernel(dk, dv, out, ktmp, kgot, vtmp, vgot, ss, rs, ls):
    x, y, z, c = place()
    net = Net(ss, rs, ls)
    right, left = dev(x, y + 1, z, c), dev(x, y - 1, z, c)
    net.greet([right, left])
    ring_scatter(net, lambda n: dk.at[n], ktmp, kgot, right, left, y, ROWS, 32)
    ring_scatter(net, lambda n: dv.at[n], vtmp, vgot, right, left, y, ROWS, 32)
    out[:, :512] = dk[y].astype(f32) + kgot[0].astype(f32) + kgot[1].astype(f32)
    out[:, 512:] = dv[y].astype(f32) + vgot[0].astype(f32) + vgot[1].astype(f32)
    net.finish()


def keys_home(dk, dv):
    return pl.pallas_call(
        keys_home_kernel,
        out_shape=shape((ROWS, D), f32),
        in_specs=[VMEM] * 2,
        out_specs=VMEM,
        scratch_shapes=[
            pltpu.VMEM((2, ROWS // 2, 512), b16),
            pltpu.VMEM((2, ROWS, 512), b16),
        ]
        * 2
        + sems(16),
        compiler_params=params(4),
        name="keys_home",
    )(dk, dv)


def project_back_kernel(dq, dkv, x, act, gh_ref, wq, tail, cos, sin, gin, qg, small, gp):
    cosine, sine = cos[...], sin[...]
    for t in range(16):
        src = dq if t < 8 else dkv
        at = slice(128 * (t % 8), 128 * (t % 8) + 128)
        tile = src[:, at]
        if t < 12:
            tile = tile * cosine - partner_lanes(tile) * sine
        gp[:, 128 * t : 128 * t + 128] = tile.astype(b16)
    ga = dot_t(gp[:, :D], wq[0]) + dot_t(gp[:, D:], wq[1])
    v = x[...].astype(f32)
    r = lax.rsqrt(jnp.mean(v * v, axis=-1, keepdims=True) + norm_epsilon)
    u = ga * tail[6:7, :].astype(f32)
    small[...] = jnp.sum(ga * v * r, axis=0, keepdims=True)
    gin[...] = gh_ref[...] + r * (u - v * (r * r * jnp.mean(u * v, axis=-1, keepdims=True)))
    a = act[...]
    for k in range(8):
        piece = t_dot(a, gp[:, 256 * k : 256 * k + 256]).astype(b16)
        for n in range(8):
            for b in range(2):
                qg[k, n, b] = piece[128 * n : 128 * n + 128, 128 * b : 128 * b + 128]


def project_back(dq, dkv, x, act, gh, wq, dn, cos, sin):
    whole = lambda *dims: pl.BlockSpec(dims, lambda i: (0,) * len(dims))
    return pl.pallas_call(
        project_back_kernel,
        grid=(1,),
        out_shape=(
            shape((ROWS, D), f32),
            shape((8, 8, 2, 128, 128), b16),
            shape((1, D), f32),
        ),
        in_specs=[
            whole(ROWS, D),
            whole(ROWS, D),
            whole(ROWS, D),
            whole(ROWS, D),
            whole(ROWS, D),
            whole(2, D, 1024),
            pl.BlockSpec((16, D), lambda i: (WIDE // 16, 0)),
            whole(ROWS, 128),
            whole(ROWS, 128),
        ],
        out_specs=(whole(ROWS, D), whole(8, 8, 2, 128, 128), whole(1, D)),
        scratch_shapes=[pltpu.VMEM((ROWS, 2 * D), b16)],
        compiler_params=params(),
        name="project_back",
    )(dq, dkv, x, act, gh, wq, dn, cos, sin)


def reduce_kernel(
    grads, og, qg, small, out, gin, ALL, SM, OUT, GIN,
    mine, o_twin, q_twin, o_tmp, o_got, q_tmp, q_got, y_tmp, y_got, z_got, half, s_twin, s_x, s_y, s_z, gin_low, gin_got,
    ss, rs, ls,
):
    x, y, z, c = place()
    z_hi, z_lo = z // 2, lax.rem(z, 2)
    net = Net(ss, rs, ls)
    twin = dev(x, y, z, 1 - c)
    xr, xl = dev(x + 1, y, z, c), dev(x - 1, y, z, c)
    x2 = dev(x + 2, y, z, c)
    yr, yl, y2 = dev(x, y + 1, z, c), dev(x, y - 1, z, c), dev(x, y + 2, z, c)
    zr, zl, z2 = dev(x, y, z + 1, c), dev(x, y, z - 1, c), dev(x, y, z + 2, c)
    net.greet([twin, xr, xl, x2, yr, yl, y2, zr, zl, z2])
    rows_of = lambda n: pl.ds(pl.multiple_of(n * 128, 128), 128)
    gin_low[...] = gin[rows_of(1 - z_hi)].astype(b16)
    net.send(out.at[rows_of(1 - z_hi)], OUT.at[z_hi], z2)
    swap = net.send(gin_low, gin_got, z2)
    OUT[z_hi] = out[rows_of(z_hi)]
    GIN[z_hi] = gin[rows_of(z_hi)]
    og_sent = [net.send(og.at[n * 2 + 1 - c], o_twin.at[n], twin) for n in range(4)]
    qg_sent = [net.send(qg.at[n * 2 + 1 - c], q_twin.at[n], twin) for n in range(4)]
    sm = net.send(small, s_twin, twin)
    for n in range(4):
        net.got(og_sent[n])
        add_into(o_twin.at[n], o_twin.at[n], og.at[n * 2 + c], 8, 1)
    for n in range(4):
        net.got(qg_sent[n])
        add_into(q_twin.at[n], q_twin.at[n], qg.at[n * 2 + c], 8, 1)
    net.got(sm)
    s_twin[...] += small[...]
    sx = [net.send(s_twin, s_x.at[i], p) for i, p in enumerate((xr, xl, x2))]
    ring_scatter(net, lambda n: o_twin.at[n], o_tmp, o_got, xr, xl, x, 8, 1)
    ring_scatter(net, lambda n: q_twin.at[n], q_tmp, q_got, xr, xl, x, 8, 1)

    def fill(n, carry):
        mine[n, 0:9] = grads[n]
        mine[n, 9:10] = (o_twin[x, n].astype(f32) + o_got[0, n].astype(f32) + o_got[1, n].astype(f32)).astype(b16)
        mine[n, 10:12] = (q_twin[x, n].astype(f32) + q_got[0, n].astype(f32) + q_got[1, n].astype(f32)).astype(b16)
        return carry

    lax.fori_loop(0, 8, fill, 0)
    for copy in sx:
        net.got(copy)
    s_y[0] = s_twin[...] + s_x[0] + s_x[1] + s_x[2]
    sy = [net.send(s_y.at[0], s_y.at[1 + i], p) for i, p in enumerate((yr, yl, y2))]
    for h in range(2):
        ring_scatter(net, lambda n: mine.at[h * 4 + n], y_tmp.at[h], y_got.at[h], yr, yl, y, 12, 1)

        def settle(b, carry):
            mine[h * 4 + y, b] = (
                mine[h * 4 + y, b].astype(f32) + y_got[h, 0, b].astype(f32) + y_got[h, 1, b].astype(f32)
            ).astype(b16)
            return carry

        lax.fori_loop(0, 12, settle, 0)
    for copy in sy:
        net.got(copy)
    s_z[0] = s_y[0] + s_y[1] + s_y[2] + s_y[3]
    sz = [net.send(s_z.at[0], s_z.at[1 + i], p) for i, p in enumerate((zr, zl, z2))]

    def piece(zz):
        return mine.at[(zz // 2) * 4 + y, pl.ds(lax.rem(zz, 2) * 6, 6)]

    zs = [
        net.send(piece(lax.rem(z + 1, 4)), z_got.at[0], zr),
        net.send(piece(lax.rem(z + 3, 4)), z_got.at[1], zl),
        net.send(piece(lax.rem(z + 2, 4)), z_got.at[2], z2),
    ]
    for copy in zs:
        net.got(copy)
    base = z_hi * 4 + y
    slot = x * 2 + c

    def settle_z(b, carry):
        at = z_lo * 6 + b
        v = mine[base, at].astype(f32) + z_got[0, b].astype(f32) + z_got[1, b].astype(f32) + z_got[2, b].astype(f32)
        ALL[slot, at] = v.astype(b16)
        return carry

    lax.fori_loop(0, 6, settle_z, 0)
    for copy in sz:
        net.got(copy)
    SM[...] = s_z[0] + s_z[1] + s_z[2] + s_z[3]
    done = ALL.at[slot, pl.ds(z_lo * 6, 6)]
    hop = dev(x, y, z + 1 - 2 * z_lo, c)
    net.got(net.send(done, done, hop))
    block = ALL.at[slot]
    net.send(block, block, twin)
    part = lambda n, h: ALL.at[n * 2 + c, pl.ds(h * 6, 6)]
    ring_gather(net, part, xr, xl, x)
    for d in range(1, 4):
        block = ALL.at[lax.rem(x + d, 4) * 2 + c]
        net.send(block, block, twin)
    net.got(swap)
    GIN[1 - z_hi] = gin_got[...].astype(f32)
    net.finish()


def reduce_all(grads, og, qg, small, out, gin):
    return pl.pallas_call(
        reduce_kernel,
        out_shape=(
            shape((8, 12, 128, 128), b16),
            shape((8, D), f32),
            shape((2, 128, D), b16),
            shape((2, 128, D), f32),
        ),
        in_specs=[VMEM] * 6,
        out_specs=(VMEM,) * 4,
        scratch_shapes=[
            pltpu.VMEM((8, 12, 128, 128), b16),
            pltpu.VMEM((4, 8, 1, 128, 128), b16),
            pltpu.VMEM((4, 8, 2, 128, 128), b16),
            pltpu.VMEM((2, 4, 1, 128, 128), b16),
            pltpu.VMEM((2, 8, 1, 128, 128), b16),
            pltpu.VMEM((2, 4, 2, 128, 128), b16),
            pltpu.VMEM((2, 8, 2, 128, 128), b16),
            pltpu.VMEM((2, 2, 6, 128, 128), b16),
            pltpu.VMEM((2, 2, 12, 128, 128), b16),
            pltpu.VMEM((3, 6, 128, 128), b16),
            pltpu.VMEM((6, 128, 128), b16),
            pltpu.VMEM((8, D), f32),
            pltpu.VMEM((3, 8, D), f32),
            pltpu.VMEM((4, 8, D), f32),
            pltpu.VMEM((4, 8, D), f32),
            pltpu.VMEM((128, D), b16),
            pltpu.VMEM((128, D), b16),
        ]
        + sems(64),
        compiler_params=params(5),
        name="reduce_all",
    )(grads, og, qg, small, out, gin)


def rotary(positions):
    freqs = 10000.0 ** (-jnp.arange(HD // 2).astype(f32) * 2.0 / HD)
    angles = positions.astype(f32)[:, None] * freqs[None, :]
    cos, sin = jnp.cos(angles), jnp.sin(angles)
    return jnp.concatenate([cos] * 4, axis=1), jnp.concatenate([-sin, sin] * 2, axis=1)


def learning_rates():
    return (D ** (-0.5), 8.0 * D ** (-0.5), D ** (-0.5), 2.0 * FF ** (-0.5), 0.5 * D ** (-0.5), 0.5)


def adamw(weight, gradient, moment, square, step_rate, decay_rate):
    moment_new = beta_one * moment + (1.0 - beta_one) * gradient
    square_new = beta_two * square + (1.0 - beta_two) * gradient * gradient
    corrected = moment_new / (1.0 - beta_one**STEP)
    spread_by = jnp.sqrt(square_new / (1.0 - beta_two**STEP)) + adam_epsilon
    updated = weight - step_rate * (corrected / spread_by + decay_rate * weight)
    return [moment_new, square_new, updated]


def on_device(
    tokens, segments, routes, cotangent, w_qkv, w_out, w_gateup, w_down, w_router, w_gains,
    qkv_first, qkv_second, out_first, out_second, gateup_first, gateup_second, down_first, down_second,
    router_first, router_second, gains_first, gains_second,
):
    x, y, z, c = place()
    z_hi = z // 2
    slot = x * 2 + c
    shard = z_hi * 4 + y
    cut = lax.dynamic_slice_in_dim
    wq = cut(w_qkv, c * 1024, 1024, 1).astype(b16)
    wo = cut(w_out, c * 512, 512, 1).astype(b16)
    gate = cut(w_gateup, slot * SLICE, SLICE, 2)
    up = cut(w_gateup, FF + slot * SLICE, SLICE, 2)
    gu = jnp.concatenate(
        [v.astype(b16).transpose(1, 0, 2).reshape(128, WIDE) for v in (gate, up)], axis=1
    )
    dn = jnp.concatenate(
        [
            cut(w_down, slot * SLICE, SLICE, 1).reshape(WIDE, 128),
            w_router.T,
            w_gains,
            jnp.zeros((8, 128), f32),
        ],
        axis=0,
    ).astype(b16)
    route_lanes = jnp.pad(routes.astype(f32), ((0, 0), (0, 0), (0, 126)))
    X, R, G, WQ, WO, GU, DN = gather(tokens, cotangent, route_lanes, wq, wo, gu, dn)

    posq = jnp.concatenate([y * 128 + jnp.arange(128), 512 + y * 128 + jnp.arange(128)])
    cos, sin = rotary(posq)
    seg = lax.dynamic_index_in_dim(segments, z_hi, 0, keepdims=False)
    segq = jnp.concatenate([cut(seg, y * 128, 128, 0), cut(seg, 512 + y * 128, 128, 0)])

    act_one, q, kv = project(X, WQ, DN, cos, sin)
    KV = gather_keys(kv)
    heads, probs = attend(q, KV, posq[:, None], segq[:, None], seg[None, :])
    hidden, act = after(X, heads, WO, DN, R)
    ACT = gather_tokens(act)
    part, grads = experts(ACT, G, GU, DN)
    total = send_home(part)
    out, gh, ghi, og, small_two = middle(slot[None], total, hidden, act, G, DN, R, heads, WO)
    dq, dk, dv = attend_back(q, KV, probs, ghi)
    dkv = keys_home(dk, dv)
    gin, qg, small_one = project_back(dq, dkv, X, act_one, gh, WQ, DN, cos, sin)
    small = jnp.concatenate([small_two[:7], small_one], axis=0)
    ALL, SM, layer_out, input_grad = reduce_all(grads, og, qg, small, out, gin)

    ALL = ALL.astype(f32)
    gate_up = [
        ALL[:, b : b + 3].reshape(8, 3, 128, 2, SLICE).transpose(1, 3, 2, 0, 4).reshape(EXPERTS, 128, FF)
        for b in (0, 3)
    ]
    mine = cut(SM, shard * 128, 128, 1)
    summed = (
        ALL[:, 10:12].transpose(2, 0, 1, 3).reshape(128, 2 * D),
        ALL[:, 9].transpose(1, 0, 2).reshape(128, D),
        jnp.concatenate(gate_up, axis=2),
        ALL[:, 6:9].reshape(8, EXPERTS, SLICE, 128).transpose(1, 0, 2, 3).reshape(EXPERTS, FF, 128),
        mine[:6].T,
        jnp.stack([mine[7], mine[6]]),
    )
    masters = (w_qkv, w_out, w_gateup, w_down, w_router, w_gains)
    firsts = (qkv_first, out_first, gateup_first, down_first, router_first, gains_first)
    seconds = (qkv_second, out_second, gateup_second, down_second, router_second, gains_second)
    decays = (0.1, 0.1, 0.1, 0.1, 0.1, 0.0)
    results = []
    for n in range(6):
        results += adamw(masters[n], summed[n], firsts[n], seconds[n], learning_rates()[n], decays[n])
    return (layer_out, input_grad, *results)


def solution(mesh):
    weight = [P("grp", None), P("grp", None), P(None, "grp", None), P(None, None, "grp"), P("grp", None), P(None, "grp")]
    tokens = P("rep", "grp", None)
    moments = [spec for spec in weight for _ in range(2)]
    results = [spec for spec in weight for _ in range(3)]
    return jax.shard_map(
        on_device,
        mesh=mesh,
        in_specs=(tokens, P("rep", None), tokens, tokens, *weight, *moments),
        out_specs=(tokens, tokens, *results),
        check_vma=False,
    )
```

```python
import functools

import jax
import jax.numpy as jnp
from jax import lax
from jax.experimental import pallas as pl
from jax.experimental.pallas import tpu as pltpu
from jax.sharding import PartitionSpec as P

D = 1024
HQ = 16
HK = 8
HD = 64
FF = 512
EXPERTS = 6
TOPK = 2
STEP = 10
ROWS = 256
SLICE = 64
WIDE = EXPERTS * SLICE

beta_one = 0.9
beta_two = 0.95
adam_epsilon = 1e-08
norm_epsilon = 1e-06

f32 = jnp.float32
b16 = jnp.bfloat16
MESH = pl.DeviceIdType.MESH
ANY = pl.BlockSpec(memory_space=pl.ANY)
VMEM = pl.BlockSpec(memory_space=pltpu.VMEM)
MIB = 2**20


def place():
    rep = lax.axis_index("rep")
    grp = lax.axis_index("grp")
    z_lo, x, c = rep // 8, lax.rem(rep // 2, 4), lax.rem(rep, 2)
    z_hi, y = grp // 4, lax.rem(grp, 4)
    return x, y, z_hi * 2 + z_lo, c


def dev(x, y, z, c):
    x, y, z = lax.rem(x + 4, 4), lax.rem(y + 4, 4), lax.rem(z + 4, 4)
    return (lax.rem(z, 2) * 8 + x * 2 + c, (z // 2) * 4 + y)


class Net:
    def __init__(self, send_sems, recv_sems, local_sems):
        self.sems = (send_sems, recv_sems, local_sems)
        self.count = 0
        self.locals = 0
        self.open = []

    def greet(self, peers):
        bar = pltpu.get_barrier_semaphore()
        for peer in peers:
            pl.semaphore_signal(bar, inc=1, device_id=peer, device_id_type=MESH)
        pl.semaphore_wait(bar, len(peers))

    def send(self, src, dst, peer):
        copy = pltpu.make_async_remote_copy(
            src_ref=src,
            dst_ref=dst,
            send_sem=self.sems[0].at[self.count],
            recv_sem=self.sems[1].at[self.count],
            device_id=peer,
            device_id_type=MESH,
        )
        copy.start()
        self.count += 1
        self.open.append(copy)
        return copy

    def local(self, src, dst):
        copy = pltpu.make_async_copy(src, dst, self.sems[2].at[self.locals])
        copy.start()
        self.locals += 1
        return copy

    def got(self, copy):
        copy.wait_recv()
        copy.seen = True

    def finish(self):
        for copy in self.open:
            if not getattr(copy, "seen", False):
                copy.wait_recv()
            copy.wait_send()


def sems(n, n_local=1):
    return [
        pltpu.SemaphoreType.DMA((n,)),
        pltpu.SemaphoreType.DMA((n,)),
        pltpu.SemaphoreType.DMA((n_local,)),
    ]


def params(cid=None, mib=56):
    if cid is None:
        return pltpu.CompilerParams(vmem_limit_bytes=mib * MIB)
    return pltpu.CompilerParams(
        vmem_limit_bytes=mib * MIB, collective_id=cid, has_side_effects=True
    )


def shape(dims, dtype):
    return jax.ShapeDtypeStruct(dims, dtype)


def ring_gather(net, part, right, left, me, src=None):
    src = src or (lambda half: part(me, half))
    a1 = net.send(src(0), part(me, 0), right)
    b1 = net.send(src(1), part(me, 1), left)
    a2 = net.send(src(1), part(me, 1), right)
    b2 = net.send(src(0), part(me, 0), left)
    before, after = lax.rem(me + 3, 4), lax.rem(me + 1, 4)
    net.got(a1)
    a3 = net.send(part(before, 0), part(before, 0), right)
    net.got(b1)
    b3 = net.send(part(after, 1), part(after, 1), left)
    for copy in (a2, b2, a3, b3):
        net.got(copy)


def add_into(dst, one, two, rows, step):
    def body(i, carry):
        at = pl.ds(pl.multiple_of(i * step, step), step)
        dst[at] = (one[at].astype(f32) + two[at].astype(f32)).astype(b16)
        return carry

    lax.fori_loop(0, rows // step, body, 0)


def ring_scatter(net, part, tmp, got, right, left, me, rows, step):
    half = rows // 2
    lo, hi = pl.ds(0, half), pl.ds(half, half)
    after, before, across = lax.rem(me + 1, 4), lax.rem(me + 3, 4), lax.rem(me + 2, 4)
    s1 = net.send(part(across).at[lo], tmp.at[0], right)
    s2 = net.send(part(across).at[hi], tmp.at[1], left)
    s3 = net.send(part(after).at[hi], got.at[0, hi], right)
    s4 = net.send(part(before).at[lo], got.at[1, lo], left)
    net.got(s1)
    add_into(tmp.at[0], tmp.at[0], part(after).at[lo], half, step)
    s5 = net.send(tmp.at[0], got.at[0, lo], right)
    net.got(s2)
    add_into(tmp.at[1], tmp.at[1], part(before).at[hi], half, step)
    s6 = net.send(tmp.at[1], got.at[1, hi], left)
    for copy in (s3, s4, s5, s6):
        net.got(copy)


def dot(a, b):
    return lax.dot_general(a, b, (((1,), (0,)), ((), ())), preferred_element_type=f32)


def dot_t(a, b):
    return lax.dot_general(a, b, (((1,), (1,)), ((), ())), preferred_element_type=f32)


def t_dot(a, b):
    return lax.dot_general(a, b, (((0,), (0,)), ((), ())), preferred_element_type=f32)


def gather_kernel(xl, gl, rl, wq, wo, gu, dn, X, R, G, WQ, WO, GU, DN, ss, rs, ls):
    x, y, z, c = place()
    z_hi = z // 2
    shard = z_hi * 4 + y
    slot = x * 2 + c
    net = Net(ss, rs, ls)
    partner = dev(x, y, z + 2, c)
    twin = dev(x, y, z, 1 - c)
    right, left = dev(x + 1, y, z, c), dev(x - 1, y, z, c)
    offsets = [(0, 1), (0, 3), (1, 0), (0, 2), (1, 1), (1, 3), (1, 2)]
    peers = [dev(x, y + dy, (3 - z) if dz else z, c) for dz, dy in offsets]
    net.greet(peers + [partner, twin, right, left])
    rows_of = lambda n: pl.ds(pl.multiple_of(n * 128, 128), 128)
    mine = rows_of(z_hi)
    swaps = [
        net.send(gl.at[1 - z_hi], G.at[slot, mine], partner),
        net.send(xl.at[1 - z_hi], X.at[mine], partner),
        net.send(rl.at[1 - z_hi], R.at[mine], partner),
    ]
    locs = [net.local(gl.at[z_hi], G.at[slot, mine])]
    at = rows_of(shard)
    wq_in = [net.send(wq, WQ.at[c, at], p) for p in peers]
    wo_in = [net.send(wo, WO.at[c, at], p) for p in peers]
    rest = [net.send(gu, GU.at[at], p) for p in peers]
    rest += [net.send(dn, DN.at[:, at], p) for p in peers]
    locs += [
        net.local(xl.at[z_hi], X.at[mine]),
        net.local(rl.at[z_hi], R.at[mine]),
        net.local(wq, WQ.at[c, at]),
        net.local(wo, WO.at[c, at]),
        net.local(gu, GU.at[at]),
        net.local(dn, DN.at[:, at]),
    ]
    net.send(wq, WQ.at[c, at], twin)
    net.send(wo, WO.at[c, at], twin)
    net.got(swaps[0])
    locs[0].wait()
    gpart = lambda n, h: G.at[n * 2 + c, pl.ds(h * 128, 128)]
    ring_gather(net, gpart, right, left, x)
    for n in range(4):
        net.send(G.at[n * 2 + c], G.at[n * 2 + c], twin)
    sources = [
        rows_of((lax.rem(1 - z_hi if dz else z_hi, 2)) * 4 + lax.rem(y + 4 - dy, 4))
        for dz, dy in offsets
    ]
    for copies, whole in ((wq_in, WQ), (wo_in, WO)):
        for copy, src in zip(copies, sources):
            net.got(copy)
            net.send(whole.at[c, src], whole.at[c, src], twin)
    for copy in locs[1:]:
        copy.wait()
    net.finish()


def gather(xl, gl, rl, wq, wo, gu, dn):
    return pl.pallas_call(
        gather_kernel,
        out_shape=(
            shape((ROWS, D), b16),
            shape((ROWS, 128), f32),
            shape((8, ROWS, D), b16),
            shape((2, D, 1024), b16),
            shape((2, D, 512), b16),
            shape((D, 2 * WIDE), b16),
            shape((WIDE + 16, D), b16),
        ),
        in_specs=[ANY] * 7,
        out_specs=(ANY,) * 7,
        scratch_shapes=sems(64, 8),
        compiler_params=params(0),
        name="gather",
    )(xl, gl, rl, wq, wo, gu, dn)


def partner_lanes(v):
    lane = lax.broadcasted_iota(jnp.int32, v.shape, 1)
    return jnp.where(lane % HD < HD // 2, pltpu.roll(v, 96, 1), pltpu.roll(v, 32, 1))


def project_kernel(x, wq, gains, cos, sin, act, q, kv):
    v = x[...].astype(f32)
    gain = gains[6:7, :].astype(f32)
    r = lax.rsqrt(jnp.mean(v * v, axis=-1, keepdims=True) + norm_epsilon)
    a = (v * r * gain).astype(b16)
    act[...] = a
    cosine, sine = cos[...], sin[...]
    for half in range(2):
        for t in range(4):
            out = dot(a, wq[half, :, 256 * t : 256 * (t + 1)])
            for u in range(2):
                tile = out[:, 128 * u : 128 * (u + 1)]
                at = slice(256 * t + 128 * u, 256 * t + 128 * (u + 1))
                if half == 0 or t < 2:
                    tile = tile * cosine + partner_lanes(tile) * sine
                if half == 0:
                    q[:, at] = (tile * 0.125).astype(b16)
                else:
                    kv[:, at] = tile.astype(b16)


def project(x, wq, dn, cos, sin):
    return pl.pallas_call(
        project_kernel,
        grid=(1,),
        out_shape=(shape((ROWS, D), b16),) * 3,
        in_specs=[
            pl.BlockSpec((ROWS, D), lambda i: (0, 0)),
            pl.BlockSpec((2, D, 1024), lambda i: (0, 0, 0)),
            pl.BlockSpec((16, D), lambda i: (WIDE // 16, 0)),
            pl.BlockSpec((ROWS, 128), lambda i: (0, 0)),
            pl.BlockSpec((ROWS, 128), lambda i: (0, 0)),
        ],
        out_specs=(pl.BlockSpec((ROWS, D), lambda i: (0, 0)),) * 3,
        compiler_params=params(),
        name="project",
    )(x, wq, dn, cos, sin)


def keys_kernel(kv, KV, ss, rs, ls):
    x, y, z, c = place()
    net = Net(ss, rs, ls)
    right, left = dev(x, y + 1, z, c), dev(x, y - 1, z, c)
    net.greet([right, left])
    own = net.local(kv, KV.at[y])
    part = lambda n, h: KV.at[n, pl.ds(h * 128, 128)]
    ring_gather(net, part, right, left, y, src=lambda h: kv.at[pl.ds(h * 128, 128)])
    own.wait()
    net.finish()


def gather_keys(kv):
    return pl.pallas_call(
        keys_kernel,
        out_shape=shape((4, ROWS, D), b16),
        in_specs=[ANY],
        out_specs=ANY,
        scratch_shapes=sems(8),
        compiler_params=params(1),
        name="gather_keys",
    )(kv)


def half_mask(rows, half):
    lane = lax.broadcasted_iota(jnp.int32, (rows, 128), 1)
    return (lane < HD) if half == 0 else (lane >= HD)


def spread(tile, half):
    keep = half_mask(ROWS, half)
    heads = []
    for g in range(2):
        v = tile if g == half else pltpu.roll(tile, HD, 1)
        heads.append(jnp.where(keep, v, 0.0).astype(b16))
    low = jnp.concatenate([h[:128] for h in heads], axis=0)
    high = jnp.concatenate([h[128:] for h in heads], axis=0)
    return low, high


def collect(low, high, half):
    heads = []
    for g in range(2):
        v = jnp.concatenate([low[g * 128 : g * 128 + 128], high[g * 128 : g * 128 + 128]], axis=0)
        heads.append(v if g == half else pltpu.roll(v, HD, 1))
    return jnp.where(half_mask(ROWS, 0), heads[0], heads[1])


def attend_kernel(q, k, v, posq, segq, segk, o, p, bias):
    @pl.when(pl.program_id(0) == 0)
    def _():
        place_k = lax.broadcasted_iota(jnp.int32, (128, D), 1)
        for h in range(2):
            at = slice(128 * h, 128 * h + 128)
            fine = (posq[at, :] >= place_k) & (segq[at, :] == segk[...])
            bias[at, :] = jnp.where(fine, 0.0, -1e30)

    keys = [k[:, :128].reshape(512, 128), k[:, 128:].reshape(512, 128)]
    vals = [v[:, :128].reshape(512, 128), v[:, 128:].reshape(512, 128)]
    keys_all = jnp.concatenate(keys, axis=0)
    vals_all = jnp.concatenate(vals, axis=0)
    low_bias = jnp.concatenate([bias[:128, :512]] * 2, axis=0)
    high_bias = jnp.concatenate([bias[128:, :]] * 2, axis=0)
    for half in range(2):
        tile = q[:, 128 * half : 128 * half + 128].astype(f32)
        low, high = spread(tile, half)
        outs = []
        for rows, kk, vv, bb, lo in (
            (low, keys[0], vals[0], low_bias, True),
            (high, keys_all, vals_all, high_bias, False),
        ):
            s = dot_t(rows, kk) + bb
            top = jnp.max(s, axis=-1, keepdims=True)
            e = jnp.exp(s - top)
            probs = (e * (1.0 / jnp.sum(e, axis=-1, keepdims=True))).astype(b16)
            if lo:
                p[half, :, :512] = probs
            else:
                p[half, :, 512:] = probs
            outs.append(dot(probs, vv))
        o[:, 128 * half : 128 * half + 128] = collect(outs[0], outs[1], half).astype(b16)


def attend(q, KV, posq, segq, segk):
    return pl.pallas_call(
        attend_kernel,
        grid=(4,),
        out_shape=(shape((ROWS, D), b16), shape((8, ROWS, 1536), b16)),
        in_specs=[
            pl.BlockSpec((ROWS, 256), lambda i: (0, i)),
            pl.BlockSpec((4, ROWS, 128), lambda i: (0, 0, i)),
            pl.BlockSpec((4, ROWS, 128), lambda i: (0, 0, 4 + i)),
            pl.BlockSpec((ROWS, 1), lambda i: (0, 0)),
            pl.BlockSpec((ROWS, 1), lambda i: (0, 0)),
            pl.BlockSpec((1, D), lambda i: (0, 0)),
        ],
        out_specs=(
            pl.BlockSpec((ROWS, 256), lambda i: (0, i)),
            pl.BlockSpec((2, ROWS, 1536), lambda i: (i, 0, 0)),
        ),
        scratch_shapes=[pltpu.VMEM((ROWS, D), f32)],
        compiler_params=params(),
        name="attend",
    )(q, KV, KV, posq, segq, segk)


def router_rows(tail):
    row = lax.broadcasted_iota(jnp.int32, (16, D), 0)
    kept = jnp.where(row < EXPERTS, tail.astype(f32), 0.0).astype(b16)
    return jnp.concatenate([kept, jnp.zeros((112, D), b16)], axis=0)


def one_hot(routes, slot):
    lane = lax.broadcasted_iota(jnp.int32, (ROWS, 128), 1).astype(f32)
    return (routes[:, slot : slot + 1] == lane).astype(f32)


def after_kernel(x, o, wo, tail, routes, hidden, act):
    heads = o[...]
    for half in range(2):
        for t in range(2):
            cols = slice(512 * half + 256 * t, 512 * half + 256 * (t + 1))
            hidden[:, cols] = x[:, cols].astype(f32) + dot(heads, wo[half, :, 256 * t : 256 * (t + 1)])
    h = hidden[...]
    r = lax.rsqrt(jnp.mean(h * h, axis=-1, keepdims=True) + norm_epsilon)
    a = (h * r * tail[7:8, :].astype(f32)).astype(b16)
    act[:, :D] = a
    logits = dot_t(a, router_rows(tail[...]))
    hots = [one_hot(routes, k) for k in range(TOPK)]
    picked = [jnp.sum(hot * logits, axis=-1, keepdims=True) for hot in hots]
    top = jnp.maximum(picked[0], picked[1])
    powers = [jnp.exp(v - top) for v in picked]
    total = powers[0] + powers[1]
    mixing = hots[0] * (powers[0] / total) + hots[1] * (powers[1] / total)
    big = mixing.astype(b16).astype(f32)
    act[:, D:] = (big + pltpu.roll(mixing - big, 16, 1)).astype(b16)


def after(x, o, wo, dn, routes):
    return pl.pallas_call(
        after_kernel,
        grid=(1,),
        out_shape=(shape((ROWS, D), f32), shape((ROWS, D + 128), b16)),
        in_specs=[
            pl.BlockSpec((ROWS, D), lambda i: (0, 0)),
            pl.BlockSpec((ROWS, D), lambda i: (0, 0)),
            pl.BlockSpec((2, D, 512), lambda i: (0, 0, 0)),
            pl.BlockSpec((16, D), lambda i: (WIDE // 16, 0)),
            pl.BlockSpec((ROWS, 128), lambda i: (0, 0)),
        ],
        out_specs=(
            pl.BlockSpec((ROWS, D), lambda i: (0, 0)),
            pl.BlockSpec((ROWS, D + 128), lambda i: (0, 0)),
        ),
        compiler_params=params(),
        name="after_attention",
    )(x, o, wo, dn, routes)


def tokens_kernel(act, ACT, ss, rs, ls):
    x, y, z, c = place()
    net = Net(ss, rs, ls)
    right, left, twin = dev(x + 1, y, z, c), dev(x - 1, y, z, c), dev(x, y, z, 1 - c)
    net.greet([right, left, twin])
    own = net.local(act, ACT.at[x * 2 + c])
    net.send(act, ACT.at[x * 2 + c], twin)
    part = lambda n, h: ACT.at[n * 2 + c, pl.ds(h * 128, 128)]
    ring_gather(net, part, right, left, x, src=lambda h: act.at[pl.ds(h * 128, 128)])
    for d in range(1, 4):
        block = ACT.at[lax.rem(x + d, 4) * 2 + c]
        net.send(block, block, twin)
    own.wait()
    net.finish()


def gather_tokens(act):
    return pl.pallas_call(
        tokens_kernel,
        out_shape=shape((8, ROWS, D + 128), b16),
        in_specs=[ANY],
        out_specs=ANY,
        scratch_shapes=sems(16),
        compiler_params=params(2),
        name="gather_tokens",
    )(act)


def experts_kernel(act, g, gu, dn, part, grads, gu_acc, dn_acc):
    step = pl.program_id(0)
    row = lax.broadcasted_iota(jnp.int32, (128, WIDE), 0)
    lane = lax.broadcasted_iota(jnp.int32, (128, WIDE), 1)
    pick = ((row % 16 == lane // SLICE) & (row < 32)).astype(b16)
    a = act[0, :, :D]
    mix = dot(act[0, :, D:], pick)
    gt = g[0]
    down = dn[:WIDE, :]
    h = dot(a, gu[...])
    gate, up = h[:, :WIDE], h[:, WIDE:]
    gw = dot_t(gt, down)
    s = 1.0 / (1.0 + jnp.exp(-gate))
    silu = gate * s
    inner = silu * up
    scaled = (inner * mix).astype(b16)
    part[0, :, :D] = dot(scaled, down).astype(b16)
    part[0, :, 2 * D :] = dot_t((inner * gw).astype(b16), pick).astype(b16)
    gi = gw * mix
    ggu = jnp.concatenate(
        [(gi * up * s * (1.0 + gate * (1.0 - s))).astype(b16), (gi * silu).astype(b16)], axis=1
    )
    part[0, :, D : 2 * D] = dot_t(ggu, gu[...]).astype(b16)

    @pl.when(step == 0)
    def _():
        gu_acc[...] = jnp.zeros_like(gu_acc)
        dn_acc[...] = jnp.zeros_like(dn_acc)

    gu_acc[...] += t_dot(a, ggu)
    dn_acc[...] += t_dot(scaled, gt)

    @pl.when(step == 7)
    def _():
        for n in range(8):
            at = slice(128 * n, 128 * n + 128)
            for b in range(6):
                grads[n, b] = gu_acc[at, 128 * b : 128 * b + 128].astype(b16)
            for b in range(3):
                grads[n, 6 + b] = dn_acc[128 * b : 128 * b + 128, at].astype(b16)


def experts(ACT, G, GU, DN):
    return pl.pallas_call(
        experts_kernel,
        grid=(8,),
        out_shape=(shape((8, ROWS, 2 * D + 128), b16), shape((8, 9, 128, 128), b16)),
        in_specs=[
            pl.BlockSpec((1, ROWS, D + 128), lambda i: (i, 0, 0)),
            pl.BlockSpec((1, ROWS, D), lambda i: (i, 0, 0)),
            pl.BlockSpec((D, 2 * WIDE), lambda i: (0, 0)),
            pl.BlockSpec((WIDE + 16, D), lambda i: (0, 0)),
        ],
        out_specs=(
            pl.BlockSpec((1, ROWS, 2 * D + 128), lambda i: (i, 0, 0)),
            pl.BlockSpec((8, 9, 128, 128), lambda i: (0, 0, 0, 0)),
        ),
        scratch_shapes=[pltpu.VMEM((D, 2 * WIDE), f32), pltpu.VMEM((WIDE, D), f32)],
        compiler_params=params(),
        name="experts",
    )(ACT, G, GU, DN)


def home_kernel(part, total, twin_got, tmp, got, ss, rs, ls):
    x, y, z, c = place()
    net = Net(ss, rs, ls)
    right, left, twin = dev(x + 1, y, z, c), dev(x - 1, y, z, c), dev(x, y, z, 1 - c)
    net.greet([right, left, twin])
    order = [lax.rem(x + d, 4) for d in (2, 1, 3, 0)]
    sent = [net.send(part.at[n * 2 + 1 - c], twin_got.at[n], twin) for n in order]
    for n, copy in zip(order, sent):
        net.got(copy)
        add_into(twin_got.at[n], twin_got.at[n], part.at[n * 2 + c], ROWS, 16)
    ring_scatter(net, lambda n: twin_got.at[n], tmp, got, right, left, x, ROWS, 16)

    def body(i, carry):
        at = pl.ds(pl.multiple_of(i * 16, 16), 16)
        total[at] = twin_got[x, at].astype(f32) + got[0, at].astype(f32) + got[1, at].astype(f32)
        return carry

    lax.fori_loop(0, ROWS // 16, body, 0)
    net.finish()


def send_home(part):
    wide = 2 * D + 128
    return pl.pallas_call(
        home_kernel,
        out_shape=shape((ROWS, wide), f32),
        in_specs=[VMEM],
        out_specs=VMEM,
        scratch_shapes=[
            pltpu.VMEM((4, ROWS, wide), b16),
            pltpu.VMEM((2, ROWS // 2, wide), b16),
            pltpu.VMEM((2, ROWS, wide), b16),
        ]
        + sems(16),
        compiler_params=params(3),
        name="send_home",
    )(part)


def middle_kernel(total, hidden, act, g, tail, routes, heads, wo, out, gh_ref, ghi, og, small):
    h = hidden[...]
    out[...] = (h + total[:, :D]).astype(b16)
    a = act[:, :D]
    mix = act[:, D:].astype(f32)
    lane = lax.broadcasted_iota(jnp.int32, (ROWS, 128), 1)
    mixing = jnp.where(lane < 16, mix + pltpu.roll(mix, 112, 1), 0.0)
    dg = total[:, 2 * D :]
    hots = [one_hot(routes, k) for k in range(TOPK)]
    probs = [jnp.sum(hot * mixing, axis=-1, keepdims=True) for hot in hots]
    dgs = [jnp.sum(hot * dg, axis=-1, keepdims=True) for hot in hots]
    mean = probs[0] * dgs[0] + probs[1] * dgs[1]
    grad_logits = sum(hot * (p * (d - mean)) for hot, p, d in zip(hots, probs, dgs)).astype(b16)
    ga = total[:, D : 2 * D] + dot(grad_logits, router_rows(tail[...]))
    small[0:6, :] = t_dot(grad_logits, a)[0:6, :]
    r = lax.rsqrt(jnp.mean(h * h, axis=-1, keepdims=True) + norm_epsilon)
    u = ga * tail[7:8, :].astype(f32)
    small[6:7, :] = jnp.sum(ga * h * r, axis=0, keepdims=True)
    small[7:8, :] = jnp.zeros((1, D), f32)
    gh = g[0].astype(f32) + r * (u - h * (r * r * jnp.mean(u * h, axis=-1, keepdims=True)))
    gh_ref[...] = gh
    low = gh.astype(b16)
    ghi[...] = (dot_t(low[:, :512], wo[0]) + dot_t(low[:, 512:], wo[1])).astype(b16)
    o = heads[...]
    for k in range(8):
        piece = t_dot(o, low[:, 128 * k : 128 * k + 128]).astype(b16)
        for n in range(8):
            og[k, n, 0] = piece[128 * n : 128 * n + 128]


def middle(slot, total, hidden, act, G, dn, routes, heads, wo):
    whole = lambda *dims: pl.BlockSpec(dims, lambda i, s: (0,) * len(dims))
    return pl.pallas_call(
        middle_kernel_with_slot,
        grid_spec=pltpu.PrefetchScalarGridSpec(
            num_scalar_prefetch=1,
            grid=(1,),
            in_specs=[
                whole(ROWS, 2 * D + 128),
                whole(ROWS, D),
                whole(ROWS, D + 128),
                pl.BlockSpec((1, ROWS, D), lambda i, s: (s[0], 0, 0)),
                pl.BlockSpec((16, D), lambda i, s: (WIDE // 16, 0)),
                whole(ROWS, 128),
                whole(ROWS, D),
                whole(2, D, 512),
            ],
            out_specs=(
                whole(ROWS, D),
                whole(ROWS, D),
                whole(ROWS, D),
                whole(8, 8, 1, 128, 128),
                whole(8, D),
            ),
        ),
        out_shape=(
            shape((ROWS, D), b16),
            shape((ROWS, D), f32),
            shape((ROWS, D), b16),
            shape((8, 8, 1, 128, 128), b16),
            shape((8, D), f32),
        ),
        compiler_params=params(),
        name="middle",
    )(slot, total, hidden, act, G, dn, routes, heads, wo)


def middle_kernel_with_slot(slot, *refs):
    middle_kernel(*refs)


def attend_back_kernel(q, k, v, p, do, dq, dk, dv):
    keys = [k[:, :128].reshape(512, 128), k[:, 128:].reshape(512, 128)]
    vals = [v[:, :128].reshape(512, 128), v[:, 128:].reshape(512, 128)]
    keys_all = jnp.concatenate(keys, axis=0)
    vals_all = jnp.concatenate(vals, axis=0)
    dk_sum = dv_sum = None
    for half in range(2):
        at = slice(128 * half, 128 * half + 128)
        q_low, q_high = spread(q[:, at].astype(f32), half)
        do_low, do_high = spread(do[:, at].astype(f32), half)
        outs, dks, dvs = [], [], []
        for qq, dd, kk, vv, cols in (
            (q_low, do_low, keys[0], vals[0], slice(0, 512)),
            (q_high, do_high, keys_all, vals_all, slice(512, 1536)),
        ):
            probs = p[half, :, cols]
            dp = dot_t(dd, vv)
            pf = probs.astype(f32)
            prod = pf * dp
            ds = (prod - pf * jnp.sum(prod, axis=-1, keepdims=True)).astype(b16)
            outs.append(dot(ds, kk) * 0.125)
            dks.append(t_dot(ds, qq))
            dvs.append(t_dot(probs, dd))
        dq[:, at] = collect(outs[0], outs[1], half)
        if half == 0:
            dk_sum, dv_sum = dks, dvs
        else:
            dk_sum = [a + b for a, b in zip(dk_sum, dks)]
            dv_sum = [a + b for a, b in zip(dv_sum, dvs)]
    for ref, (low, whole) in ((dk, dk_sum), (dv, dv_sum)):
        ref[:, :128] = (low + whole[:512]).reshape(4, 128, 128).astype(b16)
        ref[:, 128:] = whole[512:].reshape(4, 128, 128).astype(b16)


def attend_back(q, KV, p, do):
    return pl.pallas_call(
        attend_back_kernel,
        grid=(4,),
        out_shape=(shape((ROWS, D), f32), shape((4, ROWS, 512), b16), shape((4, ROWS, 512), b16)),
        in_specs=[
            pl.BlockSpec((ROWS, 256), lambda i: (0, i)),
            pl.BlockSpec((4, ROWS, 128), lambda i: (0, 0, i)),
            pl.BlockSpec((4, ROWS, 128), lambda i: (0, 0, 4 + i)),
            pl.BlockSpec((2, ROWS, 1536), lambda i: (i, 0, 0)),
            pl.BlockSpec((ROWS, 256), lambda i: (0, i)),
        ],
        out_specs=(
            pl.BlockSpec((ROWS, 256), lambda i: (0, i)),
            pl.BlockSpec((4, ROWS, 128), lambda i: (0, 0, i)),
            pl.BlockSpec((4, ROWS, 128), lambda i: (0, 0, i)),
        ),
        compiler_params=params(),
        name="attend_back",
    )(q, KV, KV, p, do)


def keys_home_kernel(dk, dv, out, ktmp, kgot, vtmp, vgot, ss, rs, ls):
    x, y, z, c = place()
    net = Net(ss, rs, ls)
    right, left = dev(x, y + 1, z, c), dev(x, y - 1, z, c)
    net.greet([right, left])
    ring_scatter(net, lambda n: dk.at[n], ktmp, kgot, right, left, y, ROWS, 32)
    ring_scatter(net, lambda n: dv.at[n], vtmp, vgot, right, left, y, ROWS, 32)
    out[:, :512] = dk[y].astype(f32) + kgot[0].astype(f32) + kgot[1].astype(f32)
    out[:, 512:] = dv[y].astype(f32) + vgot[0].astype(f32) + vgot[1].astype(f32)
    net.finish()


def keys_home(dk, dv):
    return pl.pallas_call(
        keys_home_kernel,
        out_shape=shape((ROWS, D), f32),
        in_specs=[VMEM] * 2,
        out_specs=VMEM,
        scratch_shapes=[
            pltpu.VMEM((2, ROWS // 2, 512), b16),
            pltpu.VMEM((2, ROWS, 512), b16),
        ]
        * 2
        + sems(16),
        compiler_params=params(4),
        name="keys_home",
    )(dk, dv)


def project_back_kernel(dq, dkv, x, act, gh_ref, wq, tail, cos, sin, gin, qg, small, gp):
    cosine, sine = cos[...], sin[...]
    for t in range(16):
        src = dq if t < 8 else dkv
        at = slice(128 * (t % 8), 128 * (t % 8) + 128)
        tile = src[:, at]
        if t < 12:
            tile = tile * cosine - partner_lanes(tile) * sine
        gp[:, 128 * t : 128 * t + 128] = tile.astype(b16)
    ga = dot_t(gp[:, :D], wq[0]) + dot_t(gp[:, D:], wq[1])
    v = x[...].astype(f32)
    r = lax.rsqrt(jnp.mean(v * v, axis=-1, keepdims=True) + norm_epsilon)
    u = ga * tail[6:7, :].astype(f32)
    small[...] = jnp.sum(ga * v * r, axis=0, keepdims=True)
    gin[...] = gh_ref[...] + r * (u - v * (r * r * jnp.mean(u * v, axis=-1, keepdims=True)))
    a = act[...]
    for k in range(8):
        piece = t_dot(a, gp[:, 256 * k : 256 * k + 256]).astype(b16)
        for n in range(8):
            for b in range(2):
                qg[k, n, b] = piece[128 * n : 128 * n + 128, 128 * b : 128 * b + 128]


def project_back(dq, dkv, x, act, gh, wq, dn, cos, sin):
    whole = lambda *dims: pl.BlockSpec(dims, lambda i: (0,) * len(dims))
    return pl.pallas_call(
        project_back_kernel,
        grid=(1,),
        out_shape=(
            shape((ROWS, D), f32),
            shape((8, 8, 2, 128, 128), b16),
            shape((1, D), f32),
        ),
        in_specs=[
            whole(ROWS, D),
            whole(ROWS, D),
            whole(ROWS, D),
            whole(ROWS, D),
            whole(ROWS, D),
            whole(2, D, 1024),
            pl.BlockSpec((16, D), lambda i: (WIDE // 16, 0)),
            whole(ROWS, 128),
            whole(ROWS, 128),
        ],
        out_specs=(whole(ROWS, D), whole(8, 8, 2, 128, 128), whole(1, D)),
        scratch_shapes=[pltpu.VMEM((ROWS, 2 * D), b16)],
        compiler_params=params(),
        name="project_back",
    )(dq, dkv, x, act, gh, wq, dn, cos, sin)


def reduce_kernel(
    grads, og, qg, small, out, gin, ALL, SM, OUT, GIN,
    mine, o_twin, q_twin, o_tmp, o_got, q_tmp, q_got, y_tmp, y_got, z_got, half, s_twin, s_x, s_y, s_z, gin_low, gin_got,
    ss, rs, ls,
):
    x, y, z, c = place()
    z_hi, z_lo = z // 2, lax.rem(z, 2)
    net = Net(ss, rs, ls)
    twin = dev(x, y, z, 1 - c)
    xr, xl = dev(x + 1, y, z, c), dev(x - 1, y, z, c)
    x2 = dev(x + 2, y, z, c)
    yr, yl, y2 = dev(x, y + 1, z, c), dev(x, y - 1, z, c), dev(x, y + 2, z, c)
    zr, zl, z2 = dev(x, y, z + 1, c), dev(x, y, z - 1, c), dev(x, y, z + 2, c)
    net.greet([twin, xr, xl, x2, yr, yl, y2, zr, zl, z2])
    rows_of = lambda n: pl.ds(pl.multiple_of(n * 128, 128), 128)
    gin_low[...] = gin[rows_of(1 - z_hi)].astype(b16)
    net.send(out.at[rows_of(1 - z_hi)], OUT.at[z_hi], z2)
    swap = net.send(gin_low, gin_got, z2)
    OUT[z_hi] = out[rows_of(z_hi)]
    GIN[z_hi] = gin[rows_of(z_hi)]
    og_sent = [net.send(og.at[n * 2 + 1 - c], o_twin.at[n], twin) for n in range(4)]
    qg_sent = [net.send(qg.at[n * 2 + 1 - c], q_twin.at[n], twin) for n in range(4)]
    sm = net.send(small, s_twin, twin)
    for n in range(4):
        net.got(og_sent[n])
        add_into(o_twin.at[n], o_twin.at[n], og.at[n * 2 + c], 8, 1)
    for n in range(4):
        net.got(qg_sent[n])
        add_into(q_twin.at[n], q_twin.at[n], qg.at[n * 2 + c], 8, 1)
    net.got(sm)
    s_twin[...] += small[...]
    sx = [net.send(s_twin, s_x.at[i], p) for i, p in enumerate((xr, xl, x2))]
    ring_scatter(net, lambda n: o_twin.at[n], o_tmp, o_got, xr, xl, x, 8, 1)
    ring_scatter(net, lambda n: q_twin.at[n], q_tmp, q_got, xr, xl, x, 8, 1)

    def fill(n, carry):
        mine[n, 0:9] = grads[n]
        mine[n, 9:10] = (o_twin[x, n].astype(f32) + o_got[0, n].astype(f32) + o_got[1, n].astype(f32)).astype(b16)
        mine[n, 10:12] = (q_twin[x, n].astype(f32) + q_got[0, n].astype(f32) + q_got[1, n].astype(f32)).astype(b16)
        return carry

    lax.fori_loop(0, 8, fill, 0)
    for copy in sx:
        net.got(copy)
    s_y[0] = s_twin[...] + s_x[0] + s_x[1] + s_x[2]
    sy = [net.send(s_y.at[0], s_y.at[1 + i], p) for i, p in enumerate((yr, yl, y2))]
    for h in range(2):
        ring_scatter(net, lambda n: mine.at[h * 4 + n], y_tmp.at[h], y_got.at[h], yr, yl, y, 12, 1)

        def settle(b, carry):
            mine[h * 4 + y, b] = (
                mine[h * 4 + y, b].astype(f32) + y_got[h, 0, b].astype(f32) + y_got[h, 1, b].astype(f32)
            ).astype(b16)
            return carry

        lax.fori_loop(0, 12, settle, 0)
    for copy in sy:
        net.got(copy)
    s_z[0] = s_y[0] + s_y[1] + s_y[2] + s_y[3]
    sz = [net.send(s_z.at[0], s_z.at[1 + i], p) for i, p in enumerate((zr, zl, z2))]

    def piece(zz):
        return mine.at[(zz // 2) * 4 + y, pl.ds(lax.rem(zz, 2) * 6, 6)]

    zs = [
        net.send(piece(lax.rem(z + 1, 4)), z_got.at[0], zr),
        net.send(piece(lax.rem(z + 3, 4)), z_got.at[1], zl),
        net.send(piece(lax.rem(z + 2, 4)), z_got.at[2], z2),
    ]
    for copy in zs:
        net.got(copy)
    base = z_hi * 4 + y
    slot = x * 2 + c

    def settle_z(b, carry):
        at = z_lo * 6 + b
        v = mine[base, at].astype(f32) + z_got[0, b].astype(f32) + z_got[1, b].astype(f32) + z_got[2, b].astype(f32)
        ALL[slot, at] = v.astype(b16)
        return carry

    lax.fori_loop(0, 6, settle_z, 0)
    for copy in sz:
        net.got(copy)
    SM[...] = s_z[0] + s_z[1] + s_z[2] + s_z[3]
    done = ALL.at[slot, pl.ds(z_lo * 6, 6)]
    hop = dev(x, y, z + 1 - 2 * z_lo, c)
    net.got(net.send(done, done, hop))
    block = ALL.at[slot]
    net.send(block, block, twin)
    part = lambda n, h: ALL.at[n * 2 + c, pl.ds(h * 6, 6)]
    ring_gather(net, part, xr, xl, x)
    for d in range(1, 4):
        block = ALL.at[lax.rem(x + d, 4) * 2 + c]
        net.send(block, block, twin)
    net.got(swap)
    GIN[1 - z_hi] = gin_got[...].astype(f32)
    net.finish()


def reduce_all(grads, og, qg, small, out, gin):
    return pl.pallas_call(
        reduce_kernel,
        out_shape=(
            shape((8, 12, 128, 128), b16),
            shape((8, D), f32),
            shape((2, 128, D), b16),
            shape((2, 128, D), f32),
        ),
        in_specs=[VMEM] * 6,
        out_specs=(VMEM,) * 4,
        scratch_shapes=[
            pltpu.VMEM((8, 12, 128, 128), b16),
            pltpu.VMEM((4, 8, 1, 128, 128), b16),
            pltpu.VMEM((4, 8, 2, 128, 128), b16),
            pltpu.VMEM((2, 4, 1, 128, 128), b16),
            pltpu.VMEM((2, 8, 1, 128, 128), b16),
            pltpu.VMEM((2, 4, 2, 128, 128), b16),
            pltpu.VMEM((2, 8, 2, 128, 128), b16),
            pltpu.VMEM((2, 2, 6, 128, 128), b16),
            pltpu.VMEM((2, 2, 12, 128, 128), b16),
            pltpu.VMEM((3, 6, 128, 128), b16),
            pltpu.VMEM((6, 128, 128), b16),
            pltpu.VMEM((8, D), f32),
            pltpu.VMEM((3, 8, D), f32),
            pltpu.VMEM((4, 8, D), f32),
            pltpu.VMEM((4, 8, D), f32),
            pltpu.VMEM((128, D), b16),
            pltpu.VMEM((128, D), b16),
        ]
        + sems(64),
        compiler_params=params(5),
        name="reduce_all",
    )(grads, og, qg, small, out, gin)


def rotary(positions):
    freqs = 10000.0 ** (-jnp.arange(HD // 2).astype(f32) * 2.0 / HD)
    angles = positions.astype(f32)[:, None] * freqs[None, :]
    cos, sin = jnp.cos(angles), jnp.sin(angles)
    return jnp.concatenate([cos] * 4, axis=1), jnp.concatenate([-sin, sin] * 2, axis=1)


def learning_rates():
    return (D ** (-0.5), 8.0 * D ** (-0.5), D ** (-0.5), 2.0 * FF ** (-0.5), 0.5 * D ** (-0.5), 0.5)


def adamw(weight, gradient, moment, square, step_rate, decay_rate):
    moment_new = beta_one * moment + (1.0 - beta_one) * gradient
    square_new = beta_two * square + (1.0 - beta_two) * gradient * gradient
    corrected = moment_new / (1.0 - beta_one**STEP)
    spread_by = jnp.sqrt(square_new / (1.0 - beta_two**STEP)) + adam_epsilon
    updated = weight - step_rate * (corrected / spread_by + decay_rate * weight)
    return [moment_new, square_new, updated]


def update_kernel(*refs):
    grads, ins, outs = refs[0], refs[1:13], refs[13:]
    step = pl.program_id(0)
    rates = learning_rates()
    lane = lax.broadcasted_iota(jnp.int32, (128, 128), 1)

    def apply(n, at, grad, rate):
        m, v, w = adamw(ins[3 * n][at], grad, ins[3 * n + 1][at], ins[3 * n + 2][at], rate, 0.1)
        outs[3 * n][at], outs[3 * n + 1][at], outs[3 * n + 2][at] = m, v, w

    for b in range(3):

        @pl.when(step == b)
        def _():
            for part in range(2):
                for t in range(4):
                    one = grads[2 * t, 3 * part + b].astype(f32)
                    two = grads[2 * t + 1, 3 * part + b].astype(f32)
                    cols = slice(FF * part + 128 * t, FF * part + 128 * t + 128)
                    first = jnp.where(lane < SLICE, one, pltpu.roll(two, SLICE, 1))
                    second = jnp.where(lane < SLICE, pltpu.roll(one, SLICE, 1), two)
                    apply(0, (0, slice(None), cols), first, rates[2])
                    apply(0, (1, slice(None), cols), second, rates[2])

        @pl.when(step == 3 + b)
        def _():
            for k in range(8):
                grad = grads[k, 6 + b].astype(f32)
                for e in range(2):
                    at = (e, slice(SLICE * k, SLICE * k + SLICE), slice(None))
                    apply(1, at, grad[SLICE * e : SLICE * e + SLICE], rates[3])

    for part in range(2):

        @pl.when(step == 6 + part)
        def _():
            for t in range(8):
                at = (slice(None), slice(128 * t, 128 * t + 128))
                apply(2, at, grads[4 * part + t // 2, 10 + t % 2].astype(f32), rates[0])

    @pl.when(step == 8)
    def _():
        for t in range(8):
            at = (slice(None), slice(128 * t, 128 * t + 128))
            apply(3, at, grads[t, 9].astype(f32), rates[1])


def update(ALL, *arrays):
    specs = [
        pl.BlockSpec((2, 128, D), lambda i: (jnp.minimum(i, 2), 0, 0)),
        pl.BlockSpec((2, FF, 128), lambda i: (jnp.clip(i - 3, 0, 2), 0, 0)),
        pl.BlockSpec((128, D), lambda i: (0, jnp.clip(i - 6, 0, 1))),
        pl.BlockSpec((128, D), lambda i: (0, 0)),
    ]
    dims = [(EXPERTS, 128, D), (EXPERTS, FF, 128), (128, 2 * D), (128, D)]
    return pl.pallas_call(
        update_kernel,
        grid=(9,),
        out_shape=tuple(shape(d, f32) for d in dims for _ in range(3)),
        in_specs=[pl.BlockSpec((8, 12, 128, 128), lambda i: (0, 0, 0, 0))]
        + [spec for spec in specs for _ in range(3)],
        out_specs=tuple(spec for spec in specs for _ in range(3)),
        compiler_params=params(),
        name="update",
    )(ALL, *arrays)


def on_device(
    tokens, segments, routes, cotangent, w_qkv, w_out, w_gateup, w_down, w_router, w_gains,
    qkv_first, qkv_second, out_first, out_second, gateup_first, gateup_second, down_first, down_second,
    router_first, router_second, gains_first, gains_second,
):
    x, y, z, c = place()
    z_hi = z // 2
    slot = x * 2 + c
    shard = z_hi * 4 + y
    cut = lax.dynamic_slice_in_dim
    wq = cut(w_qkv, c * 1024, 1024, 1).astype(b16)
    wo = cut(w_out, c * 512, 512, 1).astype(b16)
    gate = cut(w_gateup, slot * SLICE, SLICE, 2)
    up = cut(w_gateup, FF + slot * SLICE, SLICE, 2)
    gu = jnp.concatenate(
        [v.astype(b16).transpose(1, 0, 2).reshape(128, WIDE) for v in (gate, up)], axis=1
    )
    dn = jnp.concatenate(
        [
            cut(w_down, slot * SLICE, SLICE, 1).reshape(WIDE, 128),
            w_router.T,
            w_gains,
            jnp.zeros((8, 128), f32),
        ],
        axis=0,
    ).astype(b16)
    route_lanes = jnp.pad(routes.astype(f32), ((0, 0), (0, 0), (0, 126)))
    X, R, G, WQ, WO, GU, DN = gather(tokens, cotangent, route_lanes, wq, wo, gu, dn)

    posq = jnp.concatenate([y * 128 + jnp.arange(128), 512 + y * 128 + jnp.arange(128)])
    cos, sin = rotary(posq)
    seg = lax.dynamic_index_in_dim(segments, z_hi, 0, keepdims=False)
    segq = jnp.concatenate([cut(seg, y * 128, 128, 0), cut(seg, 512 + y * 128, 128, 0)])

    act_one, q, kv = project(X, WQ, DN, cos, sin)
    KV = gather_keys(kv)
    heads, probs = attend(q, KV, posq[:, None], segq[:, None], seg[None, :])
    hidden, act = after(X, heads, WO, DN, R)
    ACT = gather_tokens(act)
    part, grads = experts(ACT, G, GU, DN)
    total = send_home(part)
    out, gh, ghi, og, small_two = middle(slot[None], total, hidden, act, G, DN, R, heads, WO)
    dq, dk, dv = attend_back(q, KV, probs, ghi)
    dkv = keys_home(dk, dv)
    gin, qg, small_one = project_back(dq, dkv, X, act_one, gh, WQ, DN, cos, sin)
    small = jnp.concatenate([small_two[:7], small_one], axis=0)
    ALL, SM, layer_out, input_grad = reduce_all(grads, og, qg, small, out, gin)

    big = update(ALL, w_gateup, gateup_first, gateup_second, w_down, down_first, down_second,
                 w_qkv, qkv_first, qkv_second, w_out, out_first, out_second)
    mine = cut(SM, shard * 128, 128, 1)
    rates = learning_rates()
    router = adamw(w_router, mine[:6].T, router_first, router_second, rates[4], 0.1)
    gains = adamw(w_gains, jnp.stack([mine[7], mine[6]]), gains_first, gains_second, rates[5], 0.0)
    return (layer_out, input_grad, *big[6:9], *big[9:12], *big[0:3], *big[3:6], *router, *gains)


def solution(mesh):
    weight = [P("grp", None), P("grp", None), P(None, "grp", None), P(None, None, "grp"), P("grp", None), P(None, "grp")]
    tokens = P("rep", "grp", None)
    moments = [spec for spec in weight for _ in range(2)]
    results = [spec for spec in weight for _ in range(3)]
    return jax.shard_map(
        on_device,
        mesh=mesh,
        in_specs=(tokens, P("rep", None), tokens, tokens, *weight, *moments),
        out_specs=(tokens, tokens, *results),
        check_vma=False,
    )
```

```python
import functools

import jax
import jax.numpy as jnp
from jax import lax
from jax.experimental import pallas as pl
from jax.experimental.pallas import tpu as pltpu
from jax.sharding import PartitionSpec as P

D = 1024
HQ = 16
HK = 8
HD = 64
FF = 512
EXPERTS = 6
TOPK = 2
STEP = 10
ROWS = 256
SLICE = 64
WIDE = EXPERTS * SLICE

beta_one = 0.9
beta_two = 0.95
adam_epsilon = 1e-08
norm_epsilon = 1e-06

f32 = jnp.float32
b16 = jnp.bfloat16
MESH = pl.DeviceIdType.MESH
ANY = pl.BlockSpec(memory_space=pl.ANY)
VMEM = pl.BlockSpec(memory_space=pltpu.VMEM)
MIB = 2**20


def place():
    rep = lax.axis_index("rep")
    grp = lax.axis_index("grp")
    z_lo, x, c = rep // 8, lax.rem(rep // 2, 4), lax.rem(rep, 2)
    z_hi, y = grp // 4, lax.rem(grp, 4)
    return x, y, z_hi * 2 + z_lo, c


def dev(x, y, z, c):
    x, y, z = lax.rem(x + 4, 4), lax.rem(y + 4, 4), lax.rem(z + 4, 4)
    return (lax.rem(z, 2) * 8 + x * 2 + c, (z // 2) * 4 + y)


class Net:
    def __init__(self, send_sems, recv_sems, local_sems):
        self.sems = (send_sems, recv_sems, local_sems)
        self.count = 0
        self.locals = 0
        self.open = []

    def greet(self, peers):
        bar = pltpu.get_barrier_semaphore()
        for peer in peers:
            pl.semaphore_signal(bar, inc=1, device_id=peer, device_id_type=MESH)
        pl.semaphore_wait(bar, len(peers))

    def send(self, src, dst, peer):
        copy = pltpu.make_async_remote_copy(
            src_ref=src,
            dst_ref=dst,
            send_sem=self.sems[0].at[self.count],
            recv_sem=self.sems[1].at[self.count],
            device_id=peer,
            device_id_type=MESH,
        )
        copy.start()
        self.count += 1
        self.open.append(copy)
        return copy

    def local(self, src, dst):
        copy = pltpu.make_async_copy(src, dst, self.sems[2].at[self.locals])
        copy.start()
        self.locals += 1
        return copy

    def got(self, copy):
        copy.wait_recv()
        copy.seen = True

    def gone(self, copy):
        copy.wait_send()
        copy.left = True

    def finish(self):
        for copy in self.open:
            if not getattr(copy, "seen", False):
                copy.wait_recv()
            if not getattr(copy, "left", False):
                copy.wait_send()


def sems(n, n_local=1):
    return [
        pltpu.SemaphoreType.DMA((n,)),
        pltpu.SemaphoreType.DMA((n,)),
        pltpu.SemaphoreType.DMA((n_local,)),
    ]


def params(cid=None, mib=56):
    if cid is None:
        return pltpu.CompilerParams(vmem_limit_bytes=mib * MIB)
    return pltpu.CompilerParams(
        vmem_limit_bytes=mib * MIB, collective_id=cid, has_side_effects=True
    )


def shape(dims, dtype):
    return jax.ShapeDtypeStruct(dims, dtype)


class Ring:
    def __init__(self, net, part, right, left, me):
        self.net, self.part, self.right, self.left = net, part, right, left
        self.before, self.after = lax.rem(me + 3, 4), lax.rem(me + 1, 4)
        self.a1 = net.send(part(me, 0), part(me, 0), right)
        self.b1 = net.send(part(me, 1), part(me, 1), left)
        self.rest = [
            net.send(part(me, 1), part(me, 1), right),
            net.send(part(me, 0), part(me, 0), left),
        ]

    def relay(self):
        net, part = self.net, self.part
        net.got(self.a1)
        self.rest.append(net.send(part(self.before, 0), part(self.before, 0), self.right))
        net.got(self.b1)
        self.rest.append(net.send(part(self.after, 1), part(self.after, 1), self.left))

    def done(self):
        for copy in self.rest:
            self.net.got(copy)


def add_rows(dst, one, two, rows, step):
    def body(i, carry):
        at = pl.ds(pl.multiple_of(i * step, step), step)
        dst[at] = (one[at].astype(f32) + two[at].astype(f32)).astype(b16)
        return carry

    lax.fori_loop(0, rows // step, body, 0)


class Scatter:
    def __init__(self, net, part, tmp, got, right, left, me, rows, step):
        self.net, self.part, self.tmp, self.got = net, part, tmp, got
        self.right, self.left, self.me, self.step = right, left, me, step
        self.half = rows // 2
        self.lo, self.hi = pl.ds(0, self.half), pl.ds(self.half, self.half)
        self.after, self.before = lax.rem(me + 1, 4), lax.rem(me + 3, 4)
        across = lax.rem(me + 2, 4)
        self.s1 = net.send(part(across).at[self.lo], tmp.at[0], right)
        self.s2 = net.send(part(across).at[self.hi], tmp.at[1], left)
        self.rest = [
            net.send(part(self.after).at[self.hi], got.at[0, self.hi], right),
            net.send(part(self.before).at[self.lo], got.at[1, self.lo], left),
        ]

    def relay(self):
        net, tmp, got = self.net, self.tmp, self.got
        net.got(self.s1)
        add_rows(tmp.at[0], tmp.at[0], self.part(self.after).at[self.lo], self.half, self.step)
        self.rest.append(net.send(tmp.at[0], got.at[0, self.lo], self.right))
        net.got(self.s2)
        add_rows(tmp.at[1], tmp.at[1], self.part(self.before).at[self.hi], self.half, self.step)
        self.rest.append(net.send(tmp.at[1], got.at[1, self.hi], self.left))

    def done(self):
        for copy in self.rest:
            self.net.got(copy)

    def term(self, at):
        own = self.part(self.me)
        return own[at].astype(f32) + self.got[0, at].astype(f32) + self.got[1, at].astype(f32)

    def settle(self, dst, rows, step):
        def body(i, carry):
            at = pl.ds(pl.multiple_of(i * step, step), step)
            dst[at] = self.term(at).astype(dst.dtype)
            return carry

        lax.fori_loop(0, rows // step, body, 0)


def dot(a, b):
    return lax.dot_general(a, b, (((1,), (0,)), ((), ())), preferred_element_type=f32)


def dot_t(a, b):
    return lax.dot_general(a, b, (((1,), (1,)), ((), ())), preferred_element_type=f32)


def t_dot(a, b):
    return lax.dot_general(a, b, (((0,), (0,)), ((), ())), preferred_element_type=f32)


def partner_lanes(v):
    lane = lax.broadcasted_iota(jnp.int32, v.shape, 1)
    return jnp.where(lane % HD < HD // 2, pltpu.roll(v, 96, 1), pltpu.roll(v, 32, 1))


def half_mask(rows, half):
    lane = lax.broadcasted_iota(jnp.int32, (rows, 128), 1)
    return (lane < HD) if half == 0 else (lane >= HD)


def spread(tile, half):
    keep = half_mask(ROWS, half)
    heads = []
    for g in range(2):
        v = tile if g == half else pltpu.roll(tile, HD, 1)
        heads.append(jnp.where(keep, v, 0.0).astype(b16))
    low = jnp.concatenate([h[:128] for h in heads], axis=0)
    high = jnp.concatenate([h[128:] for h in heads], axis=0)
    return low, high


def collect(low, high, half):
    heads = []
    for g in range(2):
        v = jnp.concatenate([low[g * 128 : g * 128 + 128], high[g * 128 : g * 128 + 128]], axis=0)
        heads.append(v if g == half else pltpu.roll(v, HD, 1))
    return jnp.where(half_mask(ROWS, 0), heads[0], heads[1])


def router_rows(tail):
    row = lax.broadcasted_iota(jnp.int32, (16, D), 0)
    kept = jnp.where(row < EXPERTS, tail.astype(f32), 0.0).astype(b16)
    return jnp.concatenate([kept, jnp.zeros((112, D), b16)], axis=0)


def one_hot(routes, slot):
    lane = lax.broadcasted_iota(jnp.int32, (ROWS, 128), 1).astype(f32)
    return (routes[:, slot : slot + 1] == lane).astype(f32)


def lanes(n, width=128):
    return pl.ds(pl.multiple_of(n * width, width), width)


def front_kernel(
    tok, cot, rl, wqkv, wout, wgu, wdn, tail, cos, sin, posq, segq, segk,
    X_o, R_o, G, WQ_o, WKV_o, WO_o, GU, DN, TL_o, one_o, q_o, KV_o, P_o, heads_o, hidden_o, act_o,
    X, R, WQ, WKV, WO, TL, one, q, KV, probs_all, heads, hidden, act, bias,
    wq32, wkv32, wo32, gate32, up32, dn32, wq16, wkv16, wo16, gu16, dn16,
    ss, rs, ls,
):
    x, y, z, c = place()
    z_hi = z // 2
    shard = z_hi * 4 + y
    slot = x * 2 + c
    net = Net(ss, rs, ls)
    kept = []
    keep = lambda src, dst: kept.append(net.local(src, dst))
    loads = [
        net.local(wqkv.at[:, pl.ds(pl.multiple_of(D + c * 512, 512), 512)], wkv32),
        net.local(wqkv.at[:, lanes(slot)], wq32),
        net.local(wout.at[:, lanes(slot)], wo32),
        net.local(wgu.at[:, :, lanes(x)], gate32),
        net.local(wgu.at[:, :, lanes(4 + x)], up32),
        net.local(wdn.at[:, pl.ds(pl.multiple_of(slot * SLICE, SLICE), SLICE), :], dn32),
    ]
    partner = dev(x, y, z + 2, c)
    twin = dev(x, y, z, 1 - c)
    xr, xl = dev(x + 1, y, z, c), dev(x - 1, y, z, c)
    yr, yl = dev(x, y + 1, z, c), dev(x, y - 1, z, c)
    offsets = [(0, 1), (0, 3), (1, 0), (0, 2), (1, 1), (1, 3), (1, 2)]
    peers = [dev(x, y + dy, (3 - z) if dz else z, c) for dz, dy in offsets]
    sources = [
        lanes(lax.rem(z_hi + dz, 2) * 4 + lax.rem(y + 4 - dy, 4)) for dz, dy in offsets
    ]
    net.greet(peers + [partner, twin, xr, xl, dev(x + 2, y, z, c)])
    half_rows = lanes(z_hi)
    at = lanes(shard)
    x_in = net.send(tok.at[1 - z_hi], X.at[half_rows], partner)
    r_in = net.send(rl.at[1 - z_hi], R.at[half_rows], partner)
    own = [net.local(tok.at[z_hi], X.at[half_rows]), net.local(rl.at[z_hi], R.at[half_rows])]
    kv_lanes = pl.ds(pl.multiple_of(c * 512, 512), 512)
    loads[0].wait()
    wkv16[...] = wkv32[...].astype(b16)
    kv_in = [net.send(wkv16, WKV.at[at, kv_lanes], p) for p in peers]
    forwards = [net.send(wkv16, WKV.at[at, kv_lanes], twin)]
    own += [net.local(wkv16, WKV.at[at, kv_lanes]), net.local(tail, TL.at[:, at])]
    tl_in = [net.send(tail, TL.at[:, at], p) for p in peers]
    loads[1].wait()
    wq16[...] = wq32[...].astype(b16)
    q_in = [net.send(wq16, WQ.at[at, lanes(slot)], p) for p in peers]
    loads[2].wait()
    wo16[...] = wo32[...].astype(b16)
    o_in = [net.send(wo16, WO.at[at, lanes(slot)], p) for p in peers]
    own += [net.local(wq16, WQ.at[at, lanes(slot)]), net.local(wo16, WO.at[at, lanes(slot)])]
    g_in = net.send(cot.at[1 - z_hi], G.at[slot, half_rows], partner)
    g_own = net.local(cot.at[z_hi], G.at[slot, half_rows])

    for load in loads[3:]:
        load.wait()
    lane = lax.broadcasted_iota(jnp.int32, (128, 128), 1)
    mine_first = c == 0
    for part, src in enumerate((gate32, up32)):
        for b in range(3):
            one_e, two_e = src[2 * b], src[2 * b + 1]
            first = jnp.where(mine_first, one_e, pltpu.roll(one_e, SLICE, 1))
            second = jnp.where(mine_first, pltpu.roll(two_e, SLICE, 1), two_e)
            cols = slice(WIDE * part + 128 * b, WIDE * part + 128 * b + 128)
            gu16[:, cols] = jnp.where(lane < SLICE, first, second).astype(b16)
    dn16[...] = dn32[...].reshape(WIDE, 128).astype(b16)

    place_k = lax.broadcasted_iota(jnp.int32, (128, D), 1)
    for h in range(2):
        rows = slice(128 * h, 128 * h + 128)
        fine = (posq[rows, :] >= place_k) & (segq[rows, :] == segk[...])
        bias[rows, :] = jnp.where(fine, 0.0, -1e30)

    for copy in own:
        copy.wait()
    for copy in [x_in, *tl_in]:
        net.got(copy)
    v = X[...].astype(f32)
    r = lax.rsqrt(jnp.mean(v * v, axis=-1, keepdims=True) + norm_epsilon)
    one[...] = (v * r * TL[6:7, :].astype(f32)).astype(b16)
    keep(X, X_o)
    keep(one, one_o)
    keep(TL, TL_o)

    for copy, src in zip(kv_in, sources):
        net.got(copy)
        forwards.append(net.send(WKV.at[src, kv_lanes], WKV.at[src, kv_lanes], twin))
    for copy in forwards:
        net.got(copy)
    cosine, sine = cos[...], sin[...]
    a = one[...]
    for t in range(4):
        out = dot(a, WKV[:, 256 * t : 256 * t + 256])
        for u in range(2):
            tile = out[:, 128 * u : 128 * u + 128]
            if t < 2:
                tile = tile * cosine + partner_lanes(tile) * sine
            KV[y, :, 256 * t + 128 * u : 256 * t + 128 * u + 128] = tile.astype(b16)
    kv_ring = Ring(net, lambda n, h: KV.at[n, pl.ds(h * 128, 128)], yr, yl, y)
    keep(WKV, WKV_o)

    rings = []
    for copies, whole in ((q_in, WQ), (o_in, WO)):
        for copy in copies:
            net.got(copy)
        part = lambda n, h, whole=whole: whole.at[pl.ds(h * 512, 512), lanes(n * 2 + c)]
        rings.append(Ring(net, part, xr, xl, x))
    twins = [
        [net.send(whole.at[:, lanes(slot)], whole.at[:, lanes(slot)], twin)] for whole in (WQ, WO)
    ]
    kv_ring.relay()
    rings[0].relay()
    rings[1].relay()
    g_own.wait()
    net.got(g_in)
    block = G.at[slot]
    g_all = [net.send(block, block, p) for p in (xr, xl, dev(x + 2, y, z, c))]
    net.send(block, block, twin)
    for p in peers:
        net.send(gu16, GU.at[at], p)
        net.send(dn16, DN.at[:, at], p)
    keep(gu16, GU.at[at])
    keep(dn16, DN.at[:, at])

    def share(n, whole):
        rings[n].done()
        for d in range(1, 4):
            tile = whole.at[:, lanes(lax.rem(x + d, 4) * 2 + c)]
            twins[n].append(net.send(tile, tile, twin))

    share(0, WQ)
    for copy in twins[0]:
        net.got(copy)
    for t in range(4):
        out = dot(a, WQ[:, 256 * t : 256 * t + 256])
        for u in range(2):
            tile = out[:, 128 * u : 128 * u + 128]
            tile = tile * cosine + partner_lanes(tile) * sine
            q[:, 256 * t + 128 * u : 256 * t + 128 * u + 128] = (tile * 0.125).astype(b16)
    keep(q, q_o)
    keep(WQ, WQ_o)
    share(1, WO)
    kv_ring.done()
    keep(KV, KV_o)

    low_bias = jnp.concatenate([bias[:128, :512]] * 2, axis=0)
    high_bias = jnp.concatenate([bias[128:, :]] * 2, axis=0)
    for pair in range(4):
        cols = slice(128 * pair, 128 * pair + 128)
        vcols = slice(512 + 128 * pair, 512 + 128 * pair + 128)
        keys = [KV[:, :128, cols].reshape(512, 128), KV[:, 128:, cols].reshape(512, 128)]
        vals = [KV[:, :128, vcols].reshape(512, 128), KV[:, 128:, vcols].reshape(512, 128)]
        keys_all = jnp.concatenate(keys, axis=0)
        vals_all = jnp.concatenate(vals, axis=0)
        for half in range(2):
            cols = slice(256 * pair + 128 * half, 256 * pair + 128 * half + 128)
            low, high = spread(q[:, cols].astype(f32), half)
            outs = []
            for rows, kk, vv, bb, at_p in (
                (low, keys[0], vals[0], low_bias, slice(0, 512)),
                (high, keys_all, vals_all, high_bias, slice(512, 1536)),
            ):
                s = dot_t(rows, kk) + bb
                top = jnp.max(s, axis=-1, keepdims=True)
                e = jnp.exp(s - top)
                probs = (e * (1.0 / jnp.sum(e, axis=-1, keepdims=True))).astype(b16)
                probs_all[2 * pair + half, :, at_p] = probs
                outs.append(dot(probs, vv))
            heads[:, cols] = collect(outs[0], outs[1], half).astype(b16)
        keep(probs_all.at[pl.ds(2 * pair, 2)], P_o.at[pl.ds(2 * pair, 2)])
    keep(heads, heads_o)

    for copy in twins[1]:
        net.got(copy)
    keep(WO, WO_o)
    all_heads = heads[...]
    for t in range(4):
        cols = slice(256 * t, 256 * t + 256)
        hidden[:, cols] = X[:, cols].astype(f32) + dot(all_heads, WO[:, cols])
    h = hidden[...]
    r = lax.rsqrt(jnp.mean(h * h, axis=-1, keepdims=True) + norm_epsilon)
    a = (h * r * TL[7:8, :].astype(f32)).astype(b16)
    act[:, :D] = a
    logits = dot_t(a, router_rows(TL[...]))
    net.got(r_in)
    routes = R[...]
    hots = [one_hot(routes, k) for k in range(TOPK)]
    picked = [jnp.sum(hot * logits, axis=-1, keepdims=True) for hot in hots]
    top = jnp.maximum(picked[0], picked[1])
    powers = [jnp.exp(v - top) for v in picked]
    total = powers[0] + powers[1]
    mixing = hots[0] * (powers[0] / total) + hots[1] * (powers[1] / total)
    big = mixing.astype(b16).astype(f32)
    act[:, D:] = (big + pltpu.roll(mixing - big, 16, 1)).astype(b16)
    keep(hidden, hidden_o)
    keep(act, act_o)
    keep(R, R_o)
    for copy in g_all:
        net.got(copy)
    for d in range(1, 4):
        block = G.at[lax.rem(x + d, 4) * 2 + c]
        net.send(block, block, twin)
    for copy in kept:
        copy.wait()
    net.finish()


def front(tok, cot, rl, wqkv, wout, wgu, wdn, tail, cos, sin, posq, segq, segk):
    V = pltpu.VMEM
    return pl.pallas_call(
        front_kernel,
        out_shape=(
            shape((ROWS, D), b16),
            shape((ROWS, 128), f32),
            shape((8, ROWS, D), b16),
            shape((D, D), b16),
            shape((D, D), b16),
            shape((D, D), b16),
            shape((D, 2 * WIDE), b16),
            shape((WIDE, D), b16),
            shape((16, D), b16),
            shape((ROWS, D), b16),
            shape((ROWS, D), b16),
            shape((4, ROWS, D), b16),
            shape((8, ROWS, 1536), b16),
            shape((ROWS, D), b16),
            shape((ROWS, D), f32),
            shape((ROWS, D + 128), b16),
        ),
        in_specs=[ANY] * 7 + [VMEM] * 6,
        out_specs=(ANY,) * 16,
        scratch_shapes=[
            V((ROWS, D), b16),
            V((ROWS, 128), f32),
            V((D, D), b16),
            V((D, D), b16),
            V((D, D), b16),
            V((16, D), b16),
            V((ROWS, D), b16),
            V((ROWS, D), b16),
            V((4, ROWS, D), b16),
            V((8, ROWS, 1536), b16),
            V((ROWS, D), b16),
            V((ROWS, D), f32),
            V((ROWS, D + 128), b16),
            V((ROWS, D), f32),
            V((128, 128), f32),
            V((128, 512), f32),
            V((128, 128), f32),
            V((EXPERTS, 128, 128), f32),
            V((EXPERTS, 128, 128), f32),
            V((EXPERTS, SLICE, 128), f32),
            V((128, 128), b16),
            V((128, 512), b16),
            V((128, 128), b16),
            V((128, 2 * WIDE), b16),
            V((WIDE, 128), b16),
        ]
        + sems(96, 40),
        compiler_params=params(0),
        name="front",
    )(tok, cot, rl, wqkv, wout, wgu, wdn, tail, cos, sin, posq, segq, segk)


def experts_kernel(
    act, G, GU, DN, total, grads_o, PO,
    ACT, g, gu, dn, back, tw, tmp, got, out, gu_acc, dn_acc, grads,
    ss, rs, ls,
):
    x, y, z, c = place()
    slot = x * 2 + c
    net = Net(ss, rs, ls)
    loads = {}
    loads[0] = [net.local(act, ACT.at[slot]), net.local(GU, gu), net.local(DN, dn)]
    chips = {d: lax.rem(x + d, 4) for d in range(4)}
    mine = {d: chips[d] * 2 + c for d in range(4)}
    other = {d: chips[d] * 2 + 1 - c for d in range(4)}
    for d in (0, 3, 2, 1):
        loads.setdefault(d, []).extend(net.local(G.at[n], g.at[n]) for n in (mine[d], other[d]))
    xr, xl, twin = dev(x + 1, y, z, c), dev(x - 1, y, z, c), dev(x, y, z, 1 - c)
    net.greet([xr, xl, twin])
    for copy in loads[0]:
        copy.wait()
    ring = Ring(net, lambda n, h: ACT.at[n * 2 + c, pl.ds(h * 128, 128)], xr, xl, x)
    swap = net.send(ACT.at[slot], ACT.at[slot], twin)
    gu_acc[...] = jnp.zeros_like(gu_acc)
    dn_acc[...] = jnp.zeros_like(dn_acc)
    row = lax.broadcasted_iota(jnp.int32, (128, WIDE), 0)
    lane = lax.broadcasted_iota(jnp.int32, (128, WIDE), 1)
    pick = ((row % 16 == lane // SLICE) & (row < 32)).astype(b16)
    kept = []

    def compute(n):
        a = ACT[n, :, :D]
        mix = dot(ACT[n, :, D:], pick)
        gt = g[n]
        h = dot(a, gu[...])
        gate, up = h[:, :WIDE], h[:, WIDE:]
        gw = dot_t(gt, dn[...])
        s = 1.0 / (1.0 + jnp.exp(-gate))
        silu = gate * s
        inner = silu * up
        scaled = (inner * mix).astype(b16)
        gi = gw * mix
        ggu = jnp.concatenate(
            [(gi * up * s * (1.0 + gate * (1.0 - s))).astype(b16), (gi * silu).astype(b16)], axis=1
        )
        back[n, :, :D] = dot_t(ggu, gu[...]).astype(b16)
        back[n, :, D:] = dot_t((inner * gw).astype(b16), pick).astype(b16)
        out[n] = dot(scaled, dn[...]).astype(b16)
        gu_acc[...] += t_dot(a, ggu)
        dn_acc[...] += t_dot(scaled, gt)
        kept.append(net.local(out.at[n], PO.at[n]))

    def add(dst, one, two):
        def body(i, carry):
            at = pl.ds(pl.multiple_of(i * 16, 16), 16)
            dst[at] = (one[at].astype(f32) + two[at].astype(f32)).astype(b16)
            return carry

        lax.fori_loop(0, dst.shape[0] // 16, body, 0)

    def pair(d, arrive=()):
        if d:
            for copy in loads[d]:
                copy.wait()
        for copy in arrive:
            net.got(copy)
        compute(other[d])
        sent = net.send(back.at[other[d]], tw.at[chips[d]], twin)
        compute(mine[d])
        net.got(sent)
        add(tw.at[chips[d]], tw.at[chips[d]], back.at[mine[d]])

    def forward(d, arrive):
        for copy in arrive:
            net.got(copy)
        block = ACT.at[mine[d]]
        return net.send(block, block, twin)

    compute(mine[0])
    net.got(swap)
    compute(other[0])
    home = net.send(back.at[other[0]], tw.at[x], twin)
    ring.relay()
    a2, b2, a3, b3 = ring.rest
    f3 = forward(3, [a2])
    f1 = forward(1, [b2])
    net.got(home)
    add(tw.at[x], tw.at[x], back.at[mine[0]])
    pair(3, [f3])
    lo, hi = pl.ds(0, 128), pl.ds(128, 128)
    before, across, after = chips[3], chips[2], chips[1]
    last = [net.send(tw.at[before, lo], got.at[1, lo], xl)]
    f2 = forward(2, [a3, b3])
    pair(2, [f2])
    s1 = net.send(tw.at[across, lo], tmp.at[0], xr)
    s2 = net.send(tw.at[across, hi], tmp.at[1], xl)
    pair(1, [f1])
    last.append(net.send(tw.at[after, hi], got.at[0, hi], xr))
    net.got(s1)
    add(tmp.at[0], tmp.at[0], tw.at[after, lo])
    last.append(net.send(tmp.at[0], got.at[0, lo], xr))
    net.got(s2)
    add(tmp.at[1], tmp.at[1], tw.at[before, hi])
    last.append(net.send(tmp.at[1], got.at[1, hi], xl))
    for n in range(8):
        at = slice(128 * n, 128 * n + 128)
        for b in range(6):
            grads[n, 128 * b : 128 * b + 128] = gu_acc[at, 128 * b : 128 * b + 128].astype(b16)
        for b in range(3):
            rows = slice(128 * (6 + b), 128 * (6 + b) + 128)
            grads[n, rows] = dn_acc[128 * b : 128 * b + 128, at].astype(b16)
    kept.append(net.local(grads, grads_o))
    for copy in last:
        net.got(copy)

    def body(i, carry):
        at = pl.ds(pl.multiple_of(i * 16, 16), 16)
        total[at] = tw[x, at].astype(f32) + got[0, at].astype(f32) + got[1, at].astype(f32)
        return carry

    lax.fori_loop(0, ROWS // 16, body, 0)
    for copy in kept:
        copy.wait()
    net.finish()


def experts(act, G, GU, DN):
    V = pltpu.VMEM
    wide = D + 128
    return pl.pallas_call(
        experts_kernel,
        out_shape=(shape((ROWS, wide), f32), shape((8, 9 * 128, 128), b16), shape((8, ROWS, D), b16)),
        in_specs=[ANY] * 4,
        out_specs=(VMEM, ANY, ANY),
        scratch_shapes=[
            V((8, ROWS, wide), b16),
            V((8, ROWS, D), b16),
            V((D, 2 * WIDE), b16),
            V((WIDE, D), b16),
            V((8, ROWS, wide), b16),
            V((4, ROWS, wide), b16),
            V((2, ROWS // 2, wide), b16),
            V((2, ROWS, wide), b16),
            V((8, ROWS, D), b16),
            V((D, 2 * WIDE), f32),
            V((WIDE, D), f32),
            V((8, 9 * 128, 128), b16),
        ]
        + sems(24, 24),
        compiler_params=params(2),
        name="experts",
    )(act, G, GU, DN)


def back_kernel(
    total_i, hidden_i, act_i, G, TL_i, R_i, heads_i, WO_i, X_i, one_i, q_i, KV_i, P_i, WQ_i, WKV_i, grads_i, PO, cos, sin,
    OUT, gin, ALLM_o, late_o, kvg_o, small,
    total, hidden, act, g, TL, R, heads, WO, X, one, q, KV, P, WQ, WKV, gr, po,
    po_tw, po_tmp, po_got, og, og_tw, og_tmp, og_got, qg, qg_tw, qg_tmp, qg_got,
    dkv, k_tmp, k_got, gh, ghi, gp, y_tmp, y_got, z_got, ALLM, late, ob,
    ss, rs, ls,
):
    x, y, z, c = place()
    z_hi, z_lo = z // 2, lax.rem(z, 2)
    slot = x * 2 + c
    net = Net(ss, rs, ls)
    kept = []
    first = [
        net.local(*pair)
        for pair in (
            (total_i, total), (hidden_i, hidden), (act_i, act), (TL_i, TL), (R_i, R),
            (G.at[slot], g), (heads_i, heads), (WO_i, WO),
        )
    ]
    grad_load = net.local(grads_i, gr)
    po_load = [net.local(PO.at[n * 2 + c], po.at[n]) for n in range(4)]
    second = [
        net.local(*pair)
        for pair in ((KV_i, KV), (q_i, q), (P_i, P), (one_i, one), (X_i, X), (WQ_i, WQ), (WKV_i, WKV))
    ]
    twin = dev(x, y, z, 1 - c)
    xr, xl = dev(x + 1, y, z, c), dev(x - 1, y, z, c)
    yr, yl = dev(x, y + 1, z, c), dev(x, y - 1, z, c)
    zr, zl, z2 = dev(x, y, z + 1, c), dev(x, y, z - 1, c), dev(x, y, z + 2, c)
    net.greet([twin, xr, xl, yr, yl, zr, zl, z2])
    grad_load.wait()
    y_rings = [
        Scatter(net, lambda n, h=h: gr.at[h * 4 + n], y_tmp.at[h], y_got.at[h], yr, yl, y, 1152, 64)
        for h in range(2)
    ]
    po_in = [net.send(PO.at[n * 2 + 1 - c], po_tw.at[n], twin) for n in range(4)]

    for copy in first:
        copy.wait()
    h = hidden[...]
    a = act[:, :D]
    mix = act[:, D:].astype(f32)
    lane = lax.broadcasted_iota(jnp.int32, (ROWS, 128), 1)
    mixing = jnp.where(lane < 16, mix + pltpu.roll(mix, 112, 1), 0.0)
    dg = total[:, D:]
    routes = R[...]
    hots = [one_hot(routes, k) for k in range(TOPK)]
    probs = [jnp.sum(hot * mixing, axis=-1, keepdims=True) for hot in hots]
    dgs = [jnp.sum(hot * dg, axis=-1, keepdims=True) for hot in hots]
    mean = probs[0] * dgs[0] + probs[1] * dgs[1]
    grad_logits = sum(hot * (p * (d - mean)) for hot, p, d in zip(hots, probs, dgs)).astype(b16)
    ga = total[:, :D] + dot(grad_logits, router_rows(TL[...]))
    small[0:6, :] = t_dot(grad_logits, a)[0:6, :]
    r = lax.rsqrt(jnp.mean(h * h, axis=-1, keepdims=True) + norm_epsilon)
    u = ga * TL[7:8, :].astype(f32)
    small[6:7, :] = jnp.sum(ga * h * r, axis=0, keepdims=True)
    gh[...] = g[...].astype(f32) + r * (u - h * (r * r * jnp.mean(u * h, axis=-1, keepdims=True)))
    low = gh[...].astype(b16)
    ghi[...] = dot_t(low, WO[...]).astype(b16)

    for n in range(4):
        net.got(po_in[n])
        po_load[n].wait()
        add_rows(po_tw.at[n], po_tw.at[n], po.at[n], ROWS, 16)
    out_ring = Scatter(net, lambda n: po_tw.at[n], po_tmp, po_got, xr, xl, x, ROWS, 16)

    def weight_grad(dst, left, right):
        for t in range(4):
            piece = t_dot(left, right[:, 256 * t : 256 * t + 256])
            dst[2 * t] = piece[:, :128].astype(b16)
            dst[2 * t + 1] = piece[:, 128:].astype(b16)

    weight_grad(og, heads[...], low)
    og_in = [net.send(og.at[n * 2 + 1 - c], og_tw.at[n], twin) for n in range(4)]
    for ring in y_rings:
        ring.relay()
    for copy in second:
        copy.wait()
    cosine, sine = cos[...], sin[...]

    def pair(n):
        cols = slice(128 * n, 128 * n + 128)
        vcols = slice(512 + 128 * n, 512 + 128 * n + 128)
        keys = [KV[:, :128, cols].reshape(512, 128), KV[:, 128:, cols].reshape(512, 128)]
        vals = [KV[:, :128, vcols].reshape(512, 128), KV[:, 128:, vcols].reshape(512, 128)]
        keys_all = jnp.concatenate(keys, axis=0)
        vals_all = jnp.concatenate(vals, axis=0)
        sums = None
        for half in range(2):
            at = slice(256 * n + 128 * half, 256 * n + 128 * half + 128)
            q_low, q_high = spread(q[:, at].astype(f32), half)
            do_low, do_high = spread(ghi[:, at].astype(f32), half)
            outs, terms = [], []
            for qq, dd, kk, vv, at_p in (
                (q_low, do_low, keys[0], vals[0], slice(0, 512)),
                (q_high, do_high, keys_all, vals_all, slice(512, 1536)),
            ):
                pr = P[2 * n + half, :, at_p]
                dp = dot_t(dd, vv)
                pf = pr.astype(f32)
                prod = pf * dp
                ds = (prod - pf * jnp.sum(prod, axis=-1, keepdims=True)).astype(b16)
                outs.append(dot(ds, kk) * 0.125)
                terms.append((t_dot(ds, qq), t_dot(pr, dd)))
            tile = collect(outs[0], outs[1], half)
            gp[:, at] = (tile * cosine - partner_lanes(tile) * sine).astype(b16)
            sums = terms if half == 0 else [(i + k, j + m) for (i, j), (k, m) in zip(sums, terms)]
        for part, where in enumerate((cols, vcols)):
            lows, whole = sums[0][part], sums[1][part]
            dkv[:, :128, where] = (lows + whole[:512]).reshape(4, 128, 128).astype(b16)
            dkv[:, 128:, where] = whole[512:].reshape(4, 128, 128).astype(b16)

    pair(0)
    out_ring.relay()
    for n in range(4):
        net.got(og_in[n])
        add_rows(og_tw.at[n], og_tw.at[n], og.at[n * 2 + c], 1024, 64)
    og_ring = Scatter(net, lambda n: og_tw.at[n], og_tmp, og_got, xr, xl, x, 1024, 64)
    pair(1)
    pair(2)
    for n, ring in enumerate(y_rings):
        ring.done()
        ring.settle(gr.at[n * 4 + y], 1152, 64)

    def piece(zz):
        return gr.at[(zz // 2) * 4 + y, pl.ds(pl.multiple_of(lax.rem(zz, 2) * 576, 576), 576)]

    z_in = [
        net.send(piece(lax.rem(z + 1, 4)), z_got.at[0], zr),
        net.send(piece(lax.rem(z + 3, 4)), z_got.at[1], zl),
        net.send(piece(lax.rem(z + 2, 4)), z_got.at[2], z2),
    ]
    pair(3)
    k_ring = Scatter(net, lambda n: dkv.at[n], k_tmp, k_got, yr, yl, y, ROWS, 16)

    acts = one[...]
    weight_grad(qg, acts, gp[:, :D])
    qg_in = [net.send(qg.at[n * 2 + 1 - c], qg_tw.at[n], twin) for n in range(4)]
    og_ring.relay()
    for copy in z_in:
        net.got(copy)
    base = pl.multiple_of(z_lo * 576, 576)

    def settle_z(i, carry):
        at = pl.ds(pl.multiple_of(i * 64, 64), 64)
        here = pl.ds(pl.multiple_of(base + i * 64, 64), 64)
        v = gr[z_hi * 4 + y, here].astype(f32)
        for n in range(3):
            v = v + z_got[n, at].astype(f32)
        ALLM[slot, here] = v.astype(b16)
        return carry

    lax.fori_loop(0, 9, settle_z, 0)
    done = ALLM.at[slot, pl.ds(base, 576)]
    hop = net.send(done, done, dev(x, y, z + 1 - 2 * z_lo, c))
    ga = dot_t(gp[:, :D], WQ[...])
    for n in range(4):
        net.got(qg_in[n])
        add_rows(qg_tw.at[n], qg_tw.at[n], qg.at[n * 2 + c], 1024, 64)
    qg_ring = Scatter(net, lambda n: qg_tw.at[n], qg_tmp, qg_got, xr, xl, x, 1024, 64)
    out_ring.done()
    ob[...] = (hidden[...] + out_ring.term(slice(None))).astype(b16)
    rows_of = lambda n: pl.ds(pl.multiple_of(n * 128, 128), 128)
    net.send(ob.at[rows_of(1 - z_hi)], OUT.at[z_hi], z2)
    kept.append(net.local(ob.at[rows_of(z_hi)], OUT.at[z_hi]))
    k_ring.relay()
    net.got(hop)
    net.send(ALLM.at[slot], ALLM.at[slot], twin)
    m_ring = Ring(net, lambda n, h: ALLM.at[n * 2 + c, pl.ds(h * 576, 576)], xr, xl, x)
    og_ring.done()
    og_ring.settle(late.at[0], 1024, 64)
    qg_ring.relay()

    k_ring.done()
    for t in range(8):
        at = slice(128 * t, 128 * t + 128)
        tile = dkv[y, :, at].astype(f32) + k_got[0, :, at].astype(f32) + k_got[1, :, at].astype(f32)
        if t < 4:
            tile = tile * cosine - partner_lanes(tile) * sine
        gp[:, D + 128 * t : D + 128 * t + 128] = tile.astype(b16)
    for copy in og_in:
        net.gone(copy)
    weight_grad(og, acts, gp[:, D:])
    kept.append(net.local(og, kvg_o))
    m_ring.relay()
    ga = ga + dot_t(gp[:, D:], WKV[...])
    v = X[...].astype(f32)
    r = lax.rsqrt(jnp.mean(v * v, axis=-1, keepdims=True) + norm_epsilon)
    u = ga * TL[6:7, :].astype(f32)
    small[7:8, :] = jnp.sum(ga * v * r, axis=0, keepdims=True)
    gin[...] = gh[...] + r * (u - v * (r * r * jnp.mean(u * v, axis=-1, keepdims=True)))
    qg_ring.done()
    qg_ring.settle(late.at[1], 1024, 64)
    kept.append(net.local(late, late_o))
    m_ring.done()
    for d in range(1, 4):
        block = ALLM.at[lax.rem(x + d, 4) * 2 + c]
        net.send(block, block, twin)
    for copy in kept:
        copy.wait()
    net.finish()
    last = net.local(ALLM, ALLM_o)
    last.wait()


def back(*arrays):
    V = pltpu.VMEM
    wide = D + 128
    return pl.pallas_call(
        back_kernel,
        out_shape=(
            shape((2, 128, D), b16),
            shape((ROWS, D), f32),
            shape((8, 1152, 128), b16),
            shape((2, D, 128), b16),
            shape((8, D, 128), b16),
            shape((8, D), f32),
        ),
        in_specs=[ANY] * 17 + [VMEM] * 2,
        out_specs=(ANY, VMEM, ANY, ANY, ANY, VMEM),
        scratch_shapes=[
            V((ROWS, wide), f32),
            V((ROWS, D), f32),
            V((ROWS, wide), b16),
            V((ROWS, D), b16),
            V((16, D), b16),
            V((ROWS, 128), f32),
            V((ROWS, D), b16),
            V((D, D), b16),
            V((ROWS, D), b16),
            V((ROWS, D), b16),
            V((ROWS, D), b16),
            V((4, ROWS, D), b16),
            V((8, ROWS, 1536), b16),
            V((D, D), b16),
            V((D, D), b16),
            V((8, 1152, 128), b16),
            V((4, ROWS, D), b16),
            V((4, ROWS, D), b16),
            V((2, ROWS // 2, D), b16),
            V((2, ROWS, D), b16),
        ]
        + [
            V((8, D, 128), b16),
            V((4, D, 128), b16),
            V((2, D // 2, 128), b16),
            V((2, D, 128), b16),
        ]
        * 2
        + [
            V((4, ROWS, D), b16),
            V((2, ROWS // 2, D), b16),
            V((2, ROWS, D), b16),
            V((ROWS, D), f32),
            V((ROWS, D), b16),
            V((ROWS, 2 * D), b16),
            V((2, 2, 576, 128), b16),
            V((2, 2, 1152, 128), b16),
            V((3, 576, 128), b16),
            V((8, 1152, 128), b16),
            V((2, D, 128), b16),
            V((ROWS, D), b16),
        ]
        + sems(80, 32),
        compiler_params=params(3, 60),
        name="back",
    )(*arrays)


def reduce_kernel(
    kvg, late, small, gin,
    ALL, SM, GIN,
    mine, k_tw, k_tmp, k_got, y_tmp, y_got, y_in, z_got, s_twin, s_x, s_y, s_z, gin_low, gin_got,
    ss, rs, ls,
):
    x, y, z, c = place()
    z_hi, z_lo = z // 2, lax.rem(z, 2)
    slot = x * 2 + c
    net = Net(ss, rs, ls)
    twin = dev(x, y, z, 1 - c)
    xr, xl, x2 = dev(x + 1, y, z, c), dev(x - 1, y, z, c), dev(x + 2, y, z, c)
    yr, yl, y2 = dev(x, y + 1, z, c), dev(x, y - 1, z, c), dev(x, y + 2, z, c)
    zr, zl, z2 = dev(x, y, z + 1, c), dev(x, y, z - 1, c), dev(x, y, z + 2, c)
    net.greet([twin, xr, xl, x2, yr, yl, y2, zr, zl, z2])
    rows_of = lambda n: pl.ds(pl.multiple_of(n * 128, 128), 128)
    k_in = [net.send(kvg.at[n * 2 + 1 - c], k_tw.at[n], twin) for n in range(4)]
    sm = net.send(small, s_twin, twin)
    gin_low[...] = gin[rows_of(1 - z_hi)].astype(b16)
    swap = net.send(gin_low, gin_got, z2)
    for n in range(8):
        for b in range(2):
            mine[n, 128 * b : 128 * b + 128] = late[b, 128 * n : 128 * n + 128]
    early = pl.ds(0, 256)
    y_rings = [
        Scatter(net, lambda n, h=h: mine.at[h * 4 + n, early], y_tmp.at[h], y_got.at[h], yr, yl, y, 256, 64)
        for h in range(2)
    ]
    for n in range(4):
        net.got(k_in[n])
        add_rows(k_tw.at[n], k_tw.at[n], kvg.at[n * 2 + c], 1024, 64)
    k_ring = Scatter(net, lambda n: k_tw.at[n], k_tmp, k_got, xr, xl, x, 1024, 64)
    net.got(sm)
    s_twin[...] += small[...]
    sx = [net.send(s_twin, s_x.at[i], p) for i, p in enumerate((xr, xl, x2))]
    for ring in y_rings:
        ring.relay()
    k_ring.relay()
    GIN[z_hi] = gin[rows_of(z_hi)]
    for copy in sx:
        net.got(copy)
    s_y[0] = s_twin[...] + s_x[0] + s_x[1] + s_x[2]
    sy = [net.send(s_y.at[0], s_y.at[1 + i], p) for i, p in enumerate((yr, yl, y2))]
    for n, ring in enumerate(y_rings):
        ring.done()
        ring.settle(mine.at[n * 4 + y, early], 256, 64)
    k_ring.done()
    for n in range(8):
        mine[n, 256:384] = k_ring.term(slice(128 * n, 128 * n + 128)).astype(b16)
    last = pl.ds(256, 128)
    y_got3 = [
        net.send(mine.at[h * 4 + lax.rem(y + d, 4), last], y_in.at[h, i], p)
        for h in range(2)
        for i, (d, p) in enumerate(((1, yr), (3, yl), (2, y2)))
    ]
    for copy in sy:
        net.got(copy)
    s_z[0] = s_y[0] + s_y[1] + s_y[2] + s_y[3]
    sz = [net.send(s_z.at[0], s_z.at[1 + i], p) for i, p in enumerate((zr, zl, z2))]
    for copy in y_got3:
        net.got(copy)
    for h in range(2):
        v = mine[h * 4 + y, 256:384].astype(f32)
        for i in range(3):
            v = v + y_in[h, i].astype(f32)
        mine[h * 4 + y, 256:384] = v.astype(b16)

    def piece(zz):
        return mine.at[(zz // 2) * 4 + y, pl.ds(pl.multiple_of(lax.rem(zz, 2) * 192, 192), 192)]

    z_in = [
        net.send(piece(lax.rem(z + 1, 4)), z_got.at[0], zr),
        net.send(piece(lax.rem(z + 3, 4)), z_got.at[1], zl),
        net.send(piece(lax.rem(z + 2, 4)), z_got.at[2], z2),
    ]
    for copy in z_in:
        net.got(copy)
    base = pl.multiple_of(z_lo * 192, 192)
    here = pl.ds(base, 192)
    v = mine[z_hi * 4 + y, here].astype(f32)
    for i in range(3):
        v = v + z_got[i].astype(f32)
    ALL[slot, here] = v.astype(b16)
    done = ALL.at[slot, here]
    net.got(net.send(done, done, dev(x, y, z + 1 - 2 * z_lo, c)))
    block = ALL.at[slot]
    net.send(block, block, twin)
    spread_x = [net.send(block, block, p) for p in (xr, xl, x2)]
    for copy in sz:
        net.got(copy)
    SM[...] = s_z[0] + s_z[1] + s_z[2] + s_z[3]
    net.got(swap)
    GIN[1 - z_hi] = gin_got[...].astype(f32)
    for copy, d in zip(spread_x, (3, 1, 2)):
        net.got(copy)
        block = ALL.at[lax.rem(x + d, 4) * 2 + c]
        net.send(block, block, twin)
    net.finish()


def reduce_late(kvg, late, small, gin):
    V = pltpu.VMEM
    return pl.pallas_call(
        reduce_kernel,
        out_shape=(shape((8, 384, 128), b16), shape((8, D), f32), shape((2, 128, D), f32)),
        in_specs=[VMEM] * 4,
        out_specs=(VMEM,) * 3,
        scratch_shapes=[
            V((8, 384, 128), b16),
            V((4, D, 128), b16),
            V((2, D // 2, 128), b16),
            V((2, D, 128), b16),
            V((2, 2, 128, 128), b16),
            V((2, 2, 256, 128), b16),
            V((2, 3, 128, 128), b16),
            V((3, 192, 128), b16),
            V((8, D), f32),
            V((3, 8, D), f32),
            V((4, 8, D), f32),
            V((4, 8, D), f32),
            V((128, D), b16),
            V((128, D), b16),
        ]
        + sems(64),
        compiler_params=params(4),
        name="reduce_late",
    )(kvg, late, small, gin)


def rotary(positions):
    freqs = 10000.0 ** (-jnp.arange(HD // 2).astype(f32) * 2.0 / HD)
    angles = positions.astype(f32)[:, None] * freqs[None, :]
    cos, sin = jnp.cos(angles), jnp.sin(angles)
    return jnp.concatenate([cos] * 4, axis=1), jnp.concatenate([-sin, sin] * 2, axis=1)


def learning_rates():
    return (D ** (-0.5), 8.0 * D ** (-0.5), D ** (-0.5), 2.0 * FF ** (-0.5), 0.5 * D ** (-0.5), 0.5)


def adamw(weight, gradient, moment, square, step_rate, decay_rate):
    moment_new = beta_one * moment + (1.0 - beta_one) * gradient
    square_new = beta_two * square + (1.0 - beta_two) * gradient * gradient
    corrected = moment_new / (1.0 - beta_one**STEP)
    spread_by = jnp.sqrt(square_new / (1.0 - beta_two**STEP)) + adam_epsilon
    updated = weight - step_rate * (corrected / spread_by + decay_rate * weight)
    return [moment_new, square_new, updated]


def update_kernel(*refs):
    grads, late, ins, outs = refs[0], refs[1], refs[2:14], refs[14:]
    step = pl.program_id(0)
    rates = learning_rates()
    lane = lax.broadcasted_iota(jnp.int32, (128, 128), 1)

    def apply(n, at, grad, rate):
        m, v, w = adamw(ins[3 * n][at], grad, ins[3 * n + 1][at], ins[3 * n + 2][at], rate, 0.1)
        outs[3 * n][at], outs[3 * n + 1][at], outs[3 * n + 2][at] = m, v, w

    for b in range(3):

        @pl.when(step == b)
        def _():
            for part in range(2):
                for t in range(4):
                    one = grads[2 * t, 128 * (3 * part + b) : 128 * (3 * part + b) + 128].astype(f32)
                    two = grads[2 * t + 1, 128 * (3 * part + b) : 128 * (3 * part + b) + 128].astype(f32)
                    cols = slice(FF * part + 128 * t, FF * part + 128 * t + 128)
                    first = jnp.where(lane < SLICE, one, pltpu.roll(two, SLICE, 1))
                    second = jnp.where(lane < SLICE, pltpu.roll(one, SLICE, 1), two)
                    apply(0, (0, slice(None), cols), first, rates[2])
                    apply(0, (1, slice(None), cols), second, rates[2])

        @pl.when(step == 3 + b)
        def _():
            for k in range(8):
                grad = grads[k, 128 * (6 + b) : 128 * (6 + b) + 128].astype(f32)
                for e in range(2):
                    at = (e, slice(SLICE * k, SLICE * k + SLICE), slice(None))
                    apply(1, at, grad[SLICE * e : SLICE * e + SLICE], rates[3])

    for part in range(2):

        @pl.when(step == 6 + part)
        def _():
            for t in range(8):
                at = (slice(None), slice(128 * t, 128 * t + 128))
                apply(2, at, late[t, 128 * (1 + part) : 128 * (2 + part)].astype(f32), rates[0])

    @pl.when(step == 8)
    def _():
        for t in range(8):
            at = (slice(None), slice(128 * t, 128 * t + 128))
            apply(3, at, late[t, 0:128].astype(f32), rates[1])


def update(ALL, late, *arrays):
    specs = [
        pl.BlockSpec((2, 128, D), lambda i: (jnp.minimum(i, 2), 0, 0)),
        pl.BlockSpec((2, FF, 128), lambda i: (jnp.clip(i - 3, 0, 2), 0, 0)),
        pl.BlockSpec((128, D), lambda i: (0, jnp.clip(i - 6, 0, 1))),
        pl.BlockSpec((128, D), lambda i: (0, 0)),
    ]
    dims = [(EXPERTS, 128, D), (EXPERTS, FF, 128), (128, 2 * D), (128, D)]
    return pl.pallas_call(
        update_kernel,
        grid=(9,),
        out_shape=tuple(shape(d, f32) for d in dims for _ in range(3)),
        in_specs=[
            pl.BlockSpec((8, 1152, 128), lambda i: (0, 0, 0)),
            pl.BlockSpec((8, 384, 128), lambda i: (0, 0, 0)),
        ]
        + [spec for spec in specs for _ in range(3)],
        out_specs=tuple(spec for spec in specs for _ in range(3)),
        compiler_params=params(),
        name="update",
    )(ALL, late, *arrays)


def on_device(
    tokens, segments, routes, cotangent, w_qkv, w_out, w_gateup, w_down, w_router, w_gains,
    qkv_first, qkv_second, out_first, out_second, gateup_first, gateup_second, down_first, down_second,
    router_first, router_second, gains_first, gains_second,
):
    x, y, z, c = place()
    z_hi = z // 2
    shard = z_hi * 4 + y
    cut = lax.dynamic_slice_in_dim
    tail = jnp.concatenate([w_router.T, w_gains, jnp.zeros((8, 128), f32)], axis=0).astype(b16)
    route_lanes = jnp.pad(routes.astype(f32), ((0, 0), (0, 0), (0, 126)))
    posq = jnp.concatenate([y * 128 + jnp.arange(128), 512 + y * 128 + jnp.arange(128)])
    cos, sin = rotary(posq)
    seg = lax.dynamic_index_in_dim(segments, z_hi, 0, keepdims=False)
    segq = jnp.concatenate([cut(seg, y * 128, 128, 0), cut(seg, 512 + y * 128, 128, 0)])
    X, R, G, WQ, WKV, WO, GU, DN, TL, act_one, q, KV, probs, heads, hidden, act = front(
        tokens, cotangent, route_lanes, w_qkv, w_out, w_gateup, w_down, tail,
        cos, sin, posq[:, None], segq[:, None], seg[None, :],
    )
    total, grads, PO = experts(act, G, GU, DN)
    layer_out, gin, ALLM, late, kvg, small = back(
        total, hidden, act, G, TL, R, heads, WO, X, act_one, q, KV, probs, WQ, WKV, grads, PO, cos, sin
    )
    late, SM, input_grad = reduce_late(kvg, late, small, gin)
    big = update(ALLM, late, w_gateup, gateup_first, gateup_second, w_down, down_first, down_second,
                 w_qkv, qkv_first, qkv_second, w_out, out_first, out_second)
    mine = cut(SM, shard * 128, 128, 1)
    rates = learning_rates()
    router = adamw(w_router, mine[:6].T, router_first, router_second, rates[4], 0.1)
    gains = adamw(w_gains, jnp.stack([mine[7], mine[6]]), gains_first, gains_second, rates[5], 0.0)
    return (layer_out, input_grad, *big[6:9], *big[9:12], *big[0:3], *big[3:6], *router, *gains)


def solution(mesh):
    weight = [P("grp", None), P("grp", None), P(None, "grp", None), P(None, None, "grp"), P("grp", None), P(None, "grp")]
    tokens = P("rep", "grp", None)
    moments = [spec for spec in weight for _ in range(2)]
    results = [spec for spec in weight for _ in range(3)]
    return jax.shard_map(
        on_device,
        mesh=mesh,
        in_specs=(tokens, P("rep", None), tokens, tokens, *weight, *moments),
        out_specs=(tokens, tokens, *results),
        check_vma=False,
    )
```

```python
import jax
import jax.numpy as jnp
import numpy as np
from jax import lax
from jax.experimental import pallas as pl
from jax.experimental.pallas import tpu as pltpu
from jax.sharding import PartitionSpec as P

D = 1024
HQ = 16
HK = 8
HD = 64
FF = 512
EXPERTS = 6
TOPK = 2
STEP = 10
ROWS = 256
SLICE = 64
WIDE = EXPERTS * SLICE

beta_one = 0.9
beta_two = 0.95
adam_epsilon = 1e-08
norm_epsilon = 1e-06

f32 = jnp.float32
b16 = jnp.bfloat16
MESH = pl.DeviceIdType.MESH
ANY = pl.BlockSpec(memory_space=pl.ANY)
VMEM = pl.BlockSpec(memory_space=pltpu.VMEM)
MIB = 2**20


def place():
    rep = lax.axis_index("rep")
    grp = lax.axis_index("grp")
    z_lo, x, c = rep // 8, lax.rem(rep // 2, 4), lax.rem(rep, 2)
    z_hi, y = grp // 4, lax.rem(grp, 4)
    return x, y, z_hi * 2 + z_lo, c


def dev(x, y, z, c):
    x, y, z = lax.rem(x + 4, 4), lax.rem(y + 4, 4), lax.rem(z + 4, 4)
    return (lax.rem(z, 2) * 8 + x * 2 + c, (z // 2) * 4 + y)


class Net:
    def __init__(self, send_sems, recv_sems, local_sems):
        self.sems = (send_sems, recv_sems, local_sems)
        self.count = 0
        self.locals = 0
        self.open = []

    def greet(self, peers):
        bar = pltpu.get_barrier_semaphore()
        for peer in peers:
            pl.semaphore_signal(bar, inc=1, device_id=peer, device_id_type=MESH)
        pl.semaphore_wait(bar, len(peers))

    def send(self, src, dst, peer):
        copy = pltpu.make_async_remote_copy(
            src_ref=src,
            dst_ref=dst,
            send_sem=self.sems[0].at[self.count],
            recv_sem=self.sems[1].at[self.count],
            device_id=peer,
            device_id_type=MESH,
        )
        copy.start()
        self.count += 1
        self.open.append(copy)
        return copy

    def local(self, src, dst):
        copy = pltpu.make_async_copy(src, dst, self.sems[2].at[self.locals])
        copy.start()
        self.locals += 1
        return copy

    def got(self, copy):
        copy.wait_recv()
        copy.seen = True

    def gone(self, copy):
        copy.wait_send()
        copy.left = True

    def finish(self):
        for copy in self.open:
            if not getattr(copy, "seen", False):
                copy.wait_recv()
            if not getattr(copy, "left", False):
                copy.wait_send()


def sems(n, n_local=1):
    return [
        pltpu.SemaphoreType.DMA((n,)),
        pltpu.SemaphoreType.DMA((n,)),
        pltpu.SemaphoreType.DMA((n_local,)),
    ]


def params(cid=None, mib=56):
    if cid is None:
        return pltpu.CompilerParams(vmem_limit_bytes=mib * MIB)
    return pltpu.CompilerParams(
        vmem_limit_bytes=mib * MIB, collective_id=cid, has_side_effects=True
    )


def shape(dims, dtype):
    return jax.ShapeDtypeStruct(dims, dtype)


class Ring:
    def __init__(self, net, part, right, left, me):
        self.net, self.part, self.right, self.left = net, part, right, left
        self.before, self.after = lax.rem(me + 3, 4), lax.rem(me + 1, 4)
        self.a1 = net.send(part(me, 0), part(me, 0), right)
        self.b1 = net.send(part(me, 1), part(me, 1), left)
        self.rest = [
            net.send(part(me, 1), part(me, 1), right),
            net.send(part(me, 0), part(me, 0), left),
        ]

    def relay(self):
        net, part = self.net, self.part
        net.got(self.a1)
        self.rest.append(net.send(part(self.before, 0), part(self.before, 0), self.right))
        net.got(self.b1)
        self.rest.append(net.send(part(self.after, 1), part(self.after, 1), self.left))

    def done(self):
        for copy in self.rest:
            self.net.got(copy)


def add_rows(dst, one, two, rows, step):
    def body(i, carry):
        at = pl.ds(pl.multiple_of(i * step, step), step)
        dst[at] = (one[at].astype(f32) + two[at].astype(f32)).astype(b16)
        return carry

    lax.fori_loop(0, rows // step, body, 0)


class Scatter:
    def __init__(self, net, part, tmp, got, right, left, me, rows, step):
        self.net, self.part, self.tmp, self.got = net, part, tmp, got
        self.right, self.left, self.me, self.step = right, left, me, step
        self.half = rows // 2
        self.lo, self.hi = pl.ds(0, self.half), pl.ds(self.half, self.half)
        self.after, self.before = lax.rem(me + 1, 4), lax.rem(me + 3, 4)
        across = lax.rem(me + 2, 4)
        self.s1 = net.send(part(across).at[self.lo], tmp.at[0], right)
        self.s2 = net.send(part(across).at[self.hi], tmp.at[1], left)
        self.rest = [
            net.send(part(self.after).at[self.hi], got.at[0, self.hi], right),
            net.send(part(self.before).at[self.lo], got.at[1, self.lo], left),
        ]

    def relay(self):
        net, tmp, got = self.net, self.tmp, self.got
        net.got(self.s1)
        add_rows(tmp.at[0], tmp.at[0], self.part(self.after).at[self.lo], self.half, self.step)
        self.rest.append(net.send(tmp.at[0], got.at[0, self.lo], self.right))
        net.got(self.s2)
        add_rows(tmp.at[1], tmp.at[1], self.part(self.before).at[self.hi], self.half, self.step)
        self.rest.append(net.send(tmp.at[1], got.at[1, self.hi], self.left))

    def done(self):
        for copy in self.rest:
            self.net.got(copy)

    def term(self, at):
        own = self.part(self.me)
        return own[at].astype(f32) + self.got[0, at].astype(f32) + self.got[1, at].astype(f32)

    def settle(self, dst, rows, step):
        def body(i, carry):
            at = pl.ds(pl.multiple_of(i * step, step), step)
            dst[at] = self.term(at).astype(dst.dtype)
            return carry

        lax.fori_loop(0, rows // step, body, 0)


def dot(a, b):
    return lax.dot_general(a, b, (((1,), (0,)), ((), ())), preferred_element_type=f32)


def dot_t(a, b):
    return lax.dot_general(a, b, (((1,), (1,)), ((), ())), preferred_element_type=f32)


def t_dot(a, b):
    return lax.dot_general(a, b, (((0,), (0,)), ((), ())), preferred_element_type=f32)


def partner_lanes(v):
    lane = lax.broadcasted_iota(jnp.int32, v.shape, 1)
    return jnp.where(lane % HD < HD // 2, pltpu.roll(v, 96, 1), pltpu.roll(v, 32, 1))


def half_mask(rows, half):
    lane = lax.broadcasted_iota(jnp.int32, (rows, 128), 1)
    return (lane < HD) if half == 0 else (lane >= HD)


def spread(tile, half):
    keep = half_mask(ROWS, half)
    heads = []
    for g in range(2):
        v = tile if g == half else pltpu.roll(tile, HD, 1)
        heads.append(jnp.where(keep, v, 0.0).astype(b16))
    low = jnp.concatenate([h[:128] for h in heads], axis=0)
    high = jnp.concatenate([h[128:] for h in heads], axis=0)
    return low, high


def collect(low, high, half):
    heads = []
    for g in range(2):
        v = jnp.concatenate([low[g * 128 : g * 128 + 128], high[g * 128 : g * 128 + 128]], axis=0)
        heads.append(v if g == half else pltpu.roll(v, HD, 1))
    return jnp.where(half_mask(ROWS, 0), heads[0], heads[1])


def router_rows(tail):
    row = lax.broadcasted_iota(jnp.int32, (16, D), 0)
    kept = jnp.where(row < EXPERTS, tail.astype(f32), 0.0).astype(b16)
    return jnp.concatenate([kept, jnp.zeros((112, D), b16)], axis=0)


def one_hot(routes, slot):
    lane = lax.broadcasted_iota(jnp.int32, (ROWS, 128), 1).astype(f32)
    return (routes[:, slot : slot + 1] == lane).astype(f32)


def lanes(n, width=128):
    return pl.ds(pl.multiple_of(n * width, width), width)


class Fan:
    def __init__(self, net, src, at, shards, over, ys):
        self.net, self.src, self.at, self.ys, self.shards = net, src, at, ys, shards
        self.over = net.send(src, at(shards[0]), over)

    def round(self):
        self.out = [self.net.send(self.src, self.at(self.shards[0]), p) for p in self.ys]
        return self

    def forward(self):
        self.net.got(self.over)
        ref = self.at(self.shards[1])
        self.out += [self.net.send(ref, ref, p) for p in self.ys]
        return ref

    def arrivals(self):
        for copy, n in zip(self.out, self.shards[2:]):
            self.net.got(copy)
            yield self.at(n)


def front_kernel(
    tok, cot, rl, wqkv, wout, wgu, wdn, cos_t, sin_t, router, gains, segs,
    X_o, R_o, G, WQ_o, WKV_o, WO_o, GD, TL_o, one_o, q_o, KV_o, P_o, heads_o, hidden_o, act_o,
    X, R, WQ, WKV, WO, TL, one, q, KV, probs_all, heads, hidden, act, bias,
    wq32, wkv32, wo32, gate32, up32, dn32, wq16, wkv16, wo16, gd16, cos, sin, tail32, tail,
    ss, rs, ls,
):
    x, y, z, c = place()
    z_hi = z // 2
    slot = x * 2 + c
    net = Net(ss, rs, ls)
    kept = []
    keep = lambda src, dst: kept.append(net.local(src, dst))
    loads = [
        net.local(wqkv.at[:, pl.ds(pl.multiple_of(D + c * 512, 512), 512)], wkv32),
        net.local(wqkv.at[:, lanes(slot)], wq32),
        net.local(wout.at[:, lanes(slot)], wo32),
        net.local(wgu.at[:, :, lanes(x)], gate32),
        net.local(wgu.at[:, :, lanes(4 + x)], up32),
        net.local(wdn.at[:, pl.ds(pl.multiple_of(slot * SLICE, SLICE), SLICE), :], dn32),
    ]
    tables = [
        net.local(src.at[lanes(4 * h + y)], dst.at[pl.ds(128 * h, 128)])
        for src, dst in ((cos_t, cos), (sin_t, sin))
        for h in range(2)
    ]
    partner = dev(x, y, z + 2, c)
    over = dev(x, y, 3 - z, c)
    twin = dev(x, y, z, 1 - c)
    xr, xl = dev(x + 1, y, z, c), dev(x - 1, y, z, c)
    yr, yl = dev(x, y + 1, z, c), dev(x, y - 1, z, c)
    ys = [yr, yl, dev(x, y + 2, z, c)]
    net.greet(ys + [over, partner, twin, xr, xl])
    rows = [z_hi * 4, 4 - z_hi * 4]
    shards = [rows[0] + y, rows[1] + y]
    shards += [row + lax.rem(y + d, 4) for row in rows for d in (3, 1, 2)]
    half_rows = lanes(z_hi)
    kv_lanes = pl.ds(pl.multiple_of(c * 512, 512), 512)
    fan = lambda src, at: Fan(net, src, at, shards, over, ys)
    loads[0].wait()
    wkv16[...] = wkv32[...].astype(b16)
    kv_fan = fan(wkv16, lambda n: WKV.at[lanes(n), kv_lanes]).round()
    forwards = [net.send(wkv16, WKV.at[lanes(shards[0]), kv_lanes], twin)]
    own = [net.local(tok.at[z_hi], X.at[half_rows]), net.local(rl.at[z_hi], R.at[half_rows])]
    eye = lax.broadcasted_iota(jnp.int32, (128, 128), 0) == lax.broadcasted_iota(jnp.int32, (128, 128), 1)
    tail32[...] = jnp.zeros_like(tail32)
    tail32[0:6, :] = t_dot(router[...].astype(b16), eye.astype(b16))
    tail32[6:8, :] = gains[...]
    tail[...] = tail32[...].astype(b16)
    tl_fan = fan(tail, lambda n: TL.at[:, lanes(n)]).round()
    own += [
        net.local(wkv16, WKV.at[lanes(shards[0]), kv_lanes]),
        net.local(tail, TL.at[:, lanes(shards[0])]),
    ]

    place_k = lax.broadcasted_iota(jnp.int32, (128, D), 1)
    place_q = lax.broadcasted_iota(jnp.int32, (128, D), 0) + y * 128
    pick_row = lambda v: jnp.where(z_hi == 0, v[0:1], v[1:2]).astype(f32)
    seg_k = pick_row(segs[...])
    for h in range(2):
        seg_row = jnp.broadcast_to(pick_row(segs[:, lanes(4 * h + y)]), (128, 128))
        seg_q = jnp.sum(jnp.where(eye, seg_row, 0.0), axis=1, keepdims=True)
        fine = (place_q + 512 * h >= place_k) & (seg_q == seg_k)
        bias[128 * h : 128 * h + 128, :] = jnp.where(fine, 0.0, -1e30)

    ref = kv_fan.forward()
    forwards.append(net.send(ref, ref, twin))
    x_in = net.send(tok.at[1 - z_hi], X.at[half_rows], partner)
    tl_fan.forward()
    loads[1].wait()
    wq16[...] = wq32[...].astype(b16)
    q_fan = fan(wq16, lambda n: WQ.at[lanes(n), lanes(slot)])
    loads[2].wait()
    wo16[...] = wo32[...].astype(b16)
    o_fan = fan(wo16, lambda n: WO.at[lanes(n), lanes(slot)])
    more = [
        net.local(wq16, WQ.at[lanes(shards[0]), lanes(slot)]),
        net.local(wo16, WO.at[lanes(shards[0]), lanes(slot)]),
    ]
    r_in = net.send(rl.at[1 - z_hi], R.at[half_rows], partner)

    for copy in own + tables:
        copy.wait()
    for _ in tl_fan.arrivals():
        pass
    net.got(x_in)
    v = X[...].astype(f32)
    r = lax.rsqrt(jnp.mean(v * v, axis=-1, keepdims=True) + norm_epsilon)
    one[...] = (v * r * TL[6:7, :].astype(f32)).astype(b16)
    keep(X, X_o)
    keep(one, one_o)
    keep(TL, TL_o)

    for ref in kv_fan.arrivals():
        forwards.append(net.send(ref, ref, twin))
    for pieces in (q_fan, o_fan):
        pieces.round()
        pieces.forward()
    for copy in forwards:
        net.got(copy)
    cosine, sine = cos[...], sin[...]
    a = one[...]
    for t in range(4):
        out = dot(a, WKV[:, 256 * t : 256 * t + 256])
        for u in range(2):
            tile = out[:, 128 * u : 128 * u + 128]
            if t < 2:
                tile = tile * cosine + partner_lanes(tile) * sine
            KV[y, :, 256 * t + 128 * u : 256 * t + 128 * u + 128] = tile.astype(b16)
    kv_ring = Ring(net, lambda n, h: KV.at[n, pl.ds(h * 128, 128)], yr, yl, y)
    keep(WKV, WKV_o)

    for load in loads[3:]:
        load.wait()
    lane = lax.broadcasted_iota(jnp.int32, (128, 128), 1)
    mine_first = c == 0
    for part, src in enumerate((gate32, up32)):
        for b in range(3):
            one_e, two_e = src[2 * b], src[2 * b + 1]
            first = jnp.where(mine_first, one_e, pltpu.roll(one_e, SLICE, 1))
            second = jnp.where(mine_first, pltpu.roll(two_e, SLICE, 1), two_e)
            at = slice(128 * (3 * part + b), 128 * (3 * part + b) + 128)
            gd16[at, :] = jnp.where(lane < SLICE, first, second).astype(b16)
    gd16[2 * WIDE :, :] = dn32[...].reshape(WIDE, 128).astype(b16)
    gd_own = net.local(gd16, GD.at[shards[0]])
    gd_over = net.send(gd16, GD.at[shards[0]], over)
    g_in = net.send(cot.at[1 - z_hi], G.at[slot, half_rows], partner)
    g_own = net.local(cot.at[z_hi], G.at[slot, half_rows])
    for copy in more:
        copy.wait()

    rings, twins = [], []
    for pieces, whole in ((q_fan, WQ), (o_fan, WO)):
        for _ in pieces.arrivals():
            pass
        part = lambda n, h, whole=whole: whole.at[pl.ds(h * 512, 512), lanes(n * 2 + c)]
        rings.append(Ring(net, part, xr, xl, x))
        twins.append([net.send(whole.at[:, lanes(slot)], whole.at[:, lanes(slot)], twin)])
    kv_ring.relay()
    rings[0].relay()
    rings[1].relay()
    gd_own.wait()
    gd_part = lambda row: lambda n, h: GD.at[row + n, pl.ds(h * 576, 576)]
    gd_rings = [Ring(net, gd_part(rows[0]), yr, yl, y)]
    net.got(gd_over)
    gd_rings.append(Ring(net, gd_part(rows[1]), yr, yl, y))
    g_own.wait()
    net.got(g_in)
    g_ring = Ring(net, lambda n, h: G.at[n * 2 + c, pl.ds(h * 128, 128)], xr, xl, x)
    net.send(G.at[slot], G.at[slot], twin)

    def share(n, whole):
        rings[n].done()
        for d in range(1, 4):
            tile = whole.at[:, lanes(lax.rem(x + d, 4) * 2 + c)]
            twins[n].append(net.send(tile, tile, twin))

    share(0, WQ)
    for copy in twins[0]:
        net.got(copy)
    for t in range(4):
        out = dot(a, WQ[:, 256 * t : 256 * t + 256])
        for u in range(2):
            tile = out[:, 128 * u : 128 * u + 128]
            tile = tile * cosine + partner_lanes(tile) * sine
            q[:, 256 * t + 128 * u : 256 * t + 128 * u + 128] = (tile * 0.125).astype(b16)
    keep(q, q_o)
    keep(WQ, WQ_o)
    kv_ring.done()
    keep(KV, KV_o)

    low_bias = jnp.concatenate([bias[:128, :512]] * 2, axis=0)
    high_bias = jnp.concatenate([bias[128:, :]] * 2, axis=0)
    for pair in range(4):
        cols = slice(128 * pair, 128 * pair + 128)
        vcols = slice(512 + 128 * pair, 512 + 128 * pair + 128)
        keys = [KV[:, :128, cols].reshape(512, 128), KV[:, 128:, cols].reshape(512, 128)]
        vals = [KV[:, :128, vcols].reshape(512, 128), KV[:, 128:, vcols].reshape(512, 128)]
        keys_all = jnp.concatenate(keys, axis=0)
        vals_all = jnp.concatenate(vals, axis=0)
        for half in range(2):
            cols = slice(256 * pair + 128 * half, 256 * pair + 128 * half + 128)
            low, high = spread(q[:, cols].astype(f32), half)
            outs = []
            for qq, kk, vv, bb, at_p in (
                (low, keys[0], vals[0], low_bias, slice(0, 512)),
                (high, keys_all, vals_all, high_bias, slice(512, 1536)),
            ):
                s = dot_t(qq, kk) + bb
                top = jnp.max(s, axis=-1, keepdims=True)
                e = jnp.exp(s - top)
                probs = (e * (1.0 / jnp.sum(e, axis=-1, keepdims=True))).astype(b16)
                probs_all[2 * pair + half, :, at_p] = probs
                outs.append(dot(probs, vv))
            heads[:, cols] = collect(outs[0], outs[1], half).astype(b16)
        keep(probs_all.at[pl.ds(2 * pair, 2)], P_o.at[pl.ds(2 * pair, 2)])
        if pair == 0:
            share(1, WO)
        if pair == 1:
            g_ring.relay()
            gd_rings[0].relay()
        if pair == 2:
            gd_rings[1].relay()
    keep(heads, heads_o)

    for copy in twins[1]:
        net.got(copy)
    keep(WO, WO_o)
    all_heads = heads[...]
    for t in range(4):
        cols = slice(256 * t, 256 * t + 256)
        hidden[:, cols] = X[:, cols].astype(f32) + dot(all_heads, WO[:, cols])
    h = hidden[...]
    r = lax.rsqrt(jnp.mean(h * h, axis=-1, keepdims=True) + norm_epsilon)
    a = (h * r * TL[7:8, :].astype(f32)).astype(b16)
    act[:, :D] = a
    logits = dot_t(a, router_rows(TL[...]))
    net.got(r_in)
    routes = R[...]
    hots = [one_hot(routes, k) for k in range(TOPK)]
    picked = [jnp.sum(hot * logits, axis=-1, keepdims=True) for hot in hots]
    top = jnp.maximum(picked[0], picked[1])
    powers = [jnp.exp(v - top) for v in picked]
    total = powers[0] + powers[1]
    mixing = hots[0] * (powers[0] / total) + hots[1] * (powers[1] / total)
    big = mixing.astype(b16).astype(f32)
    act[:, D:] = (big + pltpu.roll(mixing - big, 16, 1)).astype(b16)
    keep(hidden, hidden_o)
    keep(act, act_o)
    keep(R, R_o)
    g_ring.done()
    for d in range(1, 4):
        block = G.at[lax.rem(x + d, 4) * 2 + c]
        net.send(block, block, twin)
    for ring in gd_rings:
        ring.done()
    for copy in kept:
        copy.wait()
    net.finish()


def front(*arrays):
    V = pltpu.VMEM
    return pl.pallas_call(
        front_kernel,
        out_shape=(
            shape((ROWS, D), b16),
            shape((ROWS, 128), f32),
            shape((8, ROWS, D), b16),
            shape((D, D), b16),
            shape((D, D), b16),
            shape((D, D), b16),
            shape((8, 3 * WIDE, 128), b16),
            shape((16, D), b16),
            shape((ROWS, D), b16),
            shape((ROWS, D), b16),
            shape((4, ROWS, D), b16),
            shape((8, ROWS, 1536), b16),
            shape((ROWS, D), b16),
            shape((ROWS, D), f32),
            shape((ROWS, D + 128), b16),
        ),
        in_specs=[ANY] * 9 + [VMEM] * 3,
        out_specs=(ANY,) * 15,
        scratch_shapes=[
            V((ROWS, D), b16),
            V((ROWS, 128), f32),
            V((D, D), b16),
            V((D, D), b16),
            V((D, D), b16),
            V((16, D), b16),
            V((ROWS, D), b16),
            V((ROWS, D), b16),
            V((4, ROWS, D), b16),
            V((8, ROWS, 1536), b16),
            V((ROWS, D), b16),
            V((ROWS, D), f32),
            V((ROWS, D + 128), b16),
            V((ROWS, D), f32),
            V((128, 128), f32),
            V((128, 512), f32),
            V((128, 128), f32),
            V((EXPERTS, 128, 128), f32),
            V((EXPERTS, 128, 128), f32),
            V((EXPERTS, SLICE, 128), f32),
            V((128, 128), b16),
            V((128, 512), b16),
            V((128, 128), b16),
            V((3 * WIDE, 128), b16),
            V((ROWS, 128), f32),
            V((ROWS, 128), f32),
            V((16, 128), f32),
            V((16, 128), b16),
        ]
        + sems(96, 40),
        compiler_params=params(0),
        name="front",
    )(*arrays)


def experts_kernel(
    act, G, GD, total, grads_o, PO,
    ACT, g, gu, dn, back, tw, tmp, got, out, gu_acc, dn_acc, grads,
    ss, rs, ls,
):
    x, y, z, c = place()
    slot = x * 2 + c
    net = Net(ss, rs, ls)
    loads = {}
    loads[0] = [net.local(act, ACT.at[slot])]
    loads[0] += [net.local(GD.at[:, pl.ds(128 * b, 128)], gu.at[:, :, pl.ds(128 * b, 128)]) for b in range(6)]
    loads[0] += [net.local(GD.at[n, pl.ds(2 * WIDE, WIDE)], dn.at[:, pl.ds(128 * n, 128)]) for n in range(8)]
    chips = {d: lax.rem(x + d, 4) for d in range(4)}
    mine = {d: chips[d] * 2 + c for d in range(4)}
    other = {d: chips[d] * 2 + 1 - c for d in range(4)}
    for d in (0, 3, 2, 1):
        loads.setdefault(d, []).extend(net.local(G.at[n], g.at[n]) for n in (mine[d], other[d]))
    xr, xl, twin = dev(x + 1, y, z, c), dev(x - 1, y, z, c), dev(x, y, z, 1 - c)
    net.greet([xr, xl, twin])
    for copy in loads[0]:
        copy.wait()
    lo, hi = pl.ds(0, 128), pl.ds(128, 128)
    before, across, after = chips[3], chips[2], chips[1]
    home_block = ACT.at[slot]
    swap = net.send(home_block, home_block, twin)
    a1 = net.send(ACT.at[slot, lo], ACT.at[slot, lo], xr)
    b1 = net.send(ACT.at[slot, hi], ACT.at[slot, hi], xl)
    gu_acc[...] = jnp.zeros_like(gu_acc)
    dn_acc[...] = jnp.zeros_like(dn_acc)
    row = lax.broadcasted_iota(jnp.int32, (128, WIDE), 0)
    lane = lax.broadcasted_iota(jnp.int32, (128, WIDE), 1)
    pick = ((row % 16 == lane // SLICE) & (row < 32)).astype(b16)
    kept = []

    def compute(parts):
        both = lambda ref, cols: jnp.concatenate([ref[n, at, cols] for n, at in parts], axis=0)
        a = both(ACT, slice(0, D))
        mix = dot(both(ACT, slice(D, D + 128)), pick)
        gt = both(g, slice(0, D))
        weights = gu[...].reshape(D, 2 * WIDE)
        h = dot(a, weights)
        gate, up = h[:, :WIDE], h[:, WIDE:]
        gw = dot_t(gt, dn[...])
        s = 1.0 / (1.0 + jnp.exp(-gate))
        silu = gate * s
        inner = silu * up
        scaled = (inner * mix).astype(b16)
        gi = gw * mix
        ggu = jnp.concatenate(
            [(gi * up * s * (1.0 + gate * (1.0 - s))).astype(b16), (gi * silu).astype(b16)], axis=1
        )
        down = dot_t(ggu, weights).astype(b16)
        dots = dot_t((inner * gw).astype(b16), pick).astype(b16)
        terms = dot(scaled, dn[...]).astype(b16)
        for i, (n, at) in enumerate(parts):
            rows = slice(128 * i, 128 * i + 128)
            back[n, at, :D] = down[rows]
            back[n, at, D:] = dots[rows]
            out[n, at] = terms[rows]
            kept.append(net.local(out.at[n, at], PO.at[n, at]))
        gu_acc[...] += t_dot(a, ggu)
        dn_acc[...] += t_dot(scaled, gt)

    def add(dst, one, two):
        add_rows(dst, one, two, dst.shape[0], 16)

    def unit(d, at, arrive):
        net.got(arrive)
        compute([(mine[d], at), (other[d], at)])
        return net.send(back.at[other[d], at], tw.at[chips[d], at], twin)

    def settle(d, at, sent):
        net.got(sent)
        add(tw.at[chips[d], at], tw.at[chips[d], at], back.at[mine[d], at])

    def forward(d, at, arrive):
        net.got(arrive)
        block = ACT.at[mine[d], at]
        return net.send(block, block, twin)

    compute([(mine[0], lo), (mine[0], hi)])
    net.got(swap)
    compute([(other[0], lo), (other[0], hi)])
    home = net.send(back.at[other[0]], tw.at[x], twin)
    net.got(a1)
    a3 = net.send(ACT.at[mine[3], lo], ACT.at[mine[3], lo], xr)
    net.got(b1)
    b3 = net.send(ACT.at[mine[1], hi], ACT.at[mine[1], hi], xl)
    a2 = net.send(ACT.at[slot, hi], ACT.at[slot, hi], xr)
    b2 = net.send(ACT.at[slot, lo], ACT.at[slot, lo], xl)
    f1, f2 = (net.send(ACT.at[mine[d], at], ACT.at[mine[d], at], twin) for d, at in ((3, lo), (1, hi)))
    for d in (3, 1, 2):
        for copy in loads[d]:
            copy.wait()
    u1 = unit(3, lo, f1)
    u2 = unit(1, hi, f2)
    f3 = forward(2, lo, a3)
    f4 = forward(2, hi, b3)
    settle(3, lo, u1)
    last = [net.send(tw.at[before, lo], got.at[1, lo], xl)]
    net.got(home)
    add(tw.at[x], tw.at[x], back.at[mine[0]])
    u3 = unit(2, lo, f3)
    settle(1, hi, u2)
    last.append(net.send(tw.at[after, hi], got.at[0, hi], xr))
    u4 = unit(2, hi, f4)
    f5 = forward(3, hi, a2)
    f6 = forward(1, lo, b2)
    settle(2, lo, u3)
    s1 = net.send(tw.at[across, lo], tmp.at[0], xr)
    u5 = unit(3, hi, f5)
    settle(2, hi, u4)
    s2 = net.send(tw.at[across, hi], tmp.at[1], xl)
    u6 = unit(1, lo, f6)
    settle(3, hi, u5)
    settle(1, lo, u6)
    net.got(s1)
    add(tmp.at[0], tmp.at[0], tw.at[after, lo])
    last.append(net.send(tmp.at[0], got.at[0, lo], xr))
    net.got(s2)
    add(tmp.at[1], tmp.at[1], tw.at[before, hi])
    last.append(net.send(tmp.at[1], got.at[1, hi], xl))
    for n in range(8):
        at = slice(128 * n, 128 * n + 128)
        for b in range(6):
            grads[n, 128 * b : 128 * b + 128] = gu_acc[at, 128 * b : 128 * b + 128].astype(b16)
        for b in range(3):
            rows = slice(128 * (6 + b), 128 * (6 + b) + 128)
            grads[n, rows] = dn_acc[128 * b : 128 * b + 128, at].astype(b16)
    kept.append(net.local(grads, grads_o))
    for copy in last:
        net.got(copy)

    def body(i, carry):
        at = pl.ds(pl.multiple_of(i * 16, 16), 16)
        total[at] = tw[x, at].astype(f32) + got[0, at].astype(f32) + got[1, at].astype(f32)
        return carry

    lax.fori_loop(0, ROWS // 16, body, 0)
    for copy in kept:
        copy.wait()
    net.finish()


def experts(act, G, GD):
    V = pltpu.VMEM
    wide = D + 128
    return pl.pallas_call(
        experts_kernel,
        out_shape=(shape((ROWS, wide), f32), shape((8, 9 * 128, 128), b16), shape((8, ROWS, D), b16)),
        in_specs=[ANY] * 3,
        out_specs=(VMEM, ANY, ANY),
        scratch_shapes=[
            V((8, ROWS, wide), b16),
            V((8, ROWS, D), b16),
            V((8, 128, 2 * WIDE), b16),
            V((WIDE, D), b16),
            V((8, ROWS, wide), b16),
            V((4, ROWS, wide), b16),
            V((2, ROWS // 2, wide), b16),
            V((2, ROWS, wide), b16),
            V((8, ROWS, D), b16),
            V((D, 2 * WIDE), f32),
            V((WIDE, D), f32),
            V((8, 9 * 128, 128), b16),
        ]
        + sems(40, 48),
        compiler_params=params(2),
        name="experts",
    )(act, G, GD)


def back_kernel(
    total_i, hidden_i, act_i, G, TL_i, R_i, heads_i, WO_i, X_i, one_i, q_i, KV_i, P_i, WQ_i, WKV_i, grads_i, PO, cos_t, sin_t,
    OUT, gin, ALLM_o, late_o, kvg_o, small,
    total, hidden, act, g, TL, R, heads, WO, X, one, q, KV, P, WQ, WKV, gr, po,
    po_tw, po_tmp, po_got, og, og_tw, og_tmp, og_got, qg, qg_tw, qg_tmp, qg_got,
    dkv, k_tmp, k_got, gh, ghi, gp, y_tmp, y_got, z_got, ALLM, late, ob, cos, sin,
    ss, rs, ls,
):
    x, y, z, c = place()
    z_hi, z_lo = z // 2, lax.rem(z, 2)
    slot = x * 2 + c
    net = Net(ss, rs, ls)
    kept = []
    first = [
        net.local(*pair)
        for pair in (
            (total_i, total), (hidden_i, hidden), (act_i, act), (TL_i, TL), (R_i, R),
            (G.at[slot], g), (heads_i, heads), (WO_i, WO),
        )
    ]
    grad_load = net.local(grads_i, gr)
    po_load = [net.local(PO.at[n * 2 + c], po.at[n]) for n in range(4)]
    second = [
        net.local(*pair)
        for pair in ((KV_i, KV), (q_i, q), (P_i, P), (one_i, one), (X_i, X), (WQ_i, WQ), (WKV_i, WKV))
    ]
    second += [
        net.local(src.at[lanes(4 * h + y)], dst.at[pl.ds(128 * h, 128)])
        for src, dst in ((cos_t, cos), (sin_t, sin))
        for h in range(2)
    ]
    twin = dev(x, y, z, 1 - c)
    xr, xl = dev(x + 1, y, z, c), dev(x - 1, y, z, c)
    yr, yl = dev(x, y + 1, z, c), dev(x, y - 1, z, c)
    zr, zl, z2 = dev(x, y, z + 1, c), dev(x, y, z - 1, c), dev(x, y, z + 2, c)
    net.greet([twin, xr, xl, yr, yl, zr, zl, z2])
    grad_load.wait()
    y_rings = [
        Scatter(net, lambda n, h=h: gr.at[h * 4 + n], y_tmp.at[h], y_got.at[h], yr, yl, y, 1152, 64)
        for h in range(2)
    ]
    po_in = [net.send(PO.at[n * 2 + 1 - c], po_tw.at[n], twin) for n in range(4)]

    for copy in first:
        copy.wait()
    h = hidden[...]
    a = act[:, :D]
    mix = act[:, D:].astype(f32)
    lane = lax.broadcasted_iota(jnp.int32, (ROWS, 128), 1)
    mixing = jnp.where(lane < 16, mix + pltpu.roll(mix, 112, 1), 0.0)
    dg = total[:, D:]
    routes = R[...]
    hots = [one_hot(routes, k) for k in range(TOPK)]
    probs = [jnp.sum(hot * mixing, axis=-1, keepdims=True) for hot in hots]
    dgs = [jnp.sum(hot * dg, axis=-1, keepdims=True) for hot in hots]
    mean = probs[0] * dgs[0] + probs[1] * dgs[1]
    grad_logits = sum(hot * (p * (d - mean)) for hot, p, d in zip(hots, probs, dgs)).astype(b16)
    ga = total[:, :D] + dot(grad_logits, router_rows(TL[...]))
    small[0:6, :] = t_dot(grad_logits, a)[0:6, :]
    r = lax.rsqrt(jnp.mean(h * h, axis=-1, keepdims=True) + norm_epsilon)
    u = ga * TL[7:8, :].astype(f32)
    small[6:7, :] = jnp.sum(ga * h * r, axis=0, keepdims=True)
    gh[...] = g[...].astype(f32) + r * (u - h * (r * r * jnp.mean(u * h, axis=-1, keepdims=True)))
    low = gh[...].astype(b16)
    ghi[...] = dot_t(low, WO[...]).astype(b16)

    for n in range(4):
        net.got(po_in[n])
        po_load[n].wait()
        add_rows(po_tw.at[n], po_tw.at[n], po.at[n], ROWS, 16)
    out_ring = Scatter(net, lambda n: po_tw.at[n], po_tmp, po_got, xr, xl, x, ROWS, 16)

    def weight_grad(dst, left, right):
        for t in range(4):
            piece = t_dot(left, right[:, 256 * t : 256 * t + 256])
            dst[2 * t] = piece[:, :128].astype(b16)
            dst[2 * t + 1] = piece[:, 128:].astype(b16)

    weight_grad(og, heads[...], low)
    og_in = [net.send(og.at[n * 2 + 1 - c], og_tw.at[n], twin) for n in range(4)]
    for ring in y_rings:
        ring.relay()
    for copy in second:
        copy.wait()
    cosine, sine = cos[...], sin[...]

    def pair(n):
        cols = slice(128 * n, 128 * n + 128)
        vcols = slice(512 + 128 * n, 512 + 128 * n + 128)
        keys = [KV[:, :128, cols].reshape(512, 128), KV[:, 128:, cols].reshape(512, 128)]
        vals = [KV[:, :128, vcols].reshape(512, 128), KV[:, 128:, vcols].reshape(512, 128)]
        keys_all = jnp.concatenate(keys, axis=0)
        vals_all = jnp.concatenate(vals, axis=0)
        sums = None
        for half in range(2):
            at = slice(256 * n + 128 * half, 256 * n + 128 * half + 128)
            q_low, q_high = spread(q[:, at].astype(f32), half)
            do_low, do_high = spread(ghi[:, at].astype(f32), half)
            outs, terms = [], []
            for qq, dd, kk, vv, at_p in (
                (q_low, do_low, keys[0], vals[0], slice(0, 512)),
                (q_high, do_high, keys_all, vals_all, slice(512, 1536)),
            ):
                pr = P[2 * n + half, :, at_p]
                dp = dot_t(dd, vv)
                pf = pr.astype(f32)
                prod = pf * dp
                ds = (prod - pf * jnp.sum(prod, axis=-1, keepdims=True)).astype(b16)
                outs.append(dot(ds, kk) * 0.125)
                terms.append((t_dot(ds, qq), t_dot(pr, dd)))
            tile = collect(outs[0], outs[1], half)
            gp[:, at] = (tile * cosine - partner_lanes(tile) * sine).astype(b16)
            sums = terms if half == 0 else [(i + k, j + m) for (i, j), (k, m) in zip(sums, terms)]
        for part, where in enumerate((cols, vcols)):
            lows, whole = sums[0][part], sums[1][part]
            dkv[:, :128, where] = (lows + whole[:512]).reshape(4, 128, 128).astype(b16)
            dkv[:, 128:, where] = whole[512:].reshape(4, 128, 128).astype(b16)

    pair(0)
    out_ring.relay()
    for n in range(4):
        net.got(og_in[n])
        add_rows(og_tw.at[n], og_tw.at[n], og.at[n * 2 + c], 1024, 64)
    og_ring = Scatter(net, lambda n: og_tw.at[n], og_tmp, og_got, xr, xl, x, 1024, 64)
    pair(1)
    pair(2)
    for n, ring in enumerate(y_rings):
        ring.done()
        ring.settle(gr.at[n * 4 + y], 1152, 64)

    def piece(zz):
        return gr.at[(zz // 2) * 4 + y, pl.ds(pl.multiple_of(lax.rem(zz, 2) * 576, 576), 576)]

    z_in = [
        net.send(piece(lax.rem(z + 1, 4)), z_got.at[0], zr),
        net.send(piece(lax.rem(z + 3, 4)), z_got.at[1], zl),
        net.send(piece(lax.rem(z + 2, 4)), z_got.at[2], z2),
    ]
    pair(3)
    k_ring = Scatter(net, lambda n: dkv.at[n], k_tmp, k_got, yr, yl, y, ROWS, 16)

    acts = one[...]
    weight_grad(qg, acts, gp[:, :D])
    qg_in = [net.send(qg.at[n * 2 + 1 - c], qg_tw.at[n], twin) for n in range(4)]
    og_ring.relay()
    for copy in z_in:
        net.got(copy)
    base = pl.multiple_of(z_lo * 576, 576)

    def settle_z(i, carry):
        at = pl.ds(pl.multiple_of(i * 64, 64), 64)
        here = pl.ds(pl.multiple_of(base + i * 64, 64), 64)
        v = gr[z_hi * 4 + y, here].astype(f32)
        for n in range(3):
            v = v + z_got[n, at].astype(f32)
        ALLM[slot, here] = v.astype(b16)
        return carry

    lax.fori_loop(0, 9, settle_z, 0)
    done = ALLM.at[slot, pl.ds(base, 576)]
    hop = net.send(done, done, dev(x, y, z + 1 - 2 * z_lo, c))
    ga = dot_t(gp[:, :D], WQ[...])
    for n in range(4):
        net.got(qg_in[n])
        add_rows(qg_tw.at[n], qg_tw.at[n], qg.at[n * 2 + c], 1024, 64)
    qg_ring = Scatter(net, lambda n: qg_tw.at[n], qg_tmp, qg_got, xr, xl, x, 1024, 64)
    out_ring.done()
    ob[...] = (hidden[...] + out_ring.term(slice(None))).astype(b16)
    rows_of = lambda n: pl.ds(pl.multiple_of(n * 128, 128), 128)
    net.send(ob.at[rows_of(1 - z_hi)], OUT.at[z_hi], z2)
    kept.append(net.local(ob.at[rows_of(z_hi)], OUT.at[z_hi]))
    k_ring.relay()
    net.got(hop)
    net.send(ALLM.at[slot], ALLM.at[slot], twin)
    m_ring = Ring(net, lambda n, h: ALLM.at[n * 2 + c, pl.ds(h * 576, 576)], xr, xl, x)
    og_ring.done()
    og_ring.settle(late.at[0], 1024, 64)
    qg_ring.relay()

    k_ring.done()
    for t in range(8):
        at = slice(128 * t, 128 * t + 128)
        tile = dkv[y, :, at].astype(f32) + k_got[0, :, at].astype(f32) + k_got[1, :, at].astype(f32)
        if t < 4:
            tile = tile * cosine - partner_lanes(tile) * sine
        gp[:, D + 128 * t : D + 128 * t + 128] = tile.astype(b16)
    for copy in og_in:
        net.gone(copy)
    weight_grad(og, acts, gp[:, D:])
    kept.append(net.local(og, kvg_o))
    m_ring.relay()
    ga = ga + dot_t(gp[:, D:], WKV[...])
    v = X[...].astype(f32)
    r = lax.rsqrt(jnp.mean(v * v, axis=-1, keepdims=True) + norm_epsilon)
    u = ga * TL[6:7, :].astype(f32)
    small[7:8, :] = jnp.sum(ga * v * r, axis=0, keepdims=True)
    gin[...] = gh[...] + r * (u - v * (r * r * jnp.mean(u * v, axis=-1, keepdims=True)))
    qg_ring.done()
    qg_ring.settle(late.at[1], 1024, 64)
    kept.append(net.local(late, late_o))
    m_ring.done()
    for d in range(1, 4):
        block = ALLM.at[lax.rem(x + d, 4) * 2 + c]
        net.send(block, block, twin)
    for copy in kept:
        copy.wait()
    net.finish()
    last = net.local(ALLM, ALLM_o)
    last.wait()


def back(*arrays):
    V = pltpu.VMEM
    wide = D + 128
    return pl.pallas_call(
        back_kernel,
        out_shape=(
            shape((2, 128, D), b16),
            shape((ROWS, D), f32),
            shape((8, 1152, 128), b16),
            shape((2, D, 128), b16),
            shape((8, D, 128), b16),
            shape((8, D), f32),
        ),
        in_specs=[ANY] * 19,
        out_specs=(ANY, VMEM, ANY, ANY, ANY, VMEM),
        scratch_shapes=[
            V((ROWS, wide), f32),
            V((ROWS, D), f32),
            V((ROWS, wide), b16),
            V((ROWS, D), b16),
            V((16, D), b16),
            V((ROWS, 128), f32),
            V((ROWS, D), b16),
            V((D, D), b16),
            V((ROWS, D), b16),
            V((ROWS, D), b16),
            V((ROWS, D), b16),
            V((4, ROWS, D), b16),
            V((8, ROWS, 1536), b16),
            V((D, D), b16),
            V((D, D), b16),
            V((8, 1152, 128), b16),
            V((4, ROWS, D), b16),
            V((4, ROWS, D), b16),
            V((2, ROWS // 2, D), b16),
            V((2, ROWS, D), b16),
        ]
        + [
            V((8, D, 128), b16),
            V((4, D, 128), b16),
            V((2, D // 2, 128), b16),
            V((2, D, 128), b16),
        ]
        * 2
        + [
            V((4, ROWS, D), b16),
            V((2, ROWS // 2, D), b16),
            V((2, ROWS, D), b16),
            V((ROWS, D), f32),
            V((ROWS, D), b16),
            V((ROWS, 2 * D), b16),
            V((2, 2, 576, 128), b16),
            V((2, 2, 1152, 128), b16),
            V((3, 576, 128), b16),
            V((8, 1152, 128), b16),
            V((2, D, 128), b16),
            V((ROWS, D), b16),
            V((ROWS, 128), f32),
            V((ROWS, 128), f32),
        ]
        + sems(80, 36),
        compiler_params=params(3, 60),
        name="back",
    )(*arrays)


def reduce_kernel(
    kvg, late, small, gin,
    ALL, SM, GIN,
    mine, k_tw, k_tmp, k_got, y_tmp, y_got, y_in, z_got, s_twin, s_x, s_y, s_z, gin_low, gin_got,
    ss, rs, ls,
):
    x, y, z, c = place()
    z_hi, z_lo = z // 2, lax.rem(z, 2)
    slot = x * 2 + c
    net = Net(ss, rs, ls)
    twin = dev(x, y, z, 1 - c)
    xr, xl, x2 = dev(x + 1, y, z, c), dev(x - 1, y, z, c), dev(x + 2, y, z, c)
    yr, yl, y2 = dev(x, y + 1, z, c), dev(x, y - 1, z, c), dev(x, y + 2, z, c)
    zr, zl, z2 = dev(x, y, z + 1, c), dev(x, y, z - 1, c), dev(x, y, z + 2, c)
    net.greet([twin, xr, xl, x2, yr, yl, y2, zr, zl, z2])
    rows_of = lambda n: pl.ds(pl.multiple_of(n * 128, 128), 128)
    k_in = [net.send(kvg.at[n * 2 + 1 - c], k_tw.at[n], twin) for n in range(4)]
    sm = net.send(small, s_twin, twin)
    gin_low[...] = gin[rows_of(1 - z_hi)].astype(b16)
    swap = net.send(gin_low, gin_got, z2)
    for n in range(8):
        for b in range(2):
            mine[n, 128 * b : 128 * b + 128] = late[b, 128 * n : 128 * n + 128]
    early = pl.ds(0, 256)
    y_rings = [
        Scatter(net, lambda n, h=h: mine.at[h * 4 + n, early], y_tmp.at[h], y_got.at[h], yr, yl, y, 256, 64)
        for h in range(2)
    ]
    for n in range(4):
        net.got(k_in[n])
        add_rows(k_tw.at[n], k_tw.at[n], kvg.at[n * 2 + c], 1024, 64)
    k_ring = Scatter(net, lambda n: k_tw.at[n], k_tmp, k_got, xr, xl, x, 1024, 64)
    net.got(sm)
    s_twin[...] += small[...]
    sx = [net.send(s_twin, s_x.at[i], p) for i, p in enumerate((xr, xl, x2))]
    for ring in y_rings:
        ring.relay()
    k_ring.relay()
    GIN[z_hi] = gin[rows_of(z_hi)]
    for copy in sx:
        net.got(copy)
    s_y[0] = s_twin[...] + s_x[0] + s_x[1] + s_x[2]
    sy = [net.send(s_y.at[0], s_y.at[1 + i], p) for i, p in enumerate((yr, yl, y2))]
    for n, ring in enumerate(y_rings):
        ring.done()
        ring.settle(mine.at[n * 4 + y, early], 256, 64)
    k_ring.done()
    for n in range(8):
        mine[n, 256:384] = k_ring.term(slice(128 * n, 128 * n + 128)).astype(b16)
    last = pl.ds(256, 128)
    y_got3 = [
        net.send(mine.at[h * 4 + lax.rem(y + d, 4), last], y_in.at[h, i], p)
        for h in range(2)
        for i, (d, p) in enumerate(((1, yr), (3, yl), (2, y2)))
    ]
    for copy in sy:
        net.got(copy)
    s_z[0] = s_y[0] + s_y[1] + s_y[2] + s_y[3]
    sz = [net.send(s_z.at[0], s_z.at[1 + i], p) for i, p in enumerate((zr, zl, z2))]
    for copy in y_got3:
        net.got(copy)
    for h in range(2):
        v = mine[h * 4 + y, 256:384].astype(f32)
        for i in range(3):
            v = v + y_in[h, i].astype(f32)
        mine[h * 4 + y, 256:384] = v.astype(b16)

    def piece(zz):
        return mine.at[(zz // 2) * 4 + y, pl.ds(pl.multiple_of(lax.rem(zz, 2) * 192, 192), 192)]

    z_in = [
        net.send(piece(lax.rem(z + 1, 4)), z_got.at[0], zr),
        net.send(piece(lax.rem(z + 3, 4)), z_got.at[1], zl),
        net.send(piece(lax.rem(z + 2, 4)), z_got.at[2], z2),
    ]
    for copy in z_in:
        net.got(copy)
    base = pl.multiple_of(z_lo * 192, 192)
    here = pl.ds(base, 192)
    v = mine[z_hi * 4 + y, here].astype(f32)
    for i in range(3):
        v = v + z_got[i].astype(f32)
    ALL[slot, here] = v.astype(b16)
    done = ALL.at[slot, here]
    net.got(net.send(done, done, dev(x, y, z + 1 - 2 * z_lo, c)))
    block = ALL.at[slot]
    net.send(block, block, twin)
    spread_x = [net.send(block, block, p) for p in (xr, xl, x2)]
    for copy in sz:
        net.got(copy)
    SM[...] = s_z[0] + s_z[1] + s_z[2] + s_z[3]
    net.got(swap)
    GIN[1 - z_hi] = gin_got[...].astype(f32)
    for copy, d in zip(spread_x, (3, 1, 2)):
        net.got(copy)
        block = ALL.at[lax.rem(x + d, 4) * 2 + c]
        net.send(block, block, twin)
    net.finish()


def reduce_late(kvg, late, small, gin):
    V = pltpu.VMEM
    return pl.pallas_call(
        reduce_kernel,
        out_shape=(shape((8, 384, 128), b16), shape((8, D), f32), shape((2, 128, D), f32)),
        in_specs=[VMEM] * 4,
        out_specs=(VMEM,) * 3,
        scratch_shapes=[
            V((8, 384, 128), b16),
            V((4, D, 128), b16),
            V((2, D // 2, 128), b16),
            V((2, D, 128), b16),
            V((2, 2, 128, 128), b16),
            V((2, 2, 256, 128), b16),
            V((2, 3, 128, 128), b16),
            V((3, 192, 128), b16),
            V((8, D), f32),
            V((3, 8, D), f32),
            V((4, 8, D), f32),
            V((4, 8, D), f32),
            V((128, D), b16),
            V((128, D), b16),
        ]
        + sems(64),
        compiler_params=params(4),
        name="reduce_late",
    )(kvg, late, small, gin)


def rotary():
    freqs = np.float32(10000.0) ** (-np.arange(HD // 2, dtype=np.float32) * np.float32(2.0) / np.float32(HD))
    angles = np.arange(D, dtype=np.float32)[:, None] * freqs[None, :]
    cos, sin = np.cos(angles), np.sin(angles)
    return np.concatenate([cos] * 4, axis=1), np.concatenate([-sin, sin] * 2, axis=1)


def learning_rates():
    return (D ** (-0.5), 8.0 * D ** (-0.5), D ** (-0.5), 2.0 * FF ** (-0.5), 0.5 * D ** (-0.5), 0.5)


def adamw(weight, gradient, moment, square, step_rate, decay_rate):
    moment_new = beta_one * moment + (1.0 - beta_one) * gradient
    square_new = beta_two * square + (1.0 - beta_two) * gradient * gradient
    corrected = moment_new / (1.0 - beta_one**STEP)
    spread_by = jnp.sqrt(square_new / (1.0 - beta_two**STEP)) + adam_epsilon
    updated = weight - step_rate * (corrected / spread_by + decay_rate * weight)
    return [moment_new, square_new, updated]


def update_kernel(*refs):
    grads, late, ins, outs = refs[0], refs[1], refs[2:14], refs[14:]
    step = pl.program_id(0)
    rates = learning_rates()
    lane = lax.broadcasted_iota(jnp.int32, (128, 128), 1)

    def apply(n, at, grad, rate):
        m, v, w = adamw(ins[3 * n][at], grad, ins[3 * n + 1][at], ins[3 * n + 2][at], rate, 0.1)
        outs[3 * n][at], outs[3 * n + 1][at], outs[3 * n + 2][at] = m, v, w

    for b in range(3):

        @pl.when(step == b)
        def _():
            for part in range(2):
                for t in range(4):
                    one = grads[2 * t, 128 * (3 * part + b) : 128 * (3 * part + b) + 128].astype(f32)
                    two = grads[2 * t + 1, 128 * (3 * part + b) : 128 * (3 * part + b) + 128].astype(f32)
                    cols = slice(FF * part + 128 * t, FF * part + 128 * t + 128)
                    first = jnp.where(lane < SLICE, one, pltpu.roll(two, SLICE, 1))
                    second = jnp.where(lane < SLICE, pltpu.roll(one, SLICE, 1), two)
                    apply(0, (0, slice(None), cols), first, rates[2])
                    apply(0, (1, slice(None), cols), second, rates[2])

        @pl.when(step == 3 + b)
        def _():
            for k in range(8):
                grad = grads[k, 128 * (6 + b) : 128 * (6 + b) + 128].astype(f32)
                for e in range(2):
                    at = (e, slice(SLICE * k, SLICE * k + SLICE), slice(None))
                    apply(1, at, grad[SLICE * e : SLICE * e + SLICE], rates[3])

    for part in range(2):

        @pl.when(step == 6 + part)
        def _():
            for t in range(8):
                at = (slice(None), slice(128 * t, 128 * t + 128))
                apply(2, at, late[t, 128 * (1 + part) : 128 * (2 + part)].astype(f32), rates[0])

    @pl.when(step == 8)
    def _():
        for t in range(8):
            at = (slice(None), slice(128 * t, 128 * t + 128))
            apply(3, at, late[t, 0:128].astype(f32), rates[1])


def update(ALL, late, *arrays):
    specs = [
        pl.BlockSpec((2, 128, D), lambda i: (jnp.minimum(i, 2), 0, 0)),
        pl.BlockSpec((2, FF, 128), lambda i: (jnp.clip(i - 3, 0, 2), 0, 0)),
        pl.BlockSpec((128, D), lambda i: (0, jnp.clip(i - 6, 0, 1))),
        pl.BlockSpec((128, D), lambda i: (0, 0)),
    ]
    dims = [(EXPERTS, 128, D), (EXPERTS, FF, 128), (128, 2 * D), (128, D)]
    return pl.pallas_call(
        update_kernel,
        grid=(9,),
        out_shape=tuple(shape(d, f32) for d in dims for _ in range(3)),
        in_specs=[
            pl.BlockSpec((8, 1152, 128), lambda i: (0, 0, 0)),
            pl.BlockSpec((8, 384, 128), lambda i: (0, 0, 0)),
        ]
        + [spec for spec in specs for _ in range(3)],
        out_specs=tuple(spec for spec in specs for _ in range(3)),
        compiler_params=params(),
        name="update",
    )(ALL, late, *arrays)


def on_device(
    tokens, segments, routes, cotangent, w_qkv, w_out, w_gateup, w_down, w_router, w_gains,
    qkv_first, qkv_second, out_first, out_second, gateup_first, gateup_second, down_first, down_second,
    router_first, router_second, gains_first, gains_second,
):
    x, y, z, c = place()
    z_hi = z // 2
    shard = z_hi * 4 + y
    route_lanes = jnp.pad(routes.astype(f32), ((0, 0), (0, 0), (0, 126)))
    cos, sin = (jnp.asarray(table) for table in rotary())
    X, R, G, WQ, WKV, WO, GD, TL, act_one, q, KV, probs, heads, hidden, act = front(
        tokens, cotangent, route_lanes, w_qkv, w_out, w_gateup, w_down, cos, sin, w_router, w_gains, segments
    )
    total, grads, PO = experts(act, G, GD)
    layer_out, gin, ALLM, late, kvg, small = back(
        total, hidden, act, G, TL, R, heads, WO, X, act_one, q, KV, probs, WQ, WKV, grads, PO, cos, sin
    )
    late, SM, input_grad = reduce_late(kvg, late, small, gin)
    big = update(ALLM, late, w_gateup, gateup_first, gateup_second, w_down, down_first, down_second,
                 w_qkv, qkv_first, qkv_second, w_out, out_first, out_second)
    mine = lax.dynamic_slice_in_dim(SM, shard * 128, 128, 1)
    rates = learning_rates()
    router = adamw(w_router, mine[:6].T, router_first, router_second, rates[4], 0.1)
    gains = adamw(w_gains, jnp.stack([mine[7], mine[6]]), gains_first, gains_second, rates[5], 0.0)
    return (layer_out, input_grad, *big[6:9], *big[9:12], *big[0:3], *big[3:6], *router, *gains)


def solution(mesh):
    weight = [P("grp", None), P("grp", None), P(None, "grp", None), P(None, None, "grp"), P("grp", None), P(None, "grp")]
    tokens = P("rep", "grp", None)
    moments = [spec for spec in weight for _ in range(2)]
    results = [spec for spec in weight for _ in range(3)]
    return jax.shard_map(
        on_device,
        mesh=mesh,
        in_specs=(tokens, P("rep", None), tokens, tokens, *weight, *moments),
        out_specs=(tokens, tokens, *results),
        check_vma=False,
    )
```

```python
import jax
import jax.numpy as jnp
import numpy as np
from jax import lax
from jax.experimental import pallas as pl
from jax.experimental.pallas import tpu as pltpu
from jax.sharding import PartitionSpec as P

D = 1024
HQ = 16
HK = 8
HD = 64
FF = 512
EXPERTS = 6
TOPK = 2
STEP = 10
ROWS = 256
SLICE = 64
WIDE = EXPERTS * SLICE

beta_one = 0.9
beta_two = 0.95
adam_epsilon = 1e-08
norm_epsilon = 1e-06

f32 = jnp.float32
b16 = jnp.bfloat16
MESH = pl.DeviceIdType.MESH
ANY = pl.BlockSpec(memory_space=pl.ANY)
VMEM = pl.BlockSpec(memory_space=pltpu.VMEM)
MIB = 2**20


def place():
    rep = lax.axis_index("rep")
    grp = lax.axis_index("grp")
    z_lo, x, c = rep // 8, lax.rem(rep // 2, 4), lax.rem(rep, 2)
    z_hi, y = grp // 4, lax.rem(grp, 4)
    return x, y, z_hi * 2 + z_lo, c


def dev(x, y, z, c):
    x, y, z = lax.rem(x + 4, 4), lax.rem(y + 4, 4), lax.rem(z + 4, 4)
    return (lax.rem(z, 2) * 8 + x * 2 + c, (z // 2) * 4 + y)


class Net:
    def __init__(self, send_sems, recv_sems, local_sems):
        self.sems = (send_sems, recv_sems, local_sems)
        self.count = 0
        self.locals = 0
        self.open = []

    def greet(self, peers):
        bar = pltpu.get_barrier_semaphore()
        for peer in peers:
            pl.semaphore_signal(bar, inc=1, device_id=peer, device_id_type=MESH)
        pl.semaphore_wait(bar, len(peers))

    def send(self, src, dst, peer):
        copy = pltpu.make_async_remote_copy(
            src_ref=src,
            dst_ref=dst,
            send_sem=self.sems[0].at[self.count],
            recv_sem=self.sems[1].at[self.count],
            device_id=peer,
            device_id_type=MESH,
        )
        copy.start()
        self.count += 1
        self.open.append(copy)
        return copy

    def local(self, src, dst):
        copy = pltpu.make_async_copy(src, dst, self.sems[2].at[self.locals])
        copy.start()
        self.locals += 1
        return copy

    def got(self, copy):
        copy.wait_recv()
        copy.seen = True

    def gone(self, copy):
        copy.wait_send()
        copy.left = True

    def finish(self):
        for copy in self.open:
            if not getattr(copy, "seen", False):
                copy.wait_recv()
            if not getattr(copy, "left", False):
                copy.wait_send()


def sems(n, n_local=1):
    return [
        pltpu.SemaphoreType.DMA((n,)),
        pltpu.SemaphoreType.DMA((n,)),
        pltpu.SemaphoreType.DMA((n_local,)),
    ]


def params(cid=None, mib=56):
    if cid is None:
        return pltpu.CompilerParams(vmem_limit_bytes=mib * MIB)
    return pltpu.CompilerParams(
        vmem_limit_bytes=mib * MIB, collective_id=cid, has_side_effects=True
    )


def shape(dims, dtype):
    return jax.ShapeDtypeStruct(dims, dtype)


class Ring:
    def __init__(self, net, part, right, left, me):
        self.net, self.part, self.right, self.left = net, part, right, left
        self.before, self.after = lax.rem(me + 3, 4), lax.rem(me + 1, 4)
        self.a1 = net.send(part(me, 0), part(me, 0), right)
        self.b1 = net.send(part(me, 1), part(me, 1), left)
        self.rest = [
            net.send(part(me, 1), part(me, 1), right),
            net.send(part(me, 0), part(me, 0), left),
        ]

    def relay(self):
        net, part = self.net, self.part
        net.got(self.a1)
        self.rest.append(net.send(part(self.before, 0), part(self.before, 0), self.right))
        net.got(self.b1)
        self.rest.append(net.send(part(self.after, 1), part(self.after, 1), self.left))

    def done(self):
        for copy in self.rest:
            self.net.got(copy)


def add_rows(dst, one, two, rows, step):
    def body(i, carry):
        at = pl.ds(pl.multiple_of(i * step, step), step)
        dst[at] = (one[at].astype(f32) + two[at].astype(f32)).astype(b16)
        return carry

    lax.fori_loop(0, rows // step, body, 0)


class Scatter:
    def __init__(self, net, part, tmp, got, right, left, me, rows, step, begin=True):
        self.net, self.part, self.tmp, self.got = net, part, tmp, got
        self.right, self.left, self.me, self.step = right, left, me, step
        self.half = rows // 2
        self.lo, self.hi = pl.ds(0, self.half), pl.ds(self.half, self.half)
        self.after, self.before = lax.rem(me + 1, 4), lax.rem(me + 3, 4)
        self.first, self.rest = [], []
        if begin:
            across = part(lax.rem(me + 2, 4))
            self.first = [net.send(across.at[self.lo], tmp.at[0], right), net.send(across.at[self.hi], tmp.at[1], left)]
            self.rest = [
                net.send(part(self.after).at[self.hi], got.at[0, self.hi], right),
                net.send(part(self.before).at[self.lo], got.at[1, self.lo], left),
            ]

    def relay(self):
        net, tmp, got = self.net, self.tmp, self.got
        for copy in self.first[:1]:
            net.got(copy)
        add_rows(tmp.at[0], tmp.at[0], self.part(self.after).at[self.lo], self.half, self.step)
        self.rest.append(net.send(tmp.at[0], got.at[0, self.lo], self.right))
        for copy in self.first[1:]:
            net.got(copy)
        add_rows(tmp.at[1], tmp.at[1], self.part(self.before).at[self.hi], self.half, self.step)
        self.rest.append(net.send(tmp.at[1], got.at[1, self.hi], self.left))

    def done(self):
        for copy in self.rest:
            self.net.got(copy)

    def term(self, at):
        own = self.part(self.me)
        return own[at].astype(f32) + self.got[0, at].astype(f32) + self.got[1, at].astype(f32)

    def settle(self, dst, rows, step):
        def body(i, carry):
            at = pl.ds(pl.multiple_of(i * step, step), step)
            dst[at] = self.term(at).astype(dst.dtype)
            return carry

        lax.fori_loop(0, rows // step, body, 0)


def dot(a, b):
    return lax.dot_general(a, b, (((1,), (0,)), ((), ())), preferred_element_type=f32)


def dot_t(a, b):
    return lax.dot_general(a, b, (((1,), (1,)), ((), ())), preferred_element_type=f32)


def t_dot(a, b):
    return lax.dot_general(a, b, (((0,), (0,)), ((), ())), preferred_element_type=f32)


def partner_lanes(v):
    lane = lax.broadcasted_iota(jnp.int32, v.shape, 1)
    return jnp.where(lane % HD < HD // 2, pltpu.roll(v, 96, 1), pltpu.roll(v, 32, 1))


def half_mask(rows, half):
    lane = lax.broadcasted_iota(jnp.int32, (rows, 128), 1)
    return (lane < HD) if half == 0 else (lane >= HD)


def spread(tile, half):
    keep = half_mask(ROWS, half)
    heads = []
    for g in range(2):
        v = tile if g == half else pltpu.roll(tile, HD, 1)
        heads.append(jnp.where(keep, v, 0.0).astype(b16))
    low = jnp.concatenate([h[:128] for h in heads], axis=0)
    high = jnp.concatenate([h[128:] for h in heads], axis=0)
    return low, high


def collect(low, high, half):
    heads = []
    for g in range(2):
        v = jnp.concatenate([low[g * 128 : g * 128 + 128], high[g * 128 : g * 128 + 128]], axis=0)
        heads.append(v if g == half else pltpu.roll(v, HD, 1))
    return jnp.where(half_mask(ROWS, 0), heads[0], heads[1])


def router_rows(tail):
    row = lax.broadcasted_iota(jnp.int32, (16, D), 0)
    kept = jnp.where(row < EXPERTS, tail.astype(f32), 0.0).astype(b16)
    return jnp.concatenate([kept, jnp.zeros((112, D), b16)], axis=0)


def one_hot(routes, slot):
    lane = lax.broadcasted_iota(jnp.int32, (ROWS, 128), 1).astype(f32)
    return (routes[:, slot : slot + 1] == lane).astype(f32)


def lanes(n, width=128):
    return pl.ds(pl.multiple_of(n * width, width), width)


class Fan:
    def __init__(self, net, src, at, shards, over, ys):
        self.net, self.src, self.at, self.ys, self.shards = net, src, at, ys, shards
        self.over = net.send(src, at(shards[0]), over)

    def round(self):
        self.out = [self.net.send(self.src, self.at(self.shards[0]), p) for p in self.ys]
        return self

    def forward(self):
        self.net.got(self.over)
        ref = self.at(self.shards[1])
        self.out += [self.net.send(ref, ref, p) for p in self.ys]
        return ref

    def arrivals(self):
        for copy, n in zip(self.out, self.shards[2:]):
            self.net.got(copy)
            yield self.at(n)


def front_kernel(
    tok, cot, rl, wqkv, wout, wgu, wdn, cos_t, sin_t, router, gains, segs,
    X_o, R_o, G, WQ_o, WKV_o, WO_o, GD, TL_o, one_o, q_o, KV_o, P_o, heads_o, hidden_o, act_o,
    X, R, WQ, WKV, WO, TL, one, q, KV, probs_all, heads, hidden, act, bias,
    wq32, wkv32, wo32, gate32, up32, dn32, wq16, wkv16, wo16, gd16, cos, sin, tail32, tail,
    ss, rs, ls,
):
    x, y, z, c = place()
    z_hi = z // 2
    slot = x * 2 + c
    net = Net(ss, rs, ls)
    kept = []
    keep = lambda src, dst: kept.append(net.local(src, dst))
    loads = [
        net.local(wqkv.at[:, pl.ds(pl.multiple_of(D + c * 512, 512), 512)], wkv32),
        net.local(wqkv.at[:, lanes(slot)], wq32),
        net.local(wout.at[:, lanes(slot)], wo32),
        net.local(wgu.at[:, :, lanes(x)], gate32),
        net.local(wgu.at[:, :, lanes(4 + x)], up32),
        net.local(wdn.at[:, pl.ds(pl.multiple_of(slot * SLICE, SLICE), SLICE), :], dn32),
    ]
    tables = [
        net.local(src.at[lanes(4 * h + y)], dst.at[pl.ds(128 * h, 128)])
        for src, dst in ((cos_t, cos), (sin_t, sin))
        for h in range(2)
    ]
    partner = dev(x, y, z + 2, c)
    over = dev(x, y, 3 - z, c)
    twin = dev(x, y, z, 1 - c)
    xr, xl = dev(x + 1, y, z, c), dev(x - 1, y, z, c)
    yr, yl = dev(x, y + 1, z, c), dev(x, y - 1, z, c)
    ys = [yr, yl, dev(x, y + 2, z, c)]
    net.greet(ys + [over, partner, twin, xr, xl])
    rows = [z_hi * 4, 4 - z_hi * 4]
    shards = [rows[0] + y, rows[1] + y]
    shards += [row + lax.rem(y + d, 4) for row in rows for d in (3, 1, 2)]
    half_rows = lanes(z_hi)
    kv_lanes = pl.ds(pl.multiple_of(c * 512, 512), 512)
    fan = lambda src, at: Fan(net, src, at, shards, over, ys)
    loads[0].wait()
    wkv16[...] = wkv32[...].astype(b16)
    kv_fan = fan(wkv16, lambda n: WKV.at[lanes(n), kv_lanes]).round()
    forwards = [net.send(wkv16, WKV.at[lanes(shards[0]), kv_lanes], twin)]
    own = [net.local(tok.at[z_hi], X.at[half_rows]), net.local(rl.at[z_hi], R.at[half_rows])]
    eye = lax.broadcasted_iota(jnp.int32, (128, 128), 0) == lax.broadcasted_iota(jnp.int32, (128, 128), 1)
    tail32[...] = jnp.zeros_like(tail32)
    tail32[0:6, :] = t_dot(router[...].astype(b16), eye.astype(b16))
    tail32[6:8, :] = gains[...]
    tail[...] = tail32[...].astype(b16)
    tl_fan = fan(tail, lambda n: TL.at[:, lanes(n)]).round()
    own += [
        net.local(wkv16, WKV.at[lanes(shards[0]), kv_lanes]),
        net.local(tail, TL.at[:, lanes(shards[0])]),
    ]

    place_k = lax.broadcasted_iota(jnp.int32, (128, D), 1)
    place_q = lax.broadcasted_iota(jnp.int32, (128, D), 0) + y * 128
    pick_row = lambda v: jnp.where(z_hi == 0, v[0:1], v[1:2]).astype(f32)
    seg_k = pick_row(segs[...])
    for h in range(2):
        seg_row = jnp.broadcast_to(pick_row(segs[:, lanes(4 * h + y)]), (128, 128))
        seg_q = jnp.sum(jnp.where(eye, seg_row, 0.0), axis=1, keepdims=True)
        fine = (place_q + 512 * h >= place_k) & (seg_q == seg_k)
        bias[128 * h : 128 * h + 128, :] = jnp.where(fine, 0.0, -1e30)

    ref = kv_fan.forward()
    forwards.append(net.send(ref, ref, twin))
    x_in = net.send(tok.at[1 - z_hi], X.at[half_rows], partner)
    tl_fan.forward()
    loads[1].wait()
    wq16[...] = wq32[...].astype(b16)
    q_fan = fan(wq16, lambda n: WQ.at[lanes(n), lanes(slot)])
    loads[2].wait()
    wo16[...] = wo32[...].astype(b16)
    o_fan = fan(wo16, lambda n: WO.at[lanes(n), lanes(slot)])
    more = [
        net.local(wq16, WQ.at[lanes(shards[0]), lanes(slot)]),
        net.local(wo16, WO.at[lanes(shards[0]), lanes(slot)]),
    ]
    r_in = net.send(rl.at[1 - z_hi], R.at[half_rows], partner)

    for copy in own + tables:
        copy.wait()
    for _ in tl_fan.arrivals():
        pass
    net.got(x_in)
    v = X[...].astype(f32)
    r = lax.rsqrt(jnp.mean(v * v, axis=-1, keepdims=True) + norm_epsilon)
    one[...] = (v * r * TL[6:7, :].astype(f32)).astype(b16)
    keep(X, X_o)
    keep(one, one_o)
    keep(TL, TL_o)

    for ref in kv_fan.arrivals():
        forwards.append(net.send(ref, ref, twin))
    for pieces in (q_fan, o_fan):
        pieces.round()
        pieces.forward()
    for copy in forwards:
        net.got(copy)
    cosine, sine = cos[...], sin[...]
    a = one[...]
    for t in range(4):
        out = dot(a, WKV[:, 256 * t : 256 * t + 256])
        for u in range(2):
            tile = out[:, 128 * u : 128 * u + 128]
            if t < 2:
                tile = tile * cosine + partner_lanes(tile) * sine
            KV[y, :, 256 * t + 128 * u : 256 * t + 128 * u + 128] = tile.astype(b16)
    kv_ring = Ring(net, lambda n, h: KV.at[n, pl.ds(h * 128, 128)], yr, yl, y)
    keep(WKV, WKV_o)

    for load in loads[3:]:
        load.wait()
    lane = lax.broadcasted_iota(jnp.int32, (128, 128), 1)
    mine_first = c == 0
    for part, src in enumerate((gate32, up32)):
        for b in range(3):
            one_e, two_e = src[2 * b], src[2 * b + 1]
            first = jnp.where(mine_first, one_e, pltpu.roll(one_e, SLICE, 1))
            second = jnp.where(mine_first, pltpu.roll(two_e, SLICE, 1), two_e)
            at = slice(128 * (3 * part + b), 128 * (3 * part + b) + 128)
            gd16[at, :] = jnp.where(lane < SLICE, first, second).astype(b16)
    gd16[2 * WIDE :, :] = dn32[...].reshape(WIDE, 128).astype(b16)
    gd_own = net.local(gd16, GD.at[shards[0]])
    gd_over = net.send(gd16, GD.at[shards[0]], over)
    g_in = net.send(cot.at[1 - z_hi], G.at[slot, half_rows], partner)
    g_own = net.local(cot.at[z_hi], G.at[slot, half_rows])
    for copy in more:
        copy.wait()

    rings, twins = [], []
    for pieces, whole in ((q_fan, WQ), (o_fan, WO)):
        for _ in pieces.arrivals():
            pass
        part = lambda n, h, whole=whole: whole.at[pl.ds(h * 512, 512), lanes(n * 2 + c)]
        rings.append(Ring(net, part, xr, xl, x))
        twins.append([net.send(whole.at[:, lanes(slot)], whole.at[:, lanes(slot)], twin)])
    kv_ring.relay()
    rings[0].relay()
    rings[1].relay()
    gd_own.wait()
    gd_part = lambda row: lambda n, h: GD.at[row + n, pl.ds(h * 576, 576)]
    gd_rings = [Ring(net, gd_part(rows[0]), yr, yl, y)]
    net.got(gd_over)
    gd_rings.append(Ring(net, gd_part(rows[1]), yr, yl, y))
    g_own.wait()
    net.got(g_in)
    g_ring = Ring(net, lambda n, h: G.at[n * 2 + c, pl.ds(h * 128, 128)], xr, xl, x)
    net.send(G.at[slot], G.at[slot], twin)

    def share(n, whole):
        rings[n].done()
        for d in range(1, 4):
            tile = whole.at[:, lanes(lax.rem(x + d, 4) * 2 + c)]
            twins[n].append(net.send(tile, tile, twin))

    share(0, WQ)
    for copy in twins[0]:
        net.got(copy)
    for t in range(4):
        out = dot(a, WQ[:, 256 * t : 256 * t + 256])
        for u in range(2):
            tile = out[:, 128 * u : 128 * u + 128]
            tile = tile * cosine + partner_lanes(tile) * sine
            q[:, 256 * t + 128 * u : 256 * t + 128 * u + 128] = (tile * 0.125).astype(b16)
    keep(q, q_o)
    keep(WQ, WQ_o)
    kv_ring.done()
    keep(KV, KV_o)

    low_bias = jnp.concatenate([bias[:128, :512]] * 2, axis=0)
    high_bias = jnp.concatenate([bias[128:, :]] * 2, axis=0)
    for pair in range(4):
        cols = slice(128 * pair, 128 * pair + 128)
        vcols = slice(512 + 128 * pair, 512 + 128 * pair + 128)
        keys = [KV[:, :128, cols].reshape(512, 128), KV[:, 128:, cols].reshape(512, 128)]
        vals = [KV[:, :128, vcols].reshape(512, 128), KV[:, 128:, vcols].reshape(512, 128)]
        keys_all = jnp.concatenate(keys, axis=0)
        vals_all = jnp.concatenate(vals, axis=0)
        for half in range(2):
            cols = slice(256 * pair + 128 * half, 256 * pair + 128 * half + 128)
            low, high = spread(q[:, cols].astype(f32), half)
            outs = []
            for qq, kk, vv, bb, at_p in (
                (low, keys[0], vals[0], low_bias, slice(0, 512)),
                (high, keys_all, vals_all, high_bias, slice(512, 1536)),
            ):
                s = dot_t(qq, kk) + bb
                top = jnp.max(s, axis=-1, keepdims=True)
                e = jnp.exp(s - top)
                probs = (e * (1.0 / jnp.sum(e, axis=-1, keepdims=True))).astype(b16)
                probs_all[2 * pair + half, :, at_p] = probs
                outs.append(dot(probs, vv))
            heads[:, cols] = collect(outs[0], outs[1], half).astype(b16)
        keep(probs_all.at[pl.ds(2 * pair, 2)], P_o.at[pl.ds(2 * pair, 2)])
        if pair == 0:
            share(1, WO)
        if pair == 1:
            g_ring.relay()
            gd_rings[0].relay()
        if pair == 2:
            gd_rings[1].relay()
    keep(heads, heads_o)

    for copy in twins[1]:
        net.got(copy)
    keep(WO, WO_o)
    all_heads = heads[...]
    for t in range(4):
        cols = slice(256 * t, 256 * t + 256)
        hidden[:, cols] = X[:, cols].astype(f32) + dot(all_heads, WO[:, cols])
    h = hidden[...]
    r = lax.rsqrt(jnp.mean(h * h, axis=-1, keepdims=True) + norm_epsilon)
    a = (h * r * TL[7:8, :].astype(f32)).astype(b16)
    act[:, :D] = a
    logits = dot_t(a, router_rows(TL[...]))
    net.got(r_in)
    routes = R[...]
    hots = [one_hot(routes, k) for k in range(TOPK)]
    picked = [jnp.sum(hot * logits, axis=-1, keepdims=True) for hot in hots]
    top = jnp.maximum(picked[0], picked[1])
    powers = [jnp.exp(v - top) for v in picked]
    total = powers[0] + powers[1]
    mixing = hots[0] * (powers[0] / total) + hots[1] * (powers[1] / total)
    big = mixing.astype(b16).astype(f32)
    act[:, D:] = (big + pltpu.roll(mixing - big, 16, 1)).astype(b16)
    keep(hidden, hidden_o)
    keep(act, act_o)
    keep(R, R_o)
    g_ring.done()
    for d in range(1, 4):
        block = G.at[lax.rem(x + d, 4) * 2 + c]
        net.send(block, block, twin)
    for ring in gd_rings:
        ring.done()
    for copy in kept:
        copy.wait()
    net.finish()


def front(*arrays):
    V = pltpu.VMEM
    return pl.pallas_call(
        front_kernel,
        out_shape=(
            shape((ROWS, D), b16),
            shape((ROWS, 128), f32),
            shape((8, ROWS, D), b16),
            shape((D, D), b16),
            shape((D, D), b16),
            shape((D, D), b16),
            shape((8, 3 * WIDE, 128), b16),
            shape((16, D), b16),
            shape((ROWS, D), b16),
            shape((ROWS, D), b16),
            shape((4, ROWS, D), b16),
            shape((8, ROWS, 1536), b16),
            shape((ROWS, D), b16),
            shape((ROWS, D), f32),
            shape((ROWS, D + 128), b16),
        ),
        in_specs=[ANY] * 9 + [VMEM] * 3,
        out_specs=(ANY,) * 15,
        scratch_shapes=[
            V((ROWS, D), b16),
            V((ROWS, 128), f32),
            V((D, D), b16),
            V((D, D), b16),
            V((D, D), b16),
            V((16, D), b16),
            V((ROWS, D), b16),
            V((ROWS, D), b16),
            V((4, ROWS, D), b16),
            V((8, ROWS, 1536), b16),
            V((ROWS, D), b16),
            V((ROWS, D), f32),
            V((ROWS, D + 128), b16),
            V((ROWS, D), f32),
            V((128, 128), f32),
            V((128, 512), f32),
            V((128, 128), f32),
            V((EXPERTS, 128, 128), f32),
            V((EXPERTS, 128, 128), f32),
            V((EXPERTS, SLICE, 128), f32),
            V((128, 128), b16),
            V((128, 512), b16),
            V((128, 128), b16),
            V((3 * WIDE, 128), b16),
            V((ROWS, 128), f32),
            V((ROWS, 128), f32),
            V((16, 128), f32),
            V((16, 128), b16),
        ]
        + sems(96, 40),
        compiler_params=params(0),
        name="front",
    )(*arrays)


def experts_kernel(
    act, G, GD, total, grads_o, PO, y_tmp, y_got,
    ACT, g, gu, dn, back, tw, tmp, got, gu_acc, dn_acc, grads,
    ss, rs, ls,
):
    x, y, z, c = place()
    slot = x * 2 + c
    net = Net(ss, rs, ls)
    loads = {}
    loads[0] = [net.local(act, ACT.at[slot])]
    loads[0] += [net.local(GD.at[:, pl.ds(128 * b, 128)], gu.at[:, :, pl.ds(128 * b, 128)]) for b in range(6)]
    loads[0] += [net.local(GD.at[n, pl.ds(2 * WIDE, WIDE)], dn.at[:, pl.ds(128 * n, 128)]) for n in range(8)]
    chips = {d: lax.rem(x + d, 4) for d in range(4)}
    mine = {d: chips[d] * 2 + c for d in range(4)}
    other = {d: chips[d] * 2 + 1 - c for d in range(4)}
    for d in (0, 3, 2, 1):
        loads.setdefault(d, []).extend(net.local(G.at[n], g.at[n]) for n in (mine[d], other[d]))
    xr, xl, twin = dev(x + 1, y, z, c), dev(x - 1, y, z, c), dev(x, y, z, 1 - c)
    yr, yl = dev(x, y + 1, z, c), dev(x, y - 1, z, c)
    net.greet([xr, xl, twin, yr, yl])
    for copy in loads[0]:
        copy.wait()
    lo, hi = pl.ds(0, 128), pl.ds(128, 128)
    ins, outs = pl.ds(0, D + 128), pl.ds(D + 128, D)
    before, across, after = chips[3], chips[2], chips[1]
    home_block = ACT.at[slot]
    swap = net.send(home_block, home_block, twin)
    a1 = net.send(ACT.at[slot, lo], ACT.at[slot, lo], xr)
    b1 = net.send(ACT.at[slot, hi], ACT.at[slot, hi], xl)
    gu_acc[...] = jnp.zeros_like(gu_acc)
    dn_acc[...] = jnp.zeros_like(dn_acc)
    row = lax.broadcasted_iota(jnp.int32, (128, WIDE), 0)
    lane = lax.broadcasted_iota(jnp.int32, (128, WIDE), 1)
    pick = ((row % 16 == lane // SLICE) & (row < 32)).astype(b16)
    kept = []

    def compute(parts):
        both = lambda ref, cols: jnp.concatenate([ref[n, at, cols] for n, at in parts], axis=0)
        a = both(ACT, slice(0, D))
        mix = dot(both(ACT, slice(D, D + 128)), pick)
        gt = both(g, slice(0, D))
        weights = gu[...].reshape(D, 2 * WIDE)
        h = dot(a, weights)
        gate, up = h[:, :WIDE], h[:, WIDE:]
        gw = dot_t(gt, dn[...])
        s = 1.0 / (1.0 + jnp.exp(-gate))
        silu = gate * s
        inner = silu * up
        scaled = (inner * mix).astype(b16)
        gi = gw * mix
        ggu = jnp.concatenate(
            [(gi * up * s * (1.0 + gate * (1.0 - s))).astype(b16), (gi * silu).astype(b16)], axis=1
        )
        down = dot_t(ggu, weights).astype(b16)
        dots = dot_t((inner * gw).astype(b16), pick).astype(b16)
        terms = dot(scaled, dn[...]).astype(b16)
        for i, (n, at) in enumerate(parts):
            rows = slice(128 * i, 128 * i + 128)
            back[n, at, :D] = down[rows]
            back[n, at, D : D + 128] = dots[rows]
            back[n, at, D + 128 :] = terms[rows]
        gu_acc[...] += t_dot(a, ggu)
        dn_acc[...] += t_dot(scaled, gt)

    def add(dst, one, two):
        add_rows(dst, one, two, dst.shape[0], 16)

    def unit(d, at, arrive):
        net.got(arrive)
        compute([(mine[d], at), (other[d], at)])
        return net.send(back.at[other[d], at], tw.at[chips[d], at], twin)

    def settle(d, at, sent):
        net.got(sent)
        add(tw.at[chips[d], at], tw.at[chips[d], at], back.at[mine[d], at])
        kept.append(net.local(tw.at[chips[d], at, outs], PO.at[chips[d], at]))

    def forward(d, at, arrive):
        net.got(arrive)
        block = ACT.at[mine[d], at]
        return net.send(block, block, twin)

    compute([(mine[0], lo), (mine[0], hi)])
    net.got(swap)
    compute([(other[0], lo), (other[0], hi)])
    home = net.send(back.at[other[0]], tw.at[x], twin)
    net.got(a1)
    a3 = net.send(ACT.at[mine[3], lo], ACT.at[mine[3], lo], xr)
    net.got(b1)
    b3 = net.send(ACT.at[mine[1], hi], ACT.at[mine[1], hi], xl)
    a2 = net.send(ACT.at[slot, hi], ACT.at[slot, hi], xr)
    b2 = net.send(ACT.at[slot, lo], ACT.at[slot, lo], xl)
    f1, f2 = (net.send(ACT.at[mine[d], at], ACT.at[mine[d], at], twin) for d, at in ((3, lo), (1, hi)))
    for d in (3, 1, 2):
        for copy in loads[d]:
            copy.wait()
    u1 = unit(3, lo, f1)
    u2 = unit(1, hi, f2)
    f3 = forward(2, lo, a3)
    f4 = forward(2, hi, b3)
    settle(3, lo, u1)
    last = [net.send(tw.at[before, lo, ins], got.at[1, lo], xl)]
    net.got(home)
    add(tw.at[x], tw.at[x], back.at[mine[0]])
    kept.append(net.local(tw.at[x, :, outs], PO.at[x]))
    u3 = unit(2, lo, f3)
    settle(1, hi, u2)
    last.append(net.send(tw.at[after, hi, ins], got.at[0, hi], xr))
    u4 = unit(2, hi, f4)
    f5 = forward(3, hi, a2)
    f6 = forward(1, lo, b2)
    settle(2, lo, u3)
    s1 = net.send(tw.at[across, lo, ins], tmp.at[0], xr)
    u5 = unit(3, hi, f5)
    settle(2, hi, u4)
    s2 = net.send(tw.at[across, hi, ins], tmp.at[1], xl)
    u6 = unit(1, lo, f6)
    for n in range(8):
        at = slice(128 * n, 128 * n + 128)
        for b in range(6):
            grads[n, 128 * b : 128 * b + 128] = gu_acc[at, 128 * b : 128 * b + 128].astype(b16)
        for b in range(3):
            rows = slice(128 * (6 + b), 128 * (6 + b) + 128)
            grads[n, rows] = dn_acc[128 * b : 128 * b + 128, at].astype(b16)
    kept.append(net.local(grads, grads_o))
    for n in range(2):
        Scatter(net, lambda k, n=n: grads.at[n * 4 + k], y_tmp.at[n], y_got.at[n], yr, yl, y, 1152, 64)
    settle(3, hi, u5)
    settle(1, lo, u6)
    net.got(s1)
    add(tmp.at[0], tmp.at[0], tw.at[after, lo, ins])
    last.append(net.send(tmp.at[0], got.at[0, lo], xr))
    net.got(s2)
    add(tmp.at[1], tmp.at[1], tw.at[before, hi, ins])
    last.append(net.send(tmp.at[1], got.at[1, hi], xl))
    for copy in last:
        net.got(copy)

    def body(i, carry):
        at = pl.ds(pl.multiple_of(i * 16, 16), 16)
        total[at] = tw[x, at, : D + 128].astype(f32) + got[0, at].astype(f32) + got[1, at].astype(f32)
        return carry

    lax.fori_loop(0, ROWS // 16, body, 0)
    for copy in kept:
        copy.wait()
    net.finish()


def experts(act, G, GD):
    V = pltpu.VMEM
    wide = D + 128
    return pl.pallas_call(
        experts_kernel,
        out_shape=(
            shape((ROWS, wide), f32),
            shape((8, 9 * 128, 128), b16),
            shape((4, ROWS, D), b16),
            shape((2, 2, 576, 128), b16),
            shape((2, 2, 1152, 128), b16),
        ),
        in_specs=[ANY] * 3,
        out_specs=(VMEM, ANY, ANY, ANY, ANY),
        scratch_shapes=[
            V((8, ROWS, wide), b16),
            V((8, ROWS, D), b16),
            V((8, 128, 2 * WIDE), b16),
            V((WIDE, D), b16),
            V((8, ROWS, wide + D), b16),
            V((4, ROWS, wide + D), b16),
            V((2, ROWS // 2, wide), b16),
            V((2, ROWS, wide), b16),
            V((D, 2 * WIDE), f32),
            V((WIDE, D), f32),
            V((8, 9 * 128, 128), b16),
        ]
        + sems(40, 48),
        compiler_params=params(2),
        name="experts",
    )(act, G, GD)


def back_kernel(
    total_i, hidden_i, act_i, G, TL_i, R_i, heads_i, WO_i, X_i, one_i, q_i, KV_i, P_i, WQ_i, WKV_i,
    grads_i, PO, y_tmp_i, y_got_i, cos_t, sin_t,
    OUT, GIN, ALLM, ALL, SM,
    total, hidden, act, g, TL, R, heads, WO, X, one, q, KV, P, WQ, WKV, gr, po, po_tmp, po_got, wg,
    o_tw, o_tmp, o_got, q_tw, q_tmp, q_got, k_tw, k_tmp, k_got,
    dkv, kv_tmp, kv_got, gh, ghi, gp, gin, gin_low, gin_got, ob, cos, sin,
    y_tmp, y_got, z_got, mine, l_tmp, l_got, l_in, l_z, small, s_twin, s_x, s_y, s_z,
    ss, rs, ls,
):
    x, y, z, c = place()
    z_hi, z_lo = z // 2, lax.rem(z, 2)
    slot = x * 2 + c
    net = Net(ss, rs, ls)
    kept = []
    grad_load = [net.local(grads_i, gr), net.local(y_tmp_i, y_tmp)]
    for n in range(2):
        at = pl.ds(576 * (1 - n), 576)
        grad_load.append(net.local(y_got_i.at[:, n, at], y_got.at[:, n, at]))
    po_load = net.local(PO, po)
    first = [
        net.local(*pair)
        for pair in (
            (total_i, total), (hidden_i, hidden), (act_i, act), (TL_i, TL), (R_i, R),
            (G.at[slot], g), (heads_i, heads), (WO_i, WO),
        )
    ]
    twin = dev(x, y, z, 1 - c)
    xs = [dev(x + d, y, z, c) for d in (1, 3, 2)]
    ys = [dev(x, y + d, z, c) for d in (1, 3, 2)]
    zs = [dev(x, y, z + d, c) for d in (1, 3, 2)]
    flip = z + 1 - 2 * z_lo
    others = [dev(x + d, y, flip, c) for d in (1, 3, 2)]
    (xr, xl, x2), (yr, yl, y2), (zr, zl, z2) = xs, ys, zs
    net.greet([twin] + xs + ys + zs + others)
    for copy in grad_load:
        copy.wait()
    y_rings = [
        Scatter(net, lambda n, h=h: gr.at[h * 4 + n], y_tmp.at[h], y_got.at[h], yr, yl, y, 1152, 64, begin=False)
        for h in range(2)
    ]
    for ring in y_rings:
        ring.relay()
    po_load.wait()
    out_ring = Scatter(net, lambda n: po.at[n], po_tmp, po_got, xr, xl, x, ROWS, 16)

    for copy in first:
        copy.wait()
    second = [
        net.local(*pair)
        for pair in ((KV_i, KV), (q_i, q), (P_i, P), (one_i, one), (X_i, X), (WQ_i, WQ), (WKV_i, WKV))
    ]
    second += [
        net.local(src.at[lanes(4 * h + y)], dst.at[pl.ds(128 * h, 128)])
        for src, dst in ((cos_t, cos), (sin_t, sin))
        for h in range(2)
    ]
    h = hidden[...]
    a = act[:, :D]
    mix = act[:, D:].astype(f32)
    lane = lax.broadcasted_iota(jnp.int32, (ROWS, 128), 1)
    mixing = jnp.where(lane < 16, mix + pltpu.roll(mix, 112, 1), 0.0)
    dg = total[:, D:]
    routes = R[...]
    hots = [one_hot(routes, k) for k in range(TOPK)]
    probs = [jnp.sum(hot * mixing, axis=-1, keepdims=True) for hot in hots]
    dgs = [jnp.sum(hot * dg, axis=-1, keepdims=True) for hot in hots]
    mean = probs[0] * dgs[0] + probs[1] * dgs[1]
    grad_logits = sum(hot * (p * (d - mean)) for hot, p, d in zip(hots, probs, dgs)).astype(b16)
    ga = total[:, :D] + dot(grad_logits, router_rows(TL[...]))
    small[0:6, :] = t_dot(grad_logits, a)[0:6, :]
    r = lax.rsqrt(jnp.mean(h * h, axis=-1, keepdims=True) + norm_epsilon)
    u = ga * TL[7:8, :].astype(f32)
    small[6:7, :] = jnp.sum(ga * h * r, axis=0, keepdims=True)
    gh[...] = g[...].astype(f32) + r * (u - h * (r * r * jnp.mean(u * h, axis=-1, keepdims=True)))
    ghi[...] = dot_t(gh[...].astype(b16), WO[...]).astype(b16)

    def weight_grad(left, right):
        for t in range(4):
            piece = t_dot(left, right[:, 256 * t : 256 * t + 256])
            wg[2 * t] = piece[:, :128].astype(b16)
            wg[2 * t + 1] = piece[:, 128:].astype(b16)

    def to_twin(tw):
        return [net.send(wg.at[n * 2 + 1 - c], tw.at[n], twin) for n in range(4)]

    def along_x(sent, tw, tmp, got):
        for n, copy in enumerate(sent):
            net.got(copy)
            add_rows(tw.at[n], tw.at[n], wg.at[n * 2 + c], 1024, 64)
            net.gone(copy)
        return Scatter(net, lambda n: tw.at[n], tmp, got, xr, xl, x, 1024, 64)

    for copy in second:
        copy.wait()
    cosine, sine = cos[...], sin[...]

    def pair(n):
        cols = slice(128 * n, 128 * n + 128)
        vcols = slice(512 + 128 * n, 512 + 128 * n + 128)
        keys = [KV[:, :128, cols].reshape(512, 128), KV[:, 128:, cols].reshape(512, 128)]
        vals = [KV[:, :128, vcols].reshape(512, 128), KV[:, 128:, vcols].reshape(512, 128)]
        keys_all = jnp.concatenate(keys, axis=0)
        vals_all = jnp.concatenate(vals, axis=0)
        sums = None
        for half in range(2):
            at = slice(256 * n + 128 * half, 256 * n + 128 * half + 128)
            q_low, q_high = spread(q[:, at].astype(f32), half)
            do_low, do_high = spread(ghi[:, at].astype(f32), half)
            outs, terms = [], []
            for qq, dd, kk, vv, at_p in (
                (q_low, do_low, keys[0], vals[0], slice(0, 512)),
                (q_high, do_high, keys_all, vals_all, slice(512, 1536)),
            ):
                pr = P[2 * n + half, :, at_p]
                dp = dot_t(dd, vv)
                pf = pr.astype(f32)
                prod = pf * dp
                ds = (prod - pf * jnp.sum(prod, axis=-1, keepdims=True)).astype(b16)
                outs.append(dot(ds, kk) * 0.125)
                terms.append((t_dot(ds, qq), t_dot(pr, dd)))
            tile = collect(outs[0], outs[1], half)
            gp[:, at] = (tile * cosine - partner_lanes(tile) * sine).astype(b16)
            sums = terms if half == 0 else [(i + k, j + m) for (i, j), (k, m) in zip(sums, terms)]
        for part in range(2):
            lows, whole = sums[0][part], sums[1][part]
            where = slice(256 * part + 128 * (n % 2), 256 * part + 128 * (n % 2) + 128)
            dkv[n // 2, :, :128, where] = (lows + whole[:512]).reshape(4, 128, 128).astype(b16)
            dkv[n // 2, :, 128:, where] = whole[512:].reshape(4, 128, 128).astype(b16)

    def keys_home(n):
        return Scatter(net, lambda k: dkv.at[n, k], kv_tmp.at[n], kv_got.at[n], yr, yl, y, ROWS, 32)

    pair(0)
    for n, ring in enumerate(y_rings):
        ring.done()
        ring.settle(gr.at[n * 4 + y], 1152, 64)

    def piece(zz):
        return gr.at[(zz // 2) * 4 + y, pl.ds(pl.multiple_of(lax.rem(zz, 2) * 576, 576), 576)]

    z_in = [net.send(piece(lax.rem(z + d, 4)), z_got.at[i], zs[i]) for i, d in enumerate((1, 3, 2))]
    pair(1)
    kv_rings = [keys_home(0)]
    out_ring.relay()
    weight_grad(heads[...], gh[...].astype(b16))
    o_in = to_twin(o_tw)
    pair(2)
    kv_rings[0].relay()
    o_ring = along_x(o_in, o_tw, o_tmp, o_got)
    pair(3)
    kv_rings.append(keys_home(1))

    acts = one[...]
    weight_grad(acts, gp[:, :D])
    q_in = to_twin(q_tw)
    for copy in z_in:
        net.got(copy)
    base = pl.multiple_of(z_lo * 576, 576)
    for i in range(9):
        at = slice(64 * i, 64 * i + 64)
        here = pl.ds(pl.multiple_of(base + 64 * i, 64), 64)
        v = gr[z_hi * 4 + y, here].astype(f32)
        for n in range(3):
            v = v + z_got[n, at].astype(f32)
        z_got[0, at] = v.astype(b16)
    half_m = ALLM.at[slot, pl.ds(base, 576)]
    own_m = net.local(z_got.at[0], half_m)
    hop = net.send(z_got.at[0], half_m, dev(x, y, flip, c))
    o_ring.relay()
    q_ring = along_x(q_in, q_tw, q_tmp, q_got)
    kv_rings[1].relay()
    ga = dot_t(gp[:, :D], WQ[...])
    out_ring.done()
    ob[...] = (hidden[...] + out_ring.term(slice(None))).astype(b16)
    rows_of = lambda n: pl.ds(pl.multiple_of(n * 128, 128), 128)
    net.send(ob.at[rows_of(1 - z_hi)], OUT.at[z_hi], z2)
    kept.append(net.local(ob.at[rows_of(z_hi)], OUT.at[z_hi]))

    for n in range(2):
        kv_rings[n].done()
        for part in range(2):
            for i in range(2):
                src = slice(256 * part + 128 * i, 256 * part + 128 * i + 128)
                tile = dkv[n, y, :, src].astype(f32)
                tile = tile + kv_got[n, 0, :, src].astype(f32) + kv_got[n, 1, :, src].astype(f32)
                if part == 0:
                    tile = tile * cosine - partner_lanes(tile) * sine
                to = D + 512 * part + 256 * n + 128 * i
                gp[:, to : to + 128] = tile.astype(b16)
    weight_grad(acts, gp[:, D:])
    k_in = to_twin(k_tw)
    ga = ga + dot_t(gp[:, D:], WKV[...])
    v = X[...].astype(f32)
    r = lax.rsqrt(jnp.mean(v * v, axis=-1, keepdims=True) + norm_epsilon)
    u = ga * TL[6:7, :].astype(f32)
    small[7:8, :] = jnp.sum(ga * v * r, axis=0, keepdims=True)
    sm = net.send(small, s_twin, twin)
    k_ring = along_x(k_in, k_tw, k_tmp, k_got)
    gin[...] = gh[...] + r * (u - v * (r * r * jnp.mean(u * v, axis=-1, keepdims=True)))
    gin_low[...] = gin[rows_of(1 - z_hi)].astype(b16)
    swap = net.send(gin_low, gin_got, z2)
    kept.append(net.local(gin.at[rows_of(z_hi)], GIN.at[z_hi]))
    o_ring.done()
    q_ring.relay()
    net.got(sm)
    s_twin[...] += small[...]
    sx = [net.send(s_twin, s_x.at[i], p) for i, p in enumerate(xs)]
    q_ring.done()
    for n in range(8):
        at = slice(128 * n, 128 * n + 128)
        mine[n, 0:128] = o_ring.term(at).astype(b16)
        mine[n, 128:256] = q_ring.term(at).astype(b16)
    early, last = pl.ds(0, 256), pl.ds(256, 128)
    l_rings = [
        Scatter(net, lambda n, h=h: mine.at[h * 4 + n, early], l_tmp.at[h], l_got.at[h], yr, yl, y, 256, 64)
        for h in range(2)
    ]
    k_ring.relay()
    own_m.wait()
    net.got(hop)
    block = ALLM.at[slot]
    net.send(block, block, twin)
    m_ring = Ring(net, lambda n, h: ALLM.at[n * 2 + c, pl.ds(h * 576, 576)], xr, xl, x)
    for copy in sx:
        net.got(copy)
    s_y[0] = s_twin[...] + s_x[0] + s_x[1] + s_x[2]
    sy = [net.send(s_y.at[0], s_y.at[1 + i], p) for i, p in enumerate(ys)]
    for ring in l_rings:
        ring.relay()
    for n, ring in enumerate(l_rings):
        ring.done()
        ring.settle(mine.at[n * 4 + y, early], 256, 64)
    k_ring.done()
    for n in range(8):
        mine[n, 256:384] = k_ring.term(slice(128 * n, 128 * n + 128)).astype(b16)
    l_sent = [
        net.send(mine.at[h * 4 + lax.rem(y + d, 4), last], l_in.at[h, i], ys[i])
        for h in range(2)
        for i, d in enumerate((1, 3, 2))
    ]
    for copy in sy:
        net.got(copy)
    s_z[0] = s_y[0] + s_y[1] + s_y[2] + s_y[3]
    sz = [net.send(s_z.at[0], s_z.at[1 + i], p) for i, p in enumerate(zs)]
    m_ring.relay()
    for copy in l_sent:
        net.got(copy)
    for n in range(2):
        v = mine[n * 4 + y, 256:384].astype(f32)
        for i in range(3):
            v = v + l_in[n, i].astype(f32)
        mine[n * 4 + y, 256:384] = v.astype(b16)

    def late_piece(zz):
        return mine.at[(zz // 2) * 4 + y, pl.ds(pl.multiple_of(lax.rem(zz, 2) * 192, 192), 192)]

    l_z_in = [net.send(late_piece(lax.rem(z + d, 4)), l_z.at[i], zs[i]) for i, d in enumerate((1, 3, 2))]
    net.got(swap)
    kept.pop().wait()
    gin[rows_of(z_hi)] = gin_got[...].astype(f32)
    for copy in l_z_in:
        net.got(copy)
    late_half = lambda chip, low: ALL.at[chip * 2 + c, pl.ds(pl.multiple_of(low * 192, 192), 192)]
    here = pl.ds(pl.multiple_of(z_lo * 192, 192), 192)
    v = mine[z_hi * 4 + y, here].astype(f32)
    for i in range(3):
        v = v + l_z[i].astype(f32)
    ALL[slot, here] = v.astype(b16)
    piece_here = late_half(x, z_lo)
    ends = [net.send(piece_here, piece_here, p) for p in xs + [dev(x, y, flip, c)] + others]
    net.send(piece_here, piece_here, twin)
    kept.append(net.local(gin.at[rows_of(z_hi)], GIN.at[1 - z_hi]))
    m_ring.done()
    for d in range(1, 4):
        block = ALLM.at[lax.rem(x + d, 4) * 2 + c]
        net.send(block, block, twin)
    for copy in sz:
        net.got(copy)
    SM[...] = s_z[0] + s_z[1] + s_z[2] + s_z[3]
    came = [(lax.rem(x + d, 4), z_lo) for d in (3, 1, 2)] + [(x, 1 - z_lo)]
    came += [(lax.rem(x + d, 4), 1 - z_lo) for d in (3, 1, 2)]
    for copy, (chip, low) in zip(ends, came):
        net.got(copy)
        block = late_half(chip, low)
        net.send(block, block, twin)
    for copy in kept:
        copy.wait()
    net.finish()


def back(*arrays):
    V = pltpu.VMEM
    wide = D + 128
    return pl.pallas_call(
        back_kernel,
        out_shape=(
            shape((2, 128, D), b16),
            shape((2, 128, D), f32),
            shape((8, 1152, 128), b16),
            shape((8, 384, 128), b16),
            shape((8, D), f32),
        ),
        in_specs=[ANY] * 21,
        out_specs=(ANY, ANY, ANY, VMEM, VMEM),
        scratch_shapes=[
            V((ROWS, wide), f32),
            V((ROWS, D), f32),
            V((ROWS, wide), b16),
            V((ROWS, D), b16),
            V((16, D), b16),
            V((ROWS, 128), f32),
            V((ROWS, D), b16),
            V((D, D), b16),
            V((ROWS, D), b16),
            V((ROWS, D), b16),
            V((ROWS, D), b16),
            V((4, ROWS, D), b16),
            V((8, ROWS, 1536), b16),
            V((D, D), b16),
            V((D, D), b16),
            V((8, 1152, 128), b16),
            V((4, ROWS, D), b16),
            V((2, ROWS // 2, D), b16),
            V((2, ROWS, D), b16),
            V((8, D, 128), b16),
        ]
        + [
            V((4, D, 128), b16),
            V((2, D // 2, 128), b16),
            V((2, D, 128), b16),
        ]
        * 3
        + [
            V((2, 4, ROWS, 512), b16),
            V((2, 2, ROWS // 2, 512), b16),
            V((2, 2, ROWS, 512), b16),
            V((ROWS, D), f32),
            V((ROWS, D), b16),
            V((ROWS, 2 * D), b16),
            V((ROWS, D), f32),
            V((128, D), b16),
            V((128, D), b16),
            V((ROWS, D), b16),
            V((ROWS, 128), f32),
            V((ROWS, 128), f32),
            V((2, 2, 576, 128), b16),
            V((2, 2, 1152, 128), b16),
            V((3, 576, 128), b16),
            V((8, 384, 128), b16),
            V((2, 2, 128, 128), b16),
            V((2, 2, 256, 128), b16),
            V((2, 3, 128, 128), b16),
            V((3, 192, 128), b16),
            V((8, D), f32),
            V((8, D), f32),
            V((3, 8, D), f32),
            V((4, 8, D), f32),
            V((4, 8, D), f32),
        ]
        + sems(128, 40),
        compiler_params=params(3, 60),
        name="back",
    )(*arrays)


def rotary():
    freqs = np.float32(10000.0) ** (-np.arange(HD // 2, dtype=np.float32) * np.float32(2.0) / np.float32(HD))
    angles = np.arange(D, dtype=np.float32)[:, None] * freqs[None, :]
    cos, sin = np.cos(angles), np.sin(angles)
    return np.concatenate([cos] * 4, axis=1), np.concatenate([-sin, sin] * 2, axis=1)


def learning_rates():
    return (D ** (-0.5), 8.0 * D ** (-0.5), D ** (-0.5), 2.0 * FF ** (-0.5), 0.5 * D ** (-0.5), 0.5)


def adamw(weight, gradient, moment, square, step_rate, decay_rate):
    moment_new = beta_one * moment + (1.0 - beta_one) * gradient
    square_new = beta_two * square + (1.0 - beta_two) * gradient * gradient
    corrected = moment_new / (1.0 - beta_one**STEP)
    spread_by = jnp.sqrt(square_new / (1.0 - beta_two**STEP)) + adam_epsilon
    updated = weight - step_rate * (corrected / spread_by + decay_rate * weight)
    return [moment_new, square_new, updated]


def update_kernel(*refs):
    moe_i, late_i, ins, outs = refs[0], refs[1], refs[2:14], refs[14:26]
    moe, late, bufs, sem = refs[26], refs[27], refs[28:40], refs[40]
    rates = learning_rates()
    lane = lax.broadcasted_iota(jnp.int32, (128, 128), 1)
    count = 0

    def copy(src, dst):
        nonlocal count
        made = pltpu.make_async_copy(src, dst, sem.at[count])
        made.start()
        count += 1
        return made

    grads = [copy(moe_i, moe), copy(late_i, late)]
    every = slice(None)
    chunks = [(0, pl.ds(2 * b, 2)) for b in range(3)] + [(1, pl.ds(2 * b, 2)) for b in range(3)]
    chunks += [(2, (every, pl.ds(1024 * p, 1024))) for p in range(2)] + [(3, every)]
    loads = [
        [copy(ins[3 * n + i].at[at], bufs[3 * n + i].at[at]) for i in range(3)] for n, at in chunks
    ]
    for load in grads:
        load.wait()
    stores = []

    def apply(n, at, grad, rate):
        w, m, v = bufs[3 * n : 3 * n + 3]
        m[at], v[at], w[at] = adamw(w[at], grad, m[at], v[at], rate, 0.1)

    for step, (n, at) in enumerate(chunks):
        for load in loads[step]:
            load.wait()
        if n == 0:
            b = step
            for part in range(2):
                for t in range(4):
                    rows = slice(128 * (3 * part + b), 128 * (3 * part + b) + 128)
                    one, two = moe[2 * t, rows].astype(f32), moe[2 * t + 1, rows].astype(f32)
                    cols = slice(FF * part + 128 * t, FF * part + 128 * t + 128)
                    first = jnp.where(lane < SLICE, one, pltpu.roll(two, SLICE, 1))
                    second = jnp.where(lane < SLICE, pltpu.roll(one, SLICE, 1), two)
                    apply(0, (2 * b, every, cols), first, rates[2])
                    apply(0, (2 * b + 1, every, cols), second, rates[2])
        elif n == 1:
            b = step - 3
            for k in range(8):
                for e in range(2):
                    row = 128 * (6 + b) + SLICE * e
                    grad = moe[k, row : row + SLICE].astype(f32)
                    apply(1, (2 * b + e, slice(SLICE * k, SLICE * k + SLICE), every), grad, rates[3])
        elif n == 2:
            part = step - 6
            for t in range(8):
                cols = slice(1024 * part + 128 * t, 1024 * part + 128 * t + 128)
                grad = late[t, 128 * (1 + part) : 128 * (2 + part)].astype(f32)
                apply(2, (every, cols), grad, rates[0])
        else:
            for t in range(8):
                apply(3, (every, slice(128 * t, 128 * t + 128)), late[t, 0:128].astype(f32), rates[1])
        for i, j in ((1, 0), (2, 1), (0, 2)):
            stores.append(copy(bufs[3 * n + i].at[at], outs[3 * n + j].at[at]))
    for store in stores:
        store.wait()


def update(*arrays):
    V = pltpu.VMEM
    dims = [(EXPERTS, 128, D), (EXPERTS, FF, 128), (128, 2 * D), (128, D)]
    return pl.pallas_call(
        update_kernel,
        out_shape=tuple(shape(d, f32) for d in dims for _ in range(3)),
        in_specs=[ANY] * 14,
        out_specs=(ANY,) * 12,
        scratch_shapes=[V((8, 1152, 128), b16), V((8, 384, 128), b16)]
        + [V(d, f32) for d in dims for _ in range(3)]
        + [pltpu.SemaphoreType.DMA((56,))],
        compiler_params=params(),
        name="update",
    )(*arrays)


def on_device(
    tokens, segments, routes, cotangent, w_qkv, w_out, w_gateup, w_down, w_router, w_gains,
    qkv_first, qkv_second, out_first, out_second, gateup_first, gateup_second, down_first, down_second,
    router_first, router_second, gains_first, gains_second,
):
    x, y, z, c = place()
    z_hi = z // 2
    shard = z_hi * 4 + y
    route_lanes = jnp.pad(routes.astype(f32), ((0, 0), (0, 0), (0, 126)))
    cos, sin = (jnp.asarray(table) for table in rotary())
    X, R, G, WQ, WKV, WO, GD, TL, act_one, q, KV, probs, heads, hidden, act = front(
        tokens, cotangent, route_lanes, w_qkv, w_out, w_gateup, w_down, cos, sin, w_router, w_gains, segments
    )
    total, grads, PO, y_tmp, y_got = experts(act, G, GD)
    layer_out, input_grad, ALLM, late, SM = back(
        total, hidden, act, G, TL, R, heads, WO, X, act_one, q, KV, probs, WQ, WKV,
        grads, PO, y_tmp, y_got, cos, sin,
    )
    big = update(ALLM, late, w_gateup, gateup_first, gateup_second, w_down, down_first, down_second,
                 w_qkv, qkv_first, qkv_second, w_out, out_first, out_second)
    mine = lax.dynamic_slice_in_dim(SM, shard * 128, 128, 1)
    rates = learning_rates()
    router = adamw(w_router, mine[:6].T, router_first, router_second, rates[4], 0.1)
    gains = adamw(w_gains, jnp.stack([mine[7], mine[6]]), gains_first, gains_second, rates[5], 0.0)
    return (layer_out, input_grad, *big[6:9], *big[9:12], *big[0:3], *big[3:6], *router, *gains)


def solution(mesh):
    weight = [P("grp", None), P("grp", None), P(None, "grp", None), P(None, None, "grp"), P("grp", None), P(None, "grp")]
    tokens = P("rep", "grp", None)
    moments = [spec for spec in weight for _ in range(2)]
    results = [spec for spec in weight for _ in range(3)]
    return jax.shard_map(
        on_device,
        mesh=mesh,
        in_specs=(tokens, P("rep", None), tokens, tokens, *weight, *moments),
        out_specs=(tokens, tokens, *results),
        check_vma=False,
    )
```

```python
import jax
import jax.numpy as jnp
import numpy as np
from jax import lax
from jax.experimental import pallas as pl
from jax.experimental.pallas import tpu as pltpu
from jax.sharding import PartitionSpec as P

D = 1024
HQ = 16
HK = 8
HD = 64
FF = 512
EXPERTS = 6
TOPK = 2
STEP = 10
ROWS = 256
SLICE = 64
WIDE = EXPERTS * SLICE

beta_one = 0.9
beta_two = 0.95
adam_epsilon = 1e-08
norm_epsilon = 1e-06

f32 = jnp.float32
b16 = jnp.bfloat16
MESH = pl.DeviceIdType.MESH
ANY = pl.BlockSpec(memory_space=pl.ANY)
VMEM = pl.BlockSpec(memory_space=pltpu.VMEM)
MIB = 2**20


def place():
    rep = lax.axis_index("rep")
    grp = lax.axis_index("grp")
    z_lo, x, c = rep // 8, lax.rem(rep // 2, 4), lax.rem(rep, 2)
    z_hi, y = grp // 4, lax.rem(grp, 4)
    return x, y, z_hi * 2 + z_lo, c


def dev(x, y, z, c):
    x, y, z = lax.rem(x + 4, 4), lax.rem(y + 4, 4), lax.rem(z + 4, 4)
    return (lax.rem(z, 2) * 8 + x * 2 + c, (z // 2) * 4 + y)


class Net:
    def __init__(self, send_sems, recv_sems, local_sems):
        self.sems = (send_sems, recv_sems, local_sems)
        self.count = 0
        self.locals = 0
        self.open = []

    def call(self, peers):
        self.peers = len(peers)
        for peer in peers:
            pl.semaphore_signal(pltpu.get_barrier_semaphore(), inc=1, device_id=peer, device_id_type=MESH)

    def answer(self):
        pl.semaphore_wait(pltpu.get_barrier_semaphore(), self.peers)

    def greet(self, peers):
        self.call(peers)
        self.answer()

    def send(self, src, dst, peer):
        copy = pltpu.make_async_remote_copy(
            src_ref=src,
            dst_ref=dst,
            send_sem=self.sems[0].at[self.count],
            recv_sem=self.sems[1].at[self.count],
            device_id=peer,
            device_id_type=MESH,
        )
        copy.start()
        self.count += 1
        self.open.append(copy)
        return copy

    def local(self, src, dst):
        copy = pltpu.make_async_copy(src, dst, self.sems[2].at[self.locals])
        copy.start()
        self.locals += 1
        return copy

    def got(self, copy):
        copy.wait_recv()
        copy.seen = True

    def gone(self, copy):
        copy.wait_send()
        copy.left = True

    def finish(self):
        for copy in self.open:
            if not getattr(copy, "seen", False):
                copy.wait_recv()
            if not getattr(copy, "left", False):
                copy.wait_send()


def sems(n, n_local=1):
    return [
        pltpu.SemaphoreType.DMA((n,)),
        pltpu.SemaphoreType.DMA((n,)),
        pltpu.SemaphoreType.DMA((n_local,)),
    ]


def params(cid=None, mib=56):
    if cid is None:
        return pltpu.CompilerParams(vmem_limit_bytes=mib * MIB)
    return pltpu.CompilerParams(
        vmem_limit_bytes=mib * MIB, collective_id=cid, has_side_effects=True
    )


def shape(dims, dtype):
    return jax.ShapeDtypeStruct(dims, dtype)


class Ring:
    def __init__(self, net, part, right, left, me):
        self.net, self.part, self.right, self.left = net, part, right, left
        self.before, self.after = lax.rem(me + 3, 4), lax.rem(me + 1, 4)
        self.a1 = net.send(part(me, 0), part(me, 0), right)
        self.b1 = net.send(part(me, 1), part(me, 1), left)
        self.rest = [
            net.send(part(me, 1), part(me, 1), right),
            net.send(part(me, 0), part(me, 0), left),
        ]

    def relay(self):
        net, part = self.net, self.part
        net.got(self.a1)
        self.rest.append(net.send(part(self.before, 0), part(self.before, 0), self.right))
        net.got(self.b1)
        self.rest.append(net.send(part(self.after, 1), part(self.after, 1), self.left))

    def done(self):
        for copy in self.rest:
            self.net.got(copy)


def add_rows(dst, one, two, rows, step):
    def body(i, carry):
        at = pl.ds(pl.multiple_of(i * step, step), step)
        dst[at] = (one[at].astype(f32) + two[at].astype(f32)).astype(b16)
        return carry

    lax.fori_loop(0, rows // step, body, 0)


class Scatter:
    def __init__(self, net, part, tmp, got, right, left, me, rows, step, begin=True):
        self.net, self.part, self.tmp, self.got = net, part, tmp, got
        self.right, self.left, self.me, self.step = right, left, me, step
        self.half = rows // 2
        self.lo, self.hi = pl.ds(0, self.half), pl.ds(self.half, self.half)
        self.after, self.before = lax.rem(me + 1, 4), lax.rem(me + 3, 4)
        self.first, self.rest = [], []
        if begin:
            across = part(lax.rem(me + 2, 4))
            self.first = [net.send(across.at[self.lo], tmp.at[0], right), net.send(across.at[self.hi], tmp.at[1], left)]
            self.rest = [
                net.send(part(self.after).at[self.hi], got.at[0, self.hi], right),
                net.send(part(self.before).at[self.lo], got.at[1, self.lo], left),
            ]

    def relay(self):
        net, tmp, got = self.net, self.tmp, self.got
        for copy in self.first[:1]:
            net.got(copy)
        add_rows(tmp.at[0], tmp.at[0], self.part(self.after).at[self.lo], self.half, self.step)
        self.rest.append(net.send(tmp.at[0], got.at[0, self.lo], self.right))
        for copy in self.first[1:]:
            net.got(copy)
        add_rows(tmp.at[1], tmp.at[1], self.part(self.before).at[self.hi], self.half, self.step)
        self.rest.append(net.send(tmp.at[1], got.at[1, self.hi], self.left))

    def done(self):
        for copy in self.rest:
            self.net.got(copy)

    def term(self, at):
        own = self.part(self.me)
        return own[at].astype(f32) + self.got[0, at].astype(f32) + self.got[1, at].astype(f32)

    def settle(self, dst, rows, step):
        def body(i, carry):
            at = pl.ds(pl.multiple_of(i * step, step), step)
            dst[at] = self.term(at).astype(dst.dtype)
            return carry

        lax.fori_loop(0, rows // step, body, 0)


def dot(a, b):
    return lax.dot_general(a, b, (((1,), (0,)), ((), ())), preferred_element_type=f32)


def dot_t(a, b):
    return lax.dot_general(a, b, (((1,), (1,)), ((), ())), preferred_element_type=f32)


def t_dot(a, b):
    return lax.dot_general(a, b, (((0,), (0,)), ((), ())), preferred_element_type=f32)


def partner_lanes(v):
    lane = lax.broadcasted_iota(jnp.int32, v.shape, 1)
    return jnp.where(lane % HD < HD // 2, pltpu.roll(v, 96, 1), pltpu.roll(v, 32, 1))


def half_mask(rows, half):
    lane = lax.broadcasted_iota(jnp.int32, (rows, 128), 1)
    return (lane < HD) if half == 0 else (lane >= HD)


def spread(tile, half):
    keep = half_mask(ROWS, half)
    heads = []
    for g in range(2):
        v = tile if g == half else pltpu.roll(tile, HD, 1)
        heads.append(jnp.where(keep, v, 0.0).astype(b16))
    low = jnp.concatenate([h[:128] for h in heads], axis=0)
    high = jnp.concatenate([h[128:] for h in heads], axis=0)
    return low, high


def collect(low, high, half):
    heads = []
    for g in range(2):
        v = jnp.concatenate([low[g * 128 : g * 128 + 128], high[g * 128 : g * 128 + 128]], axis=0)
        heads.append(v if g == half else pltpu.roll(v, HD, 1))
    return jnp.where(half_mask(ROWS, 0), heads[0], heads[1])


def router_rows(tail):
    row = lax.broadcasted_iota(jnp.int32, (16, D), 0)
    kept = jnp.where(row < EXPERTS, tail.astype(f32), 0.0).astype(b16)
    return jnp.concatenate([kept, jnp.zeros((112, D), b16)], axis=0)


def one_hot(routes, slot):
    lane = lax.broadcasted_iota(jnp.int32, (ROWS, 128), 1)
    return (routes[:, slot : slot + 1] == lane).astype(f32)


def lanes(n, width=128):
    return pl.ds(pl.multiple_of(n * width, width), width)


class Fan:
    def __init__(self, net, src, at, shards, over, ys):
        self.net, self.src, self.at, self.ys, self.shards = net, src, at, ys, shards
        self.over = net.send(src, at(shards[0]), over)

    def round(self):
        self.out = [self.net.send(self.src, self.at(self.shards[0]), p) for p in self.ys]
        return self

    def forward(self):
        self.net.got(self.over)
        ref = self.at(self.shards[1])
        self.out += [self.net.send(ref, ref, p) for p in self.ys]
        return ref

    def arrivals(self):
        for copy, n in zip(self.out, self.shards[2:]):
            self.net.got(copy)
            yield self.at(n)


def front_kernel(
    tok, cot, rl, wqkv, wout, wgu, wdn, cos_t, sin_t, router, gains, segs,
    X_o, R_o, g_o, WQ_o, WKV_o, WO_o, TL_o, one_o, q_o, KV_o, P_o, heads_o, hidden_o, act_o, total, grads_o, PO, y_tmp, y_got,
    X, R, WQ, WKV, WO, TL, one, q, KV, probs_all, heads, hidden, ACT, G, GD, back, tw, tmp, got, gu_acc, dn_acc, grads, bias,
    wq32, wkv32, wo32, gate32, up32, dn32, wq16, wkv16, wo16, gd16, cos, sin, tail32, tail,
    ss, rs, ls,
):
    x, y, z, c = place()
    z_hi = z // 2
    slot = x * 2 + c
    net = Net(ss, rs, ls)
    kept = []
    keep = lambda src, dst: kept.append(net.local(src, dst))
    loads = [
        net.local(wqkv.at[:, pl.ds(pl.multiple_of(D + c * 512, 512), 512)], wkv32),
        net.local(wqkv.at[:, lanes(slot)], wq32),
        net.local(wout.at[:, lanes(slot)], wo32),
        net.local(wgu.at[:, :, lanes(x)], gate32),
        net.local(wgu.at[:, :, lanes(4 + x)], up32),
        net.local(wdn.at[:, pl.ds(pl.multiple_of(slot * SLICE, SLICE), SLICE), :], dn32),
    ]
    tables = [
        net.local(src.at[lanes(4 * h + y)], dst.at[pl.ds(128 * h, 128)])
        for src, dst in ((cos_t, cos), (sin_t, sin))
        for h in range(2)
    ]
    partner = dev(x, y, z + 2, c)
    over = dev(x, y, 3 - z, c)
    twin = dev(x, y, z, 1 - c)
    xr, xl = dev(x + 1, y, z, c), dev(x - 1, y, z, c)
    yr, yl = dev(x, y + 1, z, c), dev(x, y - 1, z, c)
    ys = [yr, yl, dev(x, y + 2, z, c)]
    net.greet(ys + [over, partner, twin, xr, xl])
    rows = [z_hi * 4, 4 - z_hi * 4]
    shards = [rows[0] + y, rows[1] + y]
    shards += [row + lax.rem(y + d, 4) for row in rows for d in (3, 1, 2)]
    half_rows = lanes(z_hi)
    kv_lanes = pl.ds(pl.multiple_of(c * 512, 512), 512)
    fan = lambda src, at: Fan(net, src, at, shards, over, ys)
    loads[0].wait()
    wkv16[...] = wkv32[...].astype(b16)
    kv_fan = fan(wkv16, lambda n: WKV.at[lanes(n), kv_lanes]).round()
    forwards = [net.send(wkv16, WKV.at[lanes(shards[0]), kv_lanes], twin)]
    own = [net.local(tok.at[z_hi], X.at[half_rows]), net.local(rl.at[z_hi], R.at[half_rows])]
    eye = lax.broadcasted_iota(jnp.int32, (128, 128), 0) == lax.broadcasted_iota(jnp.int32, (128, 128), 1)
    tail32[...] = jnp.zeros_like(tail32)
    tail32[0:6, :] = router[...]
    tail32[6:8, :] = gains[...]
    tail[...] = tail32[...].astype(b16)
    tl_fan = fan(tail, lambda n: TL.at[:, lanes(n)]).round()
    own += [
        net.local(wkv16, WKV.at[lanes(shards[0]), kv_lanes]),
        net.local(tail, TL.at[:, lanes(shards[0])]),
    ]

    place_k = lax.broadcasted_iota(jnp.int32, (128, D), 1)
    place_q = lax.broadcasted_iota(jnp.int32, (128, D), 0) + y * 128
    pick_row = lambda v: jnp.where(z_hi == 0, v[0:1], v[1:2]).astype(f32)
    seg_k = pick_row(segs[...])
    for h in range(2):
        seg_row = jnp.broadcast_to(pick_row(segs[:, lanes(4 * h + y)]), (128, 128))
        seg_q = jnp.sum(jnp.where(eye, seg_row, 0.0), axis=1, keepdims=True)
        fine = (place_q + 512 * h >= place_k) & (seg_q == seg_k)
        bias[128 * h : 128 * h + 128, :] = jnp.where(fine, 0.0, -1e30)

    ref = kv_fan.forward()
    forwards.append(net.send(ref, ref, twin))
    x_in = net.send(tok.at[1 - z_hi], X.at[half_rows], partner)
    tl_fan.forward()
    loads[1].wait()
    wq16[...] = wq32[...].astype(b16)
    q_fan = fan(wq16, lambda n: WQ.at[lanes(n), lanes(slot)])
    loads[2].wait()
    wo16[...] = wo32[...].astype(b16)
    o_fan = fan(wo16, lambda n: WO.at[lanes(n), lanes(slot)])
    more = [
        net.local(wq16, WQ.at[lanes(shards[0]), lanes(slot)]),
        net.local(wo16, WO.at[lanes(shards[0]), lanes(slot)]),
    ]
    r_in = net.send(rl.at[1 - z_hi], R.at[half_rows], partner)

    for copy in own + tables:
        copy.wait()
    for _ in tl_fan.arrivals():
        pass
    net.got(x_in)
    v = X[...].astype(f32)
    r = lax.rsqrt(jnp.mean(v * v, axis=-1, keepdims=True) + norm_epsilon)
    one[...] = (v * r * TL[6:7, :].astype(f32)).astype(b16)
    keep(X, X_o)
    keep(one, one_o)
    keep(TL, TL_o)

    for ref in kv_fan.arrivals():
        forwards.append(net.send(ref, ref, twin))
    for pieces in (q_fan, o_fan):
        pieces.round()
        pieces.forward()
    for copy in forwards:
        net.got(copy)
    cosine, sine = cos[...], sin[...]
    a = one[...]
    for t in range(4):
        out = dot(a, WKV[:, 256 * t : 256 * t + 256])
        for u in range(2):
            tile = out[:, 128 * u : 128 * u + 128]
            if t < 2:
                tile = tile * cosine + partner_lanes(tile) * sine
            KV[y, :, 256 * t + 128 * u : 256 * t + 128 * u + 128] = tile.astype(b16)
    kv_ring = Ring(net, lambda n, h: KV.at[n, pl.ds(h * 128, 128)], yr, yl, y)
    keep(WKV, WKV_o)

    for load in loads[3:]:
        load.wait()
    lane = lax.broadcasted_iota(jnp.int32, (128, 128), 1)
    mine_first = c == 0
    for part, src in enumerate((gate32, up32)):
        for b in range(3):
            one_e, two_e = src[2 * b], src[2 * b + 1]
            first = jnp.where(mine_first, one_e, pltpu.roll(one_e, SLICE, 1))
            second = jnp.where(mine_first, pltpu.roll(two_e, SLICE, 1), two_e)
            at = slice(128 * (3 * part + b), 128 * (3 * part + b) + 128)
            gd16[at, :] = jnp.where(lane < SLICE, first, second).astype(b16)
    gd16[2 * WIDE :, :] = dn32[...].reshape(WIDE, 128).astype(b16)
    gd_own = net.local(gd16, GD.at[shards[0]])
    gd_over = net.send(gd16, GD.at[shards[0]], over)
    g_in = net.send(cot.at[1 - z_hi], G.at[slot, half_rows], partner)
    g_own = net.local(cot.at[z_hi], G.at[slot, half_rows])
    for copy in more:
        copy.wait()

    rings, twins = [], []
    for pieces, whole in ((q_fan, WQ), (o_fan, WO)):
        for _ in pieces.arrivals():
            pass
        part = lambda n, h, whole=whole: whole.at[pl.ds(h * 512, 512), lanes(n * 2 + c)]
        rings.append(Ring(net, part, xr, xl, x))
        twins.append([net.send(whole.at[:, lanes(slot)], whole.at[:, lanes(slot)], twin)])
    kv_ring.relay()
    rings[0].relay()
    rings[1].relay()
    gd_own.wait()
    gd_part = lambda row: lambda n, h: GD.at[row + n, pl.ds(h * 576, 576)]
    gd_rings = [Ring(net, gd_part(rows[0]), yr, yl, y)]
    net.got(gd_over)
    gd_rings.append(Ring(net, gd_part(rows[1]), yr, yl, y))
    g_own.wait()
    net.got(g_in)
    g_ring = Ring(net, lambda n, h: G.at[n * 2 + c, pl.ds(h * 128, 128)], xr, xl, x)
    g_twin = net.send(G.at[slot], G.at[slot], twin)
    keep(G.at[slot], g_o)

    def share(n, whole):
        rings[n].done()
        for d in range(1, 4):
            tile = whole.at[:, lanes(lax.rem(x + d, 4) * 2 + c)]
            twins[n].append(net.send(tile, tile, twin))

    share(0, WQ)
    for copy in twins[0]:
        net.got(copy)
    for t in range(4):
        out = dot(a, WQ[:, 256 * t : 256 * t + 256])
        for u in range(2):
            tile = out[:, 128 * u : 128 * u + 128]
            tile = tile * cosine + partner_lanes(tile) * sine
            q[:, 256 * t + 128 * u : 256 * t + 128 * u + 128] = (tile * 0.125).astype(b16)
    keep(q, q_o)
    keep(WQ, WQ_o)
    kv_ring.done()
    keep(KV, KV_o)

    low_bias = jnp.concatenate([bias[:128, :512]] * 2, axis=0)
    high_bias = jnp.concatenate([bias[128:, :]] * 2, axis=0)
    for pair in range(4):
        cols = slice(128 * pair, 128 * pair + 128)
        vcols = slice(512 + 128 * pair, 512 + 128 * pair + 128)
        keys = [KV[:, :128, cols].reshape(512, 128), KV[:, 128:, cols].reshape(512, 128)]
        vals = [KV[:, :128, vcols].reshape(512, 128), KV[:, 128:, vcols].reshape(512, 128)]
        keys_all = jnp.concatenate(keys, axis=0)
        vals_all = jnp.concatenate(vals, axis=0)
        for half in range(2):
            cols = slice(256 * pair + 128 * half, 256 * pair + 128 * half + 128)
            low, high = spread(q[:, cols].astype(f32), half)
            outs = []
            for qq, kk, vv, bb, at_p in (
                (low, keys[0], vals[0], low_bias, slice(0, 512)),
                (high, keys_all, vals_all, high_bias, slice(512, 1536)),
            ):
                s = dot_t(qq, kk) + bb
                top = jnp.max(s, axis=-1, keepdims=True)
                e = jnp.exp(s - top)
                probs = (e * (1.0 / jnp.sum(e, axis=-1, keepdims=True))).astype(b16)
                probs_all[2 * pair + half, :, at_p] = probs
                outs.append(dot(probs, vv))
            heads[:, cols] = collect(outs[0], outs[1], half).astype(b16)
        keep(probs_all.at[pl.ds(2 * pair, 2)], P_o.at[pl.ds(2 * pair, 2)])
        if pair == 0:
            share(1, WO)
        if pair == 1:
            g_ring.relay()
            gd_rings[0].relay()
        if pair == 2:
            gd_rings[1].relay()
    keep(heads, heads_o)

    for copy in twins[1]:
        net.got(copy)
    keep(WO, WO_o)
    all_heads = heads[...]
    for t in range(4):
        cols = slice(256 * t, 256 * t + 256)
        hidden[:, cols] = X[:, cols].astype(f32) + dot(all_heads, WO[:, cols])
    h = hidden[...]
    r = lax.rsqrt(jnp.mean(h * h, axis=-1, keepdims=True) + norm_epsilon)
    a = (h * r * TL[7:8, :].astype(f32)).astype(b16)
    ACT[slot, :, :D] = a
    logits = dot_t(a, router_rows(TL[...]))
    net.got(r_in)
    routes = R[...]
    hots = [one_hot(routes, k) for k in range(TOPK)]
    picked = [jnp.sum(hot * logits, axis=-1, keepdims=True) for hot in hots]
    top = jnp.maximum(picked[0], picked[1])
    powers = [jnp.exp(v - top) for v in picked]
    power = powers[0] + powers[1]
    mixing = hots[0] * (powers[0] / power) + hots[1] * (powers[1] / power)
    big = mixing.astype(b16).astype(f32)
    ACT[slot, :, D:] = (big + pltpu.roll(mixing - big, 16, 1)).astype(b16)
    chips = {d: lax.rem(x + d, 4) for d in range(4)}
    mine = {d: chips[d] * 2 + c for d in range(4)}
    other = {d: chips[d] * 2 + 1 - c for d in range(4)}
    lo, hi = pl.ds(0, 128), pl.ds(128, 128)
    ins, outs = pl.ds(0, D + 128), pl.ds(D + 128, D)
    before, across, after = chips[3], chips[2], chips[1]
    home_block = ACT.at[slot]
    swap = net.send(home_block, home_block, twin)
    a1 = net.send(ACT.at[slot, lo], ACT.at[slot, lo], xr)
    b1 = net.send(ACT.at[slot, hi], ACT.at[slot, hi], xl)
    gu_acc[...] = jnp.zeros_like(gu_acc)
    dn_acc[...] = jnp.zeros_like(dn_acc)
    row = lax.broadcasted_iota(jnp.int32, (128, WIDE), 0)
    lane = lax.broadcasted_iota(jnp.int32, (128, WIDE), 1)
    pick = ((row % 16 == lane // SLICE) & (row < 32)).astype(b16)

    def compute(parts):
        weights = jnp.concatenate(
            [GD[:, 128 * b : 128 * b + 128].reshape(D, 128) for b in range(6)], axis=1
        )
        down_w = jnp.concatenate([GD[n, 2 * WIDE :] for n in range(8)], axis=1)
        both = lambda ref, cols: jnp.concatenate([ref[n, at, cols] for n, at in parts], axis=0)
        a = both(ACT, slice(0, D))
        mix = dot(both(ACT, slice(D, D + 128)), pick)
        gt = both(G, slice(0, D))
        h = dot(a, weights)
        gate, up = h[:, :WIDE], h[:, WIDE:]
        gw = dot_t(gt, down_w)
        s = 1.0 / (1.0 + jnp.exp(-gate))
        silu = gate * s
        inner = silu * up
        scaled = (inner * mix).astype(b16)
        gi = gw * mix
        ggu = jnp.concatenate(
            [(gi * up * s * (1.0 + gate * (1.0 - s))).astype(b16), (gi * silu).astype(b16)], axis=1
        )
        down = dot_t(ggu, weights).astype(b16)
        dots = dot_t((inner * gw).astype(b16), pick).astype(b16)
        terms = dot(scaled, down_w).astype(b16)
        for i, (n, at) in enumerate(parts):
            rows = slice(128 * i, 128 * i + 128)
            back[n, at, :D] = down[rows]
            back[n, at, D : D + 128] = dots[rows]
            back[n, at, D + 128 :] = terms[rows]
        gu_acc[...] += t_dot(a, ggu)
        dn_acc[...] += t_dot(scaled, gt)

    def add(dst, one, two):
        add_rows(dst, one, two, dst.shape[0], 16)

    def unit(d, at, arrive):
        net.got(arrive)
        compute([(mine[d], at), (other[d], at)])
        return net.send(back.at[other[d], at], tw.at[chips[d], at], twin)

    def settle(d, at, sent):
        net.got(sent)
        add(tw.at[chips[d], at], tw.at[chips[d], at], back.at[mine[d], at])
        keep(tw.at[chips[d], at, outs], PO.at[chips[d], at])

    def forward(d, at, arrive):
        net.got(arrive)
        block = ACT.at[mine[d], at]
        return net.send(block, block, twin)

    keep(hidden, hidden_o)
    keep(ACT.at[slot], act_o)
    keep(R, R_o)
    for pieces in gd_rings:
        pieces.done()
    compute([(mine[0], lo), (mine[0], hi)])
    net.got(swap)
    net.got(g_twin)
    compute([(other[0], lo), (other[0], hi)])
    home = net.send(back.at[other[0]], tw.at[x], twin)
    net.got(a1)
    a3 = net.send(ACT.at[mine[3], lo], ACT.at[mine[3], lo], xr)
    net.got(b1)
    b3 = net.send(ACT.at[mine[1], hi], ACT.at[mine[1], hi], xl)
    a2 = net.send(ACT.at[slot, hi], ACT.at[slot, hi], xr)
    b2 = net.send(ACT.at[slot, lo], ACT.at[slot, lo], xl)
    f1, f2 = (net.send(ACT.at[mine[d], at], ACT.at[mine[d], at], twin) for d, at in ((3, lo), (1, hi)))
    g_ring.done()
    g_far = [net.send(G.at[mine[d]], G.at[mine[d]], twin) for d in (3, 1, 2)]
    for copy in g_far:
        net.got(copy)
    u1 = unit(3, lo, f1)
    u2 = unit(1, hi, f2)
    f3 = forward(2, lo, a3)
    f4 = forward(2, hi, b3)
    settle(3, lo, u1)
    last = [net.send(tw.at[before, lo, ins], got.at[1, lo], xl)]
    net.got(home)
    add(tw.at[x], tw.at[x], back.at[mine[0]])
    keep(tw.at[x, :, outs], PO.at[x])
    u3 = unit(2, lo, f3)
    settle(1, hi, u2)
    last.append(net.send(tw.at[after, hi, ins], got.at[0, hi], xr))
    u4 = unit(2, hi, f4)
    f5 = forward(3, hi, a2)
    f6 = forward(1, lo, b2)
    settle(2, lo, u3)
    s1 = net.send(tw.at[across, lo, ins], tmp.at[0], xr)
    u5 = unit(3, hi, f5)
    settle(2, hi, u4)
    s2 = net.send(tw.at[across, hi, ins], tmp.at[1], xl)
    u6 = unit(1, lo, f6)
    for n in range(8):
        at = slice(128 * n, 128 * n + 128)
        for b in range(6):
            grads[n, 128 * b : 128 * b + 128] = gu_acc[at, 128 * b : 128 * b + 128].astype(b16)
        for b in range(3):
            rows = slice(128 * (6 + b), 128 * (6 + b) + 128)
            grads[n, rows] = dn_acc[128 * b : 128 * b + 128, at].astype(b16)
    keep(grads, grads_o)
    for n in range(2):
        Scatter(net, lambda k, n=n: grads.at[n * 4 + k], y_tmp.at[n], y_got.at[n], yr, yl, y, 1152, 64)
    settle(3, hi, u5)
    settle(1, lo, u6)
    net.got(s1)
    add(tmp.at[0], tmp.at[0], tw.at[after, lo, ins])
    last.append(net.send(tmp.at[0], got.at[0, lo], xr))
    net.got(s2)
    add(tmp.at[1], tmp.at[1], tw.at[before, hi, ins])
    last.append(net.send(tmp.at[1], got.at[1, hi], xl))
    for copy in last:
        net.got(copy)

    def body(i, carry):
        at = pl.ds(pl.multiple_of(i * 16, 16), 16)
        total[at] = tw[x, at, : D + 128].astype(f32) + got[0, at].astype(f32) + got[1, at].astype(f32)
        return carry

    lax.fori_loop(0, ROWS // 16, body, 0)
    for copy in kept:
        copy.wait()
    net.finish()


def front(*arrays):
    V = pltpu.VMEM
    wide = D + 128
    return pl.pallas_call(
        front_kernel,
        out_shape=(
            shape((ROWS, D), b16),
            shape((ROWS, 128), jnp.int32),
            shape((ROWS, D), b16),
            shape((D, D), b16),
            shape((D, D), b16),
            shape((D, D), b16),
            shape((16, D), b16),
            shape((ROWS, D), b16),
            shape((ROWS, D), b16),
            shape((4, ROWS, D), b16),
            shape((8, ROWS, 1536), b16),
            shape((ROWS, D), b16),
            shape((ROWS, D), f32),
            shape((ROWS, D + 128), b16),
            shape((ROWS, wide), f32),
            shape((8, 9 * 128, 128), b16),
            shape((4, ROWS, D), b16),
            shape((2, 2, 576, 128), b16),
            shape((2, 2, 1152, 128), b16),
        ),
        in_specs=[ANY] * 9 + [VMEM] * 3,
        out_specs=(ANY,) * 14 + (VMEM,) + (ANY,) * 4,
        scratch_shapes=[
            V((ROWS, D), b16),
            V((ROWS, 128), jnp.int32),
            V((D, D), b16),
            V((D, D), b16),
            V((D, D), b16),
            V((16, D), b16),
            V((ROWS, D), b16),
            V((ROWS, D), b16),
            V((4, ROWS, D), b16),
            V((8, ROWS, 1536), b16),
            V((ROWS, D), b16),
            V((ROWS, D), f32),
            V((8, ROWS, wide), b16),
            V((8, ROWS, D), b16),
            V((8, 3 * WIDE, 128), b16),
            V((8, ROWS, wide + D), b16),
            V((4, ROWS, wide + D), b16),
            V((2, ROWS // 2, wide), b16),
            V((2, ROWS, wide), b16),
            V((D, 2 * WIDE), f32),
            V((WIDE, D), f32),
            V((8, 9 * 128, 128), b16),
            V((ROWS, D), f32),
            V((128, 128), f32),
            V((128, 512), f32),
            V((128, 128), f32),
            V((EXPERTS, 128, 128), f32),
            V((EXPERTS, 128, 128), f32),
            V((EXPERTS, SLICE, 128), f32),
            V((128, 128), b16),
            V((128, 512), b16),
            V((128, 128), b16),
            V((3 * WIDE, 128), b16),
            V((ROWS, 128), f32),
            V((ROWS, 128), f32),
            V((16, 128), f32),
            V((16, 128), b16),
        ]
        + sems(160, 64),
        compiler_params=params(0, 62),
        name="front",
    )(*arrays)


def back_kernel(
    total_i, hidden_i, act_i, g_i, TL_i, R_i, heads_i, WO_i, X_i, one_i, q_i, KV_i, P_i, WQ_i, WKV_i,
    grads_i, PO, y_tmp_i, y_got_i, cos_t, sin_t,
    OUT, GIN, ALLM, ALL, SM,
    total, hidden, act, g, TL, R, heads, heads_t, WO, X, one, one_t, q, KV, P, WQ, WKV, gr, po, po_tmp, po_got,
    o_t, o_w, o_tmp, o_got, q_t, q_w, q_tmp, q_got, k_t, k_w, k_tmp, k_got,
    dkv, kv_tmp, kv_got, gh, ghl, ghi, gp, gin, gin_low, gin_got, ob, cos, sin,
    y_tmp, y_got, z_got, o_mine, o_in, q_mine, q_in, oq, oq_in, k_mine, k_in, small, s_twin, s_x, s_y, s_z,
    ss, rs, ls,
):
    x, y, z, c = place()
    z_hi, z_lo = z // 2, lax.rem(z, 2)
    slot = x * 2 + c
    net = Net(ss, rs, ls)
    kept = []
    twin = dev(x, y, z, 1 - c)
    xs = [dev(x + d, y, z, c) for d in (1, 3, 2)]
    ys = [dev(x, y + d, z, c) for d in (1, 3, 2)]
    zs = [dev(x, y, z + d, c) for d in (1, 3, 2)]
    flip = z + 1 - 2 * z_lo
    others = [dev(x + d, y, flip, c) for d in (1, 3, 2)]
    plane = [(dy, dz) for dz in range(4) for dy in range(4) if dy or dz]
    (xr, xl, x2), (yr, yl, y2), (zr, zl, z2) = xs, ys, zs
    net.call([twin] + xs + others + [dev(x, y + dy, z + dz, c) for dy, dz in plane])
    first = [
        net.local(*pair)
        for pair in (
            (total_i, total), (hidden_i, hidden), (act_i, act), (TL_i, TL), (R_i, R),
            (g_i, g), (WO_i, WO),
        )
    ]
    grad_load = [net.local(grads_i, gr), net.local(y_tmp_i, y_tmp)]
    for n in range(2):
        at = pl.ds(576 * (1 - n), 576)
        grad_load.append(net.local(y_got_i.at[:, n, at], y_got.at[:, n, at]))
    po_load = net.local(PO, po)
    for copy in first:
        copy.wait()
    second = [
        net.local(*pair)
        for pair in ((KV_i, KV), (q_i, q), (P_i, P), (heads_i, heads), (one_i, one), (X_i, X), (WQ_i, WQ), (WKV_i, WKV))
    ]
    second += [
        net.local(src.at[lanes(4 * h + y)], dst.at[pl.ds(128 * h, 128)])
        for src, dst in ((cos_t, cos), (sin_t, sin))
        for h in range(2)
    ]

    h = hidden[...]
    a = act[:, :D]
    mix = act[:, D:].astype(f32)
    lane = lax.broadcasted_iota(jnp.int32, (ROWS, 128), 1)
    mixing = jnp.where(lane < 16, mix + pltpu.roll(mix, 112, 1), 0.0)
    dg = total[:, D:]
    routes = R[...]
    hots = [one_hot(routes, k) for k in range(TOPK)]
    probs = [jnp.sum(hot * mixing, axis=-1, keepdims=True) for hot in hots]
    dgs = [jnp.sum(hot * dg, axis=-1, keepdims=True) for hot in hots]
    mean = probs[0] * dgs[0] + probs[1] * dgs[1]
    grad_logits = sum(hot * (p * (d - mean)) for hot, p, d in zip(hots, probs, dgs)).astype(b16)
    ga = total[:, :D] + dot(grad_logits, router_rows(TL[...]))
    small[0:6, :] = t_dot(grad_logits, a)[0:6, :]
    r = lax.rsqrt(jnp.mean(h * h, axis=-1, keepdims=True) + norm_epsilon)
    u = ga * TL[7:8, :].astype(f32)
    small[6:7, :] = jnp.sum(ga * h * r, axis=0, keepdims=True)
    gh[...] = g[...].astype(f32) + r * (u - h * (r * r * jnp.mean(u * h, axis=-1, keepdims=True)))
    ghl[...] = gh[...].astype(b16)

    net.answer()
    for copy in grad_load:
        copy.wait()
    y_rings = [
        Scatter(net, lambda n, h=h: gr.at[h * 4 + n], y_tmp.at[h], y_got.at[h], yr, yl, y, 1152, 64, begin=False)
        for h in range(2)
    ]
    for ring in y_rings:
        ring.relay()
    po_load.wait()
    out_ring = Scatter(net, lambda n: po.at[n], po_tmp, po_got, xr, xl, x, ROWS, 16)

    def columns(src, dst, first=0):
        return [net.send(src.at[:, lanes(first + 2 * n + 1 - c)], dst.at[n], twin) for n in range(4)]

    o_sent = columns(ghl, o_t)
    lefts = [net.send(heads_i, heads_t, twin), net.send(one_i, one_t, twin)]
    ghi[...] = dot_t(ghl[...], WO[...]).astype(b16)

    def weight_grad(left, left_t, right, first, right_t, sent, store):
        for copy in sent:
            net.got(copy)
        for m in range(2):
            own = jnp.concatenate([right[:, lanes(first + 2 * n + c)] for n in (2 * m, 2 * m + 1)], axis=1)
            far = jnp.concatenate([right_t[2 * m], right_t[2 * m + 1]], axis=1)
            piece = (t_dot(left[...], own) + t_dot(left_t[...], far)).astype(b16)
            for i in range(2):
                store(2 * m + i, piece[:, 128 * i : 128 * i + 128])

    def store_o(n, tile):
        o_w[n] = tile

    def store_k(n, tile):
        k_w[n] = tile

    def store_q(n, tile):
        for shard in range(8):
            row = 256 * n + 128 * (shard // 4)
            q_w[shard % 4, row : row + 128] = tile[128 * shard : 128 * shard + 128]

    for copy in second:
        copy.wait()
    cosine, sine = cos[...], sin[...]

    def pair(n):
        cols = slice(128 * n, 128 * n + 128)
        vcols = slice(512 + 128 * n, 512 + 128 * n + 128)
        keys = [KV[:, :128, cols].reshape(512, 128), KV[:, 128:, cols].reshape(512, 128)]
        vals = [KV[:, :128, vcols].reshape(512, 128), KV[:, 128:, vcols].reshape(512, 128)]
        keys_all = jnp.concatenate(keys, axis=0)
        vals_all = jnp.concatenate(vals, axis=0)
        sums = None
        for half in range(2):
            at = slice(256 * n + 128 * half, 256 * n + 128 * half + 128)
            q_low, q_high = spread(q[:, at].astype(f32), half)
            do_low, do_high = spread(ghi[:, at].astype(f32), half)
            outs, terms = [], []
            for qq, dd, kk, vv, at_p in (
                (q_low, do_low, keys[0], vals[0], slice(0, 512)),
                (q_high, do_high, keys_all, vals_all, slice(512, 1536)),
            ):
                pr = P[2 * n + half, :, at_p]
                dp = dot_t(dd, vv)
                pf = pr.astype(f32)
                prod = pf * dp
                ds = (prod - pf * jnp.sum(prod, axis=-1, keepdims=True)).astype(b16)
                outs.append(dot(ds, kk) * 0.125)
                terms.append((t_dot(ds, qq), t_dot(pr, dd)))
            tile = collect(outs[0], outs[1], half)
            gp[:, at] = (tile * cosine - partner_lanes(tile) * sine).astype(b16)
            sums = terms if half == 0 else [(i + k, j + m) for (i, j), (k, m) in zip(sums, terms)]
        for part in range(2):
            lows, whole = sums[0][part], sums[1][part]
            where = slice(256 * part + 128 * (n % 2), 256 * part + 128 * (n % 2) + 128)
            dkv[n // 2, :, :128, where] = (lows + whole[:512]).reshape(4, 128, 128).astype(b16)
            dkv[n // 2, :, 128:, where] = whole[512:].reshape(4, 128, 128).astype(b16)

    def keys_home(n):
        return Scatter(net, lambda k: dkv.at[n, k], kv_tmp.at[n], kv_got.at[n], yr, yl, y, ROWS, 32)

    pair(0)
    for n, ring in enumerate(y_rings):
        ring.done()
        ring.settle(gr.at[n * 4 + y], 1152, 64)

    def piece(zz):
        return gr.at[(zz // 2) * 4 + y, pl.ds(pl.multiple_of(lax.rem(zz, 2) * 576, 576), 576)]

    z_in = [net.send(piece(lax.rem(z + d, 4)), z_got.at[i], zs[i]) for i, d in enumerate((1, 3, 2))]
    pair(1)
    kv_rings = [keys_home(0)]
    out_ring.relay()
    net.got(lefts[0])
    weight_grad(heads, heads_t, ghl, 0, o_t, o_sent, store_o)
    o_ring = Scatter(net, lambda n: o_w.at[n], o_tmp, o_got, xr, xl, x, 1024, 64)
    pair(2)
    kv_rings[0].relay()
    for copy in z_in:
        net.got(copy)
    base = pl.multiple_of(z_lo * 576, 576)
    for i in range(9):
        at = slice(64 * i, 64 * i + 64)
        here = pl.ds(pl.multiple_of(base + 64 * i, 64), 64)
        v = gr[z_hi * 4 + y, here].astype(f32)
        for n in range(3):
            v = v + z_got[n, at].astype(f32)
        z_got[0, at] = v.astype(b16)
    half_m = ALLM.at[slot, pl.ds(base, 576)]
    own_m = net.local(z_got.at[0], half_m)
    hop = net.send(z_got.at[0], half_m, dev(x, y, flip, c))
    pair(3)
    kv_rings.append(keys_home(1))

    q_sent = columns(gp, q_t)
    o_ring.relay()
    net.got(lefts[1])
    weight_grad(one, one_t, gp, 0, q_t, q_sent, store_q)
    own_m.wait()
    net.got(hop)
    block = ALLM.at[slot]
    net.send(block, block, twin)
    m_ring = Ring(net, lambda n, h: ALLM.at[n * 2 + c, pl.ds(h * 576, 576)], xr, xl, x)
    kv_rings[1].relay()
    q_ring = Scatter(net, lambda n: q_w.at[n], q_tmp, q_got, yr, yl, y, 1024, 64)
    ga = dot_t(gp[:, :D], WQ[...])
    out_ring.done()
    ob[...] = (hidden[...] + out_ring.term(slice(None))).astype(b16)
    rows_of = lambda n: pl.ds(pl.multiple_of(n * 128, 128), 128)
    net.send(ob.at[rows_of(1 - z_hi)], OUT.at[z_hi], z2)
    kept.append(net.local(ob.at[rows_of(z_hi)], OUT.at[z_hi]))

    for n in range(2):
        kv_rings[n].done()
        for part in range(2):
            for i in range(2):
                src = slice(256 * part + 128 * i, 256 * part + 128 * i + 128)
                tile = dkv[n, y, :, src].astype(f32)
                tile = tile + kv_got[n, 0, :, src].astype(f32) + kv_got[n, 1, :, src].astype(f32)
                if part == 0:
                    tile = tile * cosine - partner_lanes(tile) * sine
                to = D + 512 * part + 256 * n + 128 * i
                gp[:, to : to + 128] = tile.astype(b16)
    k_sent = columns(gp, k_t, 8)
    ga = ga + dot_t(gp[:, D:], WKV[...])
    weight_grad(one, one_t, gp, 8, k_t, k_sent, store_k)
    k_ring = Scatter(net, lambda n: k_w.at[n], k_tmp, k_got, xr, xl, x, 1024, 64)
    v = X[...].astype(f32)
    r = lax.rsqrt(jnp.mean(v * v, axis=-1, keepdims=True) + norm_epsilon)
    u = ga * TL[6:7, :].astype(f32)
    small[7:8, :] = jnp.sum(ga * v * r, axis=0, keepdims=True)
    sm = net.send(small, s_twin, twin)
    gin[...] = gh[...] + r * (u - v * (r * r * jnp.mean(u * v, axis=-1, keepdims=True)))
    gin_low[...] = gin[rows_of(1 - z_hi)].astype(b16)
    swap = net.send(gin_low, gin_got, z2)
    gin_kept = net.local(gin.at[rows_of(z_hi)], GIN.at[z_hi])
    m_ring.relay()
    q_ring.relay()
    o_ring.done()
    for n in range(8):
        o_mine[n] = o_ring.term(slice(128 * n, 128 * n + 128)).astype(b16)
    o_sent = [
        net.send(o_mine.at[h * 4 + lax.rem(y + d, 4)], o_in.at[h, i], ys[i])
        for h in range(2)
        for i, d in enumerate((1, 3, 2))
    ]
    net.got(sm)
    s_twin[...] += small[...]
    sx = [net.send(s_twin, s_x.at[i], p) for i, p in enumerate(xs)]
    k_ring.relay()
    q_ring.done()
    for n in range(4):
        q_mine[n] = q_ring.term(slice(256 * n, 256 * n + 256)).astype(b16)
    q_sent = [net.send(q_mine.at[lax.rem(x + d, 4)], q_in.at[i], xs[i]) for i, d in enumerate((1, 3, 2))]
    for copy in sx:
        net.got(copy)
    s_y[0] = s_twin[...] + s_x[0] + s_x[1] + s_x[2]
    sy = [net.send(s_y.at[0], s_y.at[1 + i], p) for i, p in enumerate(ys)]
    for copy in o_sent:
        net.got(copy)
    net.got(swap)
    gin_kept.wait()
    gin[rows_of(z_hi)] = gin_got[...].astype(f32)
    kept.append(net.local(gin.at[rows_of(z_hi)], GIN.at[1 - z_hi]))
    k_ring.done()
    for n in range(8):
        k_mine[n] = k_ring.term(slice(128 * n, 128 * n + 128)).astype(b16)

    def k_piece(dy, dz):
        zz = lax.rem(z + dz, 4)
        half = pl.ds(pl.multiple_of(lax.rem(zz, 2) * 64, 64), 64)
        return k_mine.at[(zz // 2) * 4 + lax.rem(y + dy, 4), half]

    k_sent = [
        net.send(k_piece(dy, dz), k_in.at[i], dev(x, y + dy, z + dz, c)) for i, (dy, dz) in enumerate(plane)
    ]
    for copy in sy:
        net.got(copy)
    s_z[0] = s_y[0] + s_y[1] + s_y[2] + s_y[3]
    sz = [net.send(s_z.at[0], s_z.at[1 + i], p) for i, p in enumerate(zs)]
    for copy in q_sent:
        net.got(copy)
    for h in range(2):
        o_sum = o_mine[h * 4 + y].astype(f32)
        q_sum = q_mine[x, 128 * h : 128 * h + 128].astype(f32)
        for i in range(3):
            o_sum = o_sum + o_in[h, i].astype(f32)
            q_sum = q_sum + q_in[i, 128 * h : 128 * h + 128].astype(f32)
        for low in range(2):
            oq[2 * h + low, 0:64] = o_sum[64 * low : 64 * low + 64].astype(b16)
            oq[2 * h + low, 64:128] = q_sum[64 * low : 64 * low + 64].astype(b16)
    oq_sent = [net.send(oq.at[lax.rem(z + d, 4)], oq_in.at[i], zs[i]) for i, d in enumerate((1, 3, 2))]
    m_ring.done()
    for d in range(1, 4):
        block = ALLM.at[lax.rem(x + d, 4) * 2 + c]
        net.send(block, block, twin)
    for copy in oq_sent + k_sent:
        net.got(copy)
    late_half = lambda chip, low: ALL.at[chip * 2 + c, pl.ds(pl.multiple_of(low * 192, 192), 192)]
    oq_sum = oq[z].astype(f32)
    for i in range(3):
        oq_sum = oq_sum + oq_in[i].astype(f32)
    half = pl.ds(pl.multiple_of(z_lo * 64, 64), 64)
    k_sum = k_mine[z_hi * 4 + y, half].astype(f32)
    for i in range(15):
        k_sum = k_sum + k_in[i].astype(f32)
    base = pl.multiple_of(z_lo * 192, 192)
    ALL[slot, pl.ds(base, 128)] = oq_sum.astype(b16)
    ALL[slot, pl.ds(pl.multiple_of(base + 128, 64), 64)] = k_sum.astype(b16)
    piece_here = late_half(x, z_lo)
    ends = [net.send(piece_here, piece_here, p) for p in xs + [dev(x, y, flip, c)] + others]
    net.send(piece_here, piece_here, twin)
    for copy in sz:
        net.got(copy)
    here = lanes(z_hi * 4 + y)
    SM[...] = s_z[0, :, here] + s_z[1, :, here] + s_z[2, :, here] + s_z[3, :, here]
    came = [(lax.rem(x + d, 4), z_lo) for d in (3, 1, 2)] + [(x, 1 - z_lo)]
    came += [(lax.rem(x + d, 4), 1 - z_lo) for d in (3, 1, 2)]
    for copy, (chip, low) in zip(ends, came):
        net.got(copy)
        block = late_half(chip, low)
        net.send(block, block, twin)
    for copy in kept:
        copy.wait()
    net.finish()


def back(*arrays):
    V = pltpu.VMEM
    wide = D + 128
    return pl.pallas_call(
        back_kernel,
        out_shape=(
            shape((2, 128, D), b16),
            shape((2, 128, D), f32),
            shape((8, 1152, 128), b16),
            shape((8, 384, 128), b16),
            shape((8, 128), f32),
        ),
        in_specs=[ANY] * 21,
        out_specs=(ANY, ANY, ANY, VMEM, VMEM),
        scratch_shapes=[
            V((ROWS, wide), f32),
            V((ROWS, D), f32),
            V((ROWS, wide), b16),
            V((ROWS, D), b16),
            V((16, D), b16),
            V((ROWS, 128), jnp.int32),
            V((ROWS, D), b16),
            V((ROWS, D), b16),
            V((D, D), b16),
            V((ROWS, D), b16),
            V((ROWS, D), b16),
            V((ROWS, D), b16),
            V((ROWS, D), b16),
            V((4, ROWS, D), b16),
            V((8, ROWS, 1536), b16),
            V((D, D), b16),
            V((D, D), b16),
            V((8, 1152, 128), b16),
            V((4, ROWS, D), b16),
            V((2, ROWS // 2, D), b16),
            V((2, ROWS, D), b16),
        ]
        + [
            V((4, ROWS, 128), b16),
            V((4, D, 128), b16),
            V((2, D // 2, 128), b16),
            V((2, D, 128), b16),
        ]
        * 3
        + [
            V((2, 4, ROWS, 512), b16),
            V((2, 2, ROWS // 2, 512), b16),
            V((2, 2, ROWS, 512), b16),
            V((ROWS, D), f32),
            V((ROWS, D), b16),
            V((ROWS, D), b16),
            V((ROWS, 2 * D), b16),
            V((ROWS, D), f32),
            V((128, D), b16),
            V((128, D), b16),
            V((ROWS, D), b16),
            V((ROWS, 128), f32),
            V((ROWS, 128), f32),
            V((2, 2, 576, 128), b16),
            V((2, 2, 1152, 128), b16),
            V((3, 576, 128), b16),
            V((8, 128, 128), b16),
            V((2, 3, 128, 128), b16),
            V((4, 256, 128), b16),
            V((3, 256, 128), b16),
            V((4, 128, 128), b16),
            V((3, 128, 128), b16),
            V((8, 128, 128), b16),
            V((15, 64, 128), b16),
            V((8, D), f32),
            V((8, D), f32),
            V((3, 8, D), f32),
            V((4, 8, D), f32),
            V((4, 8, D), f32),
        ]
        + sems(128, 40),
        compiler_params=params(3, 60),
        name="back",
    )(*arrays)


def rotary():
    freqs = np.float32(10000.0) ** (-np.arange(HD // 2, dtype=np.float32) * np.float32(2.0) / np.float32(HD))
    angles = np.arange(D, dtype=np.float32)[:, None] * freqs[None, :]
    cos, sin = np.cos(angles), np.sin(angles)
    return np.concatenate([cos] * 4, axis=1), np.concatenate([-sin, sin] * 2, axis=1)


def learning_rates():
    return (D ** (-0.5), 8.0 * D ** (-0.5), D ** (-0.5), 2.0 * FF ** (-0.5), 0.5 * D ** (-0.5), 0.5)


def adamw(weight, gradient, moment, square, step_rate, decay_rate):
    moment_new = beta_one * moment + (1.0 - beta_one) * gradient
    square_new = beta_two * square + (1.0 - beta_two) * gradient * gradient
    corrected = moment_new / (1.0 - beta_one**STEP)
    spread_by = jnp.sqrt(square_new / (1.0 - beta_two**STEP)) + adam_epsilon
    updated = weight - step_rate * (corrected / spread_by + decay_rate * weight)
    return [moment_new, square_new, updated]


def update_kernel(*refs):
    moe_i, late_i, out_i, gin_i, sums = refs[:5]
    ins, small_ins, outs, small_outs = refs[5:17], refs[17:23], refs[25:37], refs[37:43]
    moe, late, bufs, passing, sem = refs[43], refs[44], refs[45:57], refs[57:59], refs[59]
    rates = learning_rates()
    lane = lax.broadcasted_iota(jnp.int32, (128, 128), 1)
    count = 0

    def copy(src, dst):
        nonlocal count
        made = pltpu.make_async_copy(src, dst, sem.at[count])
        made.start()
        count += 1
        return made

    grads = [copy(moe_i, moe), copy(late_i, late)]
    every = slice(None)
    chunks = [(0, pl.ds(2 * b, 2)) for b in range(3)] + [(1, pl.ds(2 * b, 2)) for b in range(3)]
    chunks += [(2, (every, pl.ds(1024 * p, 1024))) for p in range(2)] + [(3, every)]
    loads = [
        [copy(ins[3 * n + i].at[at], bufs[3 * n + i].at[at]) for i in range(3)] for n, at in chunks
    ]
    through = [copy(src, dst) for src, dst in zip((out_i, gin_i), passing)]
    for n, (grad, rate, decay) in enumerate(
        (
            (sums[0:6, :], rates[4], 0.1),
            (jnp.concatenate([sums[7:8, :], sums[6:7, :]], axis=0), rates[5], 0.0),
        )
    ):
        w, m, v = (ref[...] for ref in small_ins[3 * n : 3 * n + 3])
        for ref, value in zip(small_outs[3 * n : 3 * n + 3], adamw(w, grad, m, v, rate, decay)):
            ref[...] = value
    for load in grads:
        load.wait()
    stores = []

    def apply(n, at, grad, rate):
        w, m, v = bufs[3 * n : 3 * n + 3]
        m[at], v[at], w[at] = adamw(w[at], grad, m[at], v[at], rate, 0.1)

    for step, (n, at) in enumerate(chunks):
        for load in loads[step]:
            load.wait()
        if n == 0:
            b = step

            def tiles(t, carry, b=b):
                for part in range(2):
                    rows = slice(128 * (3 * part + b), 128 * (3 * part + b) + 128)
                    one, two = moe[2 * t, rows].astype(f32), moe[2 * t + 1, rows].astype(f32)
                    cols = lanes(4 * part + t)
                    first = jnp.where(lane < SLICE, one, pltpu.roll(two, SLICE, 1))
                    second = jnp.where(lane < SLICE, pltpu.roll(one, SLICE, 1), two)
                    apply(0, (2 * b, every, cols), first, rates[2])
                    apply(0, (2 * b + 1, every, cols), second, rates[2])
                return carry

            lax.fori_loop(0, 4, tiles, 0)
        elif n == 1:
            b = step - 3

            def tiles(k, carry, b=b):
                for e in range(2):
                    row = 128 * (6 + b) + SLICE * e
                    grad = moe[k, row : row + SLICE].astype(f32)
                    apply(1, (2 * b + e, lanes(k, SLICE), every), grad, rates[3])
                return carry

            lax.fori_loop(0, 8, tiles, 0)
        else:
            part = step - 6
            row = 0 if n == 3 else 64 * (1 + part)

            def tiles(t, carry, n=n, part=part, row=row):
                cols = lanes(t if n == 3 else 8 * part + t)
                for h in range(2):
                    grad = late[t, 192 * h + row : 192 * h + row + 64].astype(f32)
                    apply(n, (pl.ds(64 * h, 64), cols), grad, rates[1 if n == 3 else 0])
                return carry

            lax.fori_loop(0, 8, tiles, 0)
        if step == 1:
            for load, src, dst in zip(through, passing, refs[23:25]):
                load.wait()
                stores.append(copy(src, dst))
        for i, j in ((1, 0), (2, 1), (0, 2)):
            stores.append(copy(bufs[3 * n + i].at[at], outs[3 * n + j].at[at]))
    for store in stores:
        store.wait()


def update(*arrays):
    V = pltpu.VMEM
    dims = [(EXPERTS, 128, D), (EXPERTS, FF, 128), (128, 2 * D), (128, D)]
    return pl.pallas_call(
        update_kernel,
        out_shape=(shape((2, 128, D), b16), shape((2, 128, D), f32))
        + tuple(shape(d, f32) for d in dims + [(EXPERTS, 128), (2, 128)] for _ in range(3)),
        in_specs=[ANY] * 4 + [VMEM] + [ANY] * 12 + [VMEM] * 6,
        out_specs=(ANY,) * 14 + (VMEM,) * 6,
        scratch_shapes=[V((8, 1152, 128), b16), V((8, 384, 128), b16)]
        + [V(d, f32) for d in dims for _ in range(3)]
        + [V((2, 128, D), b16), V((2, 128, D), f32), pltpu.SemaphoreType.DMA((64,))],
        compiler_params=params(),
        name="update",
    )(*arrays)


def on_device(
    tokens, segments, routes, cotangent, w_qkv, w_out, w_gateup, w_down, w_router, w_gains,
    qkv_first, qkv_second, out_first, out_second, gateup_first, gateup_second, down_first, down_second,
    router_first, router_second, gains_first, gains_second,
):
    route_lanes = jnp.pad(routes, ((0, 0), (0, 0), (0, 126)))
    cos, sin = (jnp.asarray(table) for table in rotary())
    X, R, g, WQ, WKV, WO, TL, act_one, q, KV, probs, heads, hidden, act, total, grads, PO, y_tmp, y_got = front(
        tokens, cotangent, route_lanes, w_qkv, w_out, w_gateup, w_down, cos, sin, w_router.T, w_gains, segments
    )
    layer_out, input_grad, ALLM, late, SM = back(
        total, hidden, act, g, TL, R, heads, WO, X, act_one, q, KV, probs, WQ, WKV,
        grads, PO, y_tmp, y_got, cos, sin,
    )
    done = update(
        ALLM, late, layer_out, input_grad, SM, w_gateup, gateup_first, gateup_second, w_down, down_first, down_second,
        w_qkv, qkv_first, qkv_second, w_out, out_first, out_second,
        w_router.T, router_first.T, router_second.T, w_gains, gains_first, gains_second,
    )
    router = [array.T for array in done[14:17]]
    return (*done[:2], *done[8:11], *done[11:14], *done[2:5], *done[5:8], *router, *done[17:20])


def solution(mesh):
    weight = [P("grp", None), P("grp", None), P(None, "grp", None), P(None, None, "grp"), P("grp", None), P(None, "grp")]
    tokens = P("rep", "grp", None)
    moments = [spec for spec in weight for _ in range(2)]
    results = [spec for spec in weight for _ in range(3)]
    return jax.shard_map(
        on_device,
        mesh=mesh,
        in_specs=(tokens, P("rep", None), tokens, tokens, *weight, *moments),
        out_specs=(tokens, tokens, *results),
        check_vma=False,
    )
```

```python
import jax
import jax.numpy as jnp
import numpy as np
from jax import lax
from jax.experimental import pallas as pl
from jax.experimental.pallas import tpu as pltpu
from jax.sharding import PartitionSpec as P

D = 1024
HQ = 16
HK = 8
HD = 64
FF = 512
EXPERTS = 6
TOPK = 2
STEP = 10
ROWS = 256
SLICE = 64
WIDE = EXPERTS * SLICE

beta_one = 0.9
beta_two = 0.95
adam_epsilon = 1e-08
norm_epsilon = 1e-06

f32 = jnp.float32
b16 = jnp.bfloat16
MESH = pl.DeviceIdType.MESH
ANY = pl.BlockSpec(memory_space=pl.ANY)
VMEM = pl.BlockSpec(memory_space=pltpu.VMEM)
MIB = 2**20


def place():
    rep = lax.axis_index("rep")
    grp = lax.axis_index("grp")
    z_lo, x, c = rep // 8, lax.rem(rep // 2, 4), lax.rem(rep, 2)
    z_hi, y = grp // 4, lax.rem(grp, 4)
    return x, y, z_hi * 2 + z_lo, c


def dev(x, y, z, c):
    x, y, z = lax.rem(x + 4, 4), lax.rem(y + 4, 4), lax.rem(z + 4, 4)
    return (lax.rem(z, 2) * 8 + x * 2 + c, (z // 2) * 4 + y)


class Net:
    def __init__(self, send_sems, recv_sems, local_sems):
        self.sems = (send_sems, recv_sems, local_sems)
        self.count = 0
        self.locals = 0
        self.open = []

    def call(self, peers):
        self.peers = len(peers)
        for peer in peers:
            pl.semaphore_signal(pltpu.get_barrier_semaphore(), inc=1, device_id=peer, device_id_type=MESH)

    def answer(self):
        pl.semaphore_wait(pltpu.get_barrier_semaphore(), self.peers)

    def greet(self, peers):
        self.call(peers)
        self.answer()

    def describe(self, n, src, dst, peer):
        return pltpu.make_async_remote_copy(
            src_ref=src,
            dst_ref=dst,
            send_sem=self.sems[0].at[n],
            recv_sem=self.sems[1].at[n],
            device_id=peer,
            device_id_type=MESH,
        )

    def planned(self, src, dst, peer):
        copy = self.describe(self.count, src, dst, peer)
        self.count += 1
        self.open.append(copy)
        return copy

    def send(self, src, dst, peer):
        copy = self.planned(src, dst, peer)
        copy.start()
        return copy

    def local(self, src, dst):
        copy = pltpu.make_async_copy(src, dst, self.sems[2].at[self.locals])
        copy.start()
        self.locals += 1
        return copy

    def got(self, copy):
        copy.wait_recv()
        copy.seen = True

    def gone(self, copy):
        copy.wait_send()
        copy.left = True

    def finish(self):
        for copy in self.open:
            if not getattr(copy, "seen", False):
                copy.wait_recv()
            if not getattr(copy, "left", False):
                copy.wait_send()


def sems(n, n_local=1):
    return [
        pltpu.SemaphoreType.DMA((n,)),
        pltpu.SemaphoreType.DMA((n,)),
        pltpu.SemaphoreType.DMA((n_local,)),
    ]


def params(cid=None, mib=56):
    if cid is None:
        return pltpu.CompilerParams(vmem_limit_bytes=mib * MIB)
    return pltpu.CompilerParams(
        vmem_limit_bytes=mib * MIB, collective_id=cid, has_side_effects=True
    )


def shape(dims, dtype):
    return jax.ShapeDtypeStruct(dims, dtype)


class Ring:
    def __init__(self, net, part, right, left, me):
        self.net, self.part, self.right, self.left = net, part, right, left
        self.before, self.after = lax.rem(me + 3, 4), lax.rem(me + 1, 4)
        self.a1 = net.send(part(me, 0), part(me, 0), right)
        self.b1 = net.send(part(me, 1), part(me, 1), left)
        self.rest = [
            net.send(part(me, 1), part(me, 1), right),
            net.send(part(me, 0), part(me, 0), left),
        ]

    def relay(self):
        net, part = self.net, self.part
        net.got(self.a1)
        self.rest.append(net.send(part(self.before, 0), part(self.before, 0), self.right))
        net.got(self.b1)
        self.rest.append(net.send(part(self.after, 1), part(self.after, 1), self.left))

    def done(self):
        for copy in self.rest:
            self.net.got(copy)


def add_rows(dst, one, two, rows, step):
    def body(i, carry):
        at = pl.ds(pl.multiple_of(i * step, step), step)
        dst[at] = (one[at].astype(f32) + two[at].astype(f32)).astype(b16)
        return carry

    lax.fori_loop(0, rows // step, body, 0)


class Scatter:
    def __init__(self, net, part, tmp, got, right, left, me, rows, step, begin=True):
        self.net, self.part, self.tmp, self.got = net, part, tmp, got
        self.right, self.left, self.me, self.step = right, left, me, step
        self.half = rows // 2
        self.lo, self.hi = pl.ds(0, self.half), pl.ds(self.half, self.half)
        self.after, self.before = lax.rem(me + 1, 4), lax.rem(me + 3, 4)
        self.first, self.rest = [], []
        if begin:
            across = part(lax.rem(me + 2, 4))
            self.first = [net.send(across.at[self.lo], tmp.at[0], right), net.send(across.at[self.hi], tmp.at[1], left)]
            self.rest = [
                net.send(part(self.after).at[self.hi], got.at[0, self.hi], right),
                net.send(part(self.before).at[self.lo], got.at[1, self.lo], left),
            ]

    def relay(self):
        net, tmp, got = self.net, self.tmp, self.got
        for copy in self.first[:1]:
            net.got(copy)
        add_rows(tmp.at[0], tmp.at[0], self.part(self.after).at[self.lo], self.half, self.step)
        self.rest.append(net.send(tmp.at[0], got.at[0, self.lo], self.right))
        for copy in self.first[1:]:
            net.got(copy)
        add_rows(tmp.at[1], tmp.at[1], self.part(self.before).at[self.hi], self.half, self.step)
        self.rest.append(net.send(tmp.at[1], got.at[1, self.hi], self.left))

    def done(self):
        for copy in self.rest:
            self.net.got(copy)

    def term(self, at):
        own = self.part(self.me)
        return own[at].astype(f32) + self.got[0, at].astype(f32) + self.got[1, at].astype(f32)

    def settle(self, dst, rows, step):
        def body(i, carry):
            at = pl.ds(pl.multiple_of(i * step, step), step)
            dst[at] = self.term(at).astype(dst.dtype)
            return carry

        lax.fori_loop(0, rows // step, body, 0)


def dot(a, b):
    return lax.dot_general(a, b, (((1,), (0,)), ((), ())), preferred_element_type=f32)


def dot_t(a, b):
    return lax.dot_general(a, b, (((1,), (1,)), ((), ())), preferred_element_type=f32)


def t_dot(a, b):
    return lax.dot_general(a, b, (((0,), (0,)), ((), ())), preferred_element_type=f32)


def partner_lanes(v):
    lane = lax.broadcasted_iota(jnp.int32, v.shape, 1)
    return jnp.where(lane % HD < HD // 2, pltpu.roll(v, 96, 1), pltpu.roll(v, 32, 1))


def half_mask(rows, half):
    lane = lax.broadcasted_iota(jnp.int32, (rows, 128), 1)
    return (lane < HD) if half == 0 else (lane >= HD)


def spread(tile, half):
    keep = half_mask(ROWS, half)
    heads = []
    for g in range(2):
        v = tile if g == half else pltpu.roll(tile, HD, 1)
        heads.append(jnp.where(keep, v, 0.0).astype(b16))
    low = jnp.concatenate([h[:128] for h in heads], axis=0)
    high = jnp.concatenate([h[128:] for h in heads], axis=0)
    return low, high


def collect(low, high, half):
    heads = []
    for g in range(2):
        v = jnp.concatenate([low[g * 128 : g * 128 + 128], high[g * 128 : g * 128 + 128]], axis=0)
        heads.append(v if g == half else pltpu.roll(v, HD, 1))
    return jnp.where(half_mask(ROWS, 0), heads[0], heads[1])


def router_rows(tail):
    row = lax.broadcasted_iota(jnp.int32, (16, D), 0)
    kept = jnp.where(row < EXPERTS, tail.astype(f32), 0.0).astype(b16)
    return jnp.concatenate([kept, jnp.zeros((112, D), b16)], axis=0)


def one_hot(routes, slot):
    lane = lax.broadcasted_iota(jnp.int32, (ROWS, 128), 1)
    return (routes[:, slot : slot + 1] == lane).astype(f32)


def lanes(n, width=128):
    return pl.ds(pl.multiple_of(n * width, width), width)


class Fan:
    def __init__(self, net, src, at, shards, over, ys):
        self.net, self.src, self.at, self.ys, self.shards = net, src, at, ys, shards
        self.over = net.send(src, at(shards[0]), over)

    def round(self):
        self.out = [self.net.send(self.src, self.at(self.shards[0]), p) for p in self.ys]
        return self

    def forward(self):
        self.net.got(self.over)
        ref = self.at(self.shards[1])
        self.out += [self.net.send(ref, ref, p) for p in self.ys]
        return ref

    def arrivals(self):
        for copy, n in zip(self.out, self.shards[2:]):
            self.net.got(copy)
            yield self.at(n)


def front_kernel(
    tok, cot, rl, wqkv, wout, wgu, wdn, cos_t, sin_t, router, gains, segs,
    X_o, R_o, g_o, WQ_o, WKV_o, WO_o, TL_o, one_o, q_o, KV_o, P_o, heads_o, hidden_o, act_o, total, grads_o, PO, y_tmp, y_got,
    X, R, WQ, WKV, WO, TL, one, q, KV, probs_all, heads, hidden, ACT, G, GD, back, tw, tmp, got, gu_acc, dn_acc, grads, bias,
    wq32, wkv32, wo32, gate32, up32, dn32, wq16, wkv16, wo16, gd16, cos, sin, tail32, tail,
    ss, rs, ls,
):
    x, y, z, c = place()
    z_hi = z // 2
    slot = x * 2 + c
    net = Net(ss, rs, ls)
    kept = []
    keep = lambda src, dst: kept.append(net.local(src, dst))
    loads = [
        net.local(wqkv.at[:, pl.ds(pl.multiple_of(D + c * 512, 512), 512)], wkv32),
        net.local(wqkv.at[:, lanes(slot)], wq32),
        net.local(wout.at[:, lanes(slot)], wo32),
        net.local(wgu.at[:, :, lanes(x)], gate32),
        net.local(wgu.at[:, :, lanes(4 + x)], up32),
        net.local(wdn.at[:, pl.ds(pl.multiple_of(slot * SLICE, SLICE), SLICE), :], dn32),
    ]
    tables = [
        net.local(src.at[lanes(4 * h + y)], dst.at[pl.ds(128 * h, 128)])
        for src, dst in ((cos_t, cos), (sin_t, sin))
        for h in range(2)
    ]
    partner = dev(x, y, z + 2, c)
    over = dev(x, y, 3 - z, c)
    twin = dev(x, y, z, 1 - c)
    xr, xl = dev(x + 1, y, z, c), dev(x - 1, y, z, c)
    yr, yl = dev(x, y + 1, z, c), dev(x, y - 1, z, c)
    ys = [yr, yl, dev(x, y + 2, z, c)]
    net.greet(ys + [over, partner, twin, xr, xl])
    rows = [z_hi * 4, 4 - z_hi * 4]
    shards = [rows[0] + y, rows[1] + y]
    shards += [row + lax.rem(y + d, 4) for row in rows for d in (3, 1, 2)]
    half_rows = lanes(z_hi)
    kv_lanes = pl.ds(pl.multiple_of(c * 512, 512), 512)
    fan = lambda src, at: Fan(net, src, at, shards, over, ys)
    loads[0].wait()
    wkv16[...] = wkv32[...].astype(b16)
    kv_fan = fan(wkv16, lambda n: WKV.at[lanes(n), kv_lanes]).round()
    forwards = [net.send(wkv16, WKV.at[lanes(shards[0]), kv_lanes], twin)]
    own = [net.local(tok.at[z_hi], X.at[half_rows]), net.local(rl.at[z_hi], R.at[half_rows])]
    eye = lax.broadcasted_iota(jnp.int32, (128, 128), 0) == lax.broadcasted_iota(jnp.int32, (128, 128), 1)
    tail32[...] = jnp.zeros_like(tail32)
    tail32[0:6, :] = router[...]
    tail32[6:8, :] = gains[...]
    tail[...] = tail32[...].astype(b16)
    tl_fan = fan(tail, lambda n: TL.at[:, lanes(n)]).round()
    own += [
        net.local(wkv16, WKV.at[lanes(shards[0]), kv_lanes]),
        net.local(tail, TL.at[:, lanes(shards[0])]),
    ]

    place_k = lax.broadcasted_iota(jnp.int32, (128, D), 1)
    place_q = lax.broadcasted_iota(jnp.int32, (128, D), 0) + y * 128
    pick_row = lambda v: jnp.where(z_hi == 0, v[0:1], v[1:2]).astype(f32)
    seg_k = pick_row(segs[...])
    for h in range(2):
        seg_row = jnp.broadcast_to(pick_row(segs[:, lanes(4 * h + y)]), (128, 128))
        seg_q = jnp.sum(jnp.where(eye, seg_row, 0.0), axis=1, keepdims=True)
        fine = (place_q + 512 * h >= place_k) & (seg_q == seg_k)
        bias[128 * h : 128 * h + 128, :] = jnp.where(fine, 0.0, -1e30)

    ref = kv_fan.forward()
    forwards.append(net.send(ref, ref, twin))
    x_in = net.send(tok.at[1 - z_hi], X.at[half_rows], partner)
    tl_fan.forward()
    loads[1].wait()
    wq16[...] = wq32[...].astype(b16)
    q_fan = fan(wq16, lambda n: WQ.at[lanes(n), lanes(slot)])
    loads[2].wait()
    wo16[...] = wo32[...].astype(b16)
    o_fan = fan(wo16, lambda n: WO.at[lanes(n), lanes(slot)])
    more = [
        net.local(wq16, WQ.at[lanes(shards[0]), lanes(slot)]),
        net.local(wo16, WO.at[lanes(shards[0]), lanes(slot)]),
    ]
    r_in = net.send(rl.at[1 - z_hi], R.at[half_rows], partner)

    for copy in own + tables:
        copy.wait()
    for _ in tl_fan.arrivals():
        pass
    net.got(x_in)
    v = X[...].astype(f32)
    r = lax.rsqrt(jnp.mean(v * v, axis=-1, keepdims=True) + norm_epsilon)
    one[...] = (v * r * TL[6:7, :].astype(f32)).astype(b16)
    keep(X, X_o)
    keep(one, one_o)
    keep(TL, TL_o)

    for ref in kv_fan.arrivals():
        forwards.append(net.send(ref, ref, twin))
    for pieces in (q_fan, o_fan):
        pieces.round()
        pieces.forward()
    for copy in forwards:
        net.got(copy)
    cosine, sine = cos[...], sin[...]
    a = one[...]
    for t in range(4):
        out = dot(a, WKV[:, 256 * t : 256 * t + 256])
        for u in range(2):
            tile = out[:, 128 * u : 128 * u + 128]
            if t < 2:
                tile = tile * cosine + partner_lanes(tile) * sine
            KV[y, :, 256 * t + 128 * u : 256 * t + 128 * u + 128] = tile.astype(b16)
    kv_ring = Ring(net, lambda n, h: KV.at[n, pl.ds(h * 128, 128)], yr, yl, y)
    keep(WKV, WKV_o)

    for load in loads[3:]:
        load.wait()
    lane = lax.broadcasted_iota(jnp.int32, (128, 128), 1)
    mine_first = c == 0
    for part, src in enumerate((gate32, up32)):
        for b in range(3):
            one_e, two_e = src[2 * b], src[2 * b + 1]
            first = jnp.where(mine_first, one_e, pltpu.roll(one_e, SLICE, 1))
            second = jnp.where(mine_first, pltpu.roll(two_e, SLICE, 1), two_e)
            at = slice(128 * (3 * part + b), 128 * (3 * part + b) + 128)
            gd16[at, :] = jnp.where(lane < SLICE, first, second).astype(b16)
    gd16[2 * WIDE :, :] = dn32[...].reshape(WIDE, 128).astype(b16)
    gd_own = net.local(gd16, GD.at[shards[0]])
    gd_over = net.send(gd16, GD.at[shards[0]], over)
    g_in = net.send(cot.at[1 - z_hi], G.at[slot, half_rows], partner)
    g_own = net.local(cot.at[z_hi], G.at[slot, half_rows])
    for copy in more:
        copy.wait()

    rings, twins = [], []
    for pieces, whole in ((q_fan, WQ), (o_fan, WO)):
        for _ in pieces.arrivals():
            pass
        part = lambda n, h, whole=whole: whole.at[pl.ds(h * 512, 512), lanes(n * 2 + c)]
        rings.append(Ring(net, part, xr, xl, x))
        twins.append([net.send(whole.at[:, lanes(slot)], whole.at[:, lanes(slot)], twin)])
    kv_ring.relay()
    rings[0].relay()
    rings[1].relay()
    gd_own.wait()
    gd_part = lambda row: lambda n, h: GD.at[row + n, pl.ds(h * 576, 576)]
    gd_rings = [Ring(net, gd_part(rows[0]), yr, yl, y)]
    net.got(gd_over)
    gd_rings.append(Ring(net, gd_part(rows[1]), yr, yl, y))
    g_own.wait()
    net.got(g_in)
    g_ring = Ring(net, lambda n, h: G.at[n * 2 + c, pl.ds(h * 128, 128)], xr, xl, x)
    g_twin = net.send(G.at[slot], G.at[slot], twin)
    keep(G.at[slot], g_o)

    def share(n, whole):
        rings[n].done()
        for d in range(1, 4):
            tile = whole.at[:, lanes(lax.rem(x + d, 4) * 2 + c)]
            twins[n].append(net.send(tile, tile, twin))

    share(0, WQ)
    for copy in twins[0]:
        net.got(copy)
    for t in range(4):
        out = dot(a, WQ[:, 256 * t : 256 * t + 256])
        for u in range(2):
            tile = out[:, 128 * u : 128 * u + 128]
            tile = tile * cosine + partner_lanes(tile) * sine
            q[:, 256 * t + 128 * u : 256 * t + 128 * u + 128] = (tile * 0.125).astype(b16)
    keep(q, q_o)
    keep(WQ, WQ_o)
    kv_ring.done()
    keep(KV, KV_o)

    low_bias = jnp.concatenate([bias[:128, :512]] * 2, axis=0)
    high_bias = jnp.concatenate([bias[128:, :]] * 2, axis=0)

    def attend(pair, carry):
        cols, vcols = lanes(pair), lanes(4 + pair)
        keys = [KV[:, :128, cols].reshape(512, 128), KV[:, 128:, cols].reshape(512, 128)]
        vals = [KV[:, :128, vcols].reshape(512, 128), KV[:, 128:, vcols].reshape(512, 128)]
        keys_all = jnp.concatenate(keys, axis=0)
        vals_all = jnp.concatenate(vals, axis=0)
        for half in range(2):
            cols = lanes(2 * pair + half)
            low, high = spread(q[:, cols].astype(f32), half)
            outs = []
            for qq, kk, vv, bb, at_p in (
                (low, keys[0], vals[0], low_bias, slice(0, 512)),
                (high, keys_all, vals_all, high_bias, slice(512, 1536)),
            ):
                s = dot_t(qq, kk) + bb
                top = jnp.max(s, axis=-1, keepdims=True)
                e = jnp.exp(s - top)
                probs = (e * (1.0 / jnp.sum(e, axis=-1, keepdims=True))).astype(b16)
                probs_all[2 * pair + half, :, at_p] = probs
                outs.append(dot(probs, vv))
            heads[:, cols] = collect(outs[0], outs[1], half).astype(b16)
        return carry

    for m in range(2):
        lax.fori_loop(2 * m, 2 * m + 2, attend, 0)
        keep(probs_all.at[pl.ds(4 * m, 4)], P_o.at[pl.ds(4 * m, 4)])
        if m == 0:
            share(1, WO)
            g_ring.relay()
            gd_rings[0].relay()
    gd_rings[1].relay()
    keep(heads, heads_o)

    for copy in twins[1]:
        net.got(copy)
    keep(WO, WO_o)
    all_heads = heads[...]
    for t in range(4):
        cols = slice(256 * t, 256 * t + 256)
        hidden[:, cols] = X[:, cols].astype(f32) + dot(all_heads, WO[:, cols])
    h = hidden[...]
    r = lax.rsqrt(jnp.mean(h * h, axis=-1, keepdims=True) + norm_epsilon)
    a = (h * r * TL[7:8, :].astype(f32)).astype(b16)
    ACT[slot, :, :D] = a
    logits = dot_t(a, router_rows(TL[...]))
    net.got(r_in)
    routes = R[...]
    hots = [one_hot(routes, k) for k in range(TOPK)]
    picked = [jnp.sum(hot * logits, axis=-1, keepdims=True) for hot in hots]
    top = jnp.maximum(picked[0], picked[1])
    powers = [jnp.exp(v - top) for v in picked]
    power = powers[0] + powers[1]
    mixing = hots[0] * (powers[0] / power) + hots[1] * (powers[1] / power)
    big = mixing.astype(b16).astype(f32)
    ACT[slot, :, D:] = (big + pltpu.roll(mixing - big, 16, 1)).astype(b16)
    chips = {d: lax.rem(x + d, 4) for d in range(4)}
    mine = {d: chips[d] * 2 + c for d in range(4)}
    other = {d: chips[d] * 2 + 1 - c for d in range(4)}
    lo, hi = pl.ds(0, 128), pl.ds(128, 128)
    ins, outs = pl.ds(0, D + 128), pl.ds(D + 128, D)
    before, across, after = chips[3], chips[2], chips[1]
    home_block = ACT.at[slot]
    swap = net.send(home_block, home_block, twin)
    a1 = net.send(ACT.at[slot, lo], ACT.at[slot, lo], xr)
    b1 = net.send(ACT.at[slot, hi], ACT.at[slot, hi], xl)
    gu_acc[...] = jnp.zeros_like(gu_acc)
    dn_acc[...] = jnp.zeros_like(dn_acc)
    row = lax.broadcasted_iota(jnp.int32, (128, WIDE), 0)
    lane = lax.broadcasted_iota(jnp.int32, (128, WIDE), 1)
    pick = ((row % 16 == lane // SLICE) & (row < 32)).astype(b16)

    def compute(parts):
        weights = jnp.concatenate(
            [GD[:, 128 * b : 128 * b + 128].reshape(D, 128) for b in range(6)], axis=1
        )
        down_w = jnp.concatenate([GD[n, 2 * WIDE :] for n in range(8)], axis=1)
        both = lambda ref, cols: jnp.concatenate([ref[n, at, cols] for n, at in parts], axis=0)
        a = both(ACT, slice(0, D))
        mix = dot(both(ACT, slice(D, D + 128)), pick)
        gt = both(G, slice(0, D))
        h = dot(a, weights)
        gate, up = h[:, :WIDE], h[:, WIDE:]
        gw = dot_t(gt, down_w)
        s = 1.0 / (1.0 + jnp.exp(-gate))
        silu = gate * s
        inner = silu * up
        scaled = (inner * mix).astype(b16)
        gi = gw * mix
        ggu = jnp.concatenate(
            [(gi * up * s * (1.0 + gate * (1.0 - s))).astype(b16), (gi * silu).astype(b16)], axis=1
        )
        down = dot_t(ggu, weights).astype(b16)
        dots = dot_t((inner * gw).astype(b16), pick).astype(b16)
        terms = dot(scaled, down_w).astype(b16)
        for i, (n, at) in enumerate(parts):
            rows = slice(128 * i, 128 * i + 128)
            back[n, at, :D] = down[rows]
            back[n, at, D : D + 128] = dots[rows]
            back[n, at, D + 128 :] = terms[rows]
        gu_acc[...] += t_dot(a, ggu)
        dn_acc[...] += t_dot(scaled, gt)

    def add(dst, one, two):
        add_rows(dst, one, two, dst.shape[0], 16)

    def units(chip, offset, pieces):
        first = net.count
        sent = [net.planned(back.at[other[d], at], tw.at[chips[d], at], twin) for d, at in pieces]

        def one_unit(j, carry):
            n, at = chip(j), pl.ds(pl.multiple_of(offset(j), 128), 128)
            compute([(n * 2 + c, at), (n * 2 + 1 - c, at)])
            net.describe(first + j, back.at[n * 2 + 1 - c, at], tw.at[n, at], twin).start()
            return carry

        lax.fori_loop(0, 2, one_unit, 0)
        return sent

    def settle(d, at, sent):
        net.got(sent)
        add(tw.at[chips[d], at], tw.at[chips[d], at], back.at[mine[d], at])
        keep(tw.at[chips[d], at, outs], PO.at[chips[d], at])

    def forward(d, at, arrive):
        net.got(arrive)
        block = ACT.at[mine[d], at]
        return net.send(block, block, twin)

    keep(hidden, hidden_o)
    keep(ACT.at[slot], act_o)
    keep(R, R_o)
    for pieces in gd_rings:
        pieces.done()
    net.got(swap)
    net.got(g_twin)

    def own_chip(j, carry):
        n = x * 2 + lax.rem(c + j, 2)
        compute([(n, lo), (n, hi)])
        return carry

    lax.fori_loop(0, 2, own_chip, 0)
    home = net.send(back.at[other[0]], tw.at[x], twin)
    net.got(a1)
    a3 = net.send(ACT.at[mine[3], lo], ACT.at[mine[3], lo], xr)
    net.got(b1)
    b3 = net.send(ACT.at[mine[1], hi], ACT.at[mine[1], hi], xl)
    a2 = net.send(ACT.at[slot, hi], ACT.at[slot, hi], xr)
    b2 = net.send(ACT.at[slot, lo], ACT.at[slot, lo], xl)
    f1, f2 = (net.send(ACT.at[mine[d], at], ACT.at[mine[d], at], twin) for d, at in ((3, lo), (1, hi)))
    g_ring.done()
    g_far = [net.send(G.at[mine[d]], G.at[mine[d]], twin) for d in (3, 1, 2)]
    for copy in g_far:
        net.got(copy)
    for copy in (f1, f2):
        net.got(copy)
    ends_of = lambda j: lax.rem(x + 3 - 2 * j, 4)
    u1, u2 = units(ends_of, lambda j: 128 * j, [(3, lo), (1, hi)])
    f3 = forward(2, lo, a3)
    f4 = forward(2, hi, b3)
    settle(3, lo, u1)
    last = [net.send(tw.at[before, lo, ins], got.at[1, lo], xl)]
    settle(1, hi, u2)
    last.append(net.send(tw.at[after, hi, ins], got.at[0, hi], xr))
    for copy in (f3, f4):
        net.got(copy)
    u3, u4 = units(lambda j: across, lambda j: 128 * j, [(2, lo), (2, hi)])
    f5 = forward(3, hi, a2)
    f6 = forward(1, lo, b2)
    settle(2, lo, u3)
    s1 = net.send(tw.at[across, lo, ins], tmp.at[0], xr)
    settle(2, hi, u4)
    s2 = net.send(tw.at[across, hi, ins], tmp.at[1], xl)
    for copy in (f5, f6):
        net.got(copy)
    u5, u6 = units(ends_of, lambda j: 128 - 128 * j, [(3, hi), (1, lo)])
    net.got(home)
    add(tw.at[x], tw.at[x], back.at[mine[0]])
    keep(tw.at[x, :, outs], PO.at[x])
    for n in range(8):
        at = slice(128 * n, 128 * n + 128)
        for b in range(6):
            grads[n, 128 * b : 128 * b + 128] = gu_acc[at, 128 * b : 128 * b + 128].astype(b16)
        for b in range(3):
            rows = slice(128 * (6 + b), 128 * (6 + b) + 128)
            grads[n, rows] = dn_acc[128 * b : 128 * b + 128, at].astype(b16)
    keep(grads, grads_o)
    for n in range(2):
        Scatter(net, lambda k, n=n: grads.at[n * 4 + k], y_tmp.at[n], y_got.at[n], yr, yl, y, 1152, 64)
    settle(3, hi, u5)
    settle(1, lo, u6)
    net.got(s1)
    add(tmp.at[0], tmp.at[0], tw.at[after, lo, ins])
    last.append(net.send(tmp.at[0], got.at[0, lo], xr))
    net.got(s2)
    add(tmp.at[1], tmp.at[1], tw.at[before, hi, ins])
    last.append(net.send(tmp.at[1], got.at[1, hi], xl))
    for copy in last:
        net.got(copy)

    def body(i, carry):
        at = pl.ds(pl.multiple_of(i * 16, 16), 16)
        total[at] = tw[x, at, : D + 128].astype(f32) + got[0, at].astype(f32) + got[1, at].astype(f32)
        return carry

    lax.fori_loop(0, ROWS // 16, body, 0)
    for copy in kept:
        copy.wait()
    net.finish()


def front(*arrays):
    V = pltpu.VMEM
    wide = D + 128
    return pl.pallas_call(
        front_kernel,
        out_shape=(
            shape((ROWS, D), b16),
            shape((ROWS, 128), jnp.int32),
            shape((ROWS, D), b16),
            shape((D, D), b16),
            shape((D, D), b16),
            shape((D, D), b16),
            shape((16, D), b16),
            shape((ROWS, D), b16),
            shape((ROWS, D), b16),
            shape((4, ROWS, D), b16),
            shape((8, ROWS, 1536), b16),
            shape((ROWS, D), b16),
            shape((ROWS, D), f32),
            shape((ROWS, D + 128), b16),
            shape((ROWS, wide), f32),
            shape((8, 9 * 128, 128), b16),
            shape((4, ROWS, D), b16),
            shape((2, 2, 576, 128), b16),
            shape((2, 2, 1152, 128), b16),
        ),
        in_specs=[ANY] * 9 + [VMEM] * 3,
        out_specs=(ANY,) * 14 + (VMEM,) + (ANY,) * 4,
        scratch_shapes=[
            V((ROWS, D), b16),
            V((ROWS, 128), jnp.int32),
            V((D, D), b16),
            V((D, D), b16),
            V((D, D), b16),
            V((16, D), b16),
            V((ROWS, D), b16),
            V((ROWS, D), b16),
            V((4, ROWS, D), b16),
            V((8, ROWS, 1536), b16),
            V((ROWS, D), b16),
            V((ROWS, D), f32),
            V((8, ROWS, wide), b16),
            V((8, ROWS, D), b16),
            V((8, 3 * WIDE, 128), b16),
            V((8, ROWS, wide + D), b16),
            V((4, ROWS, wide + D), b16),
            V((2, ROWS // 2, wide), b16),
            V((2, ROWS, wide), b16),
            V((D, 2 * WIDE), f32),
            V((WIDE, D), f32),
            V((8, 9 * 128, 128), b16),
            V((ROWS, D), f32),
            V((128, 128), f32),
            V((128, 512), f32),
            V((128, 128), f32),
            V((EXPERTS, 128, 128), f32),
            V((EXPERTS, 128, 128), f32),
            V((EXPERTS, SLICE, 128), f32),
            V((128, 128), b16),
            V((128, 512), b16),
            V((128, 128), b16),
            V((3 * WIDE, 128), b16),
            V((ROWS, 128), f32),
            V((ROWS, 128), f32),
            V((16, 128), f32),
            V((16, 128), b16),
        ]
        + sems(160, 64),
        compiler_params=params(0, 62),
        name="front",
    )(*arrays)


def back_kernel(
    total_i, hidden_i, act_i, g_i, TL_i, R_i, heads_i, WO_i, X_i, one_i, q_i, KV_i, P_i, WQ_i, WKV_i,
    grads_i, PO, y_tmp_i, y_got_i, cos_t, sin_t,
    OUT, GIN, ALLM, ALL, SM,
    total, hidden, act, g, TL, R, heads, heads_t, WO, X, one, one_t, q, KV, P, WQ, WKV, gr, po, po_tmp, po_got,
    o_t, o_w, o_tmp, o_got, q_t, q_w, q_tmp, q_got, k_t, k_w, k_tmp, k_got,
    dkv, kv_tmp, kv_got, gh, ghl, ghi, gp, gin, gin_low, gin_got, ob, cos, sin,
    y_tmp, y_got, z_got, o_mine, o_in, q_mine, q_in, oq, oq_in, k_mine, k_in, small, s_twin, s_x, s_y, s_z,
    ss, rs, ls,
):
    x, y, z, c = place()
    z_hi, z_lo = z // 2, lax.rem(z, 2)
    slot = x * 2 + c
    net = Net(ss, rs, ls)
    kept = []
    twin = dev(x, y, z, 1 - c)
    xs = [dev(x + d, y, z, c) for d in (1, 3, 2)]
    ys = [dev(x, y + d, z, c) for d in (1, 3, 2)]
    zs = [dev(x, y, z + d, c) for d in (1, 3, 2)]
    flip = z + 1 - 2 * z_lo
    others = [dev(x + d, y, flip, c) for d in (1, 3, 2)]
    plane = [(dy, dz) for dz in range(4) for dy in range(4) if dy or dz]
    (xr, xl, x2), (yr, yl, y2), (zr, zl, z2) = xs, ys, zs
    net.call([twin] + xs + others + [dev(x, y + dy, z + dz, c) for dy, dz in plane])
    first = [
        net.local(*pair)
        for pair in (
            (total_i, total), (hidden_i, hidden), (act_i, act), (TL_i, TL), (R_i, R),
            (g_i, g), (WO_i, WO),
        )
    ]
    grad_load = [net.local(grads_i, gr), net.local(y_tmp_i, y_tmp)]
    for n in range(2):
        at = pl.ds(576 * (1 - n), 576)
        grad_load.append(net.local(y_got_i.at[:, n, at], y_got.at[:, n, at]))
    po_load = net.local(PO, po)
    for copy in first:
        copy.wait()
    second = [
        net.local(*pair)
        for pair in ((KV_i, KV), (q_i, q), (P_i, P), (heads_i, heads), (one_i, one), (X_i, X), (WQ_i, WQ), (WKV_i, WKV))
    ]
    second += [
        net.local(src.at[lanes(4 * h + y)], dst.at[pl.ds(128 * h, 128)])
        for src, dst in ((cos_t, cos), (sin_t, sin))
        for h in range(2)
    ]

    h = hidden[...]
    a = act[:, :D]
    mix = act[:, D:].astype(f32)
    lane = lax.broadcasted_iota(jnp.int32, (ROWS, 128), 1)
    mixing = jnp.where(lane < 16, mix + pltpu.roll(mix, 112, 1), 0.0)
    dg = total[:, D:]
    routes = R[...]
    hots = [one_hot(routes, k) for k in range(TOPK)]
    probs = [jnp.sum(hot * mixing, axis=-1, keepdims=True) for hot in hots]
    dgs = [jnp.sum(hot * dg, axis=-1, keepdims=True) for hot in hots]
    mean = probs[0] * dgs[0] + probs[1] * dgs[1]
    grad_logits = sum(hot * (p * (d - mean)) for hot, p, d in zip(hots, probs, dgs)).astype(b16)
    ga = total[:, :D] + dot(grad_logits, router_rows(TL[...]))
    small[0:6, :] = t_dot(grad_logits, a)[0:6, :]
    r = lax.rsqrt(jnp.mean(h * h, axis=-1, keepdims=True) + norm_epsilon)
    u = ga * TL[7:8, :].astype(f32)
    small[6:7, :] = jnp.sum(ga * h * r, axis=0, keepdims=True)
    gh[...] = g[...].astype(f32) + r * (u - h * (r * r * jnp.mean(u * h, axis=-1, keepdims=True)))
    ghl[...] = gh[...].astype(b16)

    net.answer()
    for copy in grad_load:
        copy.wait()
    y_rings = [
        Scatter(net, lambda n, h=h: gr.at[h * 4 + n], y_tmp.at[h], y_got.at[h], yr, yl, y, 1152, 64, begin=False)
        for h in range(2)
    ]
    for ring in y_rings:
        ring.relay()
    po_load.wait()
    out_ring = Scatter(net, lambda n: po.at[n], po_tmp, po_got, xr, xl, x, ROWS, 16)

    def columns(src, dst, first=0):
        return [net.send(src.at[:, lanes(first + 2 * n + 1 - c)], dst.at[n], twin) for n in range(4)]

    o_sent = columns(ghl, o_t)
    lefts = [net.send(heads_i, heads_t, twin), net.send(one_i, one_t, twin)]
    ghi[...] = dot_t(ghl[...], WO[...]).astype(b16)

    def weight_grad(left, left_t, right, first, right_t, sent, store):
        for copy in sent:
            net.got(copy)
        for m in range(2):
            own = jnp.concatenate([right[:, lanes(first + 2 * n + c)] for n in (2 * m, 2 * m + 1)], axis=1)
            far = jnp.concatenate([right_t[2 * m], right_t[2 * m + 1]], axis=1)
            piece = (t_dot(left[...], own) + t_dot(left_t[...], far)).astype(b16)
            for i in range(2):
                store(2 * m + i, piece[:, 128 * i : 128 * i + 128])

    def store_o(n, tile):
        o_w[n] = tile

    def store_k(n, tile):
        k_w[n] = tile

    def store_q(n, tile):
        for shard in range(8):
            row = 256 * n + 128 * (shard // 4)
            q_w[shard % 4, row : row + 128] = tile[128 * shard : 128 * shard + 128]

    for copy in second:
        copy.wait()
    cosine, sine = cos[...], sin[...]

    def pair(n, carry):
        cols, vcols = lanes(n), lanes(4 + n)
        keys = [KV[:, :128, cols].reshape(512, 128), KV[:, 128:, cols].reshape(512, 128)]
        vals = [KV[:, :128, vcols].reshape(512, 128), KV[:, 128:, vcols].reshape(512, 128)]
        keys_all = jnp.concatenate(keys, axis=0)
        vals_all = jnp.concatenate(vals, axis=0)
        sums = None
        for half in range(2):
            at = lanes(2 * n + half)
            q_low, q_high = spread(q[:, at].astype(f32), half)
            do_low, do_high = spread(ghi[:, at].astype(f32), half)
            outs, terms = [], []
            for qq, dd, kk, vv, at_p in (
                (q_low, do_low, keys[0], vals[0], slice(0, 512)),
                (q_high, do_high, keys_all, vals_all, slice(512, 1536)),
            ):
                pr = P[2 * n + half, :, at_p]
                dp = dot_t(dd, vv)
                pf = pr.astype(f32)
                prod = pf * dp
                ds = (prod - pf * jnp.sum(prod, axis=-1, keepdims=True)).astype(b16)
                outs.append(dot(ds, kk) * 0.125)
                terms.append((t_dot(ds, qq), t_dot(pr, dd)))
            tile = collect(outs[0], outs[1], half)
            gp[:, at] = (tile * cosine - partner_lanes(tile) * sine).astype(b16)
            sums = terms if half == 0 else [(i + k, j + m) for (i, j), (k, m) in zip(sums, terms)]
        for part in range(2):
            lows, whole = sums[0][part], sums[1][part]
            where = lanes(2 * part + lax.rem(n, 2))
            dkv[n // 2, :, :128, where] = (lows + whole[:512]).reshape(4, 128, 128).astype(b16)
            dkv[n // 2, :, 128:, where] = whole[512:].reshape(4, 128, 128).astype(b16)
        return carry

    def keys_home(n):
        return Scatter(net, lambda k: dkv.at[n, k], kv_tmp.at[n], kv_got.at[n], yr, yl, y, ROWS, 32)

    lax.fori_loop(0, 2, pair, 0)
    kv_rings = [keys_home(0)]
    for n, ring in enumerate(y_rings):
        ring.done()
        ring.settle(gr.at[n * 4 + y], 1152, 64)

    def piece(zz):
        return gr.at[(zz // 2) * 4 + y, pl.ds(pl.multiple_of(lax.rem(zz, 2) * 576, 576), 576)]

    z_in = [net.send(piece(lax.rem(z + d, 4)), z_got.at[i], zs[i]) for i, d in enumerate((1, 3, 2))]
    out_ring.relay()
    net.got(lefts[0])
    weight_grad(heads, heads_t, ghl, 0, o_t, o_sent, store_o)
    o_ring = Scatter(net, lambda n: o_w.at[n], o_tmp, o_got, xr, xl, x, 1024, 64)
    lax.fori_loop(2, 4, pair, 0)
    kv_rings.append(keys_home(1))
    kv_rings[0].relay()
    q_sent = columns(gp, q_t)
    for copy in z_in:
        net.got(copy)
    base = pl.multiple_of(z_lo * 576, 576)
    for i in range(9):
        at = slice(64 * i, 64 * i + 64)
        here = pl.ds(pl.multiple_of(base + 64 * i, 64), 64)
        v = gr[z_hi * 4 + y, here].astype(f32)
        for n in range(3):
            v = v + z_got[n, at].astype(f32)
        z_got[0, at] = v.astype(b16)
    half_m = ALLM.at[slot, pl.ds(base, 576)]
    own_m = net.local(z_got.at[0], half_m)
    hop = net.send(z_got.at[0], half_m, dev(x, y, flip, c))

    o_ring.relay()
    net.got(lefts[1])
    weight_grad(one, one_t, gp, 0, q_t, q_sent, store_q)
    own_m.wait()
    net.got(hop)
    block = ALLM.at[slot]
    net.send(block, block, twin)
    m_ring = Ring(net, lambda n, h: ALLM.at[n * 2 + c, pl.ds(h * 576, 576)], xr, xl, x)
    kv_rings[1].relay()
    q_ring = Scatter(net, lambda n: q_w.at[n], q_tmp, q_got, yr, yl, y, 1024, 64)
    ga = dot_t(gp[:, :D], WQ[...])
    out_ring.done()
    ob[...] = (hidden[...] + out_ring.term(slice(None))).astype(b16)
    rows_of = lambda n: pl.ds(pl.multiple_of(n * 128, 128), 128)
    net.send(ob.at[rows_of(1 - z_hi)], OUT.at[z_hi], z2)
    kept.append(net.local(ob.at[rows_of(z_hi)], OUT.at[z_hi]))

    for n in range(2):
        kv_rings[n].done()
        for part in range(2):
            for i in range(2):
                src = slice(256 * part + 128 * i, 256 * part + 128 * i + 128)
                tile = dkv[n, y, :, src].astype(f32)
                tile = tile + kv_got[n, 0, :, src].astype(f32) + kv_got[n, 1, :, src].astype(f32)
                if part == 0:
                    tile = tile * cosine - partner_lanes(tile) * sine
                to = D + 512 * part + 256 * n + 128 * i
                gp[:, to : to + 128] = tile.astype(b16)
    k_sent = columns(gp, k_t, 8)
    ga = ga + dot_t(gp[:, D:], WKV[...])
    weight_grad(one, one_t, gp, 8, k_t, k_sent, store_k)
    k_ring = Scatter(net, lambda n: k_w.at[n], k_tmp, k_got, xr, xl, x, 1024, 64)
    v = X[...].astype(f32)
    r = lax.rsqrt(jnp.mean(v * v, axis=-1, keepdims=True) + norm_epsilon)
    u = ga * TL[6:7, :].astype(f32)
    small[7:8, :] = jnp.sum(ga * v * r, axis=0, keepdims=True)
    sm = net.send(small, s_twin, twin)
    gin[...] = gh[...] + r * (u - v * (r * r * jnp.mean(u * v, axis=-1, keepdims=True)))
    gin_low[...] = gin[rows_of(1 - z_hi)].astype(b16)
    swap = net.send(gin_low, gin_got, z2)
    gin_kept = net.local(gin.at[rows_of(z_hi)], GIN.at[z_hi])
    m_ring.relay()
    q_ring.relay()
    o_ring.done()
    for n in range(8):
        o_mine[n] = o_ring.term(slice(128 * n, 128 * n + 128)).astype(b16)
    o_sent = [
        net.send(o_mine.at[h * 4 + lax.rem(y + d, 4)], o_in.at[h, i], ys[i])
        for h in range(2)
        for i, d in enumerate((1, 3, 2))
    ]
    net.got(sm)
    s_twin[...] += small[...]
    sx = [net.send(s_twin, s_x.at[i], p) for i, p in enumerate(xs)]
    k_ring.relay()
    q_ring.done()
    for n in range(4):
        q_mine[n] = q_ring.term(slice(256 * n, 256 * n + 256)).astype(b16)
    q_sent = [net.send(q_mine.at[lax.rem(x + d, 4)], q_in.at[i], xs[i]) for i, d in enumerate((1, 3, 2))]
    for copy in sx:
        net.got(copy)
    s_y[0] = s_twin[...] + s_x[0] + s_x[1] + s_x[2]
    sy = [net.send(s_y.at[0], s_y.at[1 + i], p) for i, p in enumerate(ys)]
    for copy in o_sent:
        net.got(copy)
    net.got(swap)
    gin_kept.wait()
    gin[rows_of(z_hi)] = gin_got[...].astype(f32)
    kept.append(net.local(gin.at[rows_of(z_hi)], GIN.at[1 - z_hi]))
    k_ring.done()
    for n in range(8):
        k_mine[n] = k_ring.term(slice(128 * n, 128 * n + 128)).astype(b16)

    def k_piece(dy, dz):
        zz = lax.rem(z + dz, 4)
        half = pl.ds(pl.multiple_of(lax.rem(zz, 2) * 64, 64), 64)
        return k_mine.at[(zz // 2) * 4 + lax.rem(y + dy, 4), half]

    k_sent = [
        net.send(k_piece(dy, dz), k_in.at[i], dev(x, y + dy, z + dz, c)) for i, (dy, dz) in enumerate(plane)
    ]
    for copy in sy:
        net.got(copy)
    s_z[0] = s_y[0] + s_y[1] + s_y[2] + s_y[3]
    sz = [net.send(s_z.at[0], s_z.at[1 + i], p) for i, p in enumerate(zs)]
    for copy in q_sent:
        net.got(copy)
    for h in range(2):
        o_sum = o_mine[h * 4 + y].astype(f32)
        q_sum = q_mine[x, 128 * h : 128 * h + 128].astype(f32)
        for i in range(3):
            o_sum = o_sum + o_in[h, i].astype(f32)
            q_sum = q_sum + q_in[i, 128 * h : 128 * h + 128].astype(f32)
        for low in range(2):
            oq[2 * h + low, 0:64] = o_sum[64 * low : 64 * low + 64].astype(b16)
            oq[2 * h + low, 64:128] = q_sum[64 * low : 64 * low + 64].astype(b16)
    oq_sent = [net.send(oq.at[lax.rem(z + d, 4)], oq_in.at[i], zs[i]) for i, d in enumerate((1, 3, 2))]
    m_ring.done()
    for d in range(1, 4):
        block = ALLM.at[lax.rem(x + d, 4) * 2 + c]
        net.send(block, block, twin)
    for copy in oq_sent + k_sent:
        net.got(copy)
    late_half = lambda chip, low: ALL.at[chip * 2 + c, pl.ds(pl.multiple_of(low * 192, 192), 192)]
    oq_sum = oq[z].astype(f32)
    for i in range(3):
        oq_sum = oq_sum + oq_in[i].astype(f32)
    half = pl.ds(pl.multiple_of(z_lo * 64, 64), 64)
    k_sum = k_mine[z_hi * 4 + y, half].astype(f32)
    for i in range(15):
        k_sum = k_sum + k_in[i].astype(f32)
    base = pl.multiple_of(z_lo * 192, 192)
    ALL[slot, pl.ds(base, 128)] = oq_sum.astype(b16)
    ALL[slot, pl.ds(pl.multiple_of(base + 128, 64), 64)] = k_sum.astype(b16)
    piece_here = late_half(x, z_lo)
    ends = [net.send(piece_here, piece_here, p) for p in xs + [dev(x, y, flip, c)] + others]
    net.send(piece_here, piece_here, twin)
    for copy in sz:
        net.got(copy)
    here = lanes(z_hi * 4 + y)
    SM[...] = s_z[0, :, here] + s_z[1, :, here] + s_z[2, :, here] + s_z[3, :, here]
    came = [(lax.rem(x + d, 4), z_lo) for d in (3, 1, 2)] + [(x, 1 - z_lo)]
    came += [(lax.rem(x + d, 4), 1 - z_lo) for d in (3, 1, 2)]
    for copy, (chip, low) in zip(ends, came):
        net.got(copy)
        block = late_half(chip, low)
        net.send(block, block, twin)
    for copy in kept:
        copy.wait()
    net.finish()


def back(*arrays):
    V = pltpu.VMEM
    wide = D + 128
    return pl.pallas_call(
        back_kernel,
        out_shape=(
            shape((2, 128, D), b16),
            shape((2, 128, D), f32),
            shape((8, 1152, 128), b16),
            shape((8, 384, 128), b16),
            shape((8, 128), f32),
        ),
        in_specs=[ANY] * 21,
        out_specs=(ANY, ANY, ANY, VMEM, VMEM),
        scratch_shapes=[
            V((ROWS, wide), f32),
            V((ROWS, D), f32),
            V((ROWS, wide), b16),
            V((ROWS, D), b16),
            V((16, D), b16),
            V((ROWS, 128), jnp.int32),
            V((ROWS, D), b16),
            V((ROWS, D), b16),
            V((D, D), b16),
            V((ROWS, D), b16),
            V((ROWS, D), b16),
            V((ROWS, D), b16),
            V((ROWS, D), b16),
            V((4, ROWS, D), b16),
            V((8, ROWS, 1536), b16),
            V((D, D), b16),
            V((D, D), b16),
            V((8, 1152, 128), b16),
            V((4, ROWS, D), b16),
            V((2, ROWS // 2, D), b16),
            V((2, ROWS, D), b16),
        ]
        + [
            V((4, ROWS, 128), b16),
            V((4, D, 128), b16),
            V((2, D // 2, 128), b16),
            V((2, D, 128), b16),
        ]
        * 3
        + [
            V((2, 4, ROWS, 512), b16),
            V((2, 2, ROWS // 2, 512), b16),
            V((2, 2, ROWS, 512), b16),
            V((ROWS, D), f32),
            V((ROWS, D), b16),
            V((ROWS, D), b16),
            V((ROWS, 2 * D), b16),
            V((ROWS, D), f32),
            V((128, D), b16),
            V((128, D), b16),
            V((ROWS, D), b16),
            V((ROWS, 128), f32),
            V((ROWS, 128), f32),
            V((2, 2, 576, 128), b16),
            V((2, 2, 1152, 128), b16),
            V((3, 576, 128), b16),
            V((8, 128, 128), b16),
            V((2, 3, 128, 128), b16),
            V((4, 256, 128), b16),
            V((3, 256, 128), b16),
            V((4, 128, 128), b16),
            V((3, 128, 128), b16),
            V((8, 128, 128), b16),
            V((15, 64, 128), b16),
            V((8, D), f32),
            V((8, D), f32),
            V((3, 8, D), f32),
            V((4, 8, D), f32),
            V((4, 8, D), f32),
        ]
        + sems(128, 40),
        compiler_params=params(3, 60),
        name="back",
    )(*arrays)


def rotary():
    freqs = np.float32(10000.0) ** (-np.arange(HD // 2, dtype=np.float32) * np.float32(2.0) / np.float32(HD))
    angles = np.arange(D, dtype=np.float32)[:, None] * freqs[None, :]
    cos, sin = np.cos(angles), np.sin(angles)
    return np.concatenate([cos] * 4, axis=1), np.concatenate([-sin, sin] * 2, axis=1)


def learning_rates():
    return (D ** (-0.5), 8.0 * D ** (-0.5), D ** (-0.5), 2.0 * FF ** (-0.5), 0.5 * D ** (-0.5), 0.5)


def adamw(weight, gradient, moment, square, step_rate, decay_rate):
    moment_new = beta_one * moment + (1.0 - beta_one) * gradient
    square_new = beta_two * square + (1.0 - beta_two) * gradient * gradient
    corrected = moment_new / (1.0 - beta_one**STEP)
    spread_by = jnp.sqrt(square_new / (1.0 - beta_two**STEP)) + adam_epsilon
    updated = weight - step_rate * (corrected / spread_by + decay_rate * weight)
    return [moment_new, square_new, updated]


def update_kernel(*refs):
    moe_i, late_i, out_i, gin_i, sums = refs[:5]
    ins, small_ins, outs, small_outs = refs[5:17], refs[17:23], refs[25:37], refs[37:43]
    moe, late, bufs, passing, sem = refs[43], refs[44], refs[45:57], refs[57:59], refs[59]
    rates = learning_rates()
    lane = lax.broadcasted_iota(jnp.int32, (128, 128), 1)
    count = 0

    def copy(src, dst):
        nonlocal count
        made = pltpu.make_async_copy(src, dst, sem.at[count])
        made.start()
        count += 1
        return made

    grads = [copy(moe_i, moe), copy(late_i, late)]
    every = slice(None)
    chunks = [(0, pl.ds(2 * b, 2)) for b in range(3)] + [(1, pl.ds(2 * b, 2)) for b in range(3)]
    chunks += [(2, (every, pl.ds(1024 * p, 1024))) for p in range(2)] + [(3, every)]
    loads = [
        [copy(ins[3 * n + i].at[at], bufs[3 * n + i].at[at]) for i in range(3)] for n, at in chunks
    ]
    through = [copy(src, dst) for src, dst in zip((out_i, gin_i), passing)]
    for n, (grad, rate, decay) in enumerate(
        (
            (sums[0:6, :], rates[4], 0.1),
            (jnp.concatenate([sums[7:8, :], sums[6:7, :]], axis=0), rates[5], 0.0),
        )
    ):
        w, m, v = (ref[...] for ref in small_ins[3 * n : 3 * n + 3])
        for ref, value in zip(small_outs[3 * n : 3 * n + 3], adamw(w, grad, m, v, rate, decay)):
            ref[...] = value
    for load in grads:
        load.wait()
    stores = []

    def apply(n, at, grad, rate):
        w, m, v = bufs[3 * n : 3 * n + 3]
        m[at], v[at], w[at] = adamw(w[at], grad, m[at], v[at], rate, 0.1)

    for step, (n, at) in enumerate(chunks):
        for load in loads[step]:
            load.wait()
        if n == 0:
            b = step

            def tiles(t, carry, b=b):
                for part in range(2):
                    rows = slice(128 * (3 * part + b), 128 * (3 * part + b) + 128)
                    one, two = moe[2 * t, rows].astype(f32), moe[2 * t + 1, rows].astype(f32)
                    cols = lanes(4 * part + t)
                    first = jnp.where(lane < SLICE, one, pltpu.roll(two, SLICE, 1))
                    second = jnp.where(lane < SLICE, pltpu.roll(one, SLICE, 1), two)
                    apply(0, (2 * b, every, cols), first, rates[2])
                    apply(0, (2 * b + 1, every, cols), second, rates[2])
                return carry

            lax.fori_loop(0, 4, tiles, 0)
        elif n == 1:
            b = step - 3

            def tiles(k, carry, b=b):
                for e in range(2):
                    row = 128 * (6 + b) + SLICE * e
                    grad = moe[k, row : row + SLICE].astype(f32)
                    apply(1, (2 * b + e, lanes(k, SLICE), every), grad, rates[3])
                return carry

            lax.fori_loop(0, 8, tiles, 0)
        else:
            part = step - 6
            row = 0 if n == 3 else 64 * (1 + part)

            def tiles(t, carry, n=n, part=part, row=row):
                cols = lanes(t if n == 3 else 8 * part + t)
                for h in range(2):
                    grad = late[t, 192 * h + row : 192 * h + row + 64].astype(f32)
                    apply(n, (pl.ds(64 * h, 64), cols), grad, rates[1 if n == 3 else 0])
                return carry

            lax.fori_loop(0, 8, tiles, 0)
        if step == 1:
            for load, src, dst in zip(through, passing, refs[23:25]):
                load.wait()
                stores.append(copy(src, dst))
        for i, j in ((1, 0), (2, 1), (0, 2)):
            stores.append(copy(bufs[3 * n + i].at[at], outs[3 * n + j].at[at]))
    for store in stores:
        store.wait()


def update(*arrays):
    V = pltpu.VMEM
    dims = [(EXPERTS, 128, D), (EXPERTS, FF, 128), (128, 2 * D), (128, D)]
    return pl.pallas_call(
        update_kernel,
        out_shape=(shape((2, 128, D), b16), shape((2, 128, D), f32))
        + tuple(shape(d, f32) for d in dims + [(EXPERTS, 128), (2, 128)] for _ in range(3)),
        in_specs=[ANY] * 4 + [VMEM] + [ANY] * 12 + [VMEM] * 6,
        out_specs=(ANY,) * 14 + (VMEM,) * 6,
        scratch_shapes=[V((8, 1152, 128), b16), V((8, 384, 128), b16)]
        + [V(d, f32) for d in dims for _ in range(3)]
        + [V((2, 128, D), b16), V((2, 128, D), f32), pltpu.SemaphoreType.DMA((64,))],
        compiler_params=params(),
        name="update",
    )(*arrays)


def on_device(
    tokens, segments, routes, cotangent, w_qkv, w_out, w_gateup, w_down, w_router, w_gains,
    qkv_first, qkv_second, out_first, out_second, gateup_first, gateup_second, down_first, down_second,
    router_first, router_second, gains_first, gains_second,
):
    route_lanes = jnp.pad(routes, ((0, 0), (0, 0), (0, 126)))
    cos, sin = (jnp.asarray(table) for table in rotary())
    X, R, g, WQ, WKV, WO, TL, act_one, q, KV, probs, heads, hidden, act, total, grads, PO, y_tmp, y_got = front(
        tokens, cotangent, route_lanes, w_qkv, w_out, w_gateup, w_down, cos, sin, w_router.T, w_gains, segments
    )
    layer_out, input_grad, ALLM, late, SM = back(
        total, hidden, act, g, TL, R, heads, WO, X, act_one, q, KV, probs, WQ, WKV,
        grads, PO, y_tmp, y_got, cos, sin,
    )
    done = update(
        ALLM, late, layer_out, input_grad, SM, w_gateup, gateup_first, gateup_second, w_down, down_first, down_second,
        w_qkv, qkv_first, qkv_second, w_out, out_first, out_second,
        w_router.T, router_first.T, router_second.T, w_gains, gains_first, gains_second,
    )
    router = [array.T for array in done[14:17]]
    return (*done[:2], *done[8:11], *done[11:14], *done[2:5], *done[5:8], *router, *done[17:20])


def solution(mesh):
    weight = [P("grp", None), P("grp", None), P(None, "grp", None), P(None, None, "grp"), P("grp", None), P(None, "grp")]
    tokens = P("rep", "grp", None)
    moments = [spec for spec in weight for _ in range(2)]
    results = [spec for spec in weight for _ in range(3)]
    return jax.shard_map(
        on_device,
        mesh=mesh,
        in_specs=(tokens, P("rep", None), tokens, tokens, *weight, *moments),
        out_specs=(tokens, tokens, *results),
        check_vma=False,
    )
```

```python
import jax
import jax.numpy as jnp
import numpy as np
from jax import lax
from jax.experimental import pallas as pl
from jax.experimental.pallas import tpu as pltpu
from jax.sharding import PartitionSpec as P

D = 1024
HQ = 16
HK = 8
HD = 64
FF = 512
EXPERTS = 6
TOPK = 2
STEP = 10
ROWS = 256
SLICE = 64
WIDE = EXPERTS * SLICE

beta_one = 0.9
beta_two = 0.95
adam_epsilon = 1e-08
norm_epsilon = 1e-06

f32 = jnp.float32
b16 = jnp.bfloat16
MESH = pl.DeviceIdType.MESH
ANY = pl.BlockSpec(memory_space=pl.ANY)
VMEM = pl.BlockSpec(memory_space=pltpu.VMEM)
MIB = 2**20


def place():
    rep = lax.axis_index("rep")
    grp = lax.axis_index("grp")
    z_lo, x, c = rep // 8, lax.rem(rep // 2, 4), lax.rem(rep, 2)
    z_hi, y = grp // 4, lax.rem(grp, 4)
    return x, y, z_hi * 2 + z_lo, c


def dev(x, y, z, c):
    x, y, z = lax.rem(x + 4, 4), lax.rem(y + 4, 4), lax.rem(z + 4, 4)
    return (lax.rem(z, 2) * 8 + x * 2 + c, (z // 2) * 4 + y)


class Net:
    def __init__(self, send_sems, recv_sems, local_sems):
        self.sems = (send_sems, recv_sems, local_sems)
        self.count = 0
        self.locals = 0
        self.open = []

    def call(self, peers):
        self.peers = len(peers)
        for peer in peers:
            pl.semaphore_signal(pltpu.get_barrier_semaphore(), inc=1, device_id=peer, device_id_type=MESH)

    def answer(self):
        pl.semaphore_wait(pltpu.get_barrier_semaphore(), self.peers)

    def greet(self, peers):
        self.call(peers)
        self.answer()

    def describe(self, n, src, dst, peer):
        return pltpu.make_async_remote_copy(
            src_ref=src,
            dst_ref=dst,
            send_sem=self.sems[0].at[n],
            recv_sem=self.sems[1].at[n],
            device_id=peer,
            device_id_type=MESH,
        )

    def planned(self, src, dst, peer):
        copy = self.describe(self.count, src, dst, peer)
        self.count += 1
        self.open.append(copy)
        return copy

    def send(self, src, dst, peer):
        copy = self.planned(src, dst, peer)
        copy.start()
        return copy

    def local(self, src, dst):
        copy = pltpu.make_async_copy(src, dst, self.sems[2].at[self.locals])
        copy.start()
        self.locals += 1
        return copy

    def got(self, copy):
        copy.wait_recv()
        copy.seen = True

    def gone(self, copy):
        copy.wait_send()
        copy.left = True

    def finish(self):
        for copy in self.open:
            if not getattr(copy, "seen", False):
                copy.wait_recv()
            if not getattr(copy, "left", False):
                copy.wait_send()


def sems(n, n_local=1):
    return [
        pltpu.SemaphoreType.DMA((n,)),
        pltpu.SemaphoreType.DMA((n,)),
        pltpu.SemaphoreType.DMA((n_local,)),
    ]


def params(cid=None, mib=56):
    if cid is None:
        return pltpu.CompilerParams(vmem_limit_bytes=mib * MIB)
    return pltpu.CompilerParams(
        vmem_limit_bytes=mib * MIB, collective_id=cid, has_side_effects=True
    )


def shape(dims, dtype):
    return jax.ShapeDtypeStruct(dims, dtype)


class Ring:
    def __init__(self, net, part, right, left, me):
        self.net, self.part, self.right, self.left = net, part, right, left
        self.before, self.after = lax.rem(me + 3, 4), lax.rem(me + 1, 4)
        self.a1 = net.send(part(me, 0), part(me, 0), right)
        self.b1 = net.send(part(me, 1), part(me, 1), left)
        self.rest = [
            net.send(part(me, 1), part(me, 1), right),
            net.send(part(me, 0), part(me, 0), left),
        ]

    def relay(self):
        net, part = self.net, self.part
        net.got(self.a1)
        self.rest.append(net.send(part(self.before, 0), part(self.before, 0), self.right))
        net.got(self.b1)
        self.rest.append(net.send(part(self.after, 1), part(self.after, 1), self.left))

    def done(self):
        for copy in self.rest:
            self.net.got(copy)


def add_rows(dst, one, two, rows, step):
    def body(i, carry):
        at = pl.ds(pl.multiple_of(i * step, step), step)
        dst[at] = (one[at].astype(f32) + two[at].astype(f32)).astype(b16)
        return carry

    lax.fori_loop(0, rows // step, body, 0)


class Scatter:
    def __init__(self, net, part, tmp, got, right, left, me, rows, step, begin=True):
        self.net, self.part, self.tmp, self.got = net, part, tmp, got
        self.right, self.left, self.me, self.step = right, left, me, step
        self.half = rows // 2
        self.lo, self.hi = pl.ds(0, self.half), pl.ds(self.half, self.half)
        self.after, self.before = lax.rem(me + 1, 4), lax.rem(me + 3, 4)
        self.first, self.rest = [], []
        if begin:
            across = part(lax.rem(me + 2, 4))
            self.first = [net.send(across.at[self.lo], tmp.at[0], right), net.send(across.at[self.hi], tmp.at[1], left)]
            self.rest = [
                net.send(part(self.after).at[self.hi], got.at[0, self.hi], right),
                net.send(part(self.before).at[self.lo], got.at[1, self.lo], left),
            ]

    def relay(self):
        net, tmp, got = self.net, self.tmp, self.got
        for copy in self.first[:1]:
            net.got(copy)
        add_rows(tmp.at[0], tmp.at[0], self.part(self.after).at[self.lo], self.half, self.step)
        self.rest.append(net.send(tmp.at[0], got.at[0, self.lo], self.right))
        for copy in self.first[1:]:
            net.got(copy)
        add_rows(tmp.at[1], tmp.at[1], self.part(self.before).at[self.hi], self.half, self.step)
        self.rest.append(net.send(tmp.at[1], got.at[1, self.hi], self.left))

    def done(self):
        for copy in self.rest:
            self.net.got(copy)

    def term(self, at):
        own = self.part(self.me)
        return own[at].astype(f32) + self.got[0, at].astype(f32) + self.got[1, at].astype(f32)

    def settle(self, dst, rows, step):
        def body(i, carry):
            at = pl.ds(pl.multiple_of(i * step, step), step)
            dst[at] = self.term(at).astype(dst.dtype)
            return carry

        lax.fori_loop(0, rows // step, body, 0)


def dot(a, b):
    return lax.dot_general(a, b, (((1,), (0,)), ((), ())), preferred_element_type=f32)


def dot_t(a, b):
    return lax.dot_general(a, b, (((1,), (1,)), ((), ())), preferred_element_type=f32)


def t_dot(a, b):
    return lax.dot_general(a, b, (((0,), (0,)), ((), ())), preferred_element_type=f32)


def partner_lanes(v):
    lane = lax.broadcasted_iota(jnp.int32, v.shape, 1)
    return jnp.where(lane % HD < HD // 2, pltpu.roll(v, 96, 1), pltpu.roll(v, 32, 1))


def half_mask(rows, half):
    lane = lax.broadcasted_iota(jnp.int32, (rows, 128), 1)
    return (lane < HD) if half == 0 else (lane >= HD)


def spread(tile, half):
    keep = half_mask(ROWS, half)
    heads = []
    for g in range(2):
        v = tile if g == half else pltpu.roll(tile, HD, 1)
        heads.append(jnp.where(keep, v, 0.0).astype(b16))
    low = jnp.concatenate([h[:128] for h in heads], axis=0)
    high = jnp.concatenate([h[128:] for h in heads], axis=0)
    return low, high


def collect(low, high, half):
    heads = []
    for g in range(2):
        v = jnp.concatenate([low[g * 128 : g * 128 + 128], high[g * 128 : g * 128 + 128]], axis=0)
        heads.append(v if g == half else pltpu.roll(v, HD, 1))
    return jnp.where(half_mask(ROWS, 0), heads[0], heads[1])


def router_rows(tail):
    row = lax.broadcasted_iota(jnp.int32, (16, D), 0)
    kept = jnp.where(row < EXPERTS, tail.astype(f32), 0.0).astype(b16)
    return jnp.concatenate([kept, jnp.zeros((112, D), b16)], axis=0)


def one_hot(routes, slot):
    lane = lax.broadcasted_iota(jnp.int32, (ROWS, 128), 1)
    return (routes[:, slot : slot + 1] == lane).astype(f32)


def lanes(n, width=128):
    return pl.ds(pl.multiple_of(n * width, width), width)


class Fan:
    def __init__(self, net, src, at, shards, over, ys):
        self.net, self.src, self.at, self.ys, self.shards = net, src, at, ys, shards
        self.over = net.send(src, at(shards[0]), over)

    def round(self):
        self.out = [self.net.send(self.src, self.at(self.shards[0]), p) for p in self.ys]
        return self

    def forward(self):
        self.net.got(self.over)
        ref = self.at(self.shards[1])
        self.out += [self.net.send(ref, ref, p) for p in self.ys]
        return ref

    def arrivals(self):
        for copy, n in zip(self.out, self.shards[2:]):
            self.net.got(copy)
            yield self.at(n)


def front_kernel(
    tok, cot, routes_in, wqkv, wout, wgu, wdn, cos_t, sin_t, router, gains, segs,
    X_o, R_o, g_o, WQ_o, WKV_o, WO_o, TL_o, one_o, q_o, KV_o, P_o, heads_o, hidden_o, act_o, total, grads_o, PO, y_tmp, y_got,
    X, R, WQ, WKV, WO, TL, one, q, KV, probs_all, heads, hidden, ACT, G, GD, back, tw, tmp, got, gu_acc, dn_acc, grads, bias,
    wq32, wkv32, wo32, gate32, up32, dn32, wq16, wkv16, wo16, gd16, cos, sin, tail32, tail, rl,
    ss, rs, ls,
):
    x, y, z, c = place()
    z_hi = z // 2
    slot = x * 2 + c
    net = Net(ss, rs, ls)
    kept = []
    keep = lambda src, dst: kept.append(net.local(src, dst))
    rl[...] = jnp.zeros_like(rl)
    rl[:, :, 0:TOPK] = routes_in[...]
    loads = [
        net.local(wqkv.at[:, pl.ds(pl.multiple_of(D + c * 512, 512), 512)], wkv32),
        net.local(wqkv.at[:, lanes(slot)], wq32),
        net.local(wout.at[:, lanes(slot)], wo32),
        net.local(wgu.at[:, :, lanes(x)], gate32),
        net.local(wgu.at[:, :, lanes(4 + x)], up32),
        net.local(wdn.at[:, pl.ds(pl.multiple_of(slot * SLICE, SLICE), SLICE), :], dn32),
    ]
    tables = [
        net.local(src.at[lanes(4 * h + y)], dst.at[pl.ds(128 * h, 128)])
        for src, dst in ((cos_t, cos), (sin_t, sin))
        for h in range(2)
    ]
    partner = dev(x, y, z + 2, c)
    over = dev(x, y, 3 - z, c)
    twin = dev(x, y, z, 1 - c)
    xr, xl = dev(x + 1, y, z, c), dev(x - 1, y, z, c)
    yr, yl = dev(x, y + 1, z, c), dev(x, y - 1, z, c)
    ys = [yr, yl, dev(x, y + 2, z, c)]
    net.greet(ys + [over, partner, twin, xr, xl])
    rows = [z_hi * 4, 4 - z_hi * 4]
    shards = [rows[0] + y, rows[1] + y]
    shards += [row + lax.rem(y + d, 4) for row in rows for d in (3, 1, 2)]
    half_rows = lanes(z_hi)
    kv_lanes = pl.ds(pl.multiple_of(c * 512, 512), 512)
    fan = lambda src, at: Fan(net, src, at, shards, over, ys)
    loads[0].wait()
    wkv16[...] = wkv32[...].astype(b16)
    kv_fan = fan(wkv16, lambda n: WKV.at[lanes(n), kv_lanes]).round()
    forwards = [net.send(wkv16, WKV.at[lanes(shards[0]), kv_lanes], twin)]
    own = [net.local(tok.at[z_hi], X.at[half_rows]), net.local(rl.at[z_hi], R.at[half_rows])]
    eye = lax.broadcasted_iota(jnp.int32, (128, 128), 0) == lax.broadcasted_iota(jnp.int32, (128, 128), 1)
    tail32[...] = jnp.zeros_like(tail32)
    tail32[0:6, :] = router[...]
    tail32[6:8, :] = gains[...]
    tail[...] = tail32[...].astype(b16)
    tl_fan = fan(tail, lambda n: TL.at[:, lanes(n)]).round()
    own += [
        net.local(wkv16, WKV.at[lanes(shards[0]), kv_lanes]),
        net.local(tail, TL.at[:, lanes(shards[0])]),
    ]

    place_k = lax.broadcasted_iota(jnp.int32, (128, D), 1)
    place_q = lax.broadcasted_iota(jnp.int32, (128, D), 0) + y * 128
    pick_row = lambda v: jnp.where(z_hi == 0, v[0:1], v[1:2]).astype(f32)
    seg_k = pick_row(segs[...])
    for h in range(2):
        seg_row = jnp.broadcast_to(pick_row(segs[:, lanes(4 * h + y)]), (128, 128))
        seg_q = jnp.sum(jnp.where(eye, seg_row, 0.0), axis=1, keepdims=True)
        fine = (place_q + 512 * h >= place_k) & (seg_q == seg_k)
        bias[128 * h : 128 * h + 128, :] = jnp.where(fine, 0.0, -1e30)

    ref = kv_fan.forward()
    forwards.append(net.send(ref, ref, twin))
    x_in = net.send(tok.at[1 - z_hi], X.at[half_rows], partner)
    tl_fan.forward()
    loads[1].wait()
    wq16[...] = wq32[...].astype(b16)
    q_fan = fan(wq16, lambda n: WQ.at[lanes(n), lanes(slot)])
    loads[2].wait()
    wo16[...] = wo32[...].astype(b16)
    o_fan = fan(wo16, lambda n: WO.at[lanes(n), lanes(slot)])
    more = [
        net.local(wq16, WQ.at[lanes(shards[0]), lanes(slot)]),
        net.local(wo16, WO.at[lanes(shards[0]), lanes(slot)]),
    ]
    r_in = net.send(rl.at[1 - z_hi], R.at[half_rows], partner)

    for copy in own + tables:
        copy.wait()
    for _ in tl_fan.arrivals():
        pass
    net.got(x_in)
    v = X[...].astype(f32)
    r = lax.rsqrt(jnp.mean(v * v, axis=-1, keepdims=True) + norm_epsilon)
    one[...] = (v * r * TL[6:7, :].astype(f32)).astype(b16)
    keep(X, X_o)
    keep(one, one_o)
    keep(TL, TL_o)

    for ref in kv_fan.arrivals():
        forwards.append(net.send(ref, ref, twin))
    for pieces in (q_fan, o_fan):
        pieces.round()
        pieces.forward()
    for copy in forwards:
        net.got(copy)
    cosine, sine = cos[...], sin[...]
    a = one[...]
    for t in range(4):
        out = dot(a, WKV[:, 256 * t : 256 * t + 256])
        for u in range(2):
            tile = out[:, 128 * u : 128 * u + 128]
            if t < 2:
                tile = tile * cosine + partner_lanes(tile) * sine
            KV[y, :, 256 * t + 128 * u : 256 * t + 128 * u + 128] = tile.astype(b16)
    kv_ring = Ring(net, lambda n, h: KV.at[n, pl.ds(h * 128, 128)], yr, yl, y)
    keep(WKV, WKV_o)

    for load in loads[3:]:
        load.wait()
    lane = lax.broadcasted_iota(jnp.int32, (128, 128), 1)
    mine_first = c == 0
    for part, src in enumerate((gate32, up32)):
        for b in range(3):
            one_e, two_e = src[2 * b], src[2 * b + 1]
            first = jnp.where(mine_first, one_e, pltpu.roll(one_e, SLICE, 1))
            second = jnp.where(mine_first, pltpu.roll(two_e, SLICE, 1), two_e)
            at = slice(128 * (3 * part + b), 128 * (3 * part + b) + 128)
            gd16[at, :] = jnp.where(lane < SLICE, first, second).astype(b16)
    gd16[2 * WIDE :, :] = dn32[...].reshape(WIDE, 128).astype(b16)
    gd_own = net.local(gd16, GD.at[shards[0]])
    gd_over = net.send(gd16, GD.at[shards[0]], over)
    g_in = net.send(cot.at[1 - z_hi], G.at[slot, half_rows], partner)
    g_own = net.local(cot.at[z_hi], G.at[slot, half_rows])
    for copy in more:
        copy.wait()

    rings, twins = [], []
    for pieces, whole in ((q_fan, WQ), (o_fan, WO)):
        for _ in pieces.arrivals():
            pass
        part = lambda n, h, whole=whole: whole.at[pl.ds(h * 512, 512), lanes(n * 2 + c)]
        rings.append(Ring(net, part, xr, xl, x))
        twins.append([net.send(whole.at[:, lanes(slot)], whole.at[:, lanes(slot)], twin)])
    kv_ring.relay()
    rings[0].relay()
    rings[1].relay()
    gd_own.wait()
    gd_part = lambda row: lambda n, h: GD.at[row + n, pl.ds(h * 576, 576)]
    gd_rings = [Ring(net, gd_part(rows[0]), yr, yl, y)]
    net.got(gd_over)
    gd_rings.append(Ring(net, gd_part(rows[1]), yr, yl, y))
    g_own.wait()
    net.got(g_in)
    g_ring = Ring(net, lambda n, h: G.at[n * 2 + c, pl.ds(h * 128, 128)], xr, xl, x)
    g_twin = net.send(G.at[slot], G.at[slot], twin)
    keep(G.at[slot], g_o)

    def share(n, whole):
        rings[n].done()
        for d in range(1, 4):
            tile = whole.at[:, lanes(lax.rem(x + d, 4) * 2 + c)]
            twins[n].append(net.send(tile, tile, twin))

    share(0, WQ)
    for copy in twins[0]:
        net.got(copy)
    for t in range(4):
        out = dot(a, WQ[:, 256 * t : 256 * t + 256])
        for u in range(2):
            tile = out[:, 128 * u : 128 * u + 128]
            tile = tile * cosine + partner_lanes(tile) * sine
            q[:, 256 * t + 128 * u : 256 * t + 128 * u + 128] = (tile * 0.125).astype(b16)
    keep(q, q_o)
    keep(WQ, WQ_o)
    kv_ring.done()
    keep(KV, KV_o)

    low_bias = jnp.concatenate([bias[:128, :512]] * 2, axis=0)
    high_bias = jnp.concatenate([bias[128:, :]] * 2, axis=0)

    def attend(pair, carry):
        cols, vcols = lanes(pair), lanes(4 + pair)
        keys = [KV[:, :128, cols].reshape(512, 128), KV[:, 128:, cols].reshape(512, 128)]
        vals = [KV[:, :128, vcols].reshape(512, 128), KV[:, 128:, vcols].reshape(512, 128)]
        keys_all = jnp.concatenate(keys, axis=0)
        vals_all = jnp.concatenate(vals, axis=0)
        for half in range(2):
            cols = lanes(2 * pair + half)
            low, high = spread(q[:, cols].astype(f32), half)
            outs = []
            for qq, kk, vv, bb, at_p in (
                (low, keys[0], vals[0], low_bias, slice(0, 512)),
                (high, keys_all, vals_all, high_bias, slice(512, 1536)),
            ):
                s = dot_t(qq, kk) + bb
                top = jnp.max(s, axis=-1, keepdims=True)
                e = jnp.exp(s - top)
                probs = (e * (1.0 / jnp.sum(e, axis=-1, keepdims=True))).astype(b16)
                probs_all[2 * pair + half, :, at_p] = probs
                outs.append(dot(probs, vv))
            heads[:, cols] = collect(outs[0], outs[1], half).astype(b16)
        return carry

    for m in range(2):
        lax.fori_loop(2 * m, 2 * m + 2, attend, 0)
        keep(probs_all.at[pl.ds(4 * m, 4)], P_o.at[pl.ds(4 * m, 4)])
        if m == 0:
            share(1, WO)
            g_ring.relay()
            gd_rings[0].relay()
    gd_rings[1].relay()
    keep(heads, heads_o)

    for copy in twins[1]:
        net.got(copy)
    keep(WO, WO_o)
    all_heads = heads[...]
    for t in range(4):
        cols = slice(256 * t, 256 * t + 256)
        hidden[:, cols] = X[:, cols].astype(f32) + dot(all_heads, WO[:, cols])
    h = hidden[...]
    r = lax.rsqrt(jnp.mean(h * h, axis=-1, keepdims=True) + norm_epsilon)
    a = (h * r * TL[7:8, :].astype(f32)).astype(b16)
    ACT[slot, :, :D] = a
    logits = dot_t(a, router_rows(TL[...]))
    net.got(r_in)
    routes = R[...]
    hots = [one_hot(routes, k) for k in range(TOPK)]
    picked = [jnp.sum(hot * logits, axis=-1, keepdims=True) for hot in hots]
    top = jnp.maximum(picked[0], picked[1])
    powers = [jnp.exp(v - top) for v in picked]
    power = powers[0] + powers[1]
    mixing = hots[0] * (powers[0] / power) + hots[1] * (powers[1] / power)
    big = mixing.astype(b16).astype(f32)
    ACT[slot, :, D:] = (big + pltpu.roll(mixing - big, 16, 1)).astype(b16)
    chips = {d: lax.rem(x + d, 4) for d in range(4)}
    mine = {d: chips[d] * 2 + c for d in range(4)}
    other = {d: chips[d] * 2 + 1 - c for d in range(4)}
    lo, hi = pl.ds(0, 128), pl.ds(128, 128)
    ins, outs = pl.ds(0, D + 128), pl.ds(D + 128, D)
    before, across, after = chips[3], chips[2], chips[1]
    home_block = ACT.at[slot]
    swap = net.send(home_block, home_block, twin)
    a1 = net.send(ACT.at[slot, lo], ACT.at[slot, lo], xr)
    b1 = net.send(ACT.at[slot, hi], ACT.at[slot, hi], xl)
    gu_acc[...] = jnp.zeros_like(gu_acc)
    dn_acc[...] = jnp.zeros_like(dn_acc)
    row = lax.broadcasted_iota(jnp.int32, (128, WIDE), 0)
    lane = lax.broadcasted_iota(jnp.int32, (128, WIDE), 1)
    pick = ((row % 16 == lane // SLICE) & (row < 32)).astype(b16)

    def compute(parts):
        weights = jnp.concatenate(
            [GD[:, 128 * b : 128 * b + 128].reshape(D, 128) for b in range(6)], axis=1
        )
        down_w = jnp.concatenate([GD[n, 2 * WIDE :] for n in range(8)], axis=1)
        both = lambda ref, cols: jnp.concatenate([ref[n, at, cols] for n, at in parts], axis=0)
        a = both(ACT, slice(0, D))
        mix = dot(both(ACT, slice(D, D + 128)), pick)
        gt = both(G, slice(0, D))
        h = dot(a, weights)
        gate, up = h[:, :WIDE], h[:, WIDE:]
        gw = dot_t(gt, down_w)
        s = 1.0 / (1.0 + jnp.exp(-gate))
        silu = gate * s
        inner = silu * up
        scaled = (inner * mix).astype(b16)
        gi = gw * mix
        ggu = jnp.concatenate(
            [(gi * up * s * (1.0 + gate * (1.0 - s))).astype(b16), (gi * silu).astype(b16)], axis=1
        )
        down = dot_t(ggu, weights).astype(b16)
        dots = dot_t((inner * gw).astype(b16), pick).astype(b16)
        terms = dot(scaled, down_w).astype(b16)
        for i, (n, at) in enumerate(parts):
            rows = slice(128 * i, 128 * i + 128)
            back[n, at, :D] = down[rows]
            back[n, at, D : D + 128] = dots[rows]
            back[n, at, D + 128 :] = terms[rows]
        gu_acc[...] += t_dot(a, ggu)
        dn_acc[...] += t_dot(scaled, gt)

    def add(dst, one, two):
        add_rows(dst, one, two, dst.shape[0], 16)

    def units(chip, offset, pieces):
        first = net.count
        sent = [net.planned(back.at[other[d], at], tw.at[chips[d], at], twin) for d, at in pieces]

        def one_unit(j, carry):
            n, at = chip(j), pl.ds(pl.multiple_of(offset(j), 128), 128)
            compute([(n * 2 + c, at), (n * 2 + 1 - c, at)])
            net.describe(first + j, back.at[n * 2 + 1 - c, at], tw.at[n, at], twin).start()
            return carry

        lax.fori_loop(0, 2, one_unit, 0)
        return sent

    def settle(d, at, sent):
        net.got(sent)
        add(tw.at[chips[d], at], tw.at[chips[d], at], back.at[mine[d], at])
        keep(tw.at[chips[d], at, outs], PO.at[chips[d], at])

    def forward(d, at, arrive):
        net.got(arrive)
        block = ACT.at[mine[d], at]
        return net.send(block, block, twin)

    keep(hidden, hidden_o)
    keep(ACT.at[slot], act_o)
    keep(R, R_o)
    for pieces in gd_rings:
        pieces.done()
    net.got(swap)
    net.got(g_twin)

    def own_chip(j, carry):
        n = x * 2 + lax.rem(c + j, 2)
        compute([(n, lo), (n, hi)])
        return carry

    lax.fori_loop(0, 2, own_chip, 0)
    home = net.send(back.at[other[0]], tw.at[x], twin)
    net.got(a1)
    a3 = net.send(ACT.at[mine[3], lo], ACT.at[mine[3], lo], xr)
    net.got(b1)
    b3 = net.send(ACT.at[mine[1], hi], ACT.at[mine[1], hi], xl)
    a2 = net.send(ACT.at[slot, hi], ACT.at[slot, hi], xr)
    b2 = net.send(ACT.at[slot, lo], ACT.at[slot, lo], xl)
    f1, f2 = (net.send(ACT.at[mine[d], at], ACT.at[mine[d], at], twin) for d, at in ((3, lo), (1, hi)))
    g_ring.done()
    g_far = [net.send(G.at[mine[d]], G.at[mine[d]], twin) for d in (3, 1, 2)]
    for copy in g_far:
        net.got(copy)
    for copy in (f1, f2):
        net.got(copy)
    ends_of = lambda j: lax.rem(x + 3 - 2 * j, 4)
    u1, u2 = units(ends_of, lambda j: 128 * j, [(3, lo), (1, hi)])
    f3 = forward(2, lo, a3)
    f4 = forward(2, hi, b3)
    settle(3, lo, u1)
    last = [net.send(tw.at[before, lo, ins], got.at[1, lo], xl)]
    settle(1, hi, u2)
    last.append(net.send(tw.at[after, hi, ins], got.at[0, hi], xr))
    for copy in (f3, f4):
        net.got(copy)
    u3, u4 = units(lambda j: across, lambda j: 128 * j, [(2, lo), (2, hi)])
    f5 = forward(3, hi, a2)
    f6 = forward(1, lo, b2)
    settle(2, lo, u3)
    s1 = net.send(tw.at[across, lo, ins], tmp.at[0], xr)
    settle(2, hi, u4)
    s2 = net.send(tw.at[across, hi, ins], tmp.at[1], xl)
    for copy in (f5, f6):
        net.got(copy)
    u5, u6 = units(ends_of, lambda j: 128 - 128 * j, [(3, hi), (1, lo)])
    net.got(home)
    add(tw.at[x], tw.at[x], back.at[mine[0]])
    keep(tw.at[x, :, outs], PO.at[x])
    for n in range(8):
        at = slice(128 * n, 128 * n + 128)
        for b in range(6):
            grads[n, 128 * b : 128 * b + 128] = gu_acc[at, 128 * b : 128 * b + 128].astype(b16)
        for b in range(3):
            rows = slice(128 * (6 + b), 128 * (6 + b) + 128)
            grads[n, rows] = dn_acc[128 * b : 128 * b + 128, at].astype(b16)
    keep(grads, grads_o)
    for n in range(2):
        Scatter(net, lambda k, n=n: grads.at[n * 4 + k], y_tmp.at[n], y_got.at[n], yr, yl, y, 1152, 64)
    settle(3, hi, u5)
    settle(1, lo, u6)
    net.got(s1)
    add(tmp.at[0], tmp.at[0], tw.at[after, lo, ins])
    last.append(net.send(tmp.at[0], got.at[0, lo], xr))
    net.got(s2)
    add(tmp.at[1], tmp.at[1], tw.at[before, hi, ins])
    last.append(net.send(tmp.at[1], got.at[1, hi], xl))
    for copy in last:
        net.got(copy)

    def body(i, carry):
        at = pl.ds(pl.multiple_of(i * 16, 16), 16)
        total[at] = tw[x, at, : D + 128].astype(f32) + got[0, at].astype(f32) + got[1, at].astype(f32)
        return carry

    lax.fori_loop(0, ROWS // 16, body, 0)
    for copy in kept:
        copy.wait()
    net.finish()


def front(*arrays):
    V = pltpu.VMEM
    wide = D + 128
    return pl.pallas_call(
        front_kernel,
        out_shape=(
            shape((ROWS, D), b16),
            shape((ROWS, 128), jnp.int32),
            shape((ROWS, D), b16),
            shape((D, D), b16),
            shape((D, D), b16),
            shape((D, D), b16),
            shape((16, D), b16),
            shape((ROWS, D), b16),
            shape((ROWS, D), b16),
            shape((4, ROWS, D), b16),
            shape((8, ROWS, 1536), b16),
            shape((ROWS, D), b16),
            shape((ROWS, D), f32),
            shape((ROWS, D + 128), b16),
            shape((ROWS, wide), f32),
            shape((8, 9 * 128, 128), b16),
            shape((4, ROWS, D), b16),
            shape((2, 2, 576, 128), b16),
            shape((2, 2, 1152, 128), b16),
        ),
        in_specs=[ANY] * 2 + [VMEM] + [ANY] * 6 + [VMEM] * 3,
        out_specs=(ANY,) * 14 + (VMEM,) + (ANY,) * 4,
        scratch_shapes=[
            V((ROWS, D), b16),
            V((ROWS, 128), jnp.int32),
            V((D, D), b16),
            V((D, D), b16),
            V((D, D), b16),
            V((16, D), b16),
            V((ROWS, D), b16),
            V((ROWS, D), b16),
            V((4, ROWS, D), b16),
            V((8, ROWS, 1536), b16),
            V((ROWS, D), b16),
            V((ROWS, D), f32),
            V((8, ROWS, wide), b16),
            V((8, ROWS, D), b16),
            V((8, 3 * WIDE, 128), b16),
            V((8, ROWS, wide + D), b16),
            V((4, ROWS, wide + D), b16),
            V((2, ROWS // 2, wide), b16),
            V((2, ROWS, wide), b16),
            V((D, 2 * WIDE), f32),
            V((WIDE, D), f32),
            V((8, 9 * 128, 128), b16),
            V((ROWS, D), f32),
            V((128, 128), f32),
            V((128, 512), f32),
            V((128, 128), f32),
            V((EXPERTS, 128, 128), f32),
            V((EXPERTS, 128, 128), f32),
            V((EXPERTS, SLICE, 128), f32),
            V((128, 128), b16),
            V((128, 512), b16),
            V((128, 128), b16),
            V((3 * WIDE, 128), b16),
            V((ROWS, 128), f32),
            V((ROWS, 128), f32),
            V((16, 128), f32),
            V((16, 128), b16),
            V((2, 128, 128), jnp.int32),
        ]
        + sems(160, 64),
        compiler_params=params(0, 62),
        name="front",
    )(*arrays)


def back_kernel(
    total_i, hidden_i, act_i, g_i, TL_i, R_i, heads_i, WO_i, X_i, one_i, q_i, KV_i, P_i, WQ_i, WKV_i,
    grads_i, PO, y_tmp_i, y_got_i, cos_t, sin_t,
    OUT, GIN, ALLM, ALL, SM,
    total, hidden, act, g, TL, R, heads, heads_t, WO, X, one, one_t, q, KV, P, WQ, WKV, gr, po, po_tmp, po_got,
    o_t, o_w, o_tmp, o_got, q_t, q_w, q_tmp, q_got, k_t, k_w, k_tmp, k_got,
    dkv, kv_tmp, kv_got, gh, ghl, ghi, gp, gin, gin_low, gin_got, ob, cos, sin,
    y_tmp, y_got, z_got, o_mine, o_in, q_mine, q_in, oq, oq_in, k_mine, k_in, small, s_twin, s_x, s_y, s_z,
    ss, rs, ls,
):
    x, y, z, c = place()
    z_hi, z_lo = z // 2, lax.rem(z, 2)
    slot = x * 2 + c
    net = Net(ss, rs, ls)
    kept = []
    twin = dev(x, y, z, 1 - c)
    xs = [dev(x + d, y, z, c) for d in (1, 3, 2)]
    ys = [dev(x, y + d, z, c) for d in (1, 3, 2)]
    zs = [dev(x, y, z + d, c) for d in (1, 3, 2)]
    flip = z + 1 - 2 * z_lo
    others = [dev(x + d, y, flip, c) for d in (1, 3, 2)]
    plane = [(dy, dz) for dz in range(4) for dy in range(4) if dy or dz]
    (xr, xl, x2), (yr, yl, y2), (zr, zl, z2) = xs, ys, zs
    net.call([twin] + xs + others + [dev(x, y + dy, z + dz, c) for dy, dz in plane])
    first = [
        net.local(*pair)
        for pair in (
            (total_i, total), (hidden_i, hidden), (act_i, act), (TL_i, TL), (R_i, R),
            (g_i, g), (WO_i, WO),
        )
    ]
    grad_load = [net.local(grads_i, gr), net.local(y_tmp_i, y_tmp)]
    for n in range(2):
        at = pl.ds(576 * (1 - n), 576)
        grad_load.append(net.local(y_got_i.at[:, n, at], y_got.at[:, n, at]))
    po_load = net.local(PO, po)
    for copy in first:
        copy.wait()
    second = [
        net.local(*pair)
        for pair in ((KV_i, KV), (q_i, q), (P_i, P), (heads_i, heads), (one_i, one), (X_i, X), (WQ_i, WQ), (WKV_i, WKV))
    ]
    second += [
        net.local(src.at[lanes(4 * h + y)], dst.at[pl.ds(128 * h, 128)])
        for src, dst in ((cos_t, cos), (sin_t, sin))
        for h in range(2)
    ]

    h = hidden[...]
    a = act[:, :D]
    mix = act[:, D:].astype(f32)
    lane = lax.broadcasted_iota(jnp.int32, (ROWS, 128), 1)
    mixing = jnp.where(lane < 16, mix + pltpu.roll(mix, 112, 1), 0.0)
    dg = total[:, D:]
    routes = R[...]
    hots = [one_hot(routes, k) for k in range(TOPK)]
    probs = [jnp.sum(hot * mixing, axis=-1, keepdims=True) for hot in hots]
    dgs = [jnp.sum(hot * dg, axis=-1, keepdims=True) for hot in hots]
    mean = probs[0] * dgs[0] + probs[1] * dgs[1]
    grad_logits = sum(hot * (p * (d - mean)) for hot, p, d in zip(hots, probs, dgs)).astype(b16)
    ga = total[:, :D] + dot(grad_logits, router_rows(TL[...]))
    small[0:6, :] = t_dot(grad_logits, a)[0:6, :]
    r = lax.rsqrt(jnp.mean(h * h, axis=-1, keepdims=True) + norm_epsilon)
    u = ga * TL[7:8, :].astype(f32)
    small[6:7, :] = jnp.sum(ga * h * r, axis=0, keepdims=True)
    gh[...] = g[...].astype(f32) + r * (u - h * (r * r * jnp.mean(u * h, axis=-1, keepdims=True)))
    ghl[...] = gh[...].astype(b16)

    net.answer()
    for copy in grad_load:
        copy.wait()
    y_rings = [
        Scatter(net, lambda n, h=h: gr.at[h * 4 + n], y_tmp.at[h], y_got.at[h], yr, yl, y, 1152, 64, begin=False)
        for h in range(2)
    ]
    for ring in y_rings:
        ring.relay()
    po_load.wait()
    out_ring = Scatter(net, lambda n: po.at[n], po_tmp, po_got, xr, xl, x, ROWS, 16)

    def columns(src, dst, first=0):
        return [net.send(src.at[:, lanes(first + 2 * n + 1 - c)], dst.at[n], twin) for n in range(4)]

    o_sent = columns(ghl, o_t)
    lefts = [net.send(heads_i, heads_t, twin), net.send(one_i, one_t, twin)]
    ghi[...] = dot_t(ghl[...], WO[...]).astype(b16)

    def weight_grad(left, left_t, right, first, right_t, sent, store):
        for copy in sent:
            net.got(copy)
        for m in range(2):
            own = jnp.concatenate([right[:, lanes(first + 2 * n + c)] for n in (2 * m, 2 * m + 1)], axis=1)
            far = jnp.concatenate([right_t[2 * m], right_t[2 * m + 1]], axis=1)
            piece = (t_dot(left[...], own) + t_dot(left_t[...], far)).astype(b16)
            for i in range(2):
                store(2 * m + i, piece[:, 128 * i : 128 * i + 128])

    def store_o(n, tile):
        o_w[n] = tile

    def store_k(n, tile):
        k_w[n] = tile

    def store_q(n, tile):
        for shard in range(8):
            row = 256 * n + 128 * (shard // 4)
            q_w[shard % 4, row : row + 128] = tile[128 * shard : 128 * shard + 128]

    for copy in second:
        copy.wait()
    cosine, sine = cos[...], sin[...]

    def pair(n, carry):
        cols, vcols = lanes(n), lanes(4 + n)
        keys = [KV[:, :128, cols].reshape(512, 128), KV[:, 128:, cols].reshape(512, 128)]
        vals = [KV[:, :128, vcols].reshape(512, 128), KV[:, 128:, vcols].reshape(512, 128)]
        keys_all = jnp.concatenate(keys, axis=0)
        vals_all = jnp.concatenate(vals, axis=0)
        sums = None
        for half in range(2):
            at = lanes(2 * n + half)
            q_low, q_high = spread(q[:, at].astype(f32), half)
            do_low, do_high = spread(ghi[:, at].astype(f32), half)
            outs, terms = [], []
            for qq, dd, kk, vv, at_p in (
                (q_low, do_low, keys[0], vals[0], slice(0, 512)),
                (q_high, do_high, keys_all, vals_all, slice(512, 1536)),
            ):
                pr = P[2 * n + half, :, at_p]
                dp = dot_t(dd, vv)
                pf = pr.astype(f32)
                prod = pf * dp
                ds = (prod - pf * jnp.sum(prod, axis=-1, keepdims=True)).astype(b16)
                outs.append(dot(ds, kk) * 0.125)
                terms.append((t_dot(ds, qq), t_dot(pr, dd)))
            tile = collect(outs[0], outs[1], half)
            gp[:, at] = (tile * cosine - partner_lanes(tile) * sine).astype(b16)
            sums = terms if half == 0 else [(i + k, j + m) for (i, j), (k, m) in zip(sums, terms)]
        for part in range(2):
            lows, whole = sums[0][part], sums[1][part]
            where = lanes(2 * part + lax.rem(n, 2))
            dkv[n // 2, :, :128, where] = (lows + whole[:512]).reshape(4, 128, 128).astype(b16)
            dkv[n // 2, :, 128:, where] = whole[512:].reshape(4, 128, 128).astype(b16)
        return carry

    def keys_home(n):
        return Scatter(net, lambda k: dkv.at[n, k], kv_tmp.at[n], kv_got.at[n], yr, yl, y, ROWS, 32)

    lax.fori_loop(0, 2, pair, 0)
    kv_rings = [keys_home(0)]
    for n, ring in enumerate(y_rings):
        ring.done()
        ring.settle(gr.at[n * 4 + y], 1152, 64)

    def piece(zz):
        return gr.at[(zz // 2) * 4 + y, pl.ds(pl.multiple_of(lax.rem(zz, 2) * 576, 576), 576)]

    z_in = [net.send(piece(lax.rem(z + d, 4)), z_got.at[i], zs[i]) for i, d in enumerate((1, 3, 2))]
    out_ring.relay()
    net.got(lefts[0])
    weight_grad(heads, heads_t, ghl, 0, o_t, o_sent, store_o)
    o_ring = Scatter(net, lambda n: o_w.at[n], o_tmp, o_got, xr, xl, x, 1024, 64)
    lax.fori_loop(2, 4, pair, 0)
    kv_rings.append(keys_home(1))
    kv_rings[0].relay()
    q_sent = columns(gp, q_t)
    for copy in z_in:
        net.got(copy)
    base = pl.multiple_of(z_lo * 576, 576)
    for i in range(9):
        at = slice(64 * i, 64 * i + 64)
        here = pl.ds(pl.multiple_of(base + 64 * i, 64), 64)
        v = gr[z_hi * 4 + y, here].astype(f32)
        for n in range(3):
            v = v + z_got[n, at].astype(f32)
        z_got[0, at] = v.astype(b16)
    half_m = ALLM.at[slot, pl.ds(base, 576)]
    own_m = net.local(z_got.at[0], half_m)
    hop = net.send(z_got.at[0], half_m, dev(x, y, flip, c))

    o_ring.relay()
    net.got(lefts[1])
    weight_grad(one, one_t, gp, 0, q_t, q_sent, store_q)
    own_m.wait()
    net.got(hop)
    block = ALLM.at[slot]
    net.send(block, block, twin)
    m_ring = Ring(net, lambda n, h: ALLM.at[n * 2 + c, pl.ds(h * 576, 576)], xr, xl, x)
    kv_rings[1].relay()
    q_ring = Scatter(net, lambda n: q_w.at[n], q_tmp, q_got, yr, yl, y, 1024, 64)
    ga = dot_t(gp[:, :D], WQ[...])
    out_ring.done()
    ob[...] = (hidden[...] + out_ring.term(slice(None))).astype(b16)
    rows_of = lambda n: pl.ds(pl.multiple_of(n * 128, 128), 128)
    net.send(ob.at[rows_of(1 - z_hi)], OUT.at[z_hi], z2)
    kept.append(net.local(ob.at[rows_of(z_hi)], OUT.at[z_hi]))

    for n in range(2):
        kv_rings[n].done()
        for part in range(2):
            for i in range(2):
                src = slice(256 * part + 128 * i, 256 * part + 128 * i + 128)
                tile = dkv[n, y, :, src].astype(f32)
                tile = tile + kv_got[n, 0, :, src].astype(f32) + kv_got[n, 1, :, src].astype(f32)
                if part == 0:
                    tile = tile * cosine - partner_lanes(tile) * sine
                to = D + 512 * part + 256 * n + 128 * i
                gp[:, to : to + 128] = tile.astype(b16)
    k_sent = columns(gp, k_t, 8)
    ga = ga + dot_t(gp[:, D:], WKV[...])
    weight_grad(one, one_t, gp, 8, k_t, k_sent, store_k)
    k_ring = Scatter(net, lambda n: k_w.at[n], k_tmp, k_got, xr, xl, x, 1024, 64)
    v = X[...].astype(f32)
    r = lax.rsqrt(jnp.mean(v * v, axis=-1, keepdims=True) + norm_epsilon)
    u = ga * TL[6:7, :].astype(f32)
    small[7:8, :] = jnp.sum(ga * v * r, axis=0, keepdims=True)
    sm = net.send(small, s_twin, twin)
    gin[...] = gh[...] + r * (u - v * (r * r * jnp.mean(u * v, axis=-1, keepdims=True)))
    gin_low[...] = gin[rows_of(1 - z_hi)].astype(b16)
    swap = net.send(gin_low, gin_got, z2)
    gin_kept = net.local(gin.at[rows_of(z_hi)], GIN.at[z_hi])
    m_ring.relay()
    q_ring.relay()
    o_ring.done()
    for n in range(8):
        o_mine[n] = o_ring.term(slice(128 * n, 128 * n + 128)).astype(b16)
    o_sent = [
        net.send(o_mine.at[h * 4 + lax.rem(y + d, 4)], o_in.at[h, i], ys[i])
        for h in range(2)
        for i, d in enumerate((1, 3, 2))
    ]
    net.got(sm)
    s_twin[...] += small[...]
    sx = [net.send(s_twin, s_x.at[i], p) for i, p in enumerate(xs)]
    k_ring.relay()
    q_ring.done()
    for n in range(4):
        q_mine[n] = q_ring.term(slice(256 * n, 256 * n + 256)).astype(b16)
    q_sent = [net.send(q_mine.at[lax.rem(x + d, 4)], q_in.at[i], xs[i]) for i, d in enumerate((1, 3, 2))]
    for copy in sx:
        net.got(copy)
    s_y[0] = s_twin[...] + s_x[0] + s_x[1] + s_x[2]
    sy = [net.send(s_y.at[0], s_y.at[1 + i], p) for i, p in enumerate(ys)]
    for copy in o_sent:
        net.got(copy)
    net.got(swap)
    gin_kept.wait()
    gin[rows_of(z_hi)] = gin_got[...].astype(f32)
    kept.append(net.local(gin.at[rows_of(z_hi)], GIN.at[1 - z_hi]))
    k_ring.done()
    for n in range(8):
        k_mine[n] = k_ring.term(slice(128 * n, 128 * n + 128)).astype(b16)

    def k_piece(dy, dz):
        zz = lax.rem(z + dz, 4)
        half = pl.ds(pl.multiple_of(lax.rem(zz, 2) * 64, 64), 64)
        return k_mine.at[(zz // 2) * 4 + lax.rem(y + dy, 4), half]

    k_sent = [
        net.send(k_piece(dy, dz), k_in.at[i], dev(x, y + dy, z + dz, c)) for i, (dy, dz) in enumerate(plane)
    ]
    for copy in sy:
        net.got(copy)
    s_z[0] = s_y[0] + s_y[1] + s_y[2] + s_y[3]
    sz = [net.send(s_z.at[0], s_z.at[1 + i], p) for i, p in enumerate(zs)]
    for copy in q_sent:
        net.got(copy)
    for h in range(2):
        o_sum = o_mine[h * 4 + y].astype(f32)
        q_sum = q_mine[x, 128 * h : 128 * h + 128].astype(f32)
        for i in range(3):
            o_sum = o_sum + o_in[h, i].astype(f32)
            q_sum = q_sum + q_in[i, 128 * h : 128 * h + 128].astype(f32)
        for low in range(2):
            oq[2 * h + low, 0:64] = o_sum[64 * low : 64 * low + 64].astype(b16)
            oq[2 * h + low, 64:128] = q_sum[64 * low : 64 * low + 64].astype(b16)
    oq_sent = [net.send(oq.at[lax.rem(z + d, 4)], oq_in.at[i], zs[i]) for i, d in enumerate((1, 3, 2))]
    m_ring.done()
    for d in range(1, 4):
        block = ALLM.at[lax.rem(x + d, 4) * 2 + c]
        net.send(block, block, twin)
    for copy in oq_sent + k_sent:
        net.got(copy)
    late_half = lambda chip, low: ALL.at[chip * 2 + c, pl.ds(pl.multiple_of(low * 192, 192), 192)]
    oq_sum = oq[z].astype(f32)
    for i in range(3):
        oq_sum = oq_sum + oq_in[i].astype(f32)
    half = pl.ds(pl.multiple_of(z_lo * 64, 64), 64)
    k_sum = k_mine[z_hi * 4 + y, half].astype(f32)
    for i in range(15):
        k_sum = k_sum + k_in[i].astype(f32)
    base = pl.multiple_of(z_lo * 192, 192)
    ALL[slot, pl.ds(base, 128)] = oq_sum.astype(b16)
    ALL[slot, pl.ds(pl.multiple_of(base + 128, 64), 64)] = k_sum.astype(b16)
    piece_here = late_half(x, z_lo)
    ends = [net.send(piece_here, piece_here, p) for p in xs + [dev(x, y, flip, c)] + others]
    net.send(piece_here, piece_here, twin)
    for copy in sz:
        net.got(copy)
    here = lanes(z_hi * 4 + y)
    SM[...] = s_z[0, :, here] + s_z[1, :, here] + s_z[2, :, here] + s_z[3, :, here]
    came = [(lax.rem(x + d, 4), z_lo) for d in (3, 1, 2)] + [(x, 1 - z_lo)]
    came += [(lax.rem(x + d, 4), 1 - z_lo) for d in (3, 1, 2)]
    for copy, (chip, low) in zip(ends, came):
        net.got(copy)
        block = late_half(chip, low)
        net.send(block, block, twin)
    for copy in kept:
        copy.wait()
    net.finish()


def back(*arrays):
    V = pltpu.VMEM
    wide = D + 128
    return pl.pallas_call(
        back_kernel,
        out_shape=(
            shape((2, 128, D), b16),
            shape((2, 128, D), f32),
            shape((8, 1152, 128), b16),
            shape((8, 384, 128), b16),
            shape((8, 128), f32),
        ),
        in_specs=[ANY] * 21,
        out_specs=(ANY, ANY, ANY, VMEM, VMEM),
        scratch_shapes=[
            V((ROWS, wide), f32),
            V((ROWS, D), f32),
            V((ROWS, wide), b16),
            V((ROWS, D), b16),
            V((16, D), b16),
            V((ROWS, 128), jnp.int32),
            V((ROWS, D), b16),
            V((ROWS, D), b16),
            V((D, D), b16),
            V((ROWS, D), b16),
            V((ROWS, D), b16),
            V((ROWS, D), b16),
            V((ROWS, D), b16),
            V((4, ROWS, D), b16),
            V((8, ROWS, 1536), b16),
            V((D, D), b16),
            V((D, D), b16),
            V((8, 1152, 128), b16),
            V((4, ROWS, D), b16),
            V((2, ROWS // 2, D), b16),
            V((2, ROWS, D), b16),
        ]
        + [
            V((4, ROWS, 128), b16),
            V((4, D, 128), b16),
            V((2, D // 2, 128), b16),
            V((2, D, 128), b16),
        ]
        * 3
        + [
            V((2, 4, ROWS, 512), b16),
            V((2, 2, ROWS // 2, 512), b16),
            V((2, 2, ROWS, 512), b16),
            V((ROWS, D), f32),
            V((ROWS, D), b16),
            V((ROWS, D), b16),
            V((ROWS, 2 * D), b16),
            V((ROWS, D), f32),
            V((128, D), b16),
            V((128, D), b16),
            V((ROWS, D), b16),
            V((ROWS, 128), f32),
            V((ROWS, 128), f32),
            V((2, 2, 576, 128), b16),
            V((2, 2, 1152, 128), b16),
            V((3, 576, 128), b16),
            V((8, 128, 128), b16),
            V((2, 3, 128, 128), b16),
            V((4, 256, 128), b16),
            V((3, 256, 128), b16),
            V((4, 128, 128), b16),
            V((3, 128, 128), b16),
            V((8, 128, 128), b16),
            V((15, 64, 128), b16),
            V((8, D), f32),
            V((8, D), f32),
            V((3, 8, D), f32),
            V((4, 8, D), f32),
            V((4, 8, D), f32),
        ]
        + sems(128, 40),
        compiler_params=params(3, 60),
        name="back",
    )(*arrays)


def rotary():
    freqs = np.float32(10000.0) ** (-np.arange(HD // 2, dtype=np.float32) * np.float32(2.0) / np.float32(HD))
    angles = np.arange(D, dtype=np.float32)[:, None] * freqs[None, :]
    cos, sin = np.cos(angles), np.sin(angles)
    return np.concatenate([cos] * 4, axis=1), np.concatenate([-sin, sin] * 2, axis=1)


def learning_rates():
    return (D ** (-0.5), 8.0 * D ** (-0.5), D ** (-0.5), 2.0 * FF ** (-0.5), 0.5 * D ** (-0.5), 0.5)


def adamw(weight, gradient, moment, square, step_rate, decay_rate):
    moment_new = beta_one * moment + (1.0 - beta_one) * gradient
    square_new = beta_two * square + (1.0 - beta_two) * gradient * gradient
    corrected = moment_new / (1.0 - beta_one**STEP)
    spread_by = jnp.sqrt(square_new / (1.0 - beta_two**STEP)) + adam_epsilon
    updated = weight - step_rate * (corrected / spread_by + decay_rate * weight)
    return [moment_new, square_new, updated]


def update_kernel(*refs):
    moe_i, late_i, out_i, gin_i, sums = refs[:5]
    ins, small_ins, outs, small_outs = refs[5:17], refs[17:23], refs[25:37], refs[37:43]
    moe, late, bufs, passing, sem = refs[43], refs[44], refs[45:57], refs[57:59], refs[59]
    rates = learning_rates()
    lane = lax.broadcasted_iota(jnp.int32, (128, 128), 1)
    count = 0

    def copy(src, dst):
        nonlocal count
        made = pltpu.make_async_copy(src, dst, sem.at[count])
        made.start()
        count += 1
        return made

    grads = [copy(moe_i, moe), copy(late_i, late)]
    every = slice(None)
    chunks = [(0, pl.ds(2 * b, 2)) for b in range(3)] + [(1, pl.ds(2 * b, 2)) for b in range(3)]
    chunks += [(2, (every, pl.ds(1024 * p, 1024))) for p in range(2)] + [(3, every)]
    loads = [
        [copy(ins[3 * n + i].at[at], bufs[3 * n + i].at[at]) for i in range(3)] for n, at in chunks
    ]
    through = [copy(src, dst) for src, dst in zip((out_i, gin_i), passing)]
    for n, (grad, rate, decay) in enumerate(
        (
            (sums[0:6, :], rates[4], 0.1),
            (jnp.concatenate([sums[7:8, :], sums[6:7, :]], axis=0), rates[5], 0.0),
        )
    ):
        w, m, v = (ref[...] for ref in small_ins[3 * n : 3 * n + 3])
        for ref, value in zip(small_outs[3 * n : 3 * n + 3], adamw(w, grad, m, v, rate, decay)):
            ref[...] = value
    for load in grads:
        load.wait()
    stores = []

    def apply(n, at, grad, rate):
        w, m, v = bufs[3 * n : 3 * n + 3]
        m[at], v[at], w[at] = adamw(w[at], grad, m[at], v[at], rate, 0.1)

    for step, (n, at) in enumerate(chunks):
        for load in loads[step]:
            load.wait()
        if n == 0:
            b = step

            def tiles(t, carry, b=b):
                for part in range(2):
                    rows = slice(128 * (3 * part + b), 128 * (3 * part + b) + 128)
                    one, two = moe[2 * t, rows].astype(f32), moe[2 * t + 1, rows].astype(f32)
                    cols = lanes(4 * part + t)
                    first = jnp.where(lane < SLICE, one, pltpu.roll(two, SLICE, 1))
                    second = jnp.where(lane < SLICE, pltpu.roll(one, SLICE, 1), two)
                    apply(0, (2 * b, every, cols), first, rates[2])
                    apply(0, (2 * b + 1, every, cols), second, rates[2])
                return carry

            lax.fori_loop(0, 4, tiles, 0)
        elif n == 1:
            b = step - 3

            def tiles(k, carry, b=b):
                for e in range(2):
                    row = 128 * (6 + b) + SLICE * e
                    grad = moe[k, row : row + SLICE].astype(f32)
                    apply(1, (2 * b + e, lanes(k, SLICE), every), grad, rates[3])
                return carry

            lax.fori_loop(0, 8, tiles, 0)
        else:
            part = step - 6
            row = 0 if n == 3 else 64 * (1 + part)

            def tiles(t, carry, n=n, part=part, row=row):
                cols = lanes(t if n == 3 else 8 * part + t)
                for h in range(2):
                    grad = late[t, 192 * h + row : 192 * h + row + 64].astype(f32)
                    apply(n, (pl.ds(64 * h, 64), cols), grad, rates[1 if n == 3 else 0])
                return carry

            lax.fori_loop(0, 8, tiles, 0)
        if step == 1:
            for load, src, dst in zip(through, passing, refs[23:25]):
                load.wait()
                stores.append(copy(src, dst))
        for i, j in ((1, 0), (2, 1), (0, 2)):
            stores.append(copy(bufs[3 * n + i].at[at], outs[3 * n + j].at[at]))
    for store in stores:
        store.wait()


def update(*arrays):
    V = pltpu.VMEM
    dims = [(EXPERTS, 128, D), (EXPERTS, FF, 128), (128, 2 * D), (128, D)]
    return pl.pallas_call(
        update_kernel,
        out_shape=(shape((2, 128, D), b16), shape((2, 128, D), f32))
        + tuple(shape(d, f32) for d in dims + [(EXPERTS, 128), (2, 128)] for _ in range(3)),
        in_specs=[ANY] * 4 + [VMEM] + [ANY] * 12 + [VMEM] * 6,
        out_specs=(ANY,) * 14 + (VMEM,) * 6,
        scratch_shapes=[V((8, 1152, 128), b16), V((8, 384, 128), b16)]
        + [V(d, f32) for d in dims for _ in range(3)]
        + [V((2, 128, D), b16), V((2, 128, D), f32), pltpu.SemaphoreType.DMA((64,))],
        compiler_params=params(),
        name="update",
    )(*arrays)


def on_device(
    tokens, segments, routes, cotangent, w_qkv, w_out, w_gateup, w_down, w_router, w_gains,
    qkv_first, qkv_second, out_first, out_second, gateup_first, gateup_second, down_first, down_second,
    router_first, router_second, gains_first, gains_second,
):
    cos, sin = (jnp.asarray(table) for table in rotary())
    X, R, g, WQ, WKV, WO, TL, act_one, q, KV, probs, heads, hidden, act, total, grads, PO, y_tmp, y_got = front(
        tokens, cotangent, routes, w_qkv, w_out, w_gateup, w_down, cos, sin, w_router.T, w_gains, segments
    )
    layer_out, input_grad, ALLM, late, SM = back(
        total, hidden, act, g, TL, R, heads, WO, X, act_one, q, KV, probs, WQ, WKV,
        grads, PO, y_tmp, y_got, cos, sin,
    )
    done = update(
        ALLM, late, layer_out, input_grad, SM, w_gateup, gateup_first, gateup_second, w_down, down_first, down_second,
        w_qkv, qkv_first, qkv_second, w_out, out_first, out_second,
        w_router.T, router_first.T, router_second.T, w_gains, gains_first, gains_second,
    )
    router = [array.T for array in done[14:17]]
    return (*done[:2], *done[8:11], *done[11:14], *done[2:5], *done[5:8], *router, *done[17:20])


def solution(mesh):
    weight = [P("grp", None), P("grp", None), P(None, "grp", None), P(None, None, "grp"), P("grp", None), P(None, "grp")]
    tokens = P("rep", "grp", None)
    moments = [spec for spec in weight for _ in range(2)]
    results = [spec for spec in weight for _ in range(3)]
    return jax.shard_map(
        on_device,
        mesh=mesh,
        in_specs=(tokens, P("rep", None), tokens, tokens, *weight, *moments),
        out_specs=(tokens, tokens, *results),
        check_vma=False,
    )
```
